32 devices in a mesh: dp: 8 (over y, x, core), tensor: 4 (over z).
Axes of the slice: x: 2, y: 2, z: 4, core: 2. Of those that a mesh axis runs over, the one named last changes fastest.
Arguments:
- tokens: bfloat16 [8192, 768], P(('dp', 'tensor')), may hold values from -6 to 6
- memory: bfloat16 [16, 2048, 768], P('dp', 'tensor'), may hold values from -6 to 6
- table_lengths: int32 [8, 8], P('dp'), may hold values from 1 to 512, 1024 in all within a row
- table_plots: int32 [8, 8], P('dp'), may hold values from 0 to 1
- self_gain: float32 [768], replicated, may hold values from 0.25 to 1.75
- self_query: bfloat16 [768, 768], P(None, 'tensor'), may hold values from -0.21875 to 0.21875
- self_key: bfloat16 [768, 768], P(None, 'tensor'), may hold values from -0.21875 to 0.21875
- self_value: bfloat16 [768, 768], P(None, 'tensor'), may hold values from -0.21875 to 0.21875
- self_output: bfloat16 [768, 768], P('tensor'), may hold values from -0.875 to 0.875
- cross_gain: float32 [768], replicated, may hold values from 0.25 to 1.75
- cross_query: bfloat16 [768, 768], P(None, 'tensor'), may hold values from -0.21875 to 0.21875
- cross_key: bfloat16 [768, 768], P(None, 'tensor'), may hold values from -0.21875 to 0.21875
- cross_value: bfloat16 [768, 768], P(None, 'tensor'), may hold values from -0.21875 to 0.21875
- cross_output: bfloat16 [768, 768], P('tensor'), may hold values from -1.75 to 1.75
- hidden_gain: float32 [768], replicated, may hold values from 0.25 to 1.75
- hidden_gate: bfloat16 [768, 2048], P(None, 'tensor'), may hold values from -0.21875 to 0.21875
- hidden_up: bfloat16 [768, 2048], P(None, 'tensor'), may hold values from -0.21875 to 0.21875
- hidden_down: bfloat16 [2048, 768], P('tensor'), may hold values from -0.1875 to 0.1875
- cotangent: bfloat16 [8192, 768], P(('dp', 'tensor')), may hold values from -6 to 6
Outputs:
- output: bfloat16 [8192, 768], P(('dp', 'tensor'))
- grad_tokens: bfloat16 [8192, 768], P(('dp', 'tensor'))
- grad_memory: bfloat16 [16, 2048, 768], P('dp', 'tensor')
- grad_self_query: float32 [768, 768], P(None, 'tensor')
- grad_self_key: float32 [768, 768], P(None, 'tensor')
- grad_self_value: float32 [768, 768], P(None, 'tensor')
- grad_self_output: float32 [768, 768], P('tensor')
- grad_cross_query: float32 [768, 768], P(None, 'tensor')
- grad_cross_key: float32 [768, 768], P(None, 'tensor')
- grad_cross_value: float32 [768, 768], P(None, 'tensor')
- grad_cross_output: float32 [768, 768], P('tensor')
- grad_hidden_gate: float32 [768, 2048], P(None, 'tensor')
- grad_hidden_up: float32 [768, 2048], P(None, 'tensor')
- grad_hidden_down: float32 [2048, 768], P('tensor')
- grad_self_gain: float32 [768], replicated
- grad_cross_gain: float32 [768], replicated
- grad_hidden_gain: float32 [768], replicated
The draws below stay inside these ranges and needn't reach their ends.
Inputs may be any that keep to these rules, and one draw needn't show every extreme that they name: `table_lengths`: each row sums to 1024, and its largest entry is exactly 512. `table_plots`: entry t of row i names the plot, among the 2 plots of data index i, that table t of that index reads.
All inputs are finite; a program needn't handle non-finite values.
Results may differ from the reference program's by a relative error of at most 0.023.
Values may be sent and summed in bfloat16 or wider, within the bound.
A program may use at most 192 MiB of HBM per device.

```python
import math
import jax
import jax.numpy as jnp
import numpy as np
from jax import lax

D = 768
HEADS = 12
HD = 64
FF = 2048
MEM = 2048
TOK_DEV = 1024
TABLES_DEV = 8
PLOTS_DEV = 2
MOST_LEN = 512
TOKENS = 8192
PLOTS = 16
N_DP = 8


def with_ends(array, stream_key, least, top_value):
    shape = array.shape
    place = [jax.random.randint(jax.random.fold_in(stream_key, axis), (), 0, shape[axis]) for axis in range(len(shape))]
    array = array.at[tuple(place)].set(least)
    longest = shape.index(max(shape))
    place[longest] = (place[longest] + 1) % shape[longest]
    return array.at[tuple(place)].set(top_value)


def level_of(key, dims, shards, smallest, largest):
    factor_of, own = 1.0, jax.random.fold_in(key, 6)
    for position, shards_of in shards:
        heights = jnp.exp(jax.random.uniform(jax.random.fold_in(own, position), (shards_of,), jnp.float32, smallest / len(shards), largest / len(shards)))
        factor_of = factor_of * jnp.repeat(heights, dims[position] // shards_of).reshape([-1 if axis == position else 1 for axis in range(len(dims))])
    return factor_of


def length_profile(amount, total, bound, lean):
    portions = [(1 << 20) // math.isqrt(grade ** lean) + 1 for grade in range(2, amount + 1)]
    spare, counts = total - bound - (amount - 1), [1] * (amount - 1)
    while spare > 0:
        candidates = [i for i in range(amount - 1) if counts[i] < bound]
        whole, remaining = sum([portions[i] for i in candidates]), spare
        for i in candidates:
            more = min(bound - counts[i], max(1, remaining * portions[i] // whole), spare)
            counts[i] = counts[i] + more
            spare = spare - more
    return np.array([bound] + counts)


def ragged_sizes(stream_key, number_of, total, most, lean):
    if number_of == 2:
        one = jax.random.randint(stream_key, (), max(1, total - most), min(most, total - 1) + 1)
        return jnp.stack([one, total - one])
    tallies = jnp.asarray(length_profile(number_of, total, most, lean), jnp.int32)
    couples = (number_of - 1) // 2
    donor, sink = tallies[1:1 + 2 * couples:2], tallies[2:2 + 2 * couples:2]
    margin = jnp.minimum(donor - 1, most - sink)
    shifted = jax.random.randint(jax.random.fold_in(stream_key, 1), (couples,), 0, 1 << 20) % (margin + 1)
    tallies = tallies.at[1:1 + 2 * couples:2].set(donor - shifted).at[2:2 + 2 * couples:2].set(sink + shifted)
    return tallies[jax.random.permutation(jax.random.fold_in(stream_key, 2), number_of)]


def bell_draw(own_key, extent, scale, limit, split=(), held_as=jnp.bfloat16):
    result = jax.random.normal(own_key, extent, jnp.float32) * scale
    if len(split) > 0:
        result = level_of(own_key, extent, split, -0.22, 0.18) * result
    return jnp.clip(result, min=-limit, max=limit).astype(held_as)


def setup_inputs(seed: int = 0) -> dict:
    arg_keys = jax.random.split(jax.random.key(seed), 20)
    tokens = bell_draw(arg_keys[0], (TOKENS, D), 1.0, 6.0, ((0, 32),))
    memory = bell_draw(arg_keys[1], (PLOTS, MEM, D), 1.0, 6.0, ((0, 8), (1, 4)))
    table_lengths = jax.vmap(lambda own: ragged_sizes(own, TABLES_DEV, TOK_DEV, MOST_LEN, 2))(jax.random.split(arg_keys[2], N_DP)).reshape((N_DP, TABLES_DEV)).astype(jnp.int32)
    table_plots = with_ends(jax.random.randint(arg_keys[3], (N_DP, TABLES_DEV), 0, PLOTS_DEV), jax.random.fold_in(arg_keys[3], 1), 0, PLOTS_DEV - 1).astype(jnp.int32)
    self_gain = jnp.clip(1.0 + 0.15 * jax.random.normal(arg_keys[4], (D,), jnp.float32), 0.25, 1.75)
    self_query = bell_draw(arg_keys[5], (D, HEADS * HD), D ** -0.5, 0.21875, ((1, 4),))
    self_key = bell_draw(arg_keys[6], (D, HEADS * HD), D ** -0.5, 0.21875, ((1, 4),))
    self_value = bell_draw(arg_keys[7], (D, HEADS * HD), D ** -0.5, 0.21875, ((1, 4),))
    self_output = bell_draw(arg_keys[8], (HEADS * HD, D), (HEADS * HD // 16) ** -0.5, 0.875, ((0, 4),))
    cross_gain = jnp.clip(1.0 + 0.15 * jax.random.normal(arg_keys[9], (D,), jnp.float32), 0.25, 1.75)
    cross_query = bell_draw(arg_keys[10], (D, HEADS * HD), D ** -0.5, 0.21875, ((1, 4),))
    cross_key = bell_draw(arg_keys[11], (D, HEADS * HD), D ** -0.5, 0.21875, ((1, 4),))
    cross_value = bell_draw(arg_keys[12], (D, HEADS * HD), D ** -0.5, 0.21875, ((1, 4),))
    cross_output = bell_draw(arg_keys[13], (HEADS * HD, D), (HEADS * HD // 64) ** -0.5, 1.75, ((0, 4),))
    hidden_gain = jnp.clip(1.0 + 0.15 * jax.random.normal(arg_keys[14], (D,), jnp.float32), 0.25, 1.75)
    hidden_gate = bell_draw(arg_keys[15], (D, FF), D ** -0.5, 0.21875, ((1, 4),))
    hidden_up = bell_draw(arg_keys[16], (D, FF), D ** -0.5, 0.21875, ((1, 4),))
    hidden_down = bell_draw(arg_keys[17], (FF, D), (FF // 2) ** -0.5, 0.1875, ((0, 4),))
    cotangent = bell_draw(arg_keys[18], (TOKENS, D), 1.0, 6.0, ((0, 32),))
    return {"tokens": tokens, "memory": memory, "table_lengths": table_lengths, "table_plots": table_plots, "self_gain": self_gain, "self_query": self_query, "self_key": self_key, "self_value": self_value, "self_output": self_output, "cross_gain": cross_gain, "cross_query": cross_query, "cross_key": cross_key, "cross_value": cross_value, "cross_output": cross_output, "hidden_gain": hidden_gain, "hidden_gate": hidden_gate, "hidden_up": hidden_up, "hidden_down": hidden_down, "cotangent": cotangent}


@jax.custom_vjp
def low(v):
    return lax.optimization_barrier(v.astype(jnp.bfloat16)).astype(jnp.float32)

@jax.custom_vjp
def low_back(v):
    return v

def low_keep(v):
    return (low(v), None)

def low_pass(kept, grad):
    return (grad,)

def back_keep(v):
    return (v, None)

def back_low(kept, grad):
    return (low(grad),)
low.defvjp(low_keep, low_pass)
low_back.defvjp(back_keep, back_low)
epsilon = 1e-06
masked_value = -1e+30
highest = lax.Precision.HIGHEST

def norm_rows(activation, gain_vec):
    return activation * lax.rsqrt(lax.optimization_barrier(jnp.mean(activation * activation, axis=-1, keepdims=True)) + epsilon) * gain_vec

def project(activation, matrix):
    return jnp.dot(activation, matrix, precision=highest)

def by_heads(matrix):
    return matrix.reshape(matrix.shape[0], HEADS, HD).transpose(1, 0, 2)

def head_attend(query_head, key_head, value_head, allowed):
    scores = low_back(jnp.dot(query_head, key_head.T, precision=highest) * HD ** (-0.5))
    chances = jax.nn.softmax(jnp.where(allowed, scores, masked_value), axis=-1)
    return jnp.dot(low(chances), value_head, precision=highest)

def attend(queries, keys_all, values_all, allowed):

    def per_head(triple):
        return head_attend(triple[0], triple[1], triple[2], allowed)
    blended = lax.map(jax.checkpoint(per_head), (by_heads(queries), by_heads(keys_all), by_heads(values_all)))
    return blended.transpose(1, 0, 2).reshape(queries.shape[0], HEADS * HD)

def gated_unit(gate_in, up_in):
    return jax.nn.gelu(gate_in, approximate=True) * up_in

def layer_group(group_tokens, group_memory, lengths_row, plots_row, weights):
    self_gain, self_query, self_key, self_value, self_output, cross_gain, cross_query, cross_key, cross_value, cross_output, hidden_gain, hidden_gate, hidden_up, hidden_down = weights
    positions = jnp.arange(TOK_DEV, dtype=jnp.int32)
    table_ends = jnp.cumsum(lengths_row).astype(jnp.int32)
    table_of = lax.optimization_barrier(jnp.sum((positions[:, None] >= table_ends[None, :]).astype(jnp.int32), axis=1)).astype(jnp.int32)
    plot_of = plots_row[table_of]
    self_allowed = (table_of[:, None] == table_of[None, :]) & (positions[None, :] <= positions[:, None])
    key_plot = jnp.arange(PLOTS_DEV * MEM, dtype=jnp.int32) // MEM
    cross_allowed = plot_of[:, None] == key_plot[None, :]
    normed_self = low(norm_rows(group_tokens, self_gain))
    self_q = low(low_back(project(normed_self, self_query)))
    self_k = low(low_back(project(normed_self, self_key)))
    self_v = low(low_back(project(normed_self, self_value)))
    self_mix = low(low_back(attend(self_q, self_k, self_v, self_allowed)))
    first_sum = group_tokens + low_back(project(self_mix, self_output))
    normed_cross = low(norm_rows(first_sum, cross_gain))
    memory_flat = group_memory.reshape(PLOTS_DEV * MEM, D)
    cross_q = low(low_back(project(normed_cross, cross_query)))
    cross_k = low(low_back(project(memory_flat, cross_key)))
    cross_v = low(low_back(project(memory_flat, cross_value)))
    cross_mix = low(low_back(attend(cross_q, cross_k, cross_v, cross_allowed)))
    second_sum = first_sum + low_back(project(cross_mix, cross_output))
    normed_hidden = low(norm_rows(second_sum, hidden_gain))
    gate_pre = low_back(project(normed_hidden, hidden_gate))
    up_pre = low_back(project(normed_hidden, hidden_up))
    hidden_act = low(low_back(gated_unit(gate_pre, up_pre)))
    return second_sum + low_back(project(hidden_act, hidden_down))

def reference(tokens, memory, table_lengths, table_plots, self_gain, self_query, self_key, self_value, self_output, cross_gain, cross_query, cross_key, cross_value, cross_output, hidden_gain, hidden_gate, hidden_up, hidden_down, cotangent):
    weights = tuple((matrix.astype(jnp.float32) for matrix in (self_gain, self_query, self_key, self_value, self_output, cross_gain, cross_query, cross_key, cross_value, cross_output, hidden_gain, hidden_gate, hidden_up, hidden_down)))
    token_groups = tokens.astype(jnp.float32).reshape(N_DP, TOK_DEV, D)
    memory_groups = memory.astype(jnp.float32).reshape(N_DP, PLOTS_DEV, MEM, D)

    def forward(token_in, memory_in, weight_in):

        def group_step(state_in, group_data):
            result_rows = jax.checkpoint(layer_group)(group_data[0], group_data[1], group_data[2], group_data[3], weight_in)
            return (state_in, result_rows)
        _, result_groups = lax.scan(group_step, None, (token_in, memory_in, table_lengths, table_plots))
        return result_groups
    results, pullback = jax.vjp(forward, token_groups, memory_groups, weights)
    token_back, memory_back, weight_back = pullback(cotangent.astype(jnp.float32).reshape(N_DP, TOK_DEV, D))
    return (results.reshape(TOKENS, D).astype(jnp.bfloat16), token_back.reshape(TOKENS, D).astype(jnp.bfloat16), memory_back.reshape(PLOTS, MEM, D).astype(jnp.bfloat16), weight_back[1], weight_back[2], weight_back[3], weight_back[4], weight_back[6], weight_back[7], weight_back[8], weight_back[9], weight_back[11], weight_back[12], weight_back[13], weight_back[0], weight_back[5], weight_back[10])
```

```python
import functools

import jax
import jax.numpy as jnp
from jax import lax
from jax.experimental import pallas as pl
from jax.experimental.pallas import tpu as pltpu
from jax.sharding import PartitionSpec as P

HD = 64
LONGEST = 512
F32 = jnp.float32
BF16 = jnp.bfloat16
MESH = pl.DeviceIdType.MESH
ANY = pl.BlockSpec(memory_space=pl.ANY)
VMEM = pl.BlockSpec(memory_space=pltpu.VMEM)
DMA = pltpu.SemaphoreType.DMA

epsilon = 1e-06
masked_value = -1e30


def norm_rows(activation, gain_vec):
    return (
        activation
        * lax.rsqrt(jnp.mean(activation * activation, axis=-1, keepdims=True) + epsilon)
        * gain_vec
    )


def norm_back(activation, gain_vec, cotan_rows):
    _, pullback = jax.vjp(norm_rows, activation, gain_vec)
    return pullback(cotan_rows)


def gated_unit(gate_in, up_in):
    return jax.nn.gelu(gate_in, approximate=True) * up_in


def product(first_op, second_op, first_dim, second_dim):
    return lax.dot_general(
        first_op,
        second_op,
        (((first_dim,), (second_dim,)), ((), ())),
        preferred_element_type=F32,
    )


def remote(src, dst, send_sem, recv_sem, device):
    return pltpu.make_async_remote_copy(
        src_ref=src,
        dst_ref=dst,
        send_sem=send_sem,
        recv_sem=recv_sem,
        device_id=device,
        device_id_type=MESH,
    )


def place():
    dp = lax.axis_index("dp")
    z = lax.axis_index("tensor")
    return dp, z, lax.rem(dp, 2), lax.rem(dp // 2, 2), lax.rem(dp // 4, 2)


def flipped(dp, bit):
    here = lax.rem(dp // (1 << bit), 2)
    return dp + (1 << bit) * (1 - 2 * here)


def greet(devices):
    barrier = pltpu.get_barrier_semaphore()
    for device in devices:
        pl.semaphore_signal(barrier, inc=1, device_id=device, device_id_type=MESH)
    pl.semaphore_wait(barrier, len(devices))


def greet_line(dp, z, n):
    barrier = pltpu.get_barrier_semaphore()

    @pl.when(z > 0)
    def _():
        pl.semaphore_signal(barrier, inc=1, device_id=(dp, z - 1), device_id_type=MESH)

    @pl.when(z < n - 1)
    def _():
        pl.semaphore_signal(barrier, inc=1, device_id=(dp, z + 1), device_id_type=MESH)

    inner = (z > 0) & (z < n - 1)

    @pl.when(inner)
    def _():
        pl.semaphore_wait(barrier, 2)

    @pl.when(jnp.logical_not(inner))
    def _():
        pl.semaphore_wait(barrier, 1)


def gather_kernel(n, count, tok_ref, *refs):
    mine = refs[:count]
    full = refs[count : 2 * count]
    halo = refs[2 * count]
    zs, zr, s2s, s2r, s3s, s3r, s4s, s4r, hs, hr, loc = refs[2 * count + 1 :]
    dp, z, c, x, y = place()
    others = [lax.rem(z + k, n) for k in range(1, n)]
    greet([(dp, o) for o in others] + [(flipped(dp, bit), z) for bit in range(3)])
    last_halo = halo.shape[0] - 1

    own_halo = pltpu.make_async_copy(tok_ref, halo.at[last_halo], loc.at[count])
    own_halo.start()
    locals_ = []
    for g in range(count):
        copy = pltpu.make_async_copy(mine[g], full[g].at[z], loc.at[g])
        copy.start()
        locals_.append(copy)

    def halo_copy(i):
        src = tok_ref if i == 0 else halo.at[last_halo - i]
        return remote(
            src, halo.at[last_halo - 1 - i], hs.at[i], hr.at[i], (dp, lax.rem(z + 1, n))
        )

    @pl.when(z < n - 1)
    def _():
        halo_copy(0).start()

    def s1(g, k):
        return remote(
            mine[g].at[y, x, c],
            full[g].at[z, y, x, c],
            zs.at[g, k - 1],
            zr.at[g, k - 1],
            (dp, lax.rem(z + k, n)),
        )

    def s1_in(g, k):
        zk = lax.rem(z + n - k, n)
        return remote(
            mine[g].at[y, x, c],
            full[g].at[zk, y, x, c],
            zs.at[g, k - 1],
            zr.at[g, k - 1],
            (dp, lax.rem(z + k, n)),
        )

    def s2(g, k, incoming=False):
        zk = lax.rem(z + n - k, n)
        if k % 2 == 0:
            there = full[g].at[zk, y, 1 - x if incoming else x, c]
            dev = (flipped(dp, 1), z)
        else:
            there = full[g].at[zk, 1 - y if incoming else y, x, c]
            dev = (flipped(dp, 2), z)
        return remote(there, there, s2s.at[g, k - 1], s2r.at[g, k - 1], dev)

    def s3(g, k, incoming=False):
        zk = lax.rem(z + n - k, n)
        if k % 2 == 0:
            there = full[g].at[zk, 1 - y if incoming else y, :, c]
            dev = (flipped(dp, 2), z)
        else:
            there = full[g].at[zk, :, 1 - x if incoming else x, c]
            dev = (flipped(dp, 1), z)
        return remote(there, there, s3s.at[g, k - 1], s3r.at[g, k - 1], dev)

    def s4(g, k, incoming=False):
        zk = lax.rem(z + n - k, n)
        there = full[g].at[zk, :, :, 1 - c if incoming else c]
        return remote(there, there, s4s.at[g, k - 1], s4r.at[g, k - 1], (flipped(dp, 0), z))

    ks = range(1, n)
    for g in range(min(2, count)):
        for k in ks:
            s1(g, k).start()
    for i in range(last_halo):

        @pl.when(z > i)
        def _(i=i):
            halo_copy(i).wait_recv()

        if i + 1 < last_halo:

            @pl.when((z > i) & (z < n - 1))
            def _(i=i):
                halo_copy(i + 1).start()

    for t in range(count + 2):
        if t + 2 < count:
            for k in ks:
                s1(t + 2, k).start()
        if t < count:
            for k in ks:
                s1_in(t, k).wait_recv()
                s2(t, k).start()
        g = t - 1
        if 0 <= g < count:
            for k in ks:
                s2(g, k, True).wait_recv()
                s3(g, k).start()
        g = t - 2
        if 0 <= g < count:
            for k in ks:
                s3(g, k, True).wait_recv()
                s4(g, k).start()
    for g in range(count):
        for k in ks:
            s4(g, k, True).wait_recv()
    for g in range(count):
        for k in ks:
            s1(g, k).wait_send()
            s2(g, k).wait_send()
            s3(g, k).wait_send()
            s4(g, k).wait_send()
        locals_[g].wait()
    own_halo.wait()
    for i in range(last_halo):

        @pl.when((z >= i) & (z < n - 1))
        def _(i=i):
            halo_copy(i).wait_send()


def gather_all(n, tokens, shards, halo_chunks):
    count = len(shards)
    out_shape = [jax.ShapeDtypeStruct((n,) + s.shape, s.dtype) for s in shards]
    out_shape.append(jax.ShapeDtypeStruct((halo_chunks + 1,) + tokens.shape, tokens.dtype))
    sems = [DMA((count, n - 1)) for _ in range(8)] + [
        DMA((halo_chunks,)),
        DMA((halo_chunks,)),
        DMA((count + 1,)),
    ]
    out = pl.pallas_call(
        functools.partial(gather_kernel, n, count),
        out_shape=out_shape,
        in_specs=[ANY] * (count + 1),
        out_specs=[ANY] * (count + 1),
        scratch_shapes=sems,
        compiler_params=pltpu.CompilerParams(collective_id=0, has_side_effects=True),
        name="gather_weights",
    )(tokens, *shards)
    return out[:-1], out[-1]


def reduce_kernel(n, count, extra, *refs):
    part = refs[:count]
    gains, csend = refs[count : count + 2]
    fin = refs[count + 2 : 2 * count + 2]
    gain_out, crecv = refs[2 * count + 2 : 2 * count + 4]
    rest = refs[2 * count + 4 :]
    acc = rest[:count]
    rec1 = rest[count : 2 * count]
    rec2 = rest[2 * count : 3 * count]
    rec3 = rest[3 * count : 4 * count]
    rec4 = rest[4 * count : 5 * count]
    (
        recx,
        grec,
        s1s, s1r, s2s, s2r, s3s, s3r, s4s, s4r, xs, xr, a1s, a1r, a2s, a2r, a3s, a3r, gs, gr, hs, hr, loc,
    ) = rest[5 * count :]
    dp, z, c, x, y = place()
    tn_bits = n.bit_length() - 1
    others = [lax.rem(z + k, n) for k in range(1, n)]
    greet(
        [(dp, o) for o in others] + [(flipped(dp, bit), z) for bit in range(3 + extra)]
    )
    halo_chunks = csend.shape[0]

    def halo_copy(i):
        far = halo_chunks - i
        return remote(
            csend.at[i], crecv.at[i], hs.at[i], hr.at[i], (dp, lax.rem(z + n - far, n))
        )

    for i in range(halo_chunks):

        @pl.when(z >= halo_chunks - i)
        def _(i=i):
            halo_copy(i).start()

    def r1(g):
        return remote(
            part[g].at[:, :, :, 1 - c], rec1[g], s1s.at[g], s1r.at[g], (flipped(dp, 0), z)
        )

    def own(g):
        return pltpu.make_async_copy(part[g].at[:, :, :, c], acc[g], loc.at[g])

    def r2(g):
        if g % 2 == 0:
            src, bit = acc[g].at[:, :, 1 - x], 1
        else:
            src, bit = acc[g].at[:, 1 - y], 2
        return remote(src, rec2[g], s2s.at[g], s2r.at[g], (flipped(dp, bit), z))

    def r3(g):
        bit = 2 if g % 2 == 0 else 1
        src = acc[g].at[:, 1 - y, x] if g % 2 == 0 else acc[g].at[:, y, 1 - x]
        return remote(src, rec3[g], s3s.at[g], s3r.at[g], (flipped(dp, bit), z))

    def r4(g, k):
        zk = lax.rem(z + k, n)
        return remote(
            acc[g].at[zk, y, x], rec4[g].at[k - 1], s4s.at[g, k - 1], s4r.at[g, k - 1], (dp, zk)
        )

    def rx(g, e):
        return remote(
            fin[g].at[y, x, c],
            recx.at[g, e, pl.ds(0, fin[g].shape[3])],
            xs.at[g, e],
            xr.at[g, e],
            (flipped(dp, 3 + e), z),
        )

    def a1(g, incoming=False):
        if g % 2 == 0:
            there, bit = fin[g].at[1 - y if incoming else y, x, c], 2
        else:
            there, bit = fin[g].at[y, 1 - x if incoming else x, c], 1
        return remote(there, there, a1s.at[g], a1r.at[g], (flipped(dp, bit), z))

    def a2(g, incoming=False):
        if g % 2 == 0:
            there, bit = fin[g].at[:, 1 - x if incoming else x, c], 1
        else:
            there, bit = fin[g].at[1 - y if incoming else y, :, c], 2
        return remote(there, there, a2s.at[g], a2r.at[g], (flipped(dp, bit), z))

    def a3(g, incoming=False):
        there = fin[g].at[:, :, 1 - c if incoming else c]
        return remote(there, there, a3s.at[g], a3r.at[g], (flipped(dp, 0), z))

    for g in range(count):
        r1(g).start()
        own(g).start()

    def add1(g):
        def step(i, carry):
            zz, yy, xx = i // 4, lax.rem(i // 2, 2), lax.rem(i, 2)
            total = acc[g][zz, yy, xx].astype(F32) + rec1[g][zz, yy, xx].astype(F32)
            acc[g][zz, yy, xx] = total.astype(BF16)
            return carry

        lax.fori_loop(0, 4 * n, step, 0)

    def add2(g):
        def step(i, carry):
            zz, aa = i // 2, lax.rem(i, 2)
            yy, xx = (aa, x) if g % 2 == 0 else (y, aa)
            total = acc[g][zz, yy, xx].astype(F32) + rec2[g][zz, aa].astype(F32)
            acc[g][zz, yy, xx] = total.astype(BF16)
            return carry

        lax.fori_loop(0, 2 * n, step, 0)

    def add3(g):
        def step(zz, carry):
            total = acc[g][zz, y, x].astype(F32) + rec3[g][zz].astype(F32)
            acc[g][zz, y, x] = total.astype(BF16)
            return carry

        lax.fori_loop(0, n, step, 0)

    def add4(g):
        total = acc[g][z, y, x].astype(F32)
        for k in range(1, n):
            total = total + rec4[g][k - 1].astype(F32)
        fin[g][y, x, c] = total.astype(BF16)

    gain_out[...] = gains[...]
    gain_peers = [(flipped(dp, bit), z) for bit in range(3 + extra)]
    for bit in range(tn_bits):
        here = lax.rem(z // (1 << bit), 2)
        gain_peers.append((dp, z + (1 << bit) * (1 - 2 * here)))
    rounds = len(gain_peers)

    def gain_copy(i):
        src = gains if i == 0 else grec.at[2 * i]
        return remote(src, grec.at[2 * i + 1], gs.at[i], gr.at[i], gain_peers[i])

    def gain_round(i):
        gain_copy(i).wait_recv()
        gain_out[...] = gain_out[...] + grec[2 * i + 1]
        if i + 1 < rounds:
            grec[2 * i + 2] = gain_out[...]
            gain_copy(i + 1).start()

    gain_copy(0).start()

    stages = 8
    for t in range(count + stages):
        g = t
        if g < count:
            own(g).wait()
            r1(g).wait_recv()
            add1(g)
            r2(g).start()
        g = t - 1
        if 0 <= g < count:
            r2(g).wait_recv()
            add2(g)
            r3(g).start()
        g = t - 2
        if 0 <= g < count:
            r3(g).wait_recv()
            add3(g)
            for k in range(1, n):
                r4(g, k).start()
        g = t - 3
        if 0 <= g < count:
            for k in range(1, n):
                r4(g, k).wait_recv()
            add4(g)
            for e in range(extra):
                rx(g, e).start()
                rx(g, e).wait()
                rows = fin[g].shape[3]
                total = fin[g][y, x, c].astype(F32) + recx[g, e, :rows].astype(F32)
                fin[g][y, x, c] = total.astype(BF16)
            a1(g).start()
        g = t - 4
        if 0 <= g < count:
            a1(g, True).wait_recv()
            a2(g).start()
        g = t - 5
        if 0 <= g < count:
            a2(g, True).wait_recv()
            a3(g).start()
        g = t - 6
        if 0 <= g < count:
            a3(g, True).wait_recv()
        if t < rounds:
            gain_round(t)
    for i in range(halo_chunks):

        @pl.when(z + halo_chunks - i < n)
        def _(i=i):
            halo_copy(i).wait_recv()

        @pl.when(z >= halo_chunks - i)
        def _(i=i):
            halo_copy(i).wait_send()

    for i in range(rounds):
        gain_copy(i).wait_send()
    for g in range(count):
        r1(g).wait_send()
        r2(g).wait_send()
        r3(g).wait_send()
        for k in range(1, n):
            r4(g, k).wait_send()
        a1(g).wait_send()
        a2(g).wait_send()
        a3(g).wait_send()


def reduce_all(n, extra, partials, gains, csend):
    count = len(partials)
    width = partials[0].shape[-1]
    rows = [p.shape[-2] for p in partials]
    tn_bits = n.bit_length() - 1
    rounds = 3 + extra + tn_bits
    out_shape = [jax.ShapeDtypeStruct((2, 2, 2, r, width), BF16) for r in rows]
    out_shape += [
        jax.ShapeDtypeStruct(gains.shape, F32),
        jax.ShapeDtypeStruct(csend.shape, csend.dtype),
    ]
    scratch = (
        [pltpu.VMEM((n, 2, 2, r, width), BF16) for r in rows]
        + [pltpu.VMEM((n, 2, 2, r, width), BF16) for r in rows]
        + [pltpu.VMEM((n, 2, r, width), BF16) for r in rows]
        + [pltpu.VMEM((n, r, width), BF16) for r in rows]
        + [pltpu.VMEM((n - 1, r, width), BF16) for r in rows]
    )
    spare = max(extra, 1)
    scratch += [
        pltpu.VMEM((count, extra, max(rows), width) if extra else (1, 1, 16, 128), BF16),
        pltpu.VMEM((2 * rounds,) + gains.shape, F32),
    ]
    for _ in range(3):
        scratch += [DMA((count,)), DMA((count,))]
    scratch += [DMA((count, n - 1)), DMA((count, n - 1))]
    scratch += [DMA((count, spare)), DMA((count, spare))]
    for _ in range(3):
        scratch += [DMA((count,)), DMA((count,))]
    scratch += [DMA((rounds,)), DMA((rounds,))]
    scratch += [DMA((csend.shape[0],)), DMA((csend.shape[0],))]
    scratch += [DMA((count,))]
    out = pl.pallas_call(
        functools.partial(reduce_kernel, n, count, extra),
        out_shape=out_shape,
        in_specs=[ANY] * count + [VMEM, ANY],
        out_specs=[VMEM] * count + [VMEM, ANY],
        scratch_shapes=scratch,
        compiler_params=pltpu.CompilerParams(
            collective_id=1, has_side_effects=True, vmem_limit_bytes=60 << 20
        ),
        name="reduce_gradients",
    )(*partials, gains, csend)
    return out[:count], out[count], out[count + 1]


def both_plots(rows, plot_row):
    wide = rows.astype(F32)
    zero = jnp.zeros_like(wide)
    return jnp.concatenate(
        [jnp.where(plot_row == 0, wide, zero), jnp.where(plot_row == 0, zero, wide)], axis=0
    ).astype(BF16)


def own_plot(pair, plot_row):
    half = pair.shape[0] // 2
    return jnp.where(plot_row == 0, pair[:half], pair[half:])


def line_exchange(n, parts, z, dp, refs, compute, merge, finish):
    own, spread, mine, from_right, from_left, sems = refs
    ups, upr, dns, dnr, rls, rlr, rrs, rrr = sems

    def up(j, p, i, start):
        src = own[i].at[p] if start else spread[i].at[j, p]
        return remote(
            src, spread[i].at[j, p], ups.at[i, j, p], upr.at[i, j, p], (dp, lax.rem(z + 1, n))
        )

    def down(j, p, i, start):
        src = own[i].at[p] if start else spread[i].at[j, p]
        return remote(
            src,
            spread[i].at[j, p],
            dns.at[i, j, p],
            dnr.at[i, j, p],
            (dp, lax.rem(z + n - 1, n)),
        )

    def back_left(j, p, i):
        return remote(
            mine[i].at[j, p],
            from_right[i].at[j, p],
            rls.at[i, j, p],
            rlr.at[i, j, p],
            (dp, lax.rem(z + n - 1, n)),
        )

    def back_right(j, p, i):
        return remote(
            mine[i].at[j, p],
            from_left[i].at[j, p],
            rrs.at[i, j, p],
            rrr.at[i, j, p],
            (dp, lax.rem(z + 1, n)),
        )

    out_kinds = range(len(own))
    back_kinds = range(len(mine))

    def send_own(p, carry):
        for i in out_kinds:

            @pl.when(z < n - 1)
            def _():
                up(z, p, i, True).start()

            @pl.when(z > 0)
            def _():
                down(z, p, i, True).start()

        return carry

    lax.fori_loop(0, parts, send_own, 0)

    def first(p, carry):
        for i in out_kinds:
            spread[i][z, p] = own[i][p]
        compute(z, p)
        return carry

    lax.fori_loop(0, parts, first, 0)

    def tick(t, carry):
        def one_part(p, inner):
            low = z - t
            high = z + t

            @pl.when((t < n) & (low >= 0))
            def _():
                for i in out_kinds:
                    up(low, p, i, False).wait_recv()

                    @pl.when(z < n - 1)
                    def _():
                        up(low, p, i, False).start()

                compute(low, p)

                @pl.when(z == n - 1)
                def _():
                    for i in back_kinds:
                        back_left(low, p, i).start()

            @pl.when((t < n) & (high < n))
            def _():
                for i in out_kinds:
                    down(high, p, i, False).wait_recv()

                    @pl.when(z > 0)
                    def _():
                        down(high, p, i, False).start()

                compute(high, p)

                @pl.when(z == 0)
                def _():
                    for i in back_kinds:
                        back_right(high, p, i).start()

            left_chunk = 2 * (n - 1) - z - t

            @pl.when((left_chunk >= 0) & (left_chunk < z) & (z < n - 1))
            def _():
                for i in back_kinds:
                    back_left(left_chunk, p, i).wait_recv()
                merge(left_chunk, p, from_right)
                for i in back_kinds:
                    back_left(left_chunk, p, i).start()

            right_chunk = t - z

            @pl.when((right_chunk < n) & (right_chunk > z) & (z > 0))
            def _():
                for i in back_kinds:
                    back_right(right_chunk, p, i).wait_recv()
                merge(right_chunk, p, from_left)
                for i in back_kinds:
                    back_right(right_chunk, p, i).start()

            return inner

        lax.fori_loop(0, parts, one_part, 0)
        return carry

    lax.fori_loop(1, 2 * n - 2, tick, 0)

    def last(p, carry):
        @pl.when(z > 0)
        def _():
            for i in back_kinds:
                back_right(z, p, i).wait_recv()
            merge(z, p, from_left)

        @pl.when(z < n - 1)
        def _():
            for i in back_kinds:
                back_left(z, p, i).wait_recv()
            merge(z, p, from_right)

        finish(p)
        return carry

    lax.fori_loop(0, parts, last, 0)

    def drain(p, carry):
        for j in range(n):
            for i in out_kinds:

                @pl.when((z < n - 1) & (z == j))
                def _(i=i, j=j):
                    up(j, p, i, True).wait_send()

                @pl.when((z < n - 1) & (z > j))
                def _(i=i, j=j):
                    up(j, p, i, False).wait_send()

                @pl.when((z > 0) & (z == j))
                def _(i=i, j=j):
                    down(j, p, i, True).wait_send()

                @pl.when((z > 0) & (z < j))
                def _(i=i, j=j):
                    down(j, p, i, False).wait_send()

            for i in back_kinds:

                @pl.when(z > j)
                def _(i=i, j=j):
                    back_left(j, p, i).wait_send()

                @pl.when(z < j)
                def _(i=i, j=j):
                    back_right(j, p, i).wait_send()

        return carry

    lax.fori_loop(0, parts, drain, 0)


def line_sems(n, parts, out_kinds, back_kinds):
    return [DMA((out_kinds, n, parts))] * 4 + [DMA((back_kinds, n, parts))] * 4


def cross_forward_kernel(
    n, parts, heads_part, plots, q_ref, k_ref, v_ref, q_all, o_ref, l_ref,
    o_mine, l_mine, o_right, l_right, o_left, l_left, *sems
):
    dp, z = lax.axis_index("dp"), lax.axis_index("tensor")
    greet_line(dp, z, n)

    def compute(j, p):
        plot_row = plots[j]
        for hh in range(heads_part):
            h = p * heads_part + hh
            q_pair = both_plots(q_all[j, p, hh * HD : (hh + 1) * HD, :], plot_row)
            scores = jnp.dot(k_ref[h], q_pair, preferred_element_type=F32)
            top = jnp.max(scores, axis=0, keepdims=True)
            powers = jnp.exp(scores - top)
            total = jnp.sum(powers, axis=0, keepdims=True)
            mixed = jnp.dot(v_ref[h], powers.astype(BF16), preferred_element_type=F32)
            mixed = own_plot(mixed, plot_row) / total
            o_mine[j, p, hh * HD : (hh + 1) * HD, :] = mixed.astype(BF16)
            l_mine[j, p, hh : hh + 1, :] = top + jnp.log(total)

    def merge(j, p, arrived):
        for hh in range(heads_part):
            rows = slice(hh * HD, (hh + 1) * HD)
            log_a = l_mine[j, p, hh : hh + 1, :]
            log_b = arrived[1][j, p, hh : hh + 1, :]
            top = jnp.maximum(log_a, log_b)
            share_a = jnp.exp(log_a - top)
            share_b = jnp.exp(log_b - top)
            total = share_a + share_b
            mixed = (
                o_mine[j, p, rows, :].astype(F32) * (share_a / total)
                + arrived[0][j, p, rows, :].astype(F32) * (share_b / total)
            )
            o_mine[j, p, rows, :] = mixed.astype(BF16)
            l_mine[j, p, hh : hh + 1, :] = top + jnp.log(total)

    def finish(p):
        o_ref[p] = o_mine[z, p]
        l_ref[p] = l_mine[z, p]

    refs = ([q_ref], [q_all], [o_mine, l_mine], [o_right, l_right], [o_left, l_left], sems)
    line_exchange(n, parts, z, dp, refs, compute, merge, finish)


def cross_forward(n, parts, plots, q, k, v):
    rows, width = q.shape[1], q.shape[2]
    heads_part = rows // HD
    wide = jax.ShapeDtypeStruct((n, parts, rows, width), BF16)
    scratch = []
    for _ in range(3):
        scratch += [
            pltpu.VMEM((n, parts, rows, width), BF16),
            pltpu.VMEM((n, parts, 8, width), F32),
        ]
    scratch += line_sems(n, parts, 1, 2)
    return pl.pallas_call(
        functools.partial(cross_forward_kernel, n, parts, heads_part),
        out_shape=[
            wide,
            jax.ShapeDtypeStruct((parts, rows, width), BF16),
            jax.ShapeDtypeStruct((parts, 8, width), F32),
        ],
        in_specs=[VMEM] * 4,
        out_specs=[VMEM] * 3,
        scratch_shapes=scratch,
        compiler_params=pltpu.CompilerParams(
            collective_id=2, has_side_effects=True, vmem_limit_bytes=48 << 20
        ),
        name="cross_forward",
    )(plots, q, k, v)


def cross_backward_kernel(
    n, parts, heads_part, plots, do_ref, st_ref, q_all, k_ref, kt_ref, v_ref,
    dq_ref, dk_ref, dv_ref,
    do_all, st_all, q_mine, q_right, q_left, *sems
):
    dp, z = lax.axis_index("dp"), lax.axis_index("tensor")
    greet_line(dp, z, n)
    scale = HD ** (-0.5)

    def clear(h, carry):
        dk_ref[h] = jnp.zeros(dk_ref.shape[1:], F32)
        dv_ref[h] = jnp.zeros(dv_ref.shape[1:], F32)
        return carry

    lax.fori_loop(0, dk_ref.shape[0], clear, 0)

    def compute(j, p):
        plot_row = plots[j]
        for hh in range(heads_part):
            h = p * heads_part + hh
            rows = slice(hh * HD, (hh + 1) * HD)
            q_pair = both_plots(q_all[j, p, rows, :], plot_row)
            do_pair = both_plots(do_all[j, p, rows, :], plot_row)
            scores = jnp.dot(k_ref[h], q_pair, preferred_element_type=F32)
            chances = jnp.exp(scores - st_all[j, p, hh : hh + 1, :])
            prob_back = jnp.dot(v_ref[h], do_pair, preferred_element_type=F32)
            inner = st_all[j, p, heads_part + hh : heads_part + hh + 1, :]
            score_back = (chances * (prob_back - inner)).astype(BF16)
            q_back = jnp.dot(kt_ref[h], score_back, preferred_element_type=F32)
            q_mine[j, p, rows, :] = (own_plot(q_back, plot_row) * scale).astype(BF16)
            dk_ref[h] += product(score_back, q_pair, 1, 1)
            dv_ref[h] += product(chances.astype(BF16), do_pair, 1, 1)

    def merge(j, p, arrived):
        total = q_mine[j, p].astype(F32) + arrived[0][j, p].astype(F32)
        q_mine[j, p] = total.astype(BF16)

    def finish(p):
        dq_ref[p] = q_mine[z, p]

    refs = ([do_ref, st_ref], [do_all, st_all], [q_mine], [q_right], [q_left], sems)
    line_exchange(n, parts, z, dp, refs, compute, merge, finish)


def cross_backward(n, parts, plots, do, stats, q_all, k, kt, v):
    rows, width = do.shape[1], do.shape[2]
    heads_part = rows // HD
    scratch = [
        pltpu.VMEM((n, parts, rows, width), BF16),
        pltpu.VMEM((n, parts, 8, width), F32),
        pltpu.VMEM((n, parts, rows, width), BF16),
        pltpu.VMEM((n, parts, rows, width), BF16),
        pltpu.VMEM((n, parts, rows, width), BF16),
    ]
    scratch += line_sems(n, parts, 2, 1)
    return pl.pallas_call(
        functools.partial(cross_backward_kernel, n, parts, heads_part),
        out_shape=[
            jax.ShapeDtypeStruct(do.shape, BF16),
            jax.ShapeDtypeStruct(k.shape, F32),
            jax.ShapeDtypeStruct(v.shape, F32),
        ],
        in_specs=[VMEM] * 7,
        out_specs=[VMEM] * 3,
        scratch_shapes=scratch,
        compiler_params=pltpu.CompilerParams(
            collective_id=3, has_side_effects=True, vmem_limit_bytes=56 << 20
        ),
        name="cross_backward",
    )(plots, do, stats, q_all, k, kt, v)


def alone(rows, which):
    zero = jnp.zeros_like(rows)
    return jnp.concatenate([rows, zero] if which == 0 else [zero, rows], axis=0)


def self_forward_kernel(bias_ref, q_ref, k_ref, vt_ref, o_ref, l_ref):
    for which in range(2):
        rows = slice(which * HD, (which + 1) * HD)
        scores = jnp.dot(
            k_ref[...], alone(q_ref[rows, :], which), preferred_element_type=F32
        )
        scores = scores + bias_ref[...]
        top = jnp.max(scores, axis=0, keepdims=True)
        powers = jnp.exp(scores - top)
        total = jnp.sum(powers, axis=0, keepdims=True)
        mixed = jnp.dot(vt_ref[rows, :], powers.astype(BF16), preferred_element_type=F32)
        o_ref[rows, :] = (mixed / total).astype(BF16)
        l_ref[0, which : which + 1, :] = top + jnp.log(total)


def self_forward(bias, q, k, vt):
    width, rows = q.shape
    keys = k.shape[0]
    pairs = width // (2 * HD)
    return pl.pallas_call(
        self_forward_kernel,
        grid=(pairs,),
        out_shape=[
            jax.ShapeDtypeStruct((width, rows), BF16),
            jax.ShapeDtypeStruct((pairs, 8, rows), F32),
        ],
        in_specs=[
            pl.BlockSpec((keys, rows), lambda i: (0, 0)),
            pl.BlockSpec((2 * HD, rows), lambda i: (i, 0)),
            pl.BlockSpec((keys, 2 * HD), lambda i: (0, i)),
            pl.BlockSpec((2 * HD, keys), lambda i: (i, 0)),
        ],
        out_specs=[
            pl.BlockSpec((2 * HD, rows), lambda i: (i, 0)),
            pl.BlockSpec((1, 8, rows), lambda i: (i, 0, 0)),
        ],
        compiler_params=pltpu.CompilerParams(vmem_limit_bytes=32 << 20),
        name="self_forward",
    )(bias, q, k, vt)


def self_backward_kernel(
    bias_ref, q_ref, k_ref, kt_ref, v_ref, do_ref, st_ref, dq_ref, dk_ref, dv_ref
):
    scale = HD ** (-0.5)
    dk, dv = 0.0, 0.0
    for which in range(2):
        rows = slice(which * HD, (which + 1) * HD)
        q_pair = alone(q_ref[rows, :], which)
        do_pair = alone(do_ref[rows, :], which)
        scores = jnp.dot(k_ref[...], q_pair, preferred_element_type=F32)
        chances = jnp.exp(scores + bias_ref[...] - st_ref[0, which : which + 1, :])
        prob_back = jnp.dot(v_ref[...], do_pair, preferred_element_type=F32)
        score_back = (chances * (prob_back - st_ref[0, 2 + which : 3 + which, :])).astype(BF16)
        q_back = jnp.dot(kt_ref[rows, :], score_back, preferred_element_type=F32)
        dq_ref[rows, :] = (q_back * scale).astype(BF16)
        dk = dk + product(score_back, q_pair, 1, 1)
        dv = dv + product(chances.astype(BF16), do_pair, 1, 1)
    dk_ref[...] = dk.astype(BF16)
    dv_ref[...] = dv.astype(BF16)


def self_backward(bias, q, k, kt, v, do, stats):
    width, rows = q.shape
    keys = k.shape[0]
    pairs = width // (2 * HD)
    tall = pl.BlockSpec((keys, 2 * HD), lambda i: (0, i))
    flat = pl.BlockSpec((2 * HD, rows), lambda i: (i, 0))
    return pl.pallas_call(
        self_backward_kernel,
        grid=(pairs,),
        out_shape=[
            jax.ShapeDtypeStruct((width, rows), BF16),
            jax.ShapeDtypeStruct((keys, width), BF16),
            jax.ShapeDtypeStruct((keys, width), BF16),
        ],
        in_specs=[
            pl.BlockSpec((keys, rows), lambda i: (0, 0)),
            flat,
            tall,
            pl.BlockSpec((2 * HD, keys), lambda i: (i, 0)),
            tall,
            flat,
            pl.BlockSpec((1, 8, rows), lambda i: (i, 0, 0)),
        ],
        out_specs=[flat, tall, tall],
        compiler_params=pltpu.CompilerParams(vmem_limit_bytes=32 << 20),
        name="self_backward",
    )(bias, q, k, kt, v, do, stats)


def body(
    tokens, memory, table_lengths, table_plots,
    self_gain, self_query, self_key, self_value, self_output,
    cross_gain, cross_query, cross_key, cross_value, cross_output,
    hidden_gain, hidden_gate, hidden_up, hidden_down, cotangent,
):
    n = lax.axis_size("tensor")
    dp_size = lax.axis_size("dp")
    extra = dp_size.bit_length() - 1 - 3
    z = lax.axis_index("tensor")
    rows, width = tokens.shape
    plots, patches, _ = memory.shape
    heads = width // HD
    parts = n
    heads_part = heads // parts
    halo_chunks = -(-(LONGEST - 1) // rows)
    halo_rows = halo_chunks * rows
    keys = halo_rows + rows

    def group(*mats):
        flat = mats[0] if len(mats) == 1 else jnp.concatenate(mats, axis=0)
        return flat.reshape(2, 2, 2, -1, width)

    shards = [
        group(self_query.T, self_key.T),
        group(self_value.T, self_output),
        group(cross_key.T, cross_value.T),
        group(cross_query.T, cross_output),
        group(hidden_gate.T),
        group(hidden_up.T),
        group(hidden_down),
    ]
    full, halo = gather_all(n, tokens, shards, halo_chunks)

    def unit(g, index, of):
        return full[g].reshape(n, of, -1, width)[:, index].reshape(-1, width)

    w_sq, w_sk, w_sv, w_so = unit(0, 0, 2), unit(0, 1, 2), unit(1, 0, 2), unit(1, 1, 2)
    w_ck, w_cv, w_cq, w_co = unit(2, 0, 2), unit(2, 1, 2), unit(3, 0, 2), unit(3, 1, 2)
    w_gate, w_up, w_down = unit(4, 0, 1), unit(5, 0, 1), unit(6, 0, 1)

    group_tokens = rows * n
    positions = jnp.arange(group_tokens, dtype=jnp.int32)
    table_ends = jnp.cumsum(table_lengths[0])
    table_ids = jnp.sum((positions[:, None] >= table_ends[None, :]).astype(jnp.int32), axis=1)
    table_index = jnp.arange(table_ends.shape[0], dtype=jnp.int32)
    token_plot = jnp.sum(
        jnp.where(table_ids[:, None] == table_index[None, :], table_plots[0][None, :], 0), axis=1
    )
    padded = jnp.concatenate([jnp.full((halo_rows,), -1, jnp.int32), table_ids])
    key_tables = lax.dynamic_slice_in_dim(padded, z * rows, keys)
    query_tables = key_tables[halo_rows:]
    key_at = jnp.arange(keys, dtype=jnp.int32)
    allowed = (key_tables[:, None] == query_tables[None, :]) & (
        key_at[:, None] <= halo_rows + jnp.arange(rows, dtype=jnp.int32)[None, :]
    )
    bias = jnp.where(allowed, 0.0, masked_value).astype(F32)
    plot_rows = token_plot.reshape(n, 1, rows)

    present = (jnp.arange(halo_chunks + 1, dtype=jnp.int32) + z >= halo_chunks)[:, None, None]
    near = jnp.where(present, halo, 0).astype(F32).reshape(keys, width)
    inputs = tokens.astype(F32)
    scale = HD ** (-0.5)
    normed_near = norm_rows(near, self_gain).astype(BF16)
    normed_self = normed_near[halo_rows:]
    self_q = (product(w_sq, normed_self, 1, 1).astype(BF16) * scale).astype(BF16)
    self_k = product(normed_near, w_sk, 1, 1).astype(BF16)
    self_kt = product(w_sk, normed_near, 1, 1).astype(BF16)
    self_v = product(normed_near, w_sv, 1, 1).astype(BF16)
    self_vt = product(w_sv, normed_near, 1, 1).astype(BF16)
    self_mix, self_logs = self_forward(bias, self_q, self_k, self_vt)
    first_sum = inputs + product(self_mix, w_so, 0, 0)

    normed_cross = norm_rows(first_sum, cross_gain).astype(BF16)
    cross_q = (product(w_cq, normed_cross, 1, 1).astype(BF16) * scale).astype(BF16)
    cross_q = cross_q.reshape(parts, heads_part * HD, rows)
    flat_memory = memory.reshape(plots * patches, width)

    def by_head(projected):
        tall = projected.reshape(plots, patches, heads, HD)
        return tall.transpose(2, 1, 0, 3).reshape(heads, patches, plots * HD)

    def by_head_flat(projected):
        wide = projected.reshape(heads, HD, plots, patches)
        return wide.transpose(0, 2, 1, 3).reshape(heads, plots * HD, patches)

    cross_k = by_head(product(flat_memory, w_ck, 1, 1).astype(BF16))
    cross_kt = by_head_flat(product(w_ck, flat_memory, 1, 1).astype(BF16))
    cross_v = by_head(product(flat_memory, w_cv, 1, 1).astype(BF16))
    cross_vt = by_head_flat(product(w_cv, flat_memory, 1, 1).astype(BF16))
    q_all, cross_mix, cross_logs = cross_forward(n, parts, plot_rows, cross_q, cross_k, cross_vt)
    cross_mix = cross_mix.reshape(width, rows)
    second_sum = first_sum + product(cross_mix, w_co, 0, 0)

    normed_hidden = norm_rows(second_sum, hidden_gain).astype(BF16)
    gate_pre = product(normed_hidden, w_gate, 1, 1)
    up_pre = product(normed_hidden, w_up, 1, 1)
    hidden_act = gated_unit(gate_pre, up_pre).astype(BF16)
    output = (second_sum + product(hidden_act, w_down, 1, 0)).astype(BF16)
    grad_down = product(hidden_act, cotangent, 0, 0).astype(BF16)
    grad_act = product(cotangent, w_down, 1, 1).astype(BF16).astype(F32)
    _, gated_pull = jax.vjp(gated_unit, gate_pre, up_pre)
    gate_back, up_back = gated_pull(grad_act)
    gate_back = gate_back.astype(BF16)
    up_back = up_back.astype(BF16)
    grad_gate = product(gate_back, normed_hidden, 0, 0).astype(BF16)
    grad_up = product(up_back, normed_hidden, 0, 0).astype(BF16)
    normed_back = product(gate_back, w_gate, 1, 0) + product(up_back, w_up, 1, 0)
    residual_back, gain_back_hidden = norm_back(second_sum, hidden_gain, normed_back)
    second_back = cotangent.astype(F32) + residual_back

    grad_rows = second_back.astype(BF16)
    grad_co = product(cross_mix, grad_rows, 1, 0).astype(BF16)
    mixed_back = product(w_co, grad_rows, 1, 1).astype(BF16)

    def stats_of(logs, mixed, back, per):
        inner = jnp.sum(
            (mixed.astype(F32) * back.astype(F32)).reshape(heads // per, per, HD, rows), axis=2
        )
        rest = jnp.zeros((heads // per, 8 - 2 * per, rows), F32)
        return jnp.concatenate([logs[:, :per], inner, rest], axis=1)

    cross_stats = stats_of(cross_logs, cross_mix, mixed_back, heads_part)
    query_back, key_back, value_back = cross_backward(
        n, parts, plot_rows, mixed_back.reshape(parts, heads_part * HD, rows), cross_stats,
        q_all, cross_k, cross_kt, cross_v,
    )
    query_back = query_back.reshape(width, rows)

    def by_patch(back):
        tall = back.astype(BF16).reshape(heads, patches, plots, HD)
        return tall.transpose(2, 1, 0, 3).reshape(plots * patches, width)

    key_back = by_patch(key_back)
    value_back = by_patch(value_back)
    grad_cq = product(query_back, normed_cross, 1, 0).astype(BF16)
    grad_ck = product(key_back, flat_memory, 0, 0).astype(BF16)
    grad_cv = product(value_back, flat_memory, 0, 0).astype(BF16)
    grad_memory = (product(key_back, w_ck, 1, 0) + product(value_back, w_cv, 1, 0)).astype(BF16)
    residual_back, gain_back_cross = norm_back(
        first_sum, cross_gain, product(query_back, w_cq, 0, 0)
    )
    first_back = second_back + residual_back

    grad_rows = first_back.astype(BF16)
    grad_so = product(self_mix, grad_rows, 1, 0).astype(BF16)
    mixed_back = product(w_so, grad_rows, 1, 1).astype(BF16)
    self_stats = stats_of(self_logs, self_mix, mixed_back, 2)
    query_back, key_back, value_back = self_backward(
        bias, self_q, self_k, self_kt, self_v, mixed_back, self_stats
    )
    grad_sq = product(query_back, normed_self, 1, 0).astype(BF16)
    grad_sk = product(key_back, normed_near, 0, 0).astype(BF16)
    grad_sv = product(value_back, normed_near, 0, 0).astype(BF16)
    near_back = product(key_back, w_sk, 1, 0) + product(value_back, w_sv, 1, 0)
    own_back = near_back[halo_rows:] + product(query_back, w_sq, 0, 0)
    near_back = jnp.concatenate([near_back[:halo_rows], own_back], axis=0)
    near_unit = near * lax.rsqrt(jnp.mean(near * near, axis=-1, keepdims=True) + epsilon)
    gain_back_self = jnp.sum(near_back * near_unit, axis=0)

    def split(*grads):
        stacked = [g.reshape(n, -1, width) for g in grads]
        flat = stacked[0] if len(stacked) == 1 else jnp.concatenate(stacked, axis=1)
        return flat.reshape(n, 2, 2, 2, -1, width)

    partials = [
        split(grad_gate),
        split(grad_up),
        split(grad_down),
        split(grad_cq, grad_co),
        split(grad_ck, grad_cv),
        split(grad_so, grad_sv),
        split(grad_sq, grad_sk),
    ]
    gains = jnp.concatenate(
        [
            jnp.stack([gain_back_self, gain_back_cross, gain_back_hidden]),
            jnp.zeros((5, width), F32),
        ]
    )
    sent_back = near_back[:halo_rows].astype(BF16).reshape(halo_chunks, rows, width)
    summed, gains, came_back = reduce_all(n, extra, partials, gains, sent_back)
    far = halo_chunks - jnp.arange(halo_chunks, dtype=jnp.int32)
    came_back = jnp.where((z + far < n)[:, None, None], came_back, 0).astype(F32)
    normed_back = own_back + jnp.sum(came_back, axis=0)
    residual_back, _ = norm_back(inputs, self_gain, normed_back)
    grad_tokens = (first_back + residual_back).astype(BF16)

    def pair(g):
        both = summed[g].reshape(2, -1, width).astype(F32)
        return both[0], both[1]

    g_gate, g_up, g_down = (summed[g].reshape(-1, width).astype(F32) for g in range(3))
    g_cq, g_co = pair(3)
    g_ck, g_cv = pair(4)
    g_so, g_sv = pair(5)
    g_sq, g_sk = pair(6)
    return (
        output, grad_tokens, grad_memory.reshape(memory.shape),
        g_sq.T, g_sk.T, g_sv.T, g_so,
        g_cq.T, g_ck.T, g_cv.T, g_co,
        g_gate.T, g_up.T, g_down,
        gains[0], gains[1], gains[2],
    )


def solution(mesh):
    in_specs = (
        P(("dp", "tensor"), None),
        P("dp", "tensor", None),
        P("dp", None),
        P("dp", None),
        P(),
        P(None, "tensor"),
        P(None, "tensor"),
        P(None, "tensor"),
        P("tensor", None),
        P(),
        P(None, "tensor"),
        P(None, "tensor"),
        P(None, "tensor"),
        P("tensor", None),
        P(),
        P(None, "tensor"),
        P(None, "tensor"),
        P("tensor", None),
        P(("dp", "tensor"), None),
    )
    out_specs = (
        P(("dp", "tensor"), None),
        P(("dp", "tensor"), None),
        P("dp", "tensor", None),
        P(None, "tensor"),
        P(None, "tensor"),
        P(None, "tensor"),
        P("tensor", None),
        P(None, "tensor"),
        P(None, "tensor"),
        P(None, "tensor"),
        P("tensor", None),
        P(None, "tensor"),
        P(None, "tensor"),
        P("tensor", None),
        P(),
        P(),
        P(),
    )
    return jax.shard_map(body, mesh=mesh, in_specs=in_specs, out_specs=out_specs, check_vma=False)
```

```python
import functools

import jax
import jax.numpy as jnp
from jax import lax
from jax.experimental import pallas as pl
from jax.experimental.pallas import tpu as pltpu
from jax.sharding import PartitionSpec as P

HD = 64
LONGEST = 512
F32 = jnp.float32
BF16 = jnp.bfloat16
MESH = pl.DeviceIdType.MESH
ANY = pl.BlockSpec(memory_space=pl.ANY)
VMEM = pl.BlockSpec(memory_space=pltpu.VMEM)
DMA = pltpu.SemaphoreType.DMA

epsilon = 1e-06
masked_value = -1e30


def norm_rows(activation, gain_vec):
    return (
        activation
        * lax.rsqrt(jnp.mean(activation * activation, axis=-1, keepdims=True) + epsilon)
        * gain_vec
    )


def norm_back(activation, gain_vec, cotan_rows):
    _, pullback = jax.vjp(norm_rows, activation, gain_vec)
    return pullback(cotan_rows)


def gated_unit(gate_in, up_in):
    return jax.nn.gelu(gate_in, approximate=True) * up_in


def product(first_op, second_op, first_dim, second_dim):
    return lax.dot_general(
        first_op,
        second_op,
        (((first_dim,), (second_dim,)), ((), ())),
        preferred_element_type=F32,
    )


def remote(src, dst, send_sem, recv_sem, device):
    return pltpu.make_async_remote_copy(
        src_ref=src,
        dst_ref=dst,
        send_sem=send_sem,
        recv_sem=recv_sem,
        device_id=device,
        device_id_type=MESH,
    )


def place():
    dp = lax.axis_index("dp")
    z = lax.axis_index("tensor")
    return dp, z, lax.rem(dp, 2), lax.rem(dp // 2, 2), lax.rem(dp // 4, 2)


def flipped(dp, bit):
    here = lax.rem(dp // (1 << bit), 2)
    return dp + (1 << bit) * (1 - 2 * here)


def greet(devices):
    barrier = pltpu.get_barrier_semaphore()
    for device in devices:
        pl.semaphore_signal(barrier, inc=1, device_id=device, device_id_type=MESH)
    pl.semaphore_wait(barrier, len(devices))


def greet_line(dp, z, n):
    barrier = pltpu.get_barrier_semaphore()

    @pl.when(z > 0)
    def _():
        pl.semaphore_signal(barrier, inc=1, device_id=(dp, z - 1), device_id_type=MESH)

    @pl.when(z < n - 1)
    def _():
        pl.semaphore_signal(barrier, inc=1, device_id=(dp, z + 1), device_id_type=MESH)

    inner = (z > 0) & (z < n - 1)

    @pl.when(inner)
    def _():
        pl.semaphore_wait(barrier, 2)

    @pl.when(jnp.logical_not(inner))
    def _():
        pl.semaphore_wait(barrier, 1)


class Gather:
    def __init__(self, n, mine, full, sems):
        self.n, self.mine, self.full, self.count = n, mine, full, len(mine)
        self.zs, self.zr, self.as_, self.ar, self.bs, self.br, self.cs, self.cr, self.loc = sems
        self.dp, self.z, self.c, self.x, self.y = place()
        self.ks = range(1, n)

    def peers(self):
        others = [lax.rem(self.z + k, self.n) for k in self.ks]
        return [(self.dp, o) for o in others] + [(flipped(self.dp, b), self.z) for b in range(3)]

    def own(self, g):
        return pltpu.make_async_copy(self.mine[g], self.full[g].at[self.z], self.loc.at[g])

    def first(self, g, k, incoming=False):
        here = lax.rem(self.z + self.n - k, self.n) if incoming else self.z
        return remote(
            self.mine[g].at[self.y, self.x, self.c],
            self.full[g].at[here, self.y, self.x, self.c],
            self.zs.at[g, k - 1],
            self.zr.at[g, k - 1],
            (self.dp, lax.rem(self.z + k, self.n)),
        )

    def second(self, g, k, incoming=False):
        zk = lax.rem(self.z + self.n - k, self.n)
        x, y, c = self.x, self.y, self.c
        if k % 2 == 0:
            there, bit = self.full[g].at[zk, y, 1 - x if incoming else x, c], 1
        else:
            there, bit = self.full[g].at[zk, 1 - y if incoming else y, x, c], 2
        dev = (flipped(self.dp, bit), self.z)
        return remote(there, there, self.as_.at[g, k - 1], self.ar.at[g, k - 1], dev)

    def third(self, g, k, incoming=False):
        zk = lax.rem(self.z + self.n - k, self.n)
        x, y, c = self.x, self.y, self.c
        if k % 2 == 0:
            there, bit = self.full[g].at[zk, 1 - y if incoming else y, :, c], 2
        else:
            there, bit = self.full[g].at[zk, :, 1 - x if incoming else x, c], 1
        dev = (flipped(self.dp, bit), self.z)
        return remote(there, there, self.bs.at[g, k - 1], self.br.at[g, k - 1], dev)

    def fourth(self, g, k, incoming=False):
        zk = lax.rem(self.z + self.n - k, self.n)
        there = self.full[g].at[zk, :, :, 1 - self.c if incoming else self.c]
        dev = (flipped(self.dp, 0), self.z)
        return remote(there, there, self.cs.at[g, k - 1], self.cr.at[g, k - 1], dev)

    def begin(self, ahead):
        self.ahead = ahead
        for g in range(self.count):
            self.own(g).start()
        for g in range(min(ahead, self.count)):
            for k in self.ks:
                self.first(g, k).start()

    def pump(self, t):
        if t + self.ahead < self.count:
            for k in self.ks:
                self.first(t + self.ahead, k).start()
        if t < self.count:
            for k in self.ks:
                self.first(t, k, True).wait_recv()
                self.second(t, k).start()
        if 0 <= t - 1 < self.count:
            for k in self.ks:
                self.second(t - 1, k, True).wait_recv()
                self.third(t - 1, k).start()
        if 0 <= t - 2 < self.count:
            for k in self.ks:
                self.third(t - 2, k, True).wait_recv()
                self.fourth(t - 2, k).start()

    def ready(self, g):
        self.own(g).wait()
        for k in self.ks:
            self.fourth(g, k, True).wait_recv()

    def drain(self):
        for g in range(self.count):
            for k in self.ks:
                self.first(g, k).wait_send()
                self.second(g, k).wait_send()
                self.third(g, k).wait_send()
                self.fourth(g, k).wait_send()


def gather_sems(n, count):
    return [DMA((count, n - 1)) for _ in range(8)] + [DMA((count,))]


class Reduce:
    def __init__(self, n, extra, part, acc, rec1, rec2, rec3, rec4, fin, recx, sems):
        self.n, self.extra, self.count = n, extra, len(part)
        self.part, self.fin, self.recx = part, fin, recx
        self.rec1, self.rec2, self.rec3, self.rec4 = rec1, rec2, rec3, rec4
        self.sems = sems
        self.dp, self.z, self.c, self.x, self.y = place()
        self.ks = range(1, n)
        self.kept = acc
        self.acc = [
            part[g].at[:, :, :, self.c] if acc[g] is None else acc[g] for g in range(self.count)
        ]

    def peers(self):
        others = [lax.rem(self.z + k, self.n) for k in self.ks]
        bits = range(3 + self.extra)
        return [(self.dp, o) for o in others] + [(flipped(self.dp, b), self.z) for b in bits]

    def copy(self, stage, g, k=0, incoming=False):
        dp, z, c, x, y = self.dp, self.z, self.c, self.x, self.y
        even = g % 2 == 0
        acc, fin = self.acc[g], self.fin[g]
        if stage == 0:
            src, dst, dev = self.part[g].at[:, :, :, 1 - c], self.rec1[g], (flipped(dp, 0), z)
        elif stage == 1:
            src = acc.at[:, :, 1 - x] if even else acc.at[:, 1 - y]
            dst, dev = self.rec2[g], (flipped(dp, 1 if even else 2), z)
        elif stage == 2:
            src = acc.at[:, 1 - y, x] if even else acc.at[:, y, 1 - x]
            dst, dev = self.rec3[g], (flipped(dp, 2 if even else 1), z)
        elif stage == 3:
            zk = lax.rem(z + k, self.n)
            src, dst, dev = acc.at[zk, y, x], self.rec4[g].at[k - 1], (dp, zk)
        elif stage == 4:
            if even:
                src = fin.at[1 - y if incoming else y, x, c]
            else:
                src = fin.at[y, 1 - x if incoming else x, c]
            dst, dev = src, (flipped(dp, 2 if even else 1), z)
        elif stage == 5:
            if even:
                src = fin.at[:, 1 - x if incoming else x, c]
            else:
                src = fin.at[1 - y if incoming else y, :, c]
            dst, dev = src, (flipped(dp, 1 if even else 2), z)
        else:
            src = fin.at[:, :, 1 - c if incoming else c]
            dst, dev = src, (flipped(dp, 0), z)
        slot = stage if stage < 3 else stage + k - 1 if stage == 3 else stage + self.n - 2
        return remote(src, dst, self.sems[0].at[g, slot], self.sems[1].at[g, slot], dev)

    def own(self, g):
        src = self.part[g].at[:, :, :, self.c]
        return pltpu.make_async_copy(src, self.acc[g], self.sems[4].at[g])

    def further(self, g, e):
        rows = self.fin[g].shape[3]
        return remote(
            self.fin[g].at[self.y, self.x, self.c],
            self.recx.at[g, e, pl.ds(0, rows)],
            self.sems[2].at[g, e],
            self.sems[3].at[g, e],
            (flipped(self.dp, 3 + e), self.z),
        )

    def add(self, stage, g):
        n, x, y, c, z = self.n, self.x, self.y, self.c, self.z
        even = g % 2 == 0
        acc, fin = self.acc[g], self.fin[g]
        if stage == 1:

            def step(i, carry):
                zz, yy, xx = i // 4, lax.rem(i // 2, 2), lax.rem(i, 2)
                total = acc[zz, yy, xx].astype(F32) + self.rec1[g][zz, yy, xx].astype(F32)
                acc[zz, yy, xx] = total.astype(BF16)
                return carry

            lax.fori_loop(0, 4 * n, step, 0)
        elif stage == 2:

            def step(i, carry):
                zz, aa = i // 2, lax.rem(i, 2)
                yy, xx = (aa, x) if even else (y, aa)
                total = acc[zz, yy, xx].astype(F32) + self.rec2[g][zz, aa].astype(F32)
                acc[zz, yy, xx] = total.astype(BF16)
                return carry

            lax.fori_loop(0, 2 * n, step, 0)
        elif stage == 3:

            def step(zz, carry):
                total = acc[zz, y, x].astype(F32) + self.rec3[g][zz].astype(F32)
                acc[zz, y, x] = total.astype(BF16)
                return carry

            lax.fori_loop(0, n, step, 0)
        else:
            total = acc[z, y, x].astype(F32)
            for k in self.ks:
                total = total + self.rec4[g][k - 1].astype(F32)
            fin[y, x, c] = total.astype(BF16)
            for e in range(self.extra):
                self.further(g, e).start()
                self.further(g, e).wait()
                rows = fin.shape[3]
                total = fin[y, x, c].astype(F32) + self.recx[g, e, :rows].astype(F32)
                fin[y, x, c] = total.astype(BF16)

    def run(self, g, stage):
        ks = self.ks
        if stage == 0:
            if self.kept[g] is not None:
                self.own(g).start()
            self.copy(0, g).start()
            return
        if stage == 1 and self.kept[g] is not None:
            self.own(g).wait()
        for k in ks if stage == 4 else (0,):
            self.copy(stage - 1, g, k, True).wait_recv()
        if stage <= 4:
            self.add(stage, g)
        if stage <= 6:
            for k in ks if stage == 3 else (0,):
                self.copy(stage, g, k).start()

    def drain(self):
        for g in range(self.count):
            for stage in range(7):
                for k in self.ks if stage == 3 else (0,):
                    self.copy(stage, g, k).wait_send()


def reduce_scratch(n, extra, rows, width, kept):
    count = len(rows)
    scratch = [pltpu.VMEM((n, 2, 2, r, width), BF16) for r, k in zip(rows, kept) if k]
    scratch += [pltpu.VMEM((n, 2, 2, r, width), BF16) for r in rows]
    scratch += [pltpu.VMEM((n, 2, r, width), BF16) for r in rows]
    scratch += [pltpu.VMEM((n, r, width), BF16) for r in rows]
    scratch += [pltpu.VMEM((n - 1, r, width), BF16) for r in rows]
    scratch += [
        pltpu.VMEM((count, extra, max(rows), width) if extra else (1, 1, 16, 128), BF16),
        DMA((count, 6 + n - 1)),
        DMA((count, 6 + n - 1)),
        DMA((count, max(extra, 1))),
        DMA((count, max(extra, 1))),
        DMA((count,)),
    ]
    return scratch


def take_reduce(n, extra, part, fin, kept, refs):
    refs = list(refs)
    acc = [refs.pop(0) if k else None for k in kept]
    count = len(part)
    recs = [[refs.pop(0) for _ in range(count)] for _ in range(4)]
    recx = refs.pop(0)
    sems = [refs.pop(0) for _ in range(5)]
    return Reduce(n, extra, part, acc, *recs, fin, recx, sems), refs


def both_plots(rows, plot_row):
    wide = rows.astype(F32)
    zero = jnp.zeros_like(wide)
    return jnp.concatenate(
        [jnp.where(plot_row == 0, wide, zero), jnp.where(plot_row == 0, zero, wide)], axis=0
    ).astype(BF16)


def own_plot(pair, plot_row):
    half = pair.shape[0] // 2
    return jnp.where(plot_row == 0, pair[:half], pair[half:])


def line_exchange(n, parts, z, dp, refs, compute, merge, finish, hook=None):
    own, spread, mine, from_right, from_left, sems = refs
    ups, upr, dns, dnr, rls, rlr, rrs, rrr = sems

    def up(j, p, i, start):
        src = own[i].at[p] if start else spread[i].at[j, p]
        return remote(
            src, spread[i].at[j, p], ups.at[i, j, p], upr.at[i, j, p], (dp, lax.rem(z + 1, n))
        )

    def down(j, p, i, start):
        src = own[i].at[p] if start else spread[i].at[j, p]
        return remote(
            src,
            spread[i].at[j, p],
            dns.at[i, j, p],
            dnr.at[i, j, p],
            (dp, lax.rem(z + n - 1, n)),
        )

    def back_left(j, p, i):
        return remote(
            mine[i].at[j, p],
            from_right[i].at[j, p],
            rls.at[i, j, p],
            rlr.at[i, j, p],
            (dp, lax.rem(z + n - 1, n)),
        )

    def back_right(j, p, i):
        return remote(
            mine[i].at[j, p],
            from_left[i].at[j, p],
            rrs.at[i, j, p],
            rrr.at[i, j, p],
            (dp, lax.rem(z + 1, n)),
        )

    out_kinds = range(len(own))
    back_kinds = range(len(mine))

    def send_own(p, carry):
        for i in out_kinds:

            @pl.when(z < n - 1)
            def _():
                up(z, p, i, True).start()

            @pl.when(z > 0)
            def _():
                down(z, p, i, True).start()

        return carry

    lax.fori_loop(0, parts, send_own, 0)

    def first(p, carry):
        for i in out_kinds:
            spread[i][z, p] = own[i][p]
        compute(z, p)
        return carry

    lax.fori_loop(0, parts, first, 0)

    def tick(t, carry):
        def one_part(p, inner):
            low = z - t
            high = z + t

            @pl.when((t < n) & (low >= 0))
            def _():
                for i in out_kinds:
                    up(low, p, i, False).wait_recv()

                    @pl.when(z < n - 1)
                    def _():
                        up(low, p, i, False).start()

                compute(low, p)

                @pl.when(z == n - 1)
                def _():
                    for i in back_kinds:
                        back_left(low, p, i).start()

            @pl.when((t < n) & (high < n))
            def _():
                for i in out_kinds:
                    down(high, p, i, False).wait_recv()

                    @pl.when(z > 0)
                    def _():
                        down(high, p, i, False).start()

                compute(high, p)

                @pl.when(z == 0)
                def _():
                    for i in back_kinds:
                        back_right(high, p, i).start()

            left_chunk = 2 * (n - 1) - z - t

            @pl.when((left_chunk >= 0) & (left_chunk < z) & (z < n - 1))
            def _():
                for i in back_kinds:
                    back_left(left_chunk, p, i).wait_recv()
                merge(left_chunk, p, from_right)
                for i in back_kinds:
                    back_left(left_chunk, p, i).start()

            right_chunk = t - z

            @pl.when((right_chunk < n) & (right_chunk > z) & (z > 0))
            def _():
                for i in back_kinds:
                    back_right(right_chunk, p, i).wait_recv()
                merge(right_chunk, p, from_left)
                for i in back_kinds:
                    back_right(right_chunk, p, i).start()

            return inner

        lax.fori_loop(0, parts, one_part, 0)
        if hook is not None:
            hook(t)
        return carry

    if hook is not None:
        hook(0)
    lax.fori_loop(1, 2 * n - 2, tick, 0)

    def last(p, carry):
        @pl.when(z > 0)
        def _():
            for i in back_kinds:
                back_right(z, p, i).wait_recv()
            merge(z, p, from_left)

        @pl.when(z < n - 1)
        def _():
            for i in back_kinds:
                back_left(z, p, i).wait_recv()
            merge(z, p, from_right)

        finish(p)
        return carry

    lax.fori_loop(0, parts, last, 0)

    def drain(p, carry):
        for j in range(n):
            for i in out_kinds:

                @pl.when((z < n - 1) & (z == j))
                def _(i=i, j=j):
                    up(j, p, i, True).wait_send()

                @pl.when((z < n - 1) & (z > j))
                def _(i=i, j=j):
                    up(j, p, i, False).wait_send()

                @pl.when((z > 0) & (z == j))
                def _(i=i, j=j):
                    down(j, p, i, True).wait_send()

                @pl.when((z > 0) & (z < j))
                def _(i=i, j=j):
                    down(j, p, i, False).wait_send()

            for i in back_kinds:

                @pl.when(z > j)
                def _(i=i, j=j):
                    back_left(j, p, i).wait_send()

                @pl.when(z < j)
                def _(i=i, j=j):
                    back_right(j, p, i).wait_send()

        return carry

    lax.fori_loop(0, parts, drain, 0)


def line_sems(n, parts, out_kinds, back_kinds):
    return [DMA((out_kinds, n, parts))] * 4 + [DMA((back_kinds, n, parts))] * 4


def unit_rows(ref, zz, which):
    block = ref[zz, which]
    return block.reshape(-1, block.shape[-1])


def two_units(ref, pair, which):
    return jnp.concatenate(
        [unit_rows(ref, 2 * pair, which), unit_rows(ref, 2 * pair + 1, which)], axis=0
    )


def normed_rows(rows, gain):
    inverse = lax.rsqrt(jnp.mean(rows * rows, axis=-1, keepdims=True) + epsilon)
    return rows * inverse * gain


def half_lanes(first, second, which):
    lane = lax.broadcasted_iota(jnp.int32, first.shape, 1)
    if which == 0:
        return jnp.where(lane < HD, first, pltpu.roll(second, HD, 1))
    return jnp.where(lane < HD, pltpu.roll(first, HD, 1), second)


def forward_kernel(n, count, halo_chunks, *refs):
    tok, bias, plots, self_gain, cross_gain, mem = refs[:6]
    mine = refs[6 : 6 + count]
    at = 6 + count
    full_out = refs[at : at + count]
    at += count
    (
        near, normed, self_q, self_k, self_kt, self_v, self_mix, self_logs, first_sum, normed_cross,
        q_all, cross_k, cross_kt, cross_v, o_ref, l_ref,
    ) = refs[at : at + 16]
    at += 16
    full = refs[at : at + count]
    at += count
    halo, self_vt, cross_vt, cross_q, o_mine, l_mine, o_right, l_right, o_left, l_left = refs[
        at : at + 10
    ]
    at += 10
    line = refs[at : at + 8]
    at += 8
    gather_refs = refs[at : at + 9]
    hs, hr, outs = refs[at + 9 :]
    rows, width = tok.shape
    heads = width // HD
    parts = n
    heads_part = heads // parts
    scale = HD ** (-0.5)
    dp, z, c, x, y = place()
    gather = Gather(n, mine, full, gather_refs)
    greet(gather.peers())
    gather.begin(2)

    halo[halo_chunks] = tok[...]

    def halo_copy(i):
        src = tok if i == 0 else halo.at[halo_chunks - i]
        dst = halo.at[halo_chunks - 1 - i]
        return remote(src, dst, hs.at[i], hr.at[i], (dp, lax.rem(z + 1, n)))

    @pl.when(z < n - 1)
    def _():
        halo_copy(0).start()

    for i in range(halo_chunks):

        @pl.when(z <= i)
        def _(i=i):
            halo[halo_chunks - 1 - i] = jnp.zeros((rows, width), BF16)

    gather.pump(0)
    for i in range(halo_chunks):

        @pl.when(z > i)
        def _(i=i):
            halo_copy(i).wait_recv()

        if i + 1 < halo_chunks:

            @pl.when((z > i) & (z < n - 1))
            def _(i=i):
                halo_copy(i + 1).start()

    def norm_chunk(i, carry):
        at_rows = pl.ds(pl.multiple_of(i * rows, rows), rows)
        near[at_rows, :] = halo[i]
        normed[at_rows, :] = normed_rows(halo[i].astype(F32), self_gain[...]).astype(BF16)
        return carry

    lax.fori_loop(0, halo_chunks + 1, norm_chunk, 0)
    for t in range(1, 4):
        gather.pump(t)

    own_rows = slice(halo_chunks * rows, (halo_chunks + 1) * rows)
    gather.ready(0)

    def query_part(zz, carry):
        at_part = pl.ds(pl.multiple_of(zz * heads_part * HD, heads_part * HD), heads_part * HD)
        projected = product(unit_rows(full[0], zz, 0), normed[own_rows, :], 1, 1)
        self_q[at_part, :] = (projected.astype(BF16).astype(F32) * scale).astype(BF16)
        self_kt[at_part, :] = product(unit_rows(full[0], zz, 1), normed[...], 1, 1).astype(BF16)
        return carry

    lax.fori_loop(0, n, query_part, 0)

    def tall(out, g, which):
        for pair in range(n // 2):
            cols = slice(pair * 2 * heads_part * HD, (pair + 1) * 2 * heads_part * HD)

            def chunk(i, carry, pair=pair, cols=cols):
                at_rows = pl.ds(pl.multiple_of(i * rows, rows), rows)
                weights = two_units(full[g], pair, which)
                out[at_rows, cols] = product(normed[at_rows, :], weights, 1, 1).astype(BF16)
                return carry

            lax.fori_loop(0, halo_chunks + 1, chunk, 0)

    tall(self_k, 0, 1)
    gather.ready(1)

    def value_part(zz, carry):
        at_part = pl.ds(pl.multiple_of(zz * heads_part * HD, heads_part * HD), heads_part * HD)
        self_vt[at_part, :] = product(unit_rows(full[1], zz, 0), normed[...], 1, 1).astype(BF16)
        return carry

    lax.fori_loop(0, n, value_part, 0)
    tall(self_v, 1, 0)
    gather.pump(4)

    for pair in range(heads // 2):
        cols = slice(pair * 2 * HD, (pair + 1) * 2 * HD)
        for which in range(2):
            at_head = slice((2 * pair + which) * HD, (2 * pair + which + 1) * HD)
            scores = jnp.dot(
                self_k[:, cols], alone(self_q[at_head, :], which), preferred_element_type=F32
            )
            scores = scores + bias[...]
            top = jnp.max(scores, axis=0, keepdims=True)
            powers = jnp.exp(scores - top)
            total = jnp.sum(powers, axis=0, keepdims=True)
            mixed = jnp.dot(self_vt[at_head, :], powers.astype(BF16), preferred_element_type=F32)
            self_mix[at_head, :] = (mixed / total).astype(BF16)
            self_logs[pair, which : which + 1, :] = top + jnp.log(total)

    gather.pump(5)
    gather.ready(2)

    plots_held = mem.shape[0]

    def memory_part(zz, carry):
        for p in range(plots_held):
            keys_t = product(unit_rows(full[2], zz, 0), mem[p], 1, 1).astype(BF16)
            values_t = product(unit_rows(full[2], zz, 1), mem[p], 1, 1).astype(BF16)
            for hh in range(heads_part):
                at_head = slice(hh * HD, (hh + 1) * HD)
                cross_kt[zz * heads_part + hh, p * HD : (p + 1) * HD, :] = keys_t[at_head]
                cross_vt[zz * heads_part + hh, p * HD : (p + 1) * HD, :] = values_t[at_head]
        return carry

    lax.fori_loop(0, n, memory_part, 0)
    for which, out in enumerate((cross_k, cross_v)):
        for pair in range(n // 2):
            weights = two_units(full[2], pair, which)
            first = product(mem[0], weights, 1, 1)
            second = product(mem[1], weights, 1, 1)
            for hh in range(2 * heads_part):
                cols = slice((hh // 2) * 2 * HD, (hh // 2 + 1) * 2 * HD)
                both = half_lanes(first[:, cols], second[:, cols], hh % 2)
                out[pair * 2 * heads_part + hh] = both.astype(BF16)

    total = tok[...].astype(F32)
    for zz in range(n):
        at_part = slice(zz * heads_part * HD, (zz + 1) * heads_part * HD)
        total = total + product(self_mix[at_part, :], unit_rows(full[1], zz, 1), 0, 0)
    first_sum[...] = total
    normed_cross[...] = normed_rows(total, cross_gain[...]).astype(BF16)
    gather.ready(3)

    def cross_query_part(zz, carry):
        projected = product(unit_rows(full[3], zz, 0), normed_cross[...], 1, 1)
        cross_q[zz] = (projected.astype(BF16).astype(F32) * scale).astype(BF16)
        return carry

    lax.fori_loop(0, n, cross_query_part, 0)

    def compute(j, p):
        plot_row = plots[j]
        for hh in range(heads_part):
            h = p * heads_part + hh
            q_pair = both_plots(q_all[j, p, hh * HD : (hh + 1) * HD, :], plot_row)
            scores = jnp.dot(cross_k[h], q_pair, preferred_element_type=F32)
            top = jnp.max(scores, axis=0, keepdims=True)
            powers = jnp.exp(scores - top)
            total = jnp.sum(powers, axis=0, keepdims=True)
            mixed = jnp.dot(cross_vt[h], powers.astype(BF16), preferred_element_type=F32)
            mixed = own_plot(mixed, plot_row) / total
            o_mine[j, p, hh * HD : (hh + 1) * HD, :] = mixed.astype(BF16)
            l_mine[j, p, hh : hh + 1, :] = top + jnp.log(total)

    def merge(j, p, arrived):
        for hh in range(heads_part):
            at_head = slice(hh * HD, (hh + 1) * HD)
            log_a = l_mine[j, p, hh : hh + 1, :]
            log_b = arrived[1][j, p, hh : hh + 1, :]
            top = jnp.maximum(log_a, log_b)
            share_a = jnp.exp(log_a - top)
            share_b = jnp.exp(log_b - top)
            total = share_a + share_b
            mixed = o_mine[j, p, at_head, :].astype(F32) * (share_a / total)
            mixed = mixed + arrived[0][j, p, at_head, :].astype(F32) * (share_b / total)
            o_mine[j, p, at_head, :] = mixed.astype(BF16)
            l_mine[j, p, hh : hh + 1, :] = top + jnp.log(total)

    def finish(p):
        o_ref[p] = o_mine[z, p]
        l_ref[p] = l_mine[z, p]

    def keep(g):
        return pltpu.make_async_copy(full[g], full_out[g], outs.at[g])

    def hook(t):
        for step in range(4):

            @pl.when(t == step)
            def _(step=step):
                if step < 3:
                    gather.pump(6 + step)
                if step == 0:
                    for g in range(4):
                        keep(g).start()
                else:
                    gather.ready(3 + step)
                    keep(3 + step).start()

    exchange = ([cross_q], [q_all], [o_mine, l_mine], [o_right, l_right], [o_left, l_left], line)
    line_exchange(n, parts, z, dp, exchange, compute, merge, finish, hook)
    gather.drain()
    for g in range(count):
        keep(g).wait()
    for i in range(halo_chunks):

        @pl.when((z >= i) & (z < n - 1))
        def _(i=i):
            halo_copy(i).wait_send()


def forward(n, halo_chunks, tokens, bias, plots, self_gain, cross_gain, memory, shards):
    count = len(shards)
    rows, width = tokens.shape
    keys = bias.shape[0]
    heads = width // HD
    parts = n
    rows_part = width // parts
    held, patches, _ = memory.shape
    full = [(n,) + s.shape for s in shards]
    struct = jax.ShapeDtypeStruct
    out_shape = [struct(f, BF16) for f in full] + [
        struct((keys, width), BF16),
        struct((keys, width), BF16),
        struct((width, rows), BF16),
        struct((keys, width), BF16),
        struct((width, keys), BF16),
        struct((keys, width), BF16),
        struct((width, rows), BF16),
        struct((heads // 2, 8, rows), F32),
        struct((rows, width), F32),
        struct((rows, width), BF16),
        struct((n, parts, rows_part, rows), BF16),
        struct((heads, patches, held * HD), BF16),
        struct((heads, held * HD, patches), BF16),
        struct((heads, patches, held * HD), BF16),
        struct((parts, rows_part, rows), BF16),
        struct((parts, 8, rows), F32),
    ]
    scratch = [pltpu.VMEM(f, BF16) for f in full]
    scratch += [
        pltpu.VMEM((halo_chunks + 1, rows, width), BF16),
        pltpu.VMEM((width, keys), BF16),
        pltpu.VMEM((heads, held * HD, patches), BF16),
        pltpu.VMEM((parts, rows_part, rows), BF16),
    ]
    for _ in range(3):
        scratch += [
            pltpu.VMEM((n, parts, rows_part, rows), BF16),
            pltpu.VMEM((n, parts, 8, rows), F32),
        ]
    scratch += line_sems(n, parts, 1, 2)
    scratch += gather_sems(n, count)
    scratch += [DMA((halo_chunks,)), DMA((halo_chunks,)), DMA((count,))]
    out = pl.pallas_call(
        functools.partial(forward_kernel, n, count, halo_chunks),
        out_shape=out_shape,
        in_specs=[VMEM] * 6 + [ANY] * count,
        out_specs=[ANY] * count + [VMEM] * 16,
        scratch_shapes=scratch,
        compiler_params=pltpu.CompilerParams(
            collective_id=0, has_side_effects=True, vmem_limit_bytes=63 << 20
        ),
        name="forward",
    )(tokens, bias, plots, self_gain, cross_gain, memory, *shards)
    return out[:count], out[count:]


def norm_gradient(rows, gain, back):
    inverse = lax.rsqrt(jnp.mean(rows * rows, axis=-1, keepdims=True) + epsilon)
    unit = rows * inverse
    scaled = back * gain
    inner = jnp.mean(scaled * unit, axis=-1, keepdims=True)
    return inverse * (scaled - unit * inner), jnp.sum(back * unit, axis=0, keepdims=True)


def as_unit(rows_192):
    rows, width = rows_192.shape
    return rows_192.reshape(2, 2, rows // 4, width)


def cross_backward_kernel(n, count, extra, *refs):
    (
        plots, do_ref, st_ref, q_all, k_ref, kt_ref, v_ref, mem, normed_cross, cross_mix, grad_rows,
        second_back, first_sum, cross_gain, w_keys, w_query,
    ) = refs[:16]
    part = refs[16 : 16 + count]
    at = 16 + count
    fin = refs[at : at + count]
    grad_mem, part_keys, part_query, first_back, g_first, gain_cross = refs[
        at + count : at + count + 6
    ]
    rest = refs[at + count + 6 :]
    reduce, rest = take_reduce(n, extra, part, fin, [True] * count, rest)
    do_all, st_all, q_mine, q_right, q_left, dk_ref, dv_ref, k_back, v_back = rest[:9]
    line = rest[9:]
    dp, z = lax.axis_index("dp"), lax.axis_index("tensor")
    parts, rows_part, rows = do_ref.shape
    width = parts * rows_part
    heads_part = rows_part // HD
    heads = parts * heads_part
    held = mem.shape[0]
    scale = HD ** (-0.5)
    greet(reduce.peers())
    for g in range(count):
        reduce.run(g, 0)

    def clear(h, carry):
        dk_ref[h] = jnp.zeros(dk_ref.shape[1:], F32)
        dv_ref[h] = jnp.zeros(dv_ref.shape[1:], F32)
        return carry

    lax.fori_loop(0, heads, clear, 0)

    def compute(j, p):
        plot_row = plots[j]
        for hh in range(heads_part):
            h = p * heads_part + hh
            at_head = slice(hh * HD, (hh + 1) * HD)
            q_pair = both_plots(q_all[j, p, at_head, :], plot_row)
            do_pair = both_plots(do_all[j, p, at_head, :], plot_row)
            scores = jnp.dot(k_ref[h], q_pair, preferred_element_type=F32)
            chances = jnp.exp(scores - st_all[j, p, hh : hh + 1, :])
            prob_back = jnp.dot(v_ref[h], do_pair, preferred_element_type=F32)
            inner = st_all[j, p, heads_part + hh : heads_part + hh + 1, :]
            score_back = (chances * (prob_back - inner)).astype(BF16)
            q_back = jnp.dot(kt_ref[h], score_back, preferred_element_type=F32)
            q_mine[j, p, at_head, :] = (own_plot(q_back, plot_row) * scale).astype(BF16)
            dk_ref[h] += product(score_back, q_pair, 1, 1)
            dv_ref[h] += product(chances.astype(BF16), do_pair, 1, 1)

    def merge(j, p, arrived):
        total = q_mine[j, p].astype(F32) + arrived[0][j, p].astype(F32)
        q_mine[j, p] = total.astype(BF16)

    def finish(p):
        pass

    def patch_gradients():
        for source, out in ((dk_ref, k_back), (dv_ref, v_back)):

            def pair_step(i, carry, source=source, out=out):
                even, odd = source[2 * i], source[2 * i + 1]
                lane = lax.broadcasted_iota(jnp.int32, even.shape, 1)
                cols = pl.ds(pl.multiple_of(i * 2 * HD, 2 * HD), 2 * HD)
                out[0, :, cols] = jnp.where(lane < HD, even, pltpu.roll(odd, HD, 1)).astype(BF16)
                out[1, :, cols] = jnp.where(lane < HD, pltpu.roll(even, HD, 1), odd).astype(BF16)
                return carry

            lax.fori_loop(0, heads // 2, pair_step, 0)
        for which, back in enumerate((k_back, v_back)):
            for pair in range(n // 2):
                cols = slice(pair * 2 * rows_part, (pair + 1) * 2 * rows_part)
                grad = sum(product(back[p, :, cols], mem[p], 0, 0) for p in range(held))
                grad = grad.astype(BF16)
                part_keys[2 * pair, which] = as_unit(grad[:rows_part])
                part_keys[2 * pair + 1, which] = as_unit(grad[rows_part:])

        def memory_step(i, carry):
            p, at_rows = i // 2, pl.ds(pl.multiple_of(lax.rem(i, 2) * rows, rows), rows)
            total = 0.0
            for which, back in enumerate((k_back, v_back)):
                for pair in range(n // 2):
                    cols = slice(pair * 2 * rows_part, (pair + 1) * 2 * rows_part)
                    weights = two_units(w_keys, pair, which)
                    total = total + product(back[p, at_rows, cols], weights, 1, 0)
            grad_mem[p, at_rows, :] = total.astype(BF16)
            return carry

        lax.fori_loop(0, held * (mem.shape[1] // rows), memory_step, 0)

    schedule = {0: [(0, 1), (1, 1), (2, 1)], 2: [(0, 2), (1, 2)], 3: [(2, 2), (0, 3), (1, 3)]}

    def hook(t):
        for step, work in schedule.items():

            @pl.when(t == step)
            def _(work=work):
                for g, stage in work:
                    reduce.run(g, stage)

        @pl.when(t == 2 * n - 3)
        def _():
            patch_gradients()
            for g, stage in ((2, 3), (0, 4), (1, 4)):
                reduce.run(g, stage)

    exchange = ([do_ref, st_ref], [do_all, st_all], [q_mine], [q_right], [q_left], line)
    line_exchange(n, parts, z, dp, exchange, compute, merge, finish, hook)
    for g, stage in ((2, 4), (0, 5), (1, 5)):
        reduce.run(g, stage)

    back = 0.0
    for zz in range(n):
        mine = q_mine[z, zz]
        part_query[zz, 0] = as_unit(product(mine, normed_cross[...], 1, 0).astype(BF16))
        mixed = cross_mix[zz * rows_part : (zz + 1) * rows_part, :]
        part_query[zz, 1] = as_unit(product(mixed, grad_rows[...], 1, 0).astype(BF16))
        back = back + product(mine, unit_rows(w_query, zz, 0), 0, 0)
    residual, gain_back = norm_gradient(first_sum[...], cross_gain[...], back)
    total = second_back[...] + residual
    first_back[...] = total
    g_first[...] = total.astype(BF16)
    gain_cross[...] = gain_back
    for g, stage in ((2, 5), (0, 6), (1, 6), (2, 6), (0, 7), (1, 7), (2, 7)):
        reduce.run(g, stage)
    reduce.drain()


def cross_backward(n, extra, ins, part):
    do, mem = ins[1], ins[7]
    parts, rows_part, rows = do.shape
    width = parts * rows_part
    heads = width // HD
    held, patches, _ = mem.shape
    count = len(part)
    piece = [p.shape[-2] for p in part]
    struct = jax.ShapeDtypeStruct
    unit = width // n // 4
    scratch = reduce_scratch(n, extra, piece, width, [True] * count)
    scratch += [
        pltpu.VMEM((n, parts, rows_part, rows), BF16),
        pltpu.VMEM((n, parts, 8, rows), F32),
        pltpu.VMEM((n, parts, rows_part, rows), BF16),
        pltpu.VMEM((n, parts, rows_part, rows), BF16),
        pltpu.VMEM((n, parts, rows_part, rows), BF16),
        pltpu.VMEM((heads, patches, held * HD), F32),
        pltpu.VMEM((heads, patches, held * HD), F32),
        pltpu.VMEM((held, patches, width), BF16),
        pltpu.VMEM((held, patches, width), BF16),
    ]
    scratch += line_sems(n, parts, 2, 1)
    out = pl.pallas_call(
        functools.partial(cross_backward_kernel, n, count, extra),
        out_shape=[struct((2, 2, 2, r, width), BF16) for r in piece]
        + [
            struct(mem.shape, BF16),
            struct((n, 2, 2, 2, unit, width), BF16),
            struct((n, 2, 2, 2, unit, width), BF16),
            struct((rows, width), F32),
            struct((rows, width), BF16),
            struct((1, width), F32),
        ],
        in_specs=[VMEM] * 16 + [ANY] * count,
        out_specs=[VMEM] * (count + 6),
        scratch_shapes=scratch,
        compiler_params=pltpu.CompilerParams(
            collective_id=1, has_side_effects=True, vmem_limit_bytes=63 << 20
        ),
        name="cross_backward",
    )(*ins, *part)
    return out[:count], out[count:]


def alone(rows, which):
    zero = jnp.zeros_like(rows)
    return jnp.concatenate([rows, zero] if which == 0 else [zero, rows], axis=0)


def self_backward_kernel(n, extra, halo_chunks, *refs):
    (
        bias, q_ref, k_ref, kt_ref, v_ref, mix, logs, near, normed, g_first, first_back, self_gain,
        gains_in, w_qk, w_vo,
    ) = refs[:15]
    cross_parts = refs[15:17]
    fin = refs[17:21]
    grad_tokens, gain_out = refs[21:23]
    own_parts = refs[23:25]
    part = list(cross_parts) + list(own_parts)
    kept = [True, True, False, False]
    reduce, rest = take_reduce(n, extra, part, fin, kept, refs[25:])
    do_ref, dq_ref, dk_ref, dv_ref, own_back, csend, crecv, grec, hs, hr, gs, gr = rest
    dp, z, c, x, y = place()
    rows, width = g_first.shape
    heads = width // HD
    rows_part = width // n
    scale = HD ** (-0.5)
    own_rows = slice(halo_chunks * rows, (halo_chunks + 1) * rows)
    gain_peers = [(flipped(dp, bit), z) for bit in range(3 + extra)]
    for bit in range(n.bit_length() - 1):
        here = lax.rem(z // (1 << bit), 2)
        gain_peers.append((dp, z + (1 << bit) * (1 - 2 * here)))
    rounds = len(gain_peers)
    greet(reduce.peers())
    reduce.run(0, 0)
    reduce.run(1, 0)

    def do_part(zz, carry):
        at_part = pl.ds(pl.multiple_of(zz * rows_part, rows_part), rows_part)
        do_ref[at_part, :] = product(unit_rows(w_vo, zz, 1), g_first[...], 1, 1).astype(BF16)
        return carry

    lax.fori_loop(0, n, do_part, 0)
    reduce.run(0, 1)
    reduce.run(1, 1)

    def pair_step(pair, carry):
        cols = pl.ds(pl.multiple_of(pair * 2 * HD, 2 * HD), 2 * HD)
        dk, dv = 0.0, 0.0
        for which in range(2):
            at_head = pl.ds(pl.multiple_of((2 * pair + which) * HD, HD), HD)
            q_pair = alone(q_ref[at_head, :], which)
            do_head = do_ref[at_head, :]
            inner = jnp.sum(
                do_head.astype(F32) * mix[at_head, :].astype(F32), axis=0, keepdims=True
            )
            do_pair = alone(do_head, which)
            scores = jnp.dot(k_ref[:, cols], q_pair, preferred_element_type=F32)
            chances = jnp.exp(scores + bias[...] - logs[pair, which : which + 1, :])
            prob_back = jnp.dot(v_ref[:, cols], do_pair, preferred_element_type=F32)
            score_back = (chances * (prob_back - inner)).astype(BF16)
            q_back = jnp.dot(kt_ref[at_head, :], score_back, preferred_element_type=F32)
            dq_ref[at_head, :] = (q_back * scale).astype(BF16)
            dk = dk + product(score_back, q_pair, 1, 1)
            dv = dv + product(chances.astype(BF16), do_pair, 1, 1)
        dk_ref[:, cols] = dk.astype(BF16)
        dv_ref[:, cols] = dv.astype(BF16)
        return carry

    lax.fori_loop(0, heads // 2, pair_step, 0)

    def halo_copy(i):
        far = halo_chunks - i
        dev = (dp, lax.rem(z + n - far, n))
        return remote(csend.at[i], crecv.at[i], hs.at[i], hr.at[i], dev)

    gain_self = jnp.zeros((1, width), F32)
    for i in range(halo_chunks + 1):
        at_rows = slice(i * rows, (i + 1) * rows)
        back = 0.0
        for pair in range(n // 2):
            cols = slice(pair * 2 * rows_part, (pair + 1) * 2 * rows_part)
            back = back + product(dk_ref[at_rows, cols], two_units(w_qk, pair, 1), 1, 0)
            back = back + product(dv_ref[at_rows, cols], two_units(w_vo, pair, 0), 1, 0)
        if i < halo_chunks:
            csend[i] = back.astype(BF16)

            @pl.when(z >= halo_chunks - i)
            def _(i=i):
                halo_copy(i).start()

        else:
            for zz in range(n):
                at_part = slice(zz * rows_part, (zz + 1) * rows_part)
                back = back + product(dq_ref[at_part, :], unit_rows(w_qk, zz, 0), 0, 0)
            own_back[...] = back
        here = near[at_rows, :].astype(F32)
        inverse = lax.rsqrt(jnp.mean(here * here, axis=-1, keepdims=True) + epsilon)
        gain_self = gain_self + jnp.sum(back * here * inverse, axis=0, keepdims=True)

    gain_out[...] = gains_in[...]
    gain_out[0:1, :] = gain_self
    grec[0] = gain_out[...]

    def gain_copy(i):
        return remote(grec.at[2 * i], grec.at[2 * i + 1], gs.at[i], gr.at[i], gain_peers[i])

    def gain_round(i):
        gain_copy(i).wait_recv()
        gain_out[...] = gain_out[...] + grec[2 * i + 1]
        if i + 1 < rounds:
            grec[2 * i + 2] = gain_out[...]
            gain_copy(i + 1).start()

    gain_copy(0).start()
    reduce.run(0, 2)
    reduce.run(1, 2)

    for pair in range(n // 2):
        cols = slice(pair * 2 * rows_part, (pair + 1) * 2 * rows_part)
        grad = product(dv_ref[:, cols], normed[...], 0, 0).astype(BF16)
        own_parts[0][2 * pair, 1] = as_unit(grad[:rows_part])
        own_parts[0][2 * pair + 1, 1] = as_unit(grad[rows_part:])
    for zz in range(n):
        at_part = slice(zz * rows_part, (zz + 1) * rows_part)
        grad = product(mix[at_part, :], g_first[...], 1, 0)
        own_parts[0][zz, 0] = as_unit(grad.astype(BF16))
    reduce.run(2, 0)
    for pair in range(n // 2):
        cols = slice(pair * 2 * rows_part, (pair + 1) * 2 * rows_part)
        grad = product(dk_ref[:, cols], normed[...], 0, 0).astype(BF16)
        own_parts[1][2 * pair, 1] = as_unit(grad[:rows_part])
        own_parts[1][2 * pair + 1, 1] = as_unit(grad[rows_part:])
    for zz in range(n):
        at_part = slice(zz * rows_part, (zz + 1) * rows_part)
        grad = product(dq_ref[at_part, :], normed[own_rows, :], 1, 0)
        own_parts[1][zz, 0] = as_unit(grad.astype(BF16))
    reduce.run(3, 0)
    reduce.run(2, 1)
    reduce.run(3, 1)
    reduce.run(0, 3)
    reduce.run(1, 3)
    gain_round(0)
    reduce.run(2, 2)
    reduce.run(3, 2)
    reduce.run(0, 4)
    reduce.run(1, 4)
    gain_round(1)

    for i in range(halo_chunks):

        @pl.when(z + halo_chunks - i < n)
        def _(i=i):
            halo_copy(i).wait_recv()
            own_back[...] += crecv[i].astype(F32)

    here = near[own_rows, :].astype(F32)
    residual, _ = norm_gradient(here, self_gain[...], own_back[...])
    grad_tokens[...] = (first_back[...] + residual).astype(BF16)
    reduce.run(2, 3)
    reduce.run(3, 3)
    reduce.run(0, 5)
    reduce.run(1, 5)
    gain_round(2)
    reduce.run(2, 4)
    reduce.run(3, 4)
    reduce.run(0, 6)
    reduce.run(1, 6)
    for i in range(3, rounds):
        gain_round(i)
    for stage in (5, 6):
        reduce.run(2, stage)
        reduce.run(3, stage)
    for g in range(4):
        reduce.run(g, 7)
    for i in range(halo_chunks):

        @pl.when(z >= halo_chunks - i)
        def _(i=i):
            halo_copy(i).wait_send()

    for i in range(rounds):
        gain_copy(i).wait_send()
    reduce.drain()


def self_backward(n, extra, halo_chunks, ins, cross_parts):
    near, g_first = ins[7], ins[9]
    rows, width = g_first.shape
    keys = near.shape[0]
    unit = width // n // 4
    piece = [unit] * 4
    struct = jax.ShapeDtypeStruct
    rounds = 3 + extra + n.bit_length() - 1
    scratch = [pltpu.VMEM((n, 2, 2, 2, unit, width), BF16)] * 2
    scratch += reduce_scratch(n, extra, piece, width, [True, True, False, False])
    scratch += [
        pltpu.VMEM((width, rows), BF16),
        pltpu.VMEM((width, rows), BF16),
        pltpu.VMEM((keys, width), BF16),
        pltpu.VMEM((keys, width), BF16),
        pltpu.VMEM((rows, width), F32),
        pltpu.VMEM((halo_chunks, rows, width), BF16),
        pltpu.VMEM((halo_chunks, rows, width), BF16),
        pltpu.VMEM((2 * rounds, 8, width), F32),
        DMA((halo_chunks,)),
        DMA((halo_chunks,)),
        DMA((rounds,)),
        DMA((rounds,)),
    ]
    out = pl.pallas_call(
        functools.partial(self_backward_kernel, n, extra, halo_chunks),
        out_shape=[struct((2, 2, 2, r, width), BF16) for r in piece]
        + [struct((rows, width), BF16), struct((8, width), F32)],
        in_specs=[VMEM] * 15 + [ANY] * 2,
        out_specs=[VMEM] * 6,
        scratch_shapes=scratch,
        compiler_params=pltpu.CompilerParams(
            collective_id=2, has_side_effects=True, vmem_limit_bytes=63 << 20
        ),
        name="self_backward",
    )(*ins, *cross_parts)
    return out[:4], out[4], out[5]


def body(
    tokens, memory, table_lengths, table_plots,
    self_gain, self_query, self_key, self_value, self_output,
    cross_gain, cross_query, cross_key, cross_value, cross_output,
    hidden_gain, hidden_gate, hidden_up, hidden_down, cotangent,
):
    n = lax.axis_size("tensor")
    dp_size = lax.axis_size("dp")
    extra = dp_size.bit_length() - 1 - 3
    z = lax.axis_index("tensor")
    rows, width = tokens.shape
    plots, patches, _ = memory.shape
    heads = width // HD
    parts = n
    heads_part = heads // parts
    halo_chunks = -(-(LONGEST - 1) // rows)
    halo_rows = halo_chunks * rows
    keys = halo_rows + rows

    def group(*mats):
        flat = mats[0] if len(mats) == 1 else jnp.concatenate(mats, axis=0)
        return flat.reshape(2, 2, 2, -1, width)

    shards = [
        group(self_query.T, self_key.T),
        group(self_value.T, self_output),
        group(cross_key.T, cross_value.T),
        group(cross_query.T, cross_output),
        group(hidden_gate.T),
        group(hidden_up.T),
        group(hidden_down),
    ]
    group_tokens = rows * n
    positions = jnp.arange(group_tokens, dtype=jnp.int32)
    table_ends = jnp.cumsum(table_lengths[0])
    table_ids = jnp.sum((positions[:, None] >= table_ends[None, :]).astype(jnp.int32), axis=1)
    table_index = jnp.arange(table_ends.shape[0], dtype=jnp.int32)
    token_plot = jnp.sum(
        jnp.where(table_ids[:, None] == table_index[None, :], table_plots[0][None, :], 0), axis=1
    )
    padded = jnp.concatenate([jnp.full((halo_rows,), -1, jnp.int32), table_ids])
    key_tables = lax.dynamic_slice_in_dim(padded, z * rows, keys)
    query_tables = key_tables[halo_rows:]
    key_at = jnp.arange(keys, dtype=jnp.int32)
    allowed = (key_tables[:, None] == query_tables[None, :]) & (
        key_at[:, None] <= halo_rows + jnp.arange(rows, dtype=jnp.int32)[None, :]
    )
    bias = jnp.where(allowed, 0.0, masked_value).astype(F32)
    plot_rows = token_plot.reshape(n, 1, rows)

    inputs = tokens.astype(F32)
    full, saved = forward(
        n, halo_chunks, tokens, bias, plot_rows, self_gain[None], cross_gain[None], memory, shards
    )
    (
        near, normed_near, self_q, self_k, self_kt, self_v, self_mix, self_logs, first_sum,
        normed_cross, q_all, cross_k, cross_kt, cross_v, cross_mix, cross_logs,
    ) = saved

    def unit(g, index, of):
        return full[g].reshape(n, of, -1, width)[:, index].reshape(-1, width)

    w_co = unit(3, 1, 2)
    w_gate, w_up, w_down = unit(4, 0, 1), unit(5, 0, 1), unit(6, 0, 1)

    cross_mix = cross_mix.reshape(width, rows)
    second_sum = first_sum + product(cross_mix, w_co, 0, 0)

    normed_hidden = norm_rows(second_sum, hidden_gain).astype(BF16)
    gate_pre = product(normed_hidden, w_gate, 1, 1)
    up_pre = product(normed_hidden, w_up, 1, 1)
    hidden_act = gated_unit(gate_pre, up_pre).astype(BF16)
    output = (second_sum + product(hidden_act, w_down, 1, 0)).astype(BF16)
    grad_down = product(hidden_act, cotangent, 0, 0).astype(BF16)
    grad_act = product(cotangent, w_down, 1, 1).astype(BF16).astype(F32)
    _, gated_pull = jax.vjp(gated_unit, gate_pre, up_pre)
    gate_back, up_back = gated_pull(grad_act)
    gate_back = gate_back.astype(BF16)
    up_back = up_back.astype(BF16)
    grad_gate = product(gate_back, normed_hidden, 0, 0).astype(BF16)
    grad_up = product(up_back, normed_hidden, 0, 0).astype(BF16)
    normed_back = product(gate_back, w_gate, 1, 0) + product(up_back, w_up, 1, 0)
    residual_back, gain_back_hidden = norm_back(second_sum, hidden_gain, normed_back)
    second_back = cotangent.astype(F32) + residual_back

    def split(*grads):
        stacked = [g.reshape(n, -1, width) for g in grads]
        flat = stacked[0] if len(stacked) == 1 else jnp.concatenate(stacked, axis=1)
        return flat.reshape(n, 2, 2, 2, -1, width)

    grad_rows = second_back.astype(BF16)
    mixed_back = product(w_co, grad_rows, 1, 1).astype(BF16)
    inner = jnp.sum(
        (cross_mix.astype(F32) * mixed_back.astype(F32)).reshape(parts, heads_part, HD, rows),
        axis=2,
    )
    rest = jnp.zeros((parts, 8 - 2 * heads_part, rows), F32)
    cross_stats = jnp.concatenate([cross_logs[:, :heads_part], inner, rest], axis=1)
    ins = (
        plot_rows, mixed_back.reshape(parts, heads_part * HD, rows), cross_stats, q_all, cross_k,
        cross_kt, cross_v, memory, normed_cross, cross_mix, grad_rows, second_back, first_sum,
        cross_gain[None], full[2], full[3],
    )
    hidden_sums, rest = cross_backward(
        n, extra, ins, [split(grad_gate), split(grad_up), split(grad_down)]
    )
    grad_memory, part_keys, part_query, first_back, g_first, gain_cross = rest

    gains = jnp.concatenate(
        [jnp.zeros((1, width), F32), gain_cross, gain_back_hidden[None], jnp.zeros((5, width), F32)]
    )
    ins = (
        bias, self_q, self_k, self_kt, self_v, self_mix, self_logs, near, normed_near, g_first,
        first_back, self_gain[None], gains, full[0], full[1],
    )
    sums, grad_tokens, gains = self_backward(
        n, extra, halo_chunks, ins, [part_query, part_keys]
    )

    def pair(summed):
        both = summed.reshape(2, -1, width).astype(F32)
        return both[0], both[1]

    g_gate, g_up, g_down = (summed.reshape(-1, width).astype(F32) for summed in hidden_sums)
    g_cq, g_co = pair(sums[0])
    g_ck, g_cv = pair(sums[1])
    g_so, g_sv = pair(sums[2])
    g_sq, g_sk = pair(sums[3])
    return (
        output, grad_tokens, grad_memory,
        g_sq.T, g_sk.T, g_sv.T, g_so,
        g_cq.T, g_ck.T, g_cv.T, g_co,
        g_gate.T, g_up.T, g_down,
        gains[0], gains[1], gains[2],
    )


def solution(mesh):
    in_specs = (
        P(("dp", "tensor"), None),
        P("dp", "tensor", None),
        P("dp", None),
        P("dp", None),
        P(),
        P(None, "tensor"),
        P(None, "tensor"),
        P(None, "tensor"),
        P("tensor", None),
        P(),
        P(None, "tensor"),
        P(None, "tensor"),
        P(None, "tensor"),
        P("tensor", None),
        P(),
        P(None, "tensor"),
        P(None, "tensor"),
        P("tensor", None),
        P(("dp", "tensor"), None),
    )
    out_specs = (
        P(("dp", "tensor"), None),
        P(("dp", "tensor"), None),
        P("dp", "tensor", None),
        P(None, "tensor"),
        P(None, "tensor"),
        P(None, "tensor"),
        P("tensor", None),
        P(None, "tensor"),
        P(None, "tensor"),
        P(None, "tensor"),
        P("tensor", None),
        P(None, "tensor"),
        P(None, "tensor"),
        P("tensor", None),
        P(),
        P(),
        P(),
    )
    return jax.shard_map(body, mesh=mesh, in_specs=in_specs, out_specs=out_specs, check_vma=False)
```

```python
import functools

import jax
import jax.numpy as jnp
from jax import lax
from jax.experimental import pallas as pl
from jax.experimental.pallas import tpu as pltpu
from jax.sharding import PartitionSpec as P

HD = 64
LONGEST = 512
F32 = jnp.float32
BF16 = jnp.bfloat16
MESH = pl.DeviceIdType.MESH
ANY = pl.BlockSpec(memory_space=pl.ANY)
VMEM = pl.BlockSpec(memory_space=pltpu.VMEM)
DMA = pltpu.SemaphoreType.DMA

epsilon = 1e-06
masked_value = -1e30


def product(first_op, second_op, first_dim, second_dim):
    return lax.dot_general(
        first_op,
        second_op,
        (((first_dim,), (second_dim,)), ((), ())),
        preferred_element_type=F32,
    )


def remote(src, dst, send_sem, recv_sem, device):
    return pltpu.make_async_remote_copy(
        src_ref=src,
        dst_ref=dst,
        send_sem=send_sem,
        recv_sem=recv_sem,
        device_id=device,
        device_id_type=MESH,
    )


def place():
    dp = lax.axis_index("dp")
    z = lax.axis_index("tensor")
    return dp, z, lax.rem(dp, 2), lax.rem(dp // 2, 2), lax.rem(dp // 4, 2)


def flipped(dp, bit):
    here = lax.rem(dp // (1 << bit), 2)
    return dp + (1 << bit) * (1 - 2 * here)


def greet(devices):
    barrier = pltpu.get_barrier_semaphore()
    for device in devices:
        pl.semaphore_signal(barrier, inc=1, device_id=device, device_id_type=MESH)
    pl.semaphore_wait(barrier, len(devices))


def greet_line(dp, z, n):
    barrier = pltpu.get_barrier_semaphore()

    @pl.when(z > 0)
    def _():
        pl.semaphore_signal(barrier, inc=1, device_id=(dp, z - 1), device_id_type=MESH)

    @pl.when(z < n - 1)
    def _():
        pl.semaphore_signal(barrier, inc=1, device_id=(dp, z + 1), device_id_type=MESH)

    inner = (z > 0) & (z < n - 1)

    @pl.when(inner)
    def _():
        pl.semaphore_wait(barrier, 2)

    @pl.when(jnp.logical_not(inner))
    def _():
        pl.semaphore_wait(barrier, 1)


class Gather:
    def __init__(self, n, mine, full, sems):
        self.n, self.mine, self.full, self.count = n, mine, full, len(full)
        self.us, self.ds, self.zr, self.as_, self.ar, self.bs, self.br, self.cs, self.cr, self.loc = sems
        self.dp, self.z, self.c, self.x, self.y = place()
        z = self.z
        inner = [1 + s // 2 if s % 2 == 0 else n - 1 - s // 2 for s in range(n - 1)]
        self.order = [
            jnp.where(z == 0, n - 1 - s, jnp.where(z == n - 1, 1 + s, inner[s]))
            for s in range(n - 1)
        ]

    def peers(self):
        others = [lax.rem(self.z + k, self.n) for k in range(1, self.n)]
        return [(self.dp, o) for o in others] + [(flipped(self.dp, b), self.z) for b in range(3)]

    def own(self, g):
        return pltpu.make_async_copy(self.mine[g], self.full[g].at[self.z], self.loc.at[g])

    def piece(self, g, k):
        zk = lax.rem(self.z + self.n - k, self.n)
        return self.full[g].at[zk, self.y, self.x, self.c]

    def source(self, g, k, own):
        if own and self.mine[g] is not None:
            return self.mine[g].at[self.y, self.x, self.c]
        return self.piece(g, k)

    def up(self, g, k, own=False):
        dev = (self.dp, lax.rem(self.z + 1, self.n))
        src = self.source(g, k, own)
        return remote(src, self.piece(g, k), self.us.at[g, k], self.zr.at[g, k], dev)

    def down(self, g, h, own=False):
        dev = (self.dp, lax.rem(self.z + self.n - 1, self.n))
        k = lax.rem(self.n - h, self.n)
        src = self.source(g, k, own)
        return remote(
            src, self.piece(g, k), self.ds.at[g, h], self.zr.at[g, self.n - 2 - h], dev
        )

    def arrived(self, g, k):
        piece = self.piece(g, k)
        return remote(piece, piece, self.us.at[g, 0], self.zr.at[g, k - 1], (self.dp, self.z))

    def second(self, g, s, incoming=False):
        k = self.order[s]
        zk = lax.rem(self.z + self.n - k, self.n)
        x, y, c = self.x, self.y, self.c
        if s % 2 == 1:
            there, bit = self.full[g].at[zk, y, 1 - x if incoming else x, c], 1
        else:
            there, bit = self.full[g].at[zk, 1 - y if incoming else y, x, c], 2
        dev = (flipped(self.dp, bit), self.z)
        return remote(there, there, self.as_.at[g, s], self.ar.at[g, s], dev)

    def third(self, g, s, incoming=False):
        k = self.order[s]
        zk = lax.rem(self.z + self.n - k, self.n)
        x, y, c = self.x, self.y, self.c
        if s % 2 == 1:
            there, bit = self.full[g].at[zk, 1 - y if incoming else y, :, c], 2
        else:
            there, bit = self.full[g].at[zk, :, 1 - x if incoming else x, c], 1
        dev = (flipped(self.dp, bit), self.z)
        return remote(there, there, self.bs.at[g, s], self.br.at[g, s], dev)

    def fourth(self, g, s, incoming=False):
        zk = lax.rem(self.z + self.n - self.order[s], self.n)
        there = self.full[g].at[zk, :, :, 1 - self.c if incoming else self.c]
        dev = (flipped(self.dp, 0), self.z)
        return remote(there, there, self.cs.at[g, s], self.cr.at[g, s], dev)

    def run(self, g, stage):
        z, n = self.z, self.n
        steps = range(n - 1)
        if stage == 0:
            if self.mine[g] is not None:
                self.own(g).start()

            @pl.when(z < n - 1)
            def _():
                self.up(g, 0, True).start()

            @pl.when(z > 0)
            def _():
                self.down(g, 0, True).start()

        elif stage == 1:
            for s in steps:
                k = self.order[s]
                self.arrived(g, k).wait_recv()

                @pl.when((k <= z) & (z < n - 1))
                def _(k=k):
                    self.up(g, k).start()

                @pl.when((k > z) & (z > 0))
                def _(k=k):
                    self.down(g, n - k).start()

                self.second(g, s).start()
        elif stage == 2:
            for s in steps:
                self.second(g, s, True).wait_recv()
                self.third(g, s).start()
        elif stage == 3:
            for s in steps:
                self.third(g, s, True).wait_recv()
                self.fourth(g, s).start()
        else:
            if self.mine[g] is not None:
                self.own(g).wait()
            for s in steps:
                self.fourth(g, s, True).wait_recv()

    def drain(self):
        z, n = self.z, self.n

        def of_group(g):
            for h in range(n - 1):

                @pl.when((z < n - 1) & (z >= h))
                def _(h=h):
                    self.up(g, h, h == 0).wait_send()

                @pl.when((z > 0) & (z + h < n))
                def _(h=h):
                    self.down(g, h, h == 0).wait_send()

                self.second(g, h).wait_send()
                self.third(g, h).wait_send()
                self.fourth(g, h).wait_send()

        for g in range(self.count):
            of_group(g)


def gather_sems(n, count):
    return [DMA((count, n - 1)) for _ in range(9)] + [DMA((count,))]


class Reduce:
    def __init__(self, n, extra, part, acc, rec1, rec2, rec3, rec4, fin, recx, sems, quarters):
        self.n, self.extra, self.count = n, extra, len(rec4)
        self.part, self.fin, self.recx, self.quarters = part, fin, recx, quarters
        self.rec1, self.rec2, self.rec3, self.rec4 = rec1, rec2, rec3, rec4
        self.sems = sems
        self.dp, self.z, self.c, self.x, self.y = place()
        self.ks = range(1, n)
        self.kept = acc
        self.started = []
        self.acc = []
        for g in range(self.count):
            if part[g] is None:
                self.acc.append(None)
            elif acc[g] is None:
                self.acc.append(part[g].at[:, :, :, self.c])
            else:
                self.acc.append(acc[g])

    def peers(self):
        others = [lax.rem(self.z + k, self.n) for k in self.ks]
        bits = range(3 + self.extra)
        return [(self.dp, o) for o in others] + [(flipped(self.dp, b), self.z) for b in bits]

    def lanes(self, g, half):
        width = self.rec4[g].shape[-1] // 2
        return slice(half * width, (half + 1) * width)

    def copies(self, stage, g, incoming=False):
        dp, z, c, x, y, n = self.dp, self.z, self.c, self.x, self.y, self.n
        acc, fin = self.acc[g], self.fin[g] if self.fin else None
        found = []
        if stage == 0:
            src, dst, dev = self.part[g].at[:, :, :, 1 - c], self.rec1[g], (flipped(dp, 0), z)
            found.append((src, dst, dev, 0))
        elif stage == 1:
            for half in range(2):
                at = self.lanes(g, half)
                src = acc.at[:, :, 1 - x, :, at] if half == 0 else acc.at[:, 1 - y, :, :, at]
                dev = (flipped(dp, 1 if half == 0 else 2), z)
                found.append((src, self.rec2[g].at[:, :, :, at], dev, 1 + half))
        elif stage == 2:
            for half in range(2):
                at = self.lanes(g, half)
                src = acc.at[:, 1 - y, x, :, at] if half == 0 else acc.at[:, y, 1 - x, :, at]
                dev = (flipped(dp, 2 if half == 0 else 1), z)
                found.append((src, self.rec3[g].at[:, :, at], dev, 3 + half))
        elif stage == 3:
            for k in self.ks:
                zk = lax.rem(z + k, n)
                slot = lax.rem(z + n - k, n) if incoming else z
                found.append((self.quarter(g, zk), self.rec4[g].at[slot], (dp, zk), 8 + k))
        elif stage == 4:
            for half in range(2):
                at = self.lanes(g, half)
                if half == 0:
                    src = fin.at[1 - y if incoming else y, x, c, :, at]
                else:
                    src = fin.at[y, 1 - x if incoming else x, c, :, at]
                found.append((src, src, (flipped(dp, 2 if half == 0 else 1), z), 5 + half))
        elif stage == 5:
            for half in range(2):
                at = self.lanes(g, half)
                if half == 0:
                    src = fin.at[:, 1 - x if incoming else x, c, :, at]
                else:
                    src = fin.at[1 - y if incoming else y, :, c, :, at]
                found.append((src, src, (flipped(dp, 1 if half == 0 else 2), z), 7 + half))
        else:
            src = fin.at[:, :, 1 - c if incoming else c]
            found.append((src, src, (flipped(dp, 0), z), 8 + n))
        return [
            remote(src, dst, self.sems[0].at[g, slot], self.sems[1].at[g, slot], dev)
            for src, dst, dev, slot in found
        ]

    def quarter(self, g, zz):
        if self.quarters[g] is not None:
            return self.quarters[g].at[zz]
        return self.acc[g].at[zz, self.y, self.x]

    def own(self, g):
        src = self.part[g].at[:, :, :, self.c]
        return pltpu.make_async_copy(src, self.acc[g], self.sems[4].at[g])

    def further(self, g, e):
        return remote(
            self.fin[g].at[self.y, self.x, self.c],
            self.recx[g].at[e],
            self.sems[2].at[g, e],
            self.sems[3].at[g, e],
            (flipped(self.dp, 3 + e), self.z),
        )

    def add(self, stage, g):
        n, x, y, c, z = self.n, self.x, self.y, self.c, self.z
        acc, fin = self.acc[g], self.fin[g] if self.fin else None
        kind = self.rec4[g].dtype
        if stage == 1:

            def step(i, carry):
                zz, yy, xx = i // 4, lax.rem(i // 2, 2), lax.rem(i, 2)
                total = acc[zz, yy, xx].astype(F32) + self.rec1[g][zz, yy, xx].astype(F32)
                acc[zz, yy, xx] = total.astype(kind)
                return carry

            lax.fori_loop(0, 4 * n, step, 0)
        elif stage == 2:

            def step(i, carry):
                zz, aa = i // 2, lax.rem(i, 2)
                for half in range(2):
                    at = self.lanes(g, half)
                    yy, xx = (aa, x) if half == 0 else (y, aa)
                    came = self.rec2[g][zz, aa, :, at].astype(F32)
                    acc[zz, yy, xx, :, at] = (acc[zz, yy, xx, :, at].astype(F32) + came).astype(kind)
                return carry

            lax.fori_loop(0, 2 * n, step, 0)
        elif stage == 3:

            def step(zz, carry):
                total = acc[zz, y, x].astype(F32) + self.rec3[g][zz].astype(F32)
                acc[zz, y, x] = total.astype(kind)
                return carry

            lax.fori_loop(0, n, step, 0)
        else:
            self.rec4[g][z] = self.quarter(g, z)[...]
            total = self.rec4[g][0].astype(F32)
            for k in self.ks:
                total = total + self.rec4[g][k].astype(F32)
            fin[y, x, c] = total.astype(kind)
            for e in range(self.extra):
                self.further(g, e).start()
                self.further(g, e).wait()
                total = fin[y, x, c].astype(F32) + self.recx[g][e].astype(F32)
                fin[y, x, c] = total.astype(kind)

    def begin(self, stage, g):
        for copy in self.copies(stage, g):
            copy.start()
        if (stage, g) not in self.started:
            self.started.append((stage, g))

    def end(self, stage, g):
        if stage == 0 and self.kept[g] is not None:
            self.own(g).wait()
        for copy in self.copies(stage, g, True):
            copy.wait_recv()
        if stage < 4:
            self.add(stage + 1, g)

    def run(self, g, stage):
        if stage == 0 and self.kept[g] is not None:
            self.own(g).start()
        if stage > 0:
            self.end(stage - 1, g)
        if stage <= 6:
            self.begin(stage, g)

    def drain(self):
        for stage, g in self.started:
            for copy in self.copies(stage, g):
                copy.wait_send()


def reduce_scratch(n, extra, shapes, kinds, kept, from_start):
    count = len(shapes)
    every = list(zip(shapes, kinds))
    used = [s for s, f in zip(every, from_start) if f]
    scratch = [pltpu.VMEM((n, 2, 2) + s, d) for (s, d), k in zip(every, kept) if k]
    scratch += [pltpu.VMEM((n, 2, 2) + s, d) for s, d in used]
    scratch += [pltpu.VMEM((n, 2) + s, d) for s, d in used]
    scratch += [pltpu.VMEM((n,) + s, d) for s, d in used]
    scratch += [pltpu.VMEM((n,) + s, d) for s, d in every]
    if extra:
        scratch += [pltpu.VMEM((extra,) + s, d) for s, d in every]
    scratch += [
        DMA((count, 9 + n)),
        DMA((count, 9 + n)),
        DMA((count, max(extra, 1))),
        DMA((count, max(extra, 1))),
        DMA((count,)),
    ]
    return scratch


def take_reduce(n, extra, part, fin, kept, quarters, refs):
    refs = list(refs)
    acc = [refs.pop(0) if k else None for k in kept]
    recs = []
    for _ in range(3):
        recs.append([refs.pop(0) if p is not None else None for p in part])
    recs.append([refs.pop(0) for _ in part])
    recx = [refs.pop(0) for _ in part] if extra else None
    sems = [refs.pop(0) for _ in range(5)]
    return Reduce(n, extra, part, acc, *recs, fin, recx, sems, quarters), refs


def both_plots(rows, plot_row):
    wide = rows.astype(F32)
    zero = jnp.zeros_like(wide)
    return jnp.concatenate(
        [jnp.where(plot_row == 0, wide, zero), jnp.where(plot_row == 0, zero, wide)], axis=0
    ).astype(BF16)


def own_plot(pair, plot_row):
    half = pair.shape[0] // 2
    return jnp.where(plot_row == 0, pair[:half], pair[half:])


def line_exchange(n, parts, z, dp, refs, compute, merge, finish, hook, before=None):
    own, spread, mine, from_right, from_left, sems = refs
    ups, upr, dns, dnr, rls, rlr, rrs, rrr = sems

    def up(j, p, i, start):
        src = own[i].at[p] if start else spread[i].at[j, p]
        return remote(
            src, spread[i].at[j, p], ups.at[i, j, p], upr.at[i, j, p], (dp, lax.rem(z + 1, n))
        )

    def down(j, p, i, start):
        src = own[i].at[p] if start else spread[i].at[j, p]
        return remote(
            src,
            spread[i].at[j, p],
            dns.at[i, j, p],
            dnr.at[i, j, p],
            (dp, lax.rem(z + n - 1, n)),
        )

    def back_left(j, p, i):
        return remote(
            mine[i].at[j, p],
            from_right[i].at[j, p],
            rls.at[i, j, p],
            rlr.at[i, j, p],
            (dp, lax.rem(z + n - 1, n)),
        )

    def back_right(j, p, i):
        return remote(
            mine[i].at[j, p],
            from_left[i].at[j, p],
            rrs.at[i, j, p],
            rrr.at[i, j, p],
            (dp, lax.rem(z + 1, n)),
        )

    out_kinds = range(len(own))
    back_kinds = range(len(mine))

    def send_own(p, carry):
        for i in out_kinds:

            @pl.when(z < n - 1)
            def _():
                up(z, p, i, True).start()

            @pl.when(z > 0)
            def _():
                down(z, p, i, True).start()

        return carry

    lax.fori_loop(0, parts, send_own, 0)
    if before is not None:
        before()

    def first(p, carry):
        for i in out_kinds:
            spread[i][z, p] = own[i][p]
        compute(z, p)
        return carry

    lax.fori_loop(0, parts, first, 0)

    def tick(t, carry):
        def one_part(p, inner):
            low = z - t
            high = z + t

            @pl.when((t < n) & (low >= 0))
            def _():
                for i in out_kinds:
                    up(low, p, i, False).wait_recv()

                    @pl.when(z < n - 1)
                    def _():
                        up(low, p, i, False).start()

                compute(low, p)

                @pl.when(z == n - 1)
                def _():
                    for i in back_kinds:
                        back_left(low, p, i).start()

            @pl.when((t < n) & (high < n))
            def _():
                for i in out_kinds:
                    down(high, p, i, False).wait_recv()

                    @pl.when(z > 0)
                    def _():
                        down(high, p, i, False).start()

                compute(high, p)

                @pl.when(z == 0)
                def _():
                    for i in back_kinds:
                        back_right(high, p, i).start()

            left_chunk = 2 * (n - 1) - z - t

            @pl.when((left_chunk >= 0) & (left_chunk < z) & (z < n - 1))
            def _():
                for i in back_kinds:
                    back_left(left_chunk, p, i).wait_recv()
                merge(left_chunk, p, from_right)
                for i in back_kinds:
                    back_left(left_chunk, p, i).start()

            right_chunk = t - z

            @pl.when((right_chunk < n) & (right_chunk > z) & (z > 0))
            def _():
                for i in back_kinds:
                    back_right(right_chunk, p, i).wait_recv()
                merge(right_chunk, p, from_left)
                for i in back_kinds:
                    back_right(right_chunk, p, i).start()

            return inner

        lax.fori_loop(0, parts, one_part, 0)
        hook(t)
        return carry

    hook(0)
    lax.fori_loop(1, 2 * n - 2, tick, 0)

    def last(p, carry):
        @pl.when(z > 0)
        def _():
            for i in back_kinds:
                back_right(z, p, i).wait_recv()
            merge(z, p, from_left)

        @pl.when(z < n - 1)
        def _():
            for i in back_kinds:
                back_left(z, p, i).wait_recv()
            merge(z, p, from_right)

        finish(p)
        return carry

    lax.fori_loop(0, parts, last, 0)

    def drain(p, carry):
        for j in range(n):
            for i in out_kinds:

                @pl.when((z < n - 1) & (z == j))
                def _(i=i, j=j):
                    up(j, p, i, True).wait_send()

                @pl.when((z < n - 1) & (z > j))
                def _(i=i, j=j):
                    up(j, p, i, False).wait_send()

                @pl.when((z > 0) & (z == j))
                def _(i=i, j=j):
                    down(j, p, i, True).wait_send()

                @pl.when((z > 0) & (z < j))
                def _(i=i, j=j):
                    down(j, p, i, False).wait_send()

            for i in back_kinds:

                @pl.when(z > j)
                def _(i=i, j=j):
                    back_left(j, p, i).wait_send()

                @pl.when(z < j)
                def _(i=i, j=j):
                    back_right(j, p, i).wait_send()

        return carry

    lax.fori_loop(0, parts, drain, 0)


def line_sems(n, parts, out_kinds, back_kinds):
    return [DMA((out_kinds, n, parts))] * 4 + [DMA((back_kinds, n, parts))] * 4


def unit_rows(ref, zz, which):
    block = ref[zz, which]
    return block.reshape(-1, block.shape[-1])


def two_units(ref, pair, which):
    return jnp.concatenate(
        [unit_rows(ref, 2 * pair, which), unit_rows(ref, 2 * pair + 1, which)], axis=0
    )


def normed_rows(rows, gain):
    inverse = lax.rsqrt(jnp.mean(rows * rows, axis=-1, keepdims=True) + epsilon)
    return rows * inverse * gain


def half_lanes(first, second, which):
    lane = lax.broadcasted_iota(jnp.int32, first.shape, 1)
    if which == 0:
        return jnp.where(lane < HD, first, pltpu.roll(second, HD, 1))
    return jnp.where(lane < HD, pltpu.roll(first, HD, 1), second)


def table_at(position, lengths, count):
    table = jnp.zeros(position.shape, jnp.int32)
    end = 0
    for t in range(count):
        end = end + lengths[0, t]
        table = table + (position >= end).astype(jnp.int32)
    return table


def forward_kernel(n, count, halo_chunks, *refs):
    (
        lengths, table_plots, tok, cot, self_gain, cross_gain, hidden_gain, mem,
        w_ck, w_cv, w_sq, w_sk, w_sv, w_so, w_cq, w_co,
    ) = refs[:16]
    mine = [None] * 4 + list(refs[16 : 16 + count - 4])
    at = 12 + count
    full_out = refs[at : at + 4]
    at += 4
    (
        bias, plots, near, normed, self_q, self_k, self_kt, self_v, self_mix, self_logs, first_sum,
        normed_cross, q_all, cross_k, cross_kt, cross_v, o_ref,
        output, normed_hidden, hidden, gate_back, up_back, second_back, grad_rows, do_ref, stats,
        gain_hidden,
    ) = refs[at : at + 27]
    at += 27
    full = refs[at : at + count]
    at += count
    (
        halo, self_vt, cross_vt, cross_q, o_mine, l_mine, o_right, l_right, o_left, l_left,
        down_sum, back_sum, second_sum,
    ) = refs[at : at + 13]
    at += 13
    line = refs[at : at + 8]
    at += 8
    gather_refs = refs[at : at + 10]
    hs, hr, outs = refs[at + 10 :]
    rows, width = tok.shape
    heads = width // HD
    parts = n
    heads_part = heads // parts
    rows_part = heads_part * HD
    scale = HD ** (-0.5)
    dp, z, c, x, y = place()
    gather = Gather(n, mine, full, gather_refs)
    greet(gather.peers())

    def halo_copy(i):
        src = tok if i == 0 else halo.at[halo_chunks - i]
        dst = halo.at[halo_chunks - 1 - i]
        return remote(src, dst, hs.at[i], hr.at[i], (dp, lax.rem(z + 1, n)))

    def own_units(g, first, second):
        full[g][z, 0] = as_unit(first[...])
        full[g][z, 1] = as_unit(second[...])

    own_units(0, w_ck, w_cv)
    gather.run(0, 0)
    own_units(1, w_sq, w_sk)
    gather.run(1, 0)

    @pl.when(z < n - 1)
    def _():
        halo_copy(0).start()

    own_units(2, w_sv, w_so)
    gather.run(2, 0)
    own_units(3, w_cq, w_co)
    gather.run(3, 0)

    halo[halo_chunks] = tok[...]
    for i in range(halo_chunks):

        @pl.when(z <= i)
        def _(i=i):
            halo[halo_chunks - 1 - i] = jnp.zeros((rows, width), BF16)

    keys = bias.shape[0]
    held_tables = lengths.shape[1]
    first_key = z * rows - halo_chunks * rows
    key_at = lax.broadcasted_iota(jnp.int32, (keys, rows), 0) + first_key
    query_at = lax.broadcasted_iota(jnp.int32, (1, rows), 1) + z * rows
    same = table_at(key_at, lengths, held_tables) == table_at(query_at, lengths, held_tables)
    allowed = same & (key_at <= query_at) & (key_at >= 0)
    bias[...] = jnp.where(allowed, 0.0, masked_value)
    for j in range(n):
        tables = table_at(
            lax.broadcasted_iota(jnp.int32, (1, rows), 1) + j * rows, lengths, held_tables
        )
        plot = jnp.zeros((1, rows), jnp.int32)
        for t in range(held_tables):
            plot = jnp.where(tables == t, table_plots[0, t], plot)
        plots[j] = plot

    gather.run(0, 1)
    gather.run(1, 1)
    gather.run(0, 2)
    for i in range(halo_chunks):

        @pl.when(z > i)
        def _(i=i):
            halo_copy(i).wait_recv()

        if i + 1 < halo_chunks:

            @pl.when((z > i) & (z < n - 1))
            def _(i=i):
                halo_copy(i + 1).start()

        if i == 0:
            gather.run(2, 1)
            gather.run(1, 2)
            gather.run(0, 3)
    gather.run(3, 1)
    gather.run(2, 2)
    gather.run(1, 3)
    gather.run(4, 0)

    def norm_chunk(i, carry):
        at_rows = pl.ds(pl.multiple_of(i * rows, rows), rows)
        near[at_rows, :] = halo[i]
        normed[at_rows, :] = normed_rows(halo[i].astype(F32), self_gain[...]).astype(BF16)
        return carry

    gather.run(0, 4)

    plots_held = mem.shape[0]

    def flat_part(which, out):
        def step(zz, carry):
            for p in range(plots_held):
                rows_t = product(unit_rows(full[0], zz, which), mem[p], 1, 1).astype(BF16)
                for hh in range(heads_part):
                    at_head = slice(hh * HD, (hh + 1) * HD)
                    out[zz * heads_part + hh, p * HD : (p + 1) * HD, :] = rows_t[at_head]
            return carry

        lax.fori_loop(0, n, step, 0)

    def tall_part(which, out):
        for pair in range(n // 2):
            weights = two_units(full[0], pair, which)
            first = product(mem[0], weights, 1, 1)
            second = product(mem[1], weights, 1, 1)
            for hh in range(2 * heads_part):
                cols = slice((hh // 2) * 2 * HD, (hh // 2 + 1) * 2 * HD)
                both = half_lanes(first[:, cols], second[:, cols], hh % 2)
                out[pair * 2 * heads_part + hh] = both.astype(BF16)

    flat_part(1, cross_vt)
    gather.run(3, 2)
    gather.run(2, 3)
    gather.run(1, 4)
    tall_part(0, cross_k)
    lax.fori_loop(0, halo_chunks + 1, norm_chunk, 0)

    own_rows = slice(halo_chunks * rows, (halo_chunks + 1) * rows)

    def query_part(zz, carry):
        at_part = pl.ds(pl.multiple_of(zz * rows_part, rows_part), rows_part)
        projected = product(unit_rows(full[1], zz, 0), normed[own_rows, :], 1, 1)
        self_q[at_part, :] = (projected.astype(BF16).astype(F32) * scale).astype(BF16)
        return carry

    lax.fori_loop(0, n, query_part, 0)

    def tall(out, g, which):
        for pair in range(n // 2):
            cols = slice(pair * 2 * rows_part, (pair + 1) * 2 * rows_part)

            def chunk(i, carry, pair=pair, cols=cols):
                at_rows = pl.ds(pl.multiple_of(i * rows, rows), rows)
                weights = two_units(full[g], pair, which)
                out[at_rows, cols] = product(normed[at_rows, :], weights, 1, 1).astype(BF16)
                return carry

            lax.fori_loop(0, halo_chunks + 1, chunk, 0)

    tall(self_k, 1, 1)
    gather.run(3, 3)
    gather.run(2, 4)
    gather.run(5, 0)
    gather.run(4, 1)

    def flat(out, g, which):
        def step(zz, carry):
            at_part = pl.ds(pl.multiple_of(zz * rows_part, rows_part), rows_part)
            weights = unit_rows(full[g], zz, which)
            out[at_part, :] = product(weights, normed[...], 1, 1).astype(BF16)
            return carry

        lax.fori_loop(0, n, step, 0)

    flat(self_vt, 2, 0)

    def self_pair(pair, carry):
        cols = pl.ds(pl.multiple_of(pair * 2 * HD, 2 * HD), 2 * HD)
        for which in range(2):
            at_head = pl.ds(pl.multiple_of((2 * pair + which) * HD, HD), HD)
            scores = jnp.dot(
                self_k[:, cols], alone(self_q[at_head, :], which), preferred_element_type=F32
            )
            scores = scores + bias[...]
            top = jnp.max(scores, axis=0, keepdims=True)
            powers = jnp.exp(scores - top)
            total = jnp.sum(powers, axis=0, keepdims=True)
            mixed = jnp.dot(self_vt[at_head, :], powers.astype(BF16), preferred_element_type=F32)
            self_mix[at_head, :] = (mixed / total).astype(BF16)
            self_logs[pair, which : which + 1, :] = top + jnp.log(total)
        return carry

    lax.fori_loop(0, heads // 4, self_pair, 0)
    gather.run(6, 0)
    gather.run(5, 1)
    gather.run(4, 2)
    lax.fori_loop(heads // 4, heads // 2, self_pair, 0)

    total = tok[...].astype(F32)
    for zz in range(n):
        at_part = slice(zz * rows_part, (zz + 1) * rows_part)
        total = total + product(self_mix[at_part, :], unit_rows(full[2], zz, 1), 0, 0)
    first_sum[...] = total
    normed_cross[...] = normed_rows(total, cross_gain[...]).astype(BF16)
    gather.run(3, 4)

    def cross_query_part(zz, carry):
        projected = product(unit_rows(full[3], zz, 0), normed_cross[...], 1, 1)
        cross_q[zz] = (projected.astype(BF16).astype(F32) * scale).astype(BF16)
        return carry

    lax.fori_loop(0, n, cross_query_part, 0)

    def compute(j, p):
        plot_row = plots[j]
        for hh in range(heads_part):
            h = p * heads_part + hh
            q_pair = both_plots(q_all[j, p, hh * HD : (hh + 1) * HD, :], plot_row)
            scores = jnp.dot(cross_k[h], q_pair, preferred_element_type=F32)
            top = jnp.max(scores, axis=0, keepdims=True)
            powers = jnp.exp(scores - top)
            total = jnp.sum(powers, axis=0, keepdims=True)
            mixed = jnp.dot(cross_vt[h], powers.astype(BF16), preferred_element_type=F32)
            mixed = own_plot(mixed, plot_row) / total
            o_mine[j, p, hh * HD : (hh + 1) * HD, :] = mixed.astype(BF16)
            l_mine[j, p, hh : hh + 1, :] = top + jnp.log(total)

    def merge(j, p, arrived):
        for hh in range(heads_part):
            at_head = slice(hh * HD, (hh + 1) * HD)
            log_a = l_mine[j, p, hh : hh + 1, :]
            log_b = arrived[1][j, p, hh : hh + 1, :]
            top = jnp.maximum(log_a, log_b)
            share_a = jnp.exp(log_a - top)
            share_b = jnp.exp(log_b - top)
            total = share_a + share_b
            mixed = o_mine[j, p, at_head, :].astype(F32) * (share_a / total)
            mixed = mixed + arrived[0][j, p, at_head, :].astype(F32) * (share_b / total)
            o_mine[j, p, at_head, :] = mixed.astype(BF16)
            l_mine[j, p, hh : hh + 1, :] = top + jnp.log(total)

    def finish(p):
        o_ref[p] = o_mine[z, p]

    def keep(g):
        return pltpu.make_async_copy(full[g], full_out[g], outs.at[g])

    schedule = {
        0: [(6, 1), (5, 2), (4, 3)],
        1: [(6, 2), (5, 3)],
        2: [(6, 3)],
    }

    def hook(t):
        for step, work in schedule.items():

            @pl.when(t == step)
            def _(step=step, work=work):
                for g, stage in work:
                    gather.run(g, stage)
                if step == 0:
                    for g in range(4):
                        keep(g).start()

        @pl.when(t == 2 * n - 3)
        def _():
            flat_part(0, cross_kt)
            tall_part(1, cross_v)
            flat(self_kt, 1, 1)
            tall(self_v, 2, 0)

    exchange = ([cross_q], [q_all], [o_mine, l_mine], [o_right, l_right], [o_left, l_left], line)
    line_exchange(n, parts, z, dp, exchange, compute, merge, finish, hook)

    total = first_sum[...]
    for zz in range(n):
        total = total + product(o_ref[zz], unit_rows(full[3], zz, 1), 0, 0)
    second_sum[...] = total
    normed_hidden[...] = normed_rows(total, hidden_gain[...]).astype(BF16)
    down_sum[...] = jnp.zeros((rows, width), F32)
    back_sum[...] = jnp.zeros((rows, width), F32)
    for g in range(4, 7):
        gather.run(g, 4)
    slope = (2.0 / 3.141592653589793) ** 0.5
    bend = 0.044715

    def whole(g, zz):
        block = full[g][zz]
        return block.reshape(-1, block.shape[-1])

    def hidden_part(zz, carry):
        gate = product(normed_hidden[...], whole(4, zz), 1, 0)
        up = product(normed_hidden[...], whole(5, zz), 1, 0)
        act_back = product(cot[...], whole(6, zz), 1, 1).astype(BF16).astype(F32)
        square = gate * gate
        curve = jnp.tanh(slope * (gate + bend * square * gate))
        cdf = 0.5 * (1.0 + curve)
        act = gate * cdf
        turn = cdf + 0.5 * gate * (1.0 - curve * curve) * slope * (1.0 + 3.0 * bend * square)
        here = (act * up).astype(BF16)
        to_gate = (act_back * up * turn).astype(BF16)
        to_up = (act_back * act).astype(BF16)
        hidden[zz] = here
        gate_back[zz] = to_gate
        up_back[zz] = to_up
        down_sum[...] += product(here, whole(6, zz), 1, 0)
        back_sum[...] += product(to_gate, whole(4, zz), 1, 1) + product(to_up, whole(5, zz), 1, 1)
        return carry

    lax.fori_loop(0, n, hidden_part, 0)
    output[...] = (second_sum[...] + down_sum[...]).astype(BF16)
    residual, gain_back = norm_gradient(second_sum[...], hidden_gain[...], back_sum[...])
    gain_hidden[...] = gain_back
    total = cot[...].astype(F32) + residual
    second_back[...] = total
    grad_rows[...] = total.astype(BF16)

    def mixed_part(zz, carry):
        mixed = product(unit_rows(full[3], zz, 1), grad_rows[...], 1, 1).astype(BF16)
        do_ref[zz] = mixed
        for hh in range(heads_part):
            at_head = slice(hh * HD, (hh + 1) * HD)
            inner = mixed[at_head].astype(F32) * o_ref[zz, at_head, :].astype(F32)
            row = heads_part + hh
            stats[zz, row : row + 1, :] = jnp.sum(inner, axis=0, keepdims=True)
            stats[zz, hh : hh + 1, :] = l_mine[z, zz, hh : hh + 1, :]
        stats[zz, 2 * heads_part : 8, :] = jnp.zeros((8 - 2 * heads_part, rows), F32)
        return carry

    lax.fori_loop(0, n, mixed_part, 0)
    gather.drain()
    for g in range(4):
        keep(g).wait()
    for i in range(halo_chunks):

        @pl.when((z >= i) & (z < n - 1))
        def _(i=i):
            halo_copy(i).wait_send()


def forward(n, halo_chunks, ins, shards):
    tokens, memory = ins[2], ins[7]
    rows, width = tokens.shape
    keys = (halo_chunks + 1) * rows
    heads = width // HD
    parts = n
    rows_part = width // parts
    held, patches, _ = memory.shape
    unit = rows_part // 4
    full = [(n, 2, 2, 2, unit, width)] * 4 + [(n,) + s.shape for s in shards]
    count = len(full)
    struct = jax.ShapeDtypeStruct
    out_shape = [struct(f, BF16) for f in full[:4]] + [
        struct((keys, rows), F32),
        struct((n, 1, rows), jnp.int32),
        struct((keys, width), BF16),
        struct((keys, width), BF16),
        struct((width, rows), BF16),
        struct((keys, width), BF16),
        struct((width, keys), BF16),
        struct((keys, width), BF16),
        struct((width, rows), BF16),
        struct((heads // 2, 8, rows), F32),
        struct((rows, width), F32),
        struct((rows, width), BF16),
        struct((n, parts, rows_part, rows), BF16),
        struct((heads, patches, held * HD), BF16),
        struct((heads, held * HD, patches), BF16),
        struct((heads, patches, held * HD), BF16),
        struct((parts, rows_part, rows), BF16),
        struct((rows, width), BF16),
        struct((rows, width), BF16),
        struct((n, rows, shards[0].shape[-1]), BF16),
        struct((n, rows, shards[0].shape[-1]), BF16),
        struct((n, rows, shards[0].shape[-1]), BF16),
        struct((rows, width), F32),
        struct((rows, width), BF16),
        struct((parts, rows_part, rows), BF16),
        struct((parts, 8, rows), F32),
        struct((1, width), F32),
    ]
    scratch = [pltpu.VMEM(f, BF16) for f in full]
    scratch += [
        pltpu.VMEM((halo_chunks + 1, rows, width), BF16),
        pltpu.VMEM((width, keys), BF16),
        pltpu.VMEM((heads, held * HD, patches), BF16),
        pltpu.VMEM((parts, rows_part, rows), BF16),
    ]
    for _ in range(3):
        scratch += [
            pltpu.VMEM((n, parts, rows_part, rows), BF16),
            pltpu.VMEM((n, parts, 8, rows), F32),
        ]
    scratch += [pltpu.VMEM((rows, width), F32)] * 3
    scratch += line_sems(n, parts, 1, 2)
    scratch += gather_sems(n, count)
    scratch += [DMA((halo_chunks,)), DMA((halo_chunks,)), DMA((4,))]
    smem = pl.BlockSpec(memory_space=pltpu.SMEM)
    out = pl.pallas_call(
        functools.partial(forward_kernel, n, count, halo_chunks),
        out_shape=out_shape,
        in_specs=[smem] * 2 + [VMEM] * 14 + [ANY] * (count - 4),
        out_specs=[ANY] * 4 + [VMEM] * 27,
        scratch_shapes=scratch,
        compiler_params=pltpu.CompilerParams(
            collective_id=0, has_side_effects=True, vmem_limit_bytes=63 << 20
        ),
        name="forward",
    )(*ins, *shards)
    return out[:4], out[4:]


def norm_gradient(rows, gain, back):
    inverse = lax.rsqrt(jnp.mean(rows * rows, axis=-1, keepdims=True) + epsilon)
    unit = rows * inverse
    scaled = back * gain
    inner = jnp.mean(scaled * unit, axis=-1, keepdims=True)
    return inverse * (scaled - unit * inner), jnp.sum(back * unit, axis=0, keepdims=True)


def as_unit(rows_192):
    rows, width = rows_192.shape
    return rows_192.reshape(2, 2, rows // 4, width)


def cross_backward_kernel(n, count, *refs):
    (
        plots, do_ref, st_ref, q_all, k_ref, kt_ref, v_ref, mem, normed_cross, cross_mix, grad_rows,
        second_back, first_sum, cross_gain, w_keys, w_query,
        normed_hidden, hidden, gate_back, up_back, cot,
    ) = refs[:21]
    at = 21
    quarters = refs[at : at + count]
    grad_mem, part_keys, part_query, first_back, g_first, gain_cross = refs[
        at + count : at + count + 6
    ]
    rest = refs[at + count + 6 :]
    part, rest = rest[:count], rest[count:]
    reduce, rest = take_reduce(n, 0, part, None, [False] * count, [None] * count, rest)
    do_all, st_all, q_mine, q_right, q_left, dk_ref, dv_ref, k_back, v_back = rest[:9]
    line = rest[9:]
    dp, z, c, x, y = place()
    parts, rows_part, rows = do_ref.shape
    width = parts * rows_part
    heads_part = rows_part // HD
    heads = parts * heads_part
    held = mem.shape[0]
    scale = HD ** (-0.5)
    greet([(dp, lax.rem(z + k, n)) for k in range(1, n)] + [(flipped(dp, b), z) for b in range(3)])

    def clear(h, carry):
        dk_ref[h] = jnp.zeros(dk_ref.shape[1:], F32)
        dv_ref[h] = jnp.zeros(dv_ref.shape[1:], F32)
        return carry

    def compute(j, p):
        plot_row = plots[j]
        for hh in range(heads_part):
            h = p * heads_part + hh
            at_head = slice(hh * HD, (hh + 1) * HD)
            q_pair = both_plots(q_all[j, p, at_head, :], plot_row)
            do_pair = both_plots(do_all[j, p, at_head, :], plot_row)
            scores = jnp.dot(k_ref[h], q_pair, preferred_element_type=F32)
            chances = jnp.exp(scores - st_all[j, p, hh : hh + 1, :])
            prob_back = jnp.dot(v_ref[h], do_pair, preferred_element_type=F32)
            inner = st_all[j, p, heads_part + hh : heads_part + hh + 1, :]
            score_back = (chances * (prob_back - inner)).astype(BF16)
            q_back = jnp.dot(kt_ref[h], score_back, preferred_element_type=F32)
            q_mine[j, p, at_head, :] = (own_plot(q_back, plot_row) * scale).astype(BF16)
            dk_ref[h] += product(score_back, q_pair, 1, 1)
            dv_ref[h] += product(chances.astype(BF16), do_pair, 1, 1)

    def merge(j, p, arrived):
        total = q_mine[j, p].astype(F32) + arrived[0][j, p].astype(F32)
        q_mine[j, p] = total.astype(BF16)

    def finish(p):
        pass

    def hidden_gradients():
        def step(zz, carry):
            grad = product(normed_hidden[...], gate_back[zz], 0, 0)
            part[0][zz] = grad.astype(BF16).reshape(part[0].shape[1:])
            grad = product(normed_hidden[...], up_back[zz], 0, 0)
            part[1][zz] = grad.astype(BF16).reshape(part[1].shape[1:])
            grad = product(hidden[zz], cot[...], 0, 0)
            part[2][zz] = grad.astype(BF16).reshape(part[2].shape[1:])
            return carry

        lax.fori_loop(0, n, step, 0)

    def patch_gradients():
        for source, out in ((dk_ref, k_back), (dv_ref, v_back)):

            def pair_step(i, carry, source=source, out=out):
                even, odd = source[2 * i], source[2 * i + 1]
                lane = lax.broadcasted_iota(jnp.int32, even.shape, 1)
                cols = pl.ds(pl.multiple_of(i * 2 * HD, 2 * HD), 2 * HD)
                out[0, :, cols] = jnp.where(lane < HD, even, pltpu.roll(odd, HD, 1)).astype(BF16)
                out[1, :, cols] = jnp.where(lane < HD, pltpu.roll(even, HD, 1), odd).astype(BF16)
                return carry

            lax.fori_loop(0, heads // 2, pair_step, 0)
        for which, back in enumerate((k_back, v_back)):
            for pair in range(n // 2):
                cols = slice(pair * 2 * rows_part, (pair + 1) * 2 * rows_part)
                grad = sum(product(back[p, :, cols], mem[p], 0, 0) for p in range(held))
                grad = grad.astype(BF16)
                part_keys[2 * pair, which] = as_unit(grad[:rows_part])
                part_keys[2 * pair + 1, which] = as_unit(grad[rows_part:])

        def memory_step(i, carry):
            p, at_rows = i // 2, pl.ds(pl.multiple_of(lax.rem(i, 2) * rows, rows), rows)
            total = 0.0
            for which, back in enumerate((k_back, v_back)):
                for pair in range(n // 2):
                    cols = slice(pair * 2 * rows_part, (pair + 1) * 2 * rows_part)
                    weights = two_units(w_keys, pair, which)
                    total = total + product(back[p, at_rows, cols], weights, 1, 0)
            grad_mem[p, at_rows, :] = total.astype(BF16)
            return carry

        lax.fori_loop(0, held * (mem.shape[1] // rows), memory_step, 0)

    def hook(t):
        @pl.when(t == 0)
        def _():
            for g in range(count):
                reduce.run(g, 1)

        @pl.when(t == 2 * n - 4)
        def _():
            for g in range(count):
                reduce.run(g, 2)

        @pl.when(t == 2 * n - 3)
        def _():
            patch_gradients()

    def before():
        lax.fori_loop(0, heads, clear, 0)
        hidden_gradients()
        for g in range(count):
            reduce.run(g, 0)

    exchange = ([do_ref, st_ref], [do_all, st_all], [q_mine], [q_right], [q_left], line)
    line_exchange(n, parts, z, dp, exchange, compute, merge, finish, hook, before)

    back = 0.0
    for zz in range(n):
        mine = q_mine[z, zz]
        part_query[zz, 0] = as_unit(product(mine, normed_cross[...], 1, 0).astype(BF16))
        part_query[zz, 1] = as_unit(product(cross_mix[zz], grad_rows[...], 1, 0).astype(BF16))
        back = back + product(mine, unit_rows(w_query, zz, 0), 0, 0)
    residual, gain_back = norm_gradient(first_sum[...], cross_gain[...], back)
    total = second_back[...] + residual
    first_back[...] = total
    g_first[...] = total.astype(BF16)
    gain_cross[...] = gain_back
    for g in range(count):
        reduce.end(2, g)
        quarters[g][...] = reduce.acc[g][:, y, x]
    reduce.drain()


def cross_backward(n, ins, shapes):
    do, mem = ins[1], ins[7]
    parts, rows_part, rows = do.shape
    width = parts * rows_part
    heads = width // HD
    held, patches, _ = mem.shape
    count = len(shapes)
    struct = jax.ShapeDtypeStruct
    unit = width // n // 4
    scratch = [pltpu.VMEM((n, 2, 2, 2) + s, BF16) for s in shapes]
    scratch += reduce_scratch(n, 0, shapes, [BF16] * count, [False] * count, [True] * count)
    scratch += [
        pltpu.VMEM((n, parts, rows_part, rows), BF16),
        pltpu.VMEM((n, parts, 8, rows), F32),
        pltpu.VMEM((n, parts, rows_part, rows), BF16),
        pltpu.VMEM((n, parts, rows_part, rows), BF16),
        pltpu.VMEM((n, parts, rows_part, rows), BF16),
        pltpu.VMEM((heads, patches, held * HD), F32),
        pltpu.VMEM((heads, patches, held * HD), F32),
        pltpu.VMEM((held, patches, width), BF16),
        pltpu.VMEM((held, patches, width), BF16),
    ]
    scratch += line_sems(n, parts, 2, 1)
    out = pl.pallas_call(
        functools.partial(cross_backward_kernel, n, count),
        out_shape=[struct((n,) + s, BF16) for s in shapes]
        + [
            struct(mem.shape, BF16),
            struct((n, 2, 2, 2, unit, width), BF16),
            struct((n, 2, 2, 2, unit, width), BF16),
            struct((rows, width), F32),
            struct((rows, width), BF16),
            struct((1, width), F32),
        ],
        in_specs=[VMEM] * 21,
        out_specs=[VMEM] * (count + 6),
        scratch_shapes=scratch,
        compiler_params=pltpu.CompilerParams(
            collective_id=1, has_side_effects=True, vmem_limit_bytes=63 << 20
        ),
        name="cross_backward",
    )(*ins)
    return out[:count], out[count:]


def alone(rows, which):
    zero = jnp.zeros_like(rows)
    return jnp.concatenate([rows, zero] if which == 0 else [zero, rows], axis=0)


def self_backward_kernel(n, extra, halo_chunks, *refs):
    (
        bias, q_ref, k_ref, kt_ref, v_ref, mix, logs, near, normed, g_first, first_back, self_gain,
        gain_cross, gain_hidden, w_qk, w_vo,
    ) = refs[:16]
    cross_parts = refs[16:18]
    sums = refs[18:21]
    fin = list(refs[21:28])
    grad_tokens, gain_out = refs[28:30]
    own_parts = refs[30:32]
    gain_part, gain_fin = refs[32:34]
    part = list(cross_parts) + list(own_parts) + [None] * 3 + [gain_part]
    kept = [True, True] + [False] * 6
    quarters = [None] * 4 + list(sums) + [None]
    reduce, rest = take_reduce(n, extra, part, fin + [gain_fin], kept, quarters, refs[34:])
    do_ref, dq_ref, dk_ref, dv_ref, own_back, csend, crecv, gain_rows, hs, hr = rest
    dp, z, c, x, y = place()
    rows, width = g_first.shape
    heads = width // HD
    rows_part = width // n
    scale = HD ** (-0.5)
    own_rows = slice(halo_chunks * rows, (halo_chunks + 1) * rows)
    hidden_groups, cross_groups, self_groups = (4, 5, 6), (0, 1), (2, 3, 7)

    def all_run(groups, stage):
        for g in groups:
            reduce.run(g, stage)

    greet(reduce.peers())
    all_run(cross_groups, 0)
    for g in hidden_groups:
        reduce.begin(3, g)

    def do_part(zz, carry):
        at_part = pl.ds(pl.multiple_of(zz * rows_part, rows_part), rows_part)
        do_ref[at_part, :] = product(unit_rows(w_vo, zz, 1), g_first[...], 1, 1).astype(BF16)
        return carry

    lax.fori_loop(0, n, do_part, 0)
    all_run(cross_groups, 1)

    def pair_step(pair, carry):
        cols = pl.ds(pl.multiple_of(pair * 2 * HD, 2 * HD), 2 * HD)
        dk, dv = 0.0, 0.0
        for which in range(2):
            at_head = pl.ds(pl.multiple_of((2 * pair + which) * HD, HD), HD)
            q_pair = alone(q_ref[at_head, :], which)
            do_head = do_ref[at_head, :]
            inner = jnp.sum(
                do_head.astype(F32) * mix[at_head, :].astype(F32), axis=0, keepdims=True
            )
            do_pair = alone(do_head, which)
            scores = jnp.dot(k_ref[:, cols], q_pair, preferred_element_type=F32)
            chances = jnp.exp(scores + bias[...] - logs[pair, which : which + 1, :])
            prob_back = jnp.dot(v_ref[:, cols], do_pair, preferred_element_type=F32)
            score_back = (chances * (prob_back - inner)).astype(BF16)
            q_back = jnp.dot(kt_ref[at_head, :], score_back, preferred_element_type=F32)
            dq_ref[at_head, :] = (q_back * scale).astype(BF16)
            dk = dk + product(score_back, q_pair, 1, 1)
            dv = dv + product(chances.astype(BF16), do_pair, 1, 1)
        dk_ref[:, cols] = dk.astype(BF16)
        dv_ref[:, cols] = dv.astype(BF16)
        return carry

    lax.fori_loop(0, heads // 3, pair_step, 0)
    all_run(cross_groups, 2)
    lax.fori_loop(heads // 3, heads // 2, pair_step, 0)

    def halo_copy(i):
        far = halo_chunks - i
        dev = (dp, lax.rem(z + n - far, n))
        return remote(csend.at[i], crecv.at[i], hs.at[i], hr.at[i], dev)

    gain_self = jnp.zeros((1, width), F32)
    for i in range(halo_chunks + 1):
        at_rows = slice(i * rows, (i + 1) * rows)
        back = 0.0
        for pair in range(n // 2):
            cols = slice(pair * 2 * rows_part, (pair + 1) * 2 * rows_part)
            back = back + product(dk_ref[at_rows, cols], two_units(w_qk, pair, 1), 1, 0)
            back = back + product(dv_ref[at_rows, cols], two_units(w_vo, pair, 0), 1, 0)
        if i < halo_chunks:
            csend[i] = back.astype(BF16)

            @pl.when(z >= halo_chunks - i)
            def _(i=i):
                halo_copy(i).start()

        else:
            for zz in range(n):
                at_part = slice(zz * rows_part, (zz + 1) * rows_part)
                back = back + product(dq_ref[at_part, :], unit_rows(w_qk, zz, 0), 0, 0)
            own_back[...] = back
        here = near[at_rows, :].astype(F32)
        inverse = lax.rsqrt(jnp.mean(here * here, axis=-1, keepdims=True) + epsilon)
        gain_self = gain_self + jnp.sum(back * here * inverse, axis=0, keepdims=True)

    all_run(hidden_groups, 4)
    all_run(cross_groups, 3)

    lanes = gain_rows.shape[1]
    gain_rows[...] = jnp.zeros(gain_rows.shape, F32)
    for i, gain in enumerate((gain_self, gain_cross[...], gain_hidden[...])):
        for j in range(width // lanes):
            row = i * (width // lanes) + j
            gain_rows[row : row + 1, :] = gain[:, j * lanes : (j + 1) * lanes]
    gain_part[...] = jnp.zeros(gain_part.shape, F32)
    for zz in range(n):
        gain_part[zz, 0, 0, 0] = gain_rows[...]
    reduce.run(7, 0)

    for pair in range(n // 2):
        cols = slice(pair * 2 * rows_part, (pair + 1) * 2 * rows_part)
        grad = product(dv_ref[:, cols], normed[...], 0, 0).astype(BF16)
        own_parts[0][2 * pair, 1] = as_unit(grad[:rows_part])
        own_parts[0][2 * pair + 1, 1] = as_unit(grad[rows_part:])
    for zz in range(n):
        at_part = slice(zz * rows_part, (zz + 1) * rows_part)
        grad = product(mix[at_part, :], g_first[...], 1, 0)
        own_parts[0][zz, 0] = as_unit(grad.astype(BF16))
    reduce.run(2, 0)
    for pair in range(n // 2):
        cols = slice(pair * 2 * rows_part, (pair + 1) * 2 * rows_part)
        grad = product(dk_ref[:, cols], normed[...], 0, 0).astype(BF16)
        own_parts[1][2 * pair, 1] = as_unit(grad[:rows_part])
        own_parts[1][2 * pair + 1, 1] = as_unit(grad[rows_part:])
    for zz in range(n):
        at_part = slice(zz * rows_part, (zz + 1) * rows_part)
        grad = product(dq_ref[at_part, :], normed[own_rows, :], 1, 0)
        own_parts[1][zz, 0] = as_unit(grad.astype(BF16))
    reduce.run(3, 0)
    all_run(self_groups, 1)
    all_run(hidden_groups, 5)
    for i in range(halo_chunks):

        @pl.when(z + halo_chunks - i < n)
        def _(i=i):
            halo_copy(i).wait_recv()
            own_back[...] += crecv[i].astype(F32)

    here = near[own_rows, :].astype(F32)
    residual, _ = norm_gradient(here, self_gain[...], own_back[...])
    grad_tokens[...] = (first_back[...] + residual).astype(BF16)
    all_run(hidden_groups, 6)
    all_run(self_groups, 2)
    all_run(cross_groups, 4)
    all_run(self_groups, 3)
    all_run(cross_groups, 5)
    all_run(self_groups, 4)
    all_run(cross_groups, 6)
    all_run(self_groups, 5)
    all_run(self_groups, 6)
    all_run(range(8), 7)
    for i in range(3):
        for j in range(width // lanes):
            row = i * (width // lanes) + j
            cols = slice(j * lanes, (j + 1) * lanes)
            gain_out[i : i + 1, cols] = gain_fin[0, 0, 0, row : row + 1, :]
    gain_out[3:8, :] = jnp.zeros((5, width), F32)
    for i in range(halo_chunks):

        @pl.when(z >= halo_chunks - i)
        def _(i=i):
            halo_copy(i).wait_send()

    reduce.drain()


def self_backward(n, extra, halo_chunks, ins, cross_parts, sums):
    near, g_first = ins[7], ins[9]
    rows, width = g_first.shape
    keys = near.shape[0]
    unit = width // n // 4
    gain_shape = (16, 256)
    shapes = [(unit, width)] * 4 + [p.shape[1:] for p in sums]
    struct = jax.ShapeDtypeStruct
    scratch = [pltpu.VMEM((n, 2, 2, 2, unit, width), BF16)] * 2
    scratch += [pltpu.VMEM((n, 2, 2, 2) + gain_shape, F32), pltpu.VMEM((2, 2, 2) + gain_shape, F32)]
    scratch += reduce_scratch(
        n, extra, shapes + [gain_shape], [BF16] * 7 + [F32],
        [True, True] + [False] * 6, [True] * 4 + [False] * 3 + [True],
    )
    scratch += [
        pltpu.VMEM((width, rows), BF16),
        pltpu.VMEM((width, rows), BF16),
        pltpu.VMEM((keys, width), BF16),
        pltpu.VMEM((keys, width), BF16),
        pltpu.VMEM((rows, width), F32),
        pltpu.VMEM((halo_chunks, rows, width), BF16),
        pltpu.VMEM((halo_chunks, rows, width), BF16),
        pltpu.VMEM(gain_shape, F32),
        DMA((halo_chunks,)),
        DMA((halo_chunks,)),
    ]
    out = pl.pallas_call(
        functools.partial(self_backward_kernel, n, extra, halo_chunks),
        out_shape=[struct((2, 2, 2) + s, BF16) for s in shapes]
        + [struct((rows, width), BF16), struct((8, width), F32)],
        in_specs=[VMEM] * 16 + [ANY] * 2 + [VMEM] * 3,
        out_specs=[VMEM] * 9,
        scratch_shapes=scratch,
        compiler_params=pltpu.CompilerParams(
            collective_id=2, has_side_effects=True, vmem_limit_bytes=63 << 20
        ),
        name="self_backward",
    )(*ins, *cross_parts, *sums)
    return out[:7], out[7], out[8]


def body(
    tokens, memory, table_lengths, table_plots,
    self_gain, self_query, self_key, self_value, self_output,
    cross_gain, cross_query, cross_key, cross_value, cross_output,
    hidden_gain, hidden_gate, hidden_up, hidden_down, cotangent,
):
    n = lax.axis_size("tensor")
    extra = lax.axis_size("dp").bit_length() - 1 - 3
    rows, width = tokens.shape
    halo_chunks = -(-(LONGEST - 1) // rows)

    def pieces(shard):
        return shard.reshape(2, 2, 2, -1, shard.shape[-1])

    shards = [pieces(hidden_gate), pieces(hidden_up), pieces(hidden_down)]
    ins = (
        table_lengths, table_plots, tokens, cotangent,
        self_gain[None], cross_gain[None], hidden_gain[None], memory,
        cross_key.T, cross_value.T, self_query.T, self_key.T, self_value.T, self_output,
        cross_query.T, cross_output,
    )
    full, saved = forward(n, halo_chunks, ins, shards)
    (
        bias, plots, near, normed_near, self_q, self_k, self_kt, self_v, self_mix, self_logs,
        first_sum, normed_cross, q_all, cross_k, cross_kt, cross_v, cross_mix,
        output, normed_hidden, hidden, gate_back, up_back, second_back, grad_rows, mixed_back,
        cross_stats, gain_hidden,
    ) = saved
    ins = (
        plots, mixed_back, cross_stats, q_all, cross_k, cross_kt, cross_v, memory, normed_cross,
        cross_mix, grad_rows, second_back, first_sum, cross_gain[None], full[0], full[3],
        normed_hidden, hidden, gate_back, up_back, cotangent,
    )
    hidden_pieces, rest = cross_backward(n, ins, [s.shape[3:] for s in shards])
    grad_memory, part_keys, part_query, first_back, g_first, gain_cross = rest
    ins = (
        bias, self_q, self_k, self_kt, self_v, self_mix, self_logs, near, normed_near, g_first,
        first_back, self_gain[None], gain_cross, gain_hidden, full[1], full[2],
    )
    sums, grad_tokens, gains = self_backward(
        n, extra, halo_chunks, ins, [part_query, part_keys], hidden_pieces
    )

    def pair(summed):
        both = summed.reshape(2, -1, width).astype(F32)
        return both[0], both[1]

    def whole(summed):
        return summed.reshape(-1, summed.shape[-1]).astype(F32)

    g_cq, g_co = pair(sums[0])
    g_ck, g_cv = pair(sums[1])
    g_so, g_sv = pair(sums[2])
    g_sq, g_sk = pair(sums[3])
    return (
        output, grad_tokens, grad_memory,
        g_sq.T, g_sk.T, g_sv.T, g_so,
        g_cq.T, g_ck.T, g_cv.T, g_co,
        whole(sums[4]), whole(sums[5]), whole(sums[6]),
        gains[0], gains[1], gains[2],
    )


def solution(mesh):
    in_specs = (
        P(("dp", "tensor"), None),
        P("dp", "tensor", None),
        P("dp", None),
        P("dp", None),
        P(),
        P(None, "tensor"),
        P(None, "tensor"),
        P(None, "tensor"),
        P("tensor", None),
        P(),
        P(None, "tensor"),
        P(None, "tensor"),
        P(None, "tensor"),
        P("tensor", None),
        P(),
        P(None, "tensor"),
        P(None, "tensor"),
        P("tensor", None),
        P(("dp", "tensor"), None),
    )
    out_specs = (
        P(("dp", "tensor"), None),
        P(("dp", "tensor"), None),
        P("dp", "tensor", None),
        P(None, "tensor"),
        P(None, "tensor"),
        P(None, "tensor"),
        P("tensor", None),
        P(None, "tensor"),
        P(None, "tensor"),
        P(None, "tensor"),
        P("tensor", None),
        P(None, "tensor"),
        P(None, "tensor"),
        P("tensor", None),
        P(),
        P(),
        P(),
    )
    return jax.shard_map(body, mesh=mesh, in_specs=in_specs, out_specs=out_specs, check_vma=False)
```

```python
import functools

import jax
import jax.numpy as jnp
from jax import lax
from jax.experimental import pallas as pl
from jax.experimental.pallas import tpu as pltpu
from jax.sharding import PartitionSpec as P

HD = 64
LONGEST = 512
F32 = jnp.float32
BF16 = jnp.bfloat16
MESH = pl.DeviceIdType.MESH
ANY = pl.BlockSpec(memory_space=pl.ANY)
VMEM = pl.BlockSpec(memory_space=pltpu.VMEM)
DMA = pltpu.SemaphoreType.DMA

epsilon = 1e-06
masked_value = -1e30


def product(first_op, second_op, first_dim, second_dim):
    return lax.dot_general(
        first_op,
        second_op,
        (((first_dim,), (second_dim,)), ((), ())),
        preferred_element_type=F32,
    )


def remote(src, dst, send_sem, recv_sem, device):
    return pltpu.make_async_remote_copy(
        src_ref=src,
        dst_ref=dst,
        send_sem=send_sem,
        recv_sem=recv_sem,
        device_id=device,
        device_id_type=MESH,
    )


class Moves:
    def __init__(self, pairs, sems):
        self.copies = [
            pltpu.make_async_copy(src, dst, sems.at[i]) for i, (src, dst) in enumerate(pairs)
        ]

    def start(self, *which):
        for i in which:
            self.copies[i].start()

    def wait(self, *which):
        for i in which:
            self.copies[i].wait()


def held(struct):
    return pltpu.VMEM(struct.shape, struct.dtype)


def place():
    dp = lax.axis_index("dp")
    z = lax.axis_index("tensor")
    return dp, z, lax.rem(dp, 2), lax.rem(dp // 2, 2), lax.rem(dp // 4, 2)


def flipped(dp, bit):
    here = lax.rem(dp // (1 << bit), 2)
    return dp + (1 << bit) * (1 - 2 * here)


def greet(devices):
    barrier = pltpu.get_barrier_semaphore()
    for device in devices:
        pl.semaphore_signal(barrier, inc=1, device_id=device, device_id_type=MESH)
    pl.semaphore_wait(barrier, len(devices))


def greet_line(dp, z, n):
    barrier = pltpu.get_barrier_semaphore()

    @pl.when(z > 0)
    def _():
        pl.semaphore_signal(barrier, inc=1, device_id=(dp, z - 1), device_id_type=MESH)

    @pl.when(z < n - 1)
    def _():
        pl.semaphore_signal(barrier, inc=1, device_id=(dp, z + 1), device_id_type=MESH)

    inner = (z > 0) & (z < n - 1)

    @pl.when(inner)
    def _():
        pl.semaphore_wait(barrier, 2)

    @pl.when(jnp.logical_not(inner))
    def _():
        pl.semaphore_wait(barrier, 1)


class Gather:
    def __init__(self, n, mine, full, sems):
        self.n, self.mine, self.full, self.count = n, mine, full, len(full)
        self.zs, self.zr, self.as_, self.ar, self.bs, self.br, self.cs, self.cr, self.loc = sems
        self.dp, self.z, self.c, self.x, self.y = place()
        z = self.z
        inner = [1 + s // 2 if s % 2 == 0 else n - 1 - s // 2 for s in range(n - 1)]
        self.order = [
            jnp.where(z == 0, n - 1 - s, jnp.where(z == n - 1, 1 + s, inner[s]))
            for s in range(n - 1)
        ]

    def peers(self):
        others = [lax.rem(self.z + k, self.n) for k in range(1, self.n)]
        return [(self.dp, o) for o in others] + [(flipped(self.dp, b), self.z) for b in range(3)]

    def own(self, g):
        return pltpu.make_async_copy(self.mine[g], self.full[g].at[self.z], self.loc.at[g])

    def piece(self, g, k):
        zk = lax.rem(self.z + self.n - k, self.n)
        return self.full[g].at[zk, self.y, self.x, self.c]

    def first(self, g, k):
        src = self.piece(g, 0) if self.mine[g] is None else self.mine[g].at[self.y, self.x, self.c]
        dev = (self.dp, lax.rem(self.z + k, self.n))
        return remote(src, self.piece(g, 0), self.zs.at[g, k - 1], self.zr.at[g, k - 1], dev)

    def passed(self, g, up):
        k = self.n - 2 if up else 2
        dev = (self.dp, lax.rem(self.z + (1 if up else self.n - 1), self.n))
        slot = self.n - 2 if up else 0
        piece = self.piece(g, k)
        return remote(piece, piece, self.zs.at[g, self.n - 1], self.zr.at[g, slot], dev)

    def straight(self, k, start):
        ends = ((self.z == 0) & (k == self.n - 1)) | ((self.z == self.n - 1) & (k == 1))
        pl.when(jnp.logical_not(ends) if self.n > 2 else self.z >= 0)(start)

    def arrived(self, g, k):
        piece = self.piece(g, k)
        dev = (self.dp, lax.rem(self.z + k, self.n))
        return remote(piece, piece, self.zs.at[g, 0], self.zr.at[g, k - 1], dev)

    def second(self, g, s, incoming=False):
        k = self.order[s]
        zk = lax.rem(self.z + self.n - k, self.n)
        x, y, c = self.x, self.y, self.c
        if s % 2 == 1:
            there, bit = self.full[g].at[zk, y, 1 - x if incoming else x, c], 1
        else:
            there, bit = self.full[g].at[zk, 1 - y if incoming else y, x, c], 2
        dev = (flipped(self.dp, bit), self.z)
        return remote(there, there, self.as_.at[g, s], self.ar.at[g, s], dev)

    def third(self, g, s, incoming=False):
        k = self.order[s]
        zk = lax.rem(self.z + self.n - k, self.n)
        x, y, c = self.x, self.y, self.c
        if s % 2 == 1:
            there, bit = self.full[g].at[zk, 1 - y if incoming else y, :, c], 2
        else:
            there, bit = self.full[g].at[zk, :, 1 - x if incoming else x, c], 1
        dev = (flipped(self.dp, bit), self.z)
        return remote(there, there, self.bs.at[g, s], self.br.at[g, s], dev)

    def fourth(self, g, s, incoming=False):
        zk = lax.rem(self.z + self.n - self.order[s], self.n)
        there = self.full[g].at[zk, :, :, 1 - self.c if incoming else self.c]
        dev = (flipped(self.dp, 0), self.z)
        return remote(there, there, self.cs.at[g, s], self.cr.at[g, s], dev)

    def run(self, g, stage):
        n = self.n
        steps = range(n - 1)
        if stage == 0:
            if self.mine[g] is not None:
                self.own(g).start()

            for k in sorted(range(1, n), key=lambda k: min(k, n - k)):
                self.straight(k, lambda k=k: self.first(g, k).start())
        elif stage == 1:
            for s in steps:
                k = self.order[s]
                self.arrived(g, k).wait_recv()
                if n > 2:

                    @pl.when((self.z == n - 2) & (k == n - 2))
                    def _():
                        self.passed(g, True).start()

                    @pl.when((self.z == 1) & (k == 2))
                    def _():
                        self.passed(g, False).start()

                self.second(g, s).start()
        elif stage == 2:
            for s in steps:
                self.second(g, s, True).wait_recv()
                self.third(g, s).start()
        elif stage == 3:
            for s in steps:
                self.third(g, s, True).wait_recv()
                self.fourth(g, s).start()
        else:
            if self.mine[g] is not None:
                self.own(g).wait()
            for s in steps:
                self.fourth(g, s, True).wait_recv()

    def drain(self):
        for g in range(self.count):
            if self.n > 2:

                @pl.when((self.z == self.n - 2) | (self.z == 1))
                def _(g=g):
                    self.passed(g, True).wait_send()

            for s in range(self.n - 1):
                self.straight(s + 1, lambda s=s, g=g: self.first(g, s + 1).wait_send())
                self.second(g, s).wait_send()
                self.third(g, s).wait_send()
                self.fourth(g, s).wait_send()


def gather_sems(n, count):
    return [DMA((count, n)) for _ in range(8)] + [DMA((count,))]


class Reduce:
    def __init__(self, n, extra, part, acc, rec1, rec2, rec3, rec4, fin, recx, sems, quarters):
        self.n, self.extra, self.count = n, extra, len(rec4)
        self.part, self.fin, self.recx, self.quarters = part, fin, recx, quarters
        self.rec1, self.rec2, self.rec3, self.rec4 = rec1, rec2, rec3, rec4
        self.sems = sems
        self.dp, self.z, self.c, self.x, self.y = place()
        self.ks = range(1, n)
        self.kept = acc
        self.started = []
        self.acc = []
        for g in range(self.count):
            if part[g] is None:
                self.acc.append(None)
            elif acc[g] is None:
                self.acc.append(part[g].at[:, :, :, self.c])
            else:
                self.acc.append(acc[g])

    def peers(self):
        others = [lax.rem(self.z + k, self.n) for k in self.ks]
        bits = range(3 + self.extra)
        return [(self.dp, o) for o in others] + [(flipped(self.dp, b), self.z) for b in bits]

    def lanes(self, g, half):
        width = self.rec4[g].shape[-1]
        middle = width // 256 * 128 + (128 if width % 256 and g % 2 == 0 else 0)
        return slice(0, middle) if half == 0 else slice(middle, width)

    def copies(self, stage, g, incoming=False):
        dp, z, c, x, y, n = self.dp, self.z, self.c, self.x, self.y, self.n
        acc, fin = self.acc[g], self.fin[g] if self.fin else None
        found = []
        if stage == 0:
            src, dst, dev = self.part[g].at[:, :, :, 1 - c], self.rec1[g], (flipped(dp, 0), z)
            found.append((src, dst, dev, 0))
        elif stage == 1:
            for half in range(2):
                at = self.lanes(g, half)
                src = acc.at[:, :, 1 - x, :, at] if half == 0 else acc.at[:, 1 - y, :, :, at]
                dev = (flipped(dp, 1 if half == 0 else 2), z)
                found.append((src, self.rec2[g].at[:, :, :, at], dev, 1 + half))
        elif stage == 2:
            for half in range(2):
                at = self.lanes(g, half)
                src = acc.at[:, 1 - y, x, :, at] if half == 0 else acc.at[:, y, 1 - x, :, at]
                dev = (flipped(dp, 2 if half == 0 else 1), z)
                found.append((src, self.rec3[g].at[:, :, at], dev, 3 + half))
        elif stage == 3:
            for k in self.ks:
                zk = lax.rem(z + k, n)
                slot = lax.rem(z + n - k, n) if incoming else z
                found.append((self.quarter(g, zk), self.rec4[g].at[slot], (dp, zk), 8 + k))
        elif stage == 4:
            for half in range(2):
                at = self.lanes(g, half)
                if half == 0:
                    src = fin.at[1 - y if incoming else y, x, c, :, at]
                else:
                    src = fin.at[y, 1 - x if incoming else x, c, :, at]
                found.append((src, src, (flipped(dp, 2 if half == 0 else 1), z), 5 + half))
        elif stage == 5:
            for half in range(2):
                at = self.lanes(g, half)
                if half == 0:
                    src = fin.at[:, 1 - x if incoming else x, c, :, at]
                else:
                    src = fin.at[1 - y if incoming else y, :, c, :, at]
                found.append((src, src, (flipped(dp, 1 if half == 0 else 2), z), 7 + half))
        else:
            src = fin.at[:, :, 1 - c if incoming else c]
            found.append((src, src, (flipped(dp, 0), z), 8 + n))
        return [
            remote(src, dst, self.sems[0].at[g, slot], self.sems[1].at[g, slot], dev)
            for src, dst, dev, slot in found
        ]

    def quarter(self, g, zz):
        if self.quarters[g] is not None:
            return self.quarters[g].at[zz]
        return self.acc[g].at[zz, self.y, self.x]

    def own(self, g):
        src = self.part[g].at[:, :, :, self.c]
        return pltpu.make_async_copy(src, self.acc[g], self.sems[4].at[g])

    def further(self, g, e):
        return remote(
            self.fin[g].at[self.y, self.x, self.c],
            self.recx[g].at[e],
            self.sems[2].at[g, e],
            self.sems[3].at[g, e],
            (flipped(self.dp, 3 + e), self.z),
        )

    def add(self, stage, g):
        n, x, y, c, z = self.n, self.x, self.y, self.c, self.z
        acc, fin = self.acc[g], self.fin[g] if self.fin else None
        kind = self.rec4[g].dtype
        if stage == 1:

            def step(i, carry):
                zz, yy, xx = i // 4, lax.rem(i // 2, 2), lax.rem(i, 2)
                total = acc[zz, yy, xx].astype(F32) + self.rec1[g][zz, yy, xx].astype(F32)
                acc[zz, yy, xx] = total.astype(kind)
                return carry

            lax.fori_loop(0, 4 * n, step, 0)
        elif stage == 2:

            def step(i, carry):
                zz, aa = i // 2, lax.rem(i, 2)
                for half in range(2):
                    at = self.lanes(g, half)
                    yy, xx = (aa, x) if half == 0 else (y, aa)
                    came = self.rec2[g][zz, aa, :, at].astype(F32)
                    acc[zz, yy, xx, :, at] = (acc[zz, yy, xx, :, at].astype(F32) + came).astype(kind)
                return carry

            lax.fori_loop(0, 2 * n, step, 0)
        elif stage == 3:

            def step(zz, carry):
                total = acc[zz, y, x].astype(F32) + self.rec3[g][zz].astype(F32)
                acc[zz, y, x] = total.astype(kind)
                return carry

            lax.fori_loop(0, n, step, 0)
        else:
            self.rec4[g][z] = self.quarter(g, z)[...]
            total = self.rec4[g][0].astype(F32)
            for k in self.ks:
                total = total + self.rec4[g][k].astype(F32)
            fin[y, x, c] = total.astype(kind)
            for e in range(self.extra):
                self.further(g, e).start()
                self.further(g, e).wait()
                total = fin[y, x, c].astype(F32) + self.recx[g][e].astype(F32)
                fin[y, x, c] = total.astype(kind)

    def begin(self, stage, g):
        for copy in self.copies(stage, g):
            copy.start()
        if (stage, g) not in self.started:
            self.started.append((stage, g))

    def end(self, stage, g):
        if stage == 0 and self.kept[g] is not None:
            self.own(g).wait()
        for copy in self.copies(stage, g, True):
            copy.wait_recv()
        if stage < 4:
            self.add(stage + 1, g)

    def run(self, g, stage):
        if stage == 0 and self.kept[g] is not None:
            self.own(g).start()
        if stage > 0:
            self.end(stage - 1, g)
        if stage <= 6:
            self.begin(stage, g)

    def drain(self):
        for stage, g in self.started:
            for copy in self.copies(stage, g):
                copy.wait_send()


def reduce_scratch(n, extra, shapes, kinds, kept, from_start):
    count = len(shapes)
    every = list(zip(shapes, kinds))
    used = [s for s, f in zip(every, from_start) if f]
    scratch = [pltpu.VMEM((n, 2, 2) + s, d) for (s, d), k in zip(every, kept) if k]
    scratch += [pltpu.VMEM((n, 2, 2) + s, d) for s, d in used]
    scratch += [pltpu.VMEM((n, 2) + s, d) for s, d in used]
    scratch += [pltpu.VMEM((n,) + s, d) for s, d in used]
    scratch += [pltpu.VMEM((n,) + s, d) for s, d in every]
    if extra:
        scratch += [pltpu.VMEM((extra,) + s, d) for s, d in every]
    scratch += [
        DMA((count, 9 + n)),
        DMA((count, 9 + n)),
        DMA((count, max(extra, 1))),
        DMA((count, max(extra, 1))),
        DMA((count,)),
    ]
    return scratch


def take_reduce(n, extra, part, fin, kept, quarters, refs):
    refs = list(refs)
    acc = [refs.pop(0) if k else None for k in kept]
    recs = []
    for _ in range(3):
        recs.append([refs.pop(0) if p is not None else None for p in part])
    recs.append([refs.pop(0) for _ in part])
    recx = [refs.pop(0) for _ in part] if extra else None
    sems = [refs.pop(0) for _ in range(5)]
    return Reduce(n, extra, part, acc, *recs, fin, recx, sems, quarters), refs


def both_plots(rows, plot_row):
    wide = rows.astype(F32)
    zero = jnp.zeros_like(wide)
    return jnp.concatenate(
        [jnp.where(plot_row == 0, wide, zero), jnp.where(plot_row == 0, zero, wide)], axis=0
    ).astype(BF16)


def own_plot(pair, plot_row):
    half = pair.shape[0] // 2
    return jnp.where(plot_row == 0, pair[:half], pair[half:])


def line_exchange(n, parts, z, dp, refs, compute, merge, finish, hook, before=None):
    own, spread, mine, from_right, from_left, sems = refs
    ups, upr, dns, dnr, rls, rlr, rrs, rrr = sems

    def up(j, p, i, start):
        src = own[i].at[p] if start else spread[i].at[j, p]
        return remote(
            src, spread[i].at[j, p], ups.at[i, j, p], upr.at[i, j, p], (dp, lax.rem(z + 1, n))
        )

    def down(j, p, i, start):
        src = own[i].at[p] if start else spread[i].at[j, p]
        return remote(
            src,
            spread[i].at[j, p],
            dns.at[i, j, p],
            dnr.at[i, j, p],
            (dp, lax.rem(z + n - 1, n)),
        )

    def back_left(j, p, i):
        return remote(
            mine[i].at[j, p],
            from_right[i].at[j, p],
            rls.at[i, j, p],
            rlr.at[i, j, p],
            (dp, lax.rem(z + n - 1, n)),
        )

    def back_right(j, p, i):
        return remote(
            mine[i].at[j, p],
            from_left[i].at[j, p],
            rrs.at[i, j, p],
            rrr.at[i, j, p],
            (dp, lax.rem(z + 1, n)),
        )

    out_kinds = range(len(own))
    back_kinds = range(len(mine))

    def send_own(p, carry):
        for i in out_kinds:

            @pl.when(z < n - 1)
            def _():
                up(z, p, i, True).start()

            @pl.when(z > 0)
            def _():
                down(z, p, i, True).start()

        return carry

    lax.fori_loop(0, parts, send_own, 0)
    if before is not None:
        before()

    def slot(t, carry):
        def one_part(p, inner):
            low = z - t
            high = z + t

            @pl.when(t == 0)
            def _():
                for i in out_kinds:
                    spread[i][z, p] = own[i][p]
                compute(z, p)

            @pl.when((t > 0) & (t < n) & (low >= 0))
            def _():
                compute(low, p)

                @pl.when(z == n - 1)
                def _():
                    for i in back_kinds:
                        back_left(low, p, i).start()

            @pl.when((t > 0) & (t < n) & (high < n))
            def _():
                compute(high, p)

                @pl.when(z == 0)
                def _():
                    for i in back_kinds:
                        back_right(high, p, i).start()

            @pl.when((t + 1 < n) & (low - 1 >= 0))
            def _():
                for i in out_kinds:
                    up(low - 1, p, i, False).wait_recv()

                    @pl.when(z < n - 1)
                    def _():
                        up(low - 1, p, i, False).start()

            @pl.when((t + 1 < n) & (high + 1 < n))
            def _():
                for i in out_kinds:
                    down(high + 1, p, i, False).wait_recv()

                    @pl.when(z > 0)
                    def _():
                        down(high + 1, p, i, False).start()

            left_chunk = 2 * (n - 1) - z - t

            @pl.when((t > 0) & (left_chunk >= 0) & (left_chunk < z) & (z < n - 1))
            def _():
                for i in back_kinds:
                    back_left(left_chunk, p, i).wait_recv()
                merge(left_chunk, p, from_right)
                for i in back_kinds:
                    back_left(left_chunk, p, i).start()

            right_chunk = t - z

            @pl.when((t > 0) & (right_chunk < n) & (right_chunk > z) & (z > 0))
            def _():
                for i in back_kinds:
                    back_right(right_chunk, p, i).wait_recv()
                merge(right_chunk, p, from_left)
                for i in back_kinds:
                    back_right(right_chunk, p, i).start()

            return inner

        lax.fori_loop(0, parts, one_part, 0)
        hook(t)
        return carry

    lax.fori_loop(0, 2 * n - 2, slot, 0)

    def last(p, carry):
        @pl.when(z > 0)
        def _():
            for i in back_kinds:
                back_right(z, p, i).wait_recv()
            merge(z, p, from_left)

        @pl.when(z < n - 1)
        def _():
            for i in back_kinds:
                back_left(z, p, i).wait_recv()
            merge(z, p, from_right)

        finish(p)
        return carry

    lax.fori_loop(0, parts, last, 0)

    def drain(p, carry):
        for j in range(n):
            for i in out_kinds:

                @pl.when((z < n - 1) & (z == j))
                def _(i=i, j=j):
                    up(j, p, i, True).wait_send()

                @pl.when((z < n - 1) & (z > j))
                def _(i=i, j=j):
                    up(j, p, i, False).wait_send()

                @pl.when((z > 0) & (z == j))
                def _(i=i, j=j):
                    down(j, p, i, True).wait_send()

                @pl.when((z > 0) & (z < j))
                def _(i=i, j=j):
                    down(j, p, i, False).wait_send()

            for i in back_kinds:

                @pl.when(z > j)
                def _(i=i, j=j):
                    back_left(j, p, i).wait_send()

                @pl.when(z < j)
                def _(i=i, j=j):
                    back_right(j, p, i).wait_send()

        return carry

    lax.fori_loop(0, parts, drain, 0)


def line_sems(n, parts, out_kinds, back_kinds):
    return [DMA((out_kinds, n, parts))] * 4 + [DMA((back_kinds, n, parts))] * 4


def unit_rows(ref, zz, which):
    block = ref[zz, which]
    return block.reshape(-1, block.shape[-1])


def two_units(ref, pair, which):
    return jnp.concatenate(
        [unit_rows(ref, 2 * pair, which), unit_rows(ref, 2 * pair + 1, which)], axis=0
    )


def normed_rows(rows, gain):
    inverse = lax.rsqrt(jnp.mean(rows * rows, axis=-1, keepdims=True) + epsilon)
    return rows * inverse * gain


def half_lanes(first, second, which):
    lane = lax.broadcasted_iota(jnp.int32, first.shape, 1)
    if which == 0:
        return jnp.where(lane < HD, first, pltpu.roll(second, HD, 1))
    return jnp.where(lane < HD, pltpu.roll(first, HD, 1), second)


def table_at(position, lengths, count):
    table = jnp.zeros(position.shape, jnp.int32)
    end = 0
    for t in range(count):
        end = end + lengths[0, t]
        table = table + (position >= end).astype(jnp.int32)
    return table


KEPT = 16


def forward_kernel(n, count, halo_chunks, *refs):
    (
        lengths, table_plots, tok, cot, self_gain, cross_gain, hidden_gain, mem,
        w_ck, w_cv, w_sq, w_sk, w_sv, w_so, w_cq, w_co,
    ) = refs[:16]
    mine = [None] * 4 + list(refs[16 : 16 + count - 4])
    at = 12 + count
    full_out = refs[at : at + 4]
    at += 4
    out_refs = refs[at : at + 27]
    at += 27
    kept_refs = refs[at : at + KEPT]
    at += KEPT
    (
        bias, plots, near, normed, self_q, self_k, self_kt, self_v, self_mix, self_logs, first_sum,
        normed_cross, q_all, cross_k, cross_kt, cross_v, o_ref,
        output, normed_hidden, hidden, gate_back, up_back, second_back, grad_rows, do_ref, stats,
        gain_hidden,
    ) = kept_refs + out_refs[KEPT:]
    full = refs[at : at + count]
    at += count
    (
        halo, self_vt, cross_vt, cross_q, o_mine, l_mine, o_right, l_right, o_left, l_left,
        down_sum, back_sum, second_sum,
    ) = refs[at : at + 13]
    at += 13
    line = refs[at : at + 8]
    at += 8
    gather_refs = refs[at : at + 9]
    hs, hr, outs, out_sems = refs[at + 9 :]
    leaving = Moves(list(zip(kept_refs, out_refs[:KEPT])), out_sems)
    rows, width = tok.shape
    heads = width // HD
    parts = n
    heads_part = heads // parts
    rows_part = heads_part * HD
    scale = HD ** (-0.5)
    dp, z, c, x, y = place()
    gather = Gather(n, mine, full, gather_refs)
    greet(gather.peers())

    def halo_copy(i):
        src = tok if i == 0 else halo.at[halo_chunks - i]
        dst = halo.at[halo_chunks - 1 - i]
        return remote(src, dst, hs.at[i], hr.at[i], (dp, lax.rem(z + 1, n)))

    def own_units(g, first, second):
        full[g][z, 0] = as_unit(first[...])
        full[g][z, 1] = as_unit(second[...])

    own_units(0, w_ck, w_cv)
    gather.run(0, 0)
    own_units(1, w_sq, w_sk)
    gather.run(1, 0)
    own_units(2, w_sv, w_so)
    own_units(3, w_cq, w_co)

    halo[halo_chunks] = tok[...]
    for i in range(halo_chunks):

        @pl.when(z <= i)
        def _(i=i):
            halo[halo_chunks - 1 - i] = jnp.zeros((rows, width), BF16)

    keys = bias.shape[0]
    held_tables = lengths.shape[1]
    first_key = z * rows - halo_chunks * rows
    key_at = lax.broadcasted_iota(jnp.int32, (keys, rows), 0) + first_key
    query_at = lax.broadcasted_iota(jnp.int32, (1, rows), 1) + z * rows
    same = table_at(key_at, lengths, held_tables) == table_at(query_at, lengths, held_tables)
    allowed = same & (key_at <= query_at) & (key_at >= 0)
    bias[...] = jnp.where(allowed, 0.0, masked_value)
    for j in range(n):
        tables = table_at(
            lax.broadcasted_iota(jnp.int32, (1, rows), 1) + j * rows, lengths, held_tables
        )
        plot = jnp.zeros((1, rows), jnp.int32)
        for t in range(held_tables):
            plot = jnp.where(tables == t, table_plots[0, t], plot)
        plots[j] = plot

    gather.run(0, 1)

    @pl.when(z < n - 1)
    def _():
        halo_copy(0).start()

    gather.run(2, 0)
    gather.run(0, 2)
    gather.run(1, 1)
    gather.run(0, 3)
    gather.run(1, 2)
    gather.run(3, 0)

    def halo_pass(i):
        @pl.when(z > i)
        def _():
            halo_copy(i).wait_recv()

        if i + 1 < halo_chunks:

            @pl.when((z > i) & (z < n - 1))
            def _():
                halo_copy(i + 1).start()

    halo_pass(0)
    gather.run(2, 1)

    def norm_chunk(i, carry):
        at_rows = pl.ds(pl.multiple_of(i * rows, rows), rows)
        near[at_rows, :] = halo[i]
        normed[at_rows, :] = normed_rows(halo[i].astype(F32), self_gain[...]).astype(BF16)
        return carry

    gather.run(0, 4)

    plots_held = mem.shape[0]

    def flat_part(which, out):
        def step(zz, carry):
            for p in range(plots_held):
                rows_t = product(unit_rows(full[0], zz, which), mem[p], 1, 1).astype(BF16)
                for hh in range(heads_part):
                    at_head = slice(hh * HD, (hh + 1) * HD)
                    out[zz * heads_part + hh, p * HD : (p + 1) * HD, :] = rows_t[at_head]
            return carry

        lax.fori_loop(0, n, step, 0)

    def tall_part(which, out):
        for pair in range(n // 2):
            weights = two_units(full[0], pair, which)
            first = product(mem[0], weights, 1, 1)
            second = product(mem[1], weights, 1, 1)
            for hh in range(2 * heads_part):
                cols = slice((hh // 2) * 2 * HD, (hh // 2 + 1) * 2 * HD)
                both = half_lanes(first[:, cols], second[:, cols], hh % 2)
                out[pair * 2 * heads_part + hh] = both.astype(BF16)

    flat_part(1, cross_vt)
    gather.run(1, 3)
    gather.run(2, 2)
    flat_part(0, cross_kt)
    gather.run(3, 1)
    gather.run(4, 0)
    tall_part(0, cross_k)
    for i in range(1, halo_chunks):
        halo_pass(i)
    gather.run(1, 4)
    gather.run(2, 3)
    gather.run(3, 2)
    lax.fori_loop(0, halo_chunks + 1, norm_chunk, 0)

    own_rows = slice(halo_chunks * rows, (halo_chunks + 1) * rows)

    def query_part(zz, carry):
        at_part = pl.ds(pl.multiple_of(zz * rows_part, rows_part), rows_part)
        projected = product(unit_rows(full[1], zz, 0), normed[own_rows, :], 1, 1)
        self_q[at_part, :] = (projected.astype(BF16).astype(F32) * scale).astype(BF16)
        return carry

    lax.fori_loop(0, n, query_part, 0)

    def tall(out, g, which):
        for pair in range(n // 2):
            cols = slice(pair * 2 * rows_part, (pair + 1) * 2 * rows_part)

            def chunk(i, carry, pair=pair, cols=cols):
                at_rows = pl.ds(pl.multiple_of(i * rows, rows), rows)
                weights = two_units(full[g], pair, which)
                out[at_rows, cols] = product(normed[at_rows, :], weights, 1, 1).astype(BF16)
                return carry

            lax.fori_loop(0, halo_chunks + 1, chunk, 0)

    tall(self_k, 1, 1)
    gather.run(5, 0)
    gather.run(2, 4)

    def flat(out, g, which):
        def step(zz, carry):
            at_part = pl.ds(pl.multiple_of(zz * rows_part, rows_part), rows_part)
            weights = unit_rows(full[g], zz, which)
            out[at_part, :] = product(weights, normed[...], 1, 1).astype(BF16)
            return carry

        lax.fori_loop(0, n, step, 0)

    flat(self_vt, 2, 0)
    gather.run(3, 3)

    def self_pair(pair, carry):
        cols = pl.ds(pl.multiple_of(pair * 2 * HD, 2 * HD), 2 * HD)
        for which in range(2):
            at_head = pl.ds(pl.multiple_of((2 * pair + which) * HD, HD), HD)
            scores = jnp.dot(
                self_k[:, cols], alone(self_q[at_head, :], which), preferred_element_type=F32
            )
            scores = scores + bias[...]
            top = jnp.max(scores, axis=0, keepdims=True)
            powers = jnp.exp(scores - top)
            total = jnp.sum(powers, axis=0, keepdims=True)
            mixed = jnp.dot(self_vt[at_head, :], powers.astype(BF16), preferred_element_type=F32)
            self_mix[at_head, :] = (mixed / total).astype(BF16)
            self_logs[pair, which : which + 1, :] = top + jnp.log(total)
        return carry

    lax.fori_loop(0, heads // 4, self_pair, 0)
    lax.fori_loop(heads // 4, heads // 2, self_pair, 0)

    total = tok[...].astype(F32)
    for zz in range(n):
        at_part = slice(zz * rows_part, (zz + 1) * rows_part)
        total = total + product(self_mix[at_part, :], unit_rows(full[2], zz, 1), 0, 0)
    first_sum[...] = total
    normed_cross[...] = normed_rows(total, cross_gain[...]).astype(BF16)
    gather.run(3, 4)

    def cross_query_part(zz, carry):
        projected = product(unit_rows(full[3], zz, 0), normed_cross[...], 1, 1)
        cross_q[zz] = (projected.astype(BF16).astype(F32) * scale).astype(BF16)
        return carry

    lax.fori_loop(0, n, cross_query_part, 0)

    def compute(j, p):
        plot_row = plots[j]
        for hh in range(heads_part):
            h = p * heads_part + hh
            q_pair = both_plots(q_all[j, p, hh * HD : (hh + 1) * HD, :], plot_row)
            scores = jnp.dot(cross_k[h], q_pair, preferred_element_type=F32)
            top = jnp.max(scores, axis=0, keepdims=True)
            powers = jnp.exp(scores - top)
            total = jnp.sum(powers, axis=0, keepdims=True)
            mixed = jnp.dot(cross_vt[h], powers.astype(BF16), preferred_element_type=F32)
            mixed = own_plot(mixed, plot_row) / total
            o_mine[j, p, hh * HD : (hh + 1) * HD, :] = mixed.astype(BF16)
            l_mine[j, p, hh : hh + 1, :] = top + jnp.log(total)

    def merge(j, p, arrived):
        for hh in range(heads_part):
            at_head = slice(hh * HD, (hh + 1) * HD)
            log_a = l_mine[j, p, hh : hh + 1, :]
            log_b = arrived[1][j, p, hh : hh + 1, :]
            top = jnp.maximum(log_a, log_b)
            share_a = jnp.exp(log_a - top)
            share_b = jnp.exp(log_b - top)
            total = share_a + share_b
            mixed = o_mine[j, p, at_head, :].astype(F32) * (share_a / total)
            mixed = mixed + arrived[0][j, p, at_head, :].astype(F32) * (share_b / total)
            o_mine[j, p, at_head, :] = mixed.astype(BF16)
            l_mine[j, p, hh : hh + 1, :] = top + jnp.log(total)

    def finish(p):
        o_ref[p] = o_mine[z, p]

    def keep(g):
        return pltpu.make_async_copy(full[g], full_out[g], outs.at[g])

    schedule = {
        0: [(4, 1)],
        1: [(6, 0), (4, 2), (5, 1)],
        2: [(4, 3), (5, 2)],
        3: [(6, 1)],
        4: [(6, 2), (5, 3)],
        5: [(6, 3)],
    }

    def hook(t):
        for step, work in schedule.items():

            @pl.when(t == step)
            def _(step=step, work=work):
                for g, stage in work:
                    gather.run(g, stage)
                if step == 0:
                    for g in range(4):
                        keep(g).start()

        @pl.when(t == 2 * n - 3)
        def _():
            tall_part(1, cross_v)
            tall(self_v, 2, 0)
            flat(self_kt, 1, 1)
            leaving.start(*range(KEPT))

    exchange = ([cross_q], [q_all], [o_mine, l_mine], [o_right, l_right], [o_left, l_left], line)
    line_exchange(n, parts, z, dp, exchange, compute, merge, finish, hook)

    total = first_sum[...]
    for zz in range(n):
        total = total + product(o_ref[zz], unit_rows(full[3], zz, 1), 0, 0)
    second_sum[...] = total
    normed_hidden[...] = normed_rows(total, hidden_gain[...]).astype(BF16)
    down_sum[...] = jnp.zeros((rows, width), F32)
    back_sum[...] = jnp.zeros((rows, width), F32)
    for g in range(4, 7):
        gather.run(g, 4)
    slope = (2.0 / 3.141592653589793) ** 0.5
    bend = 0.044715

    def whole(g, zz):
        block = full[g][zz]
        return block.reshape(-1, block.shape[-1])

    def hidden_part(zz, carry):
        gate = product(normed_hidden[...], whole(4, zz), 1, 0)
        up = product(normed_hidden[...], whole(5, zz), 1, 0)
        act_back = product(cot[...], whole(6, zz), 1, 1).astype(BF16).astype(F32)
        square = gate * gate
        curve = jnp.tanh(slope * (gate + bend * square * gate))
        cdf = 0.5 * (1.0 + curve)
        act = gate * cdf
        turn = cdf + 0.5 * gate * (1.0 - curve * curve) * slope * (1.0 + 3.0 * bend * square)
        here = (act * up).astype(BF16)
        to_gate = (act_back * up * turn).astype(BF16)
        to_up = (act_back * act).astype(BF16)
        hidden[zz] = here
        gate_back[zz] = to_gate
        up_back[zz] = to_up
        down_sum[...] += product(here, whole(6, zz), 1, 0)
        back_sum[...] += product(to_gate, whole(4, zz), 1, 1) + product(to_up, whole(5, zz), 1, 1)
        return carry

    lax.fori_loop(0, n, hidden_part, 0)
    output[...] = (second_sum[...] + down_sum[...]).astype(BF16)
    residual, gain_back = norm_gradient(second_sum[...], hidden_gain[...], back_sum[...])
    gain_hidden[...] = gain_back
    total = cot[...].astype(F32) + residual
    second_back[...] = total
    grad_rows[...] = total.astype(BF16)

    def mixed_part(zz, carry):
        mixed = product(unit_rows(full[3], zz, 1), grad_rows[...], 1, 1).astype(BF16)
        do_ref[zz] = mixed
        for hh in range(heads_part):
            at_head = slice(hh * HD, (hh + 1) * HD)
            inner = mixed[at_head].astype(F32) * o_ref[zz, at_head, :].astype(F32)
            row = heads_part + hh
            stats[zz, row : row + 1, :] = jnp.sum(inner, axis=0, keepdims=True)
            stats[zz, hh : hh + 1, :] = l_mine[z, zz, hh : hh + 1, :]
        stats[zz, 2 * heads_part : 8, :] = jnp.zeros((8 - 2 * heads_part, rows), F32)
        return carry

    lax.fori_loop(0, n, mixed_part, 0)
    gather.drain()
    leaving.wait(*range(KEPT))
    for g in range(4):
        keep(g).wait()
    for i in range(halo_chunks):

        @pl.when((z >= i) & (z < n - 1))
        def _(i=i):
            halo_copy(i).wait_send()


def forward(n, halo_chunks, ins, shards):
    tokens, memory = ins[2], ins[7]
    rows, width = tokens.shape
    keys = (halo_chunks + 1) * rows
    heads = width // HD
    parts = n
    rows_part = width // parts
    held_plots, patches, _ = memory.shape
    unit = rows_part // 4
    full = [(n, 2, 2, 2, unit, width)] * 4 + [(n,) + s.shape for s in shards]
    count = len(full)
    struct = jax.ShapeDtypeStruct
    out_shape = [struct(f, BF16) for f in full[:4]] + [
        struct((keys, rows), F32),
        struct((n, 1, rows), jnp.int32),
        struct((keys, width), BF16),
        struct((keys, width), BF16),
        struct((width, rows), BF16),
        struct((keys, width), BF16),
        struct((width, keys), BF16),
        struct((keys, width), BF16),
        struct((width, rows), BF16),
        struct((heads // 2, 8, rows), F32),
        struct((rows, width), F32),
        struct((rows, width), BF16),
        struct((n, parts, rows_part, rows), BF16),
        struct((heads, patches, held_plots * HD), BF16),
        struct((heads, held_plots * HD, patches), BF16),
        struct((heads, patches, held_plots * HD), BF16),
        struct((parts, rows_part, rows), BF16),
        struct((rows, width), BF16),
        struct((rows, width), BF16),
        struct((n, rows, shards[0].shape[-1]), BF16),
        struct((n, rows, shards[0].shape[-1]), BF16),
        struct((n, rows, shards[0].shape[-1]), BF16),
        struct((rows, width), F32),
        struct((rows, width), BF16),
        struct((parts, rows_part, rows), BF16),
        struct((parts, 8, rows), F32),
        struct((1, width), F32),
    ]
    scratch = [held(o) for o in out_shape[4 : 4 + KEPT]]
    scratch += [pltpu.VMEM(f, BF16) for f in full]
    scratch += [
        pltpu.VMEM((halo_chunks + 1, rows, width), BF16),
        pltpu.VMEM((width, keys), BF16),
        pltpu.VMEM((heads, held_plots * HD, patches), BF16),
        pltpu.VMEM((parts, rows_part, rows), BF16),
    ]
    for _ in range(3):
        scratch += [
            pltpu.VMEM((n, parts, rows_part, rows), BF16),
            pltpu.VMEM((n, parts, 8, rows), F32),
        ]
    scratch += [pltpu.VMEM((rows, width), F32)] * 3
    scratch += line_sems(n, parts, 1, 2)
    scratch += gather_sems(n, count)
    scratch += [DMA((halo_chunks,)), DMA((halo_chunks,)), DMA((4,)), DMA((KEPT,))]
    smem = pl.BlockSpec(memory_space=pltpu.SMEM)
    out = pl.pallas_call(
        functools.partial(forward_kernel, n, count, halo_chunks),
        out_shape=out_shape,
        in_specs=[smem] * 2 + [VMEM] * 14 + [ANY] * (count - 4),
        out_specs=[ANY] * (4 + KEPT) + [VMEM] * (27 - KEPT),
        scratch_shapes=scratch,
        compiler_params=pltpu.CompilerParams(
            collective_id=0, has_side_effects=True, vmem_limit_bytes=63 << 20
        ),
        name="forward",
    )(*ins, *shards)
    return out[:4], out[4:]


def norm_gradient(rows, gain, back):
    inverse = lax.rsqrt(jnp.mean(rows * rows, axis=-1, keepdims=True) + epsilon)
    unit = rows * inverse
    scaled = back * gain
    inner = jnp.mean(scaled * unit, axis=-1, keepdims=True)
    return inverse * (scaled - unit * inner), jnp.sum(back * unit, axis=0, keepdims=True)


def as_unit(rows_192):
    rows, width = rows_192.shape
    return rows_192.reshape(2, 2, rows // 4, width)


def cross_backward_kernel(n, count, *refs):
    plots, do_ref, st_ref, cross_gain = refs[:4]
    late, at = refs[4:21], 21
    quarters = refs[at : at + count]
    grad_mem, part_keys, part_query, first_back, g_first, gain_cross = refs[
        at + count : at + count + 6
    ]
    rest = refs[at + count + 6 :]
    part, rest = rest[:count], rest[count:]
    reduce, rest = take_reduce(n, 0, part, None, [False] * count, [None] * count, rest)
    do_all, st_all, q_mine, q_right, q_left, dk_ref, dv_ref, k_back, v_back = rest[:9]
    line = rest[9:17]
    inside, load_sems = rest[17:34], rest[34]
    (
        normed_hidden, gate_back, up_back, hidden, cot, q_all, k_ref, v_ref, kt_ref,
        mem, w_keys, w_query, cross_mix, grad_rows, normed_cross, second_back, first_sum,
    ) = inside
    loads = Moves(list(zip(late, inside)), load_sems)
    loads.start(*range(17))
    dp, z, c, x, y = place()
    parts, rows_part, rows = do_ref.shape
    width = parts * rows_part
    heads_part = rows_part // HD
    heads = parts * heads_part
    held_plots = mem.shape[0]
    scale = HD ** (-0.5)
    greet(reduce.peers())

    def clear(h, carry):
        dk_ref[h] = jnp.zeros(dk_ref.shape[1:], F32)
        dv_ref[h] = jnp.zeros(dv_ref.shape[1:], F32)
        return carry

    def compute(j, p):
        plot_row = plots[j]
        for hh in range(heads_part):
            h = p * heads_part + hh
            at_head = slice(hh * HD, (hh + 1) * HD)
            q_pair = both_plots(q_all[j, p, at_head, :], plot_row)
            do_pair = both_plots(do_all[j, p, at_head, :], plot_row)
            scores = jnp.dot(k_ref[h], q_pair, preferred_element_type=F32)
            chances = jnp.exp(scores - st_all[j, p, hh : hh + 1, :])
            prob_back = jnp.dot(v_ref[h], do_pair, preferred_element_type=F32)
            inner = st_all[j, p, heads_part + hh : heads_part + hh + 1, :]
            score_back = (chances * (prob_back - inner)).astype(BF16)
            q_back = jnp.dot(kt_ref[h], score_back, preferred_element_type=F32)
            q_mine[j, p, at_head, :] = (own_plot(q_back, plot_row) * scale).astype(BF16)
            dk_ref[h] += product(score_back, q_pair, 1, 1)
            dv_ref[h] += product(chances.astype(BF16), do_pair, 1, 1)

    def merge(j, p, arrived):
        total = q_mine[j, p].astype(F32) + arrived[0][j, p].astype(F32)
        q_mine[j, p] = total.astype(BF16)

    def finish(p):
        pass

    def hidden_gradients():
        firsts = (normed_hidden, normed_hidden, None)
        for g, seconds in enumerate((gate_back, up_back, None)):

            def step(zz, carry, g=g, seconds=seconds):
                if seconds is None:
                    grad = product(hidden[zz], cot[...], 0, 0)
                else:
                    grad = product(firsts[g][...], seconds[zz], 0, 0)
                part[g][zz] = grad.astype(BF16).reshape(part[g].shape[1:])
                return carry

            loads.wait(*((0, 1), (2,), (3, 4))[g])
            lax.fori_loop(0, n, step, 0)
            reduce.run(g, 0)

        loads.wait(5, 6, 7, 8)

    def patch_gradients():
        for source, out in ((dk_ref, k_back), (dv_ref, v_back)):

            def pair_step(i, carry, source=source, out=out):
                even, odd = source[2 * i], source[2 * i + 1]
                lane = lax.broadcasted_iota(jnp.int32, even.shape, 1)
                cols = pl.ds(pl.multiple_of(i * 2 * HD, 2 * HD), 2 * HD)
                out[0, :, cols] = jnp.where(lane < HD, even, pltpu.roll(odd, HD, 1)).astype(BF16)
                out[1, :, cols] = jnp.where(lane < HD, pltpu.roll(even, HD, 1), odd).astype(BF16)
                return carry

            lax.fori_loop(0, heads // 2, pair_step, 0)
        for which, back in enumerate((k_back, v_back)):
            for pair in range(n // 2):
                cols = slice(pair * 2 * rows_part, (pair + 1) * 2 * rows_part)
                grad = sum(product(back[p, :, cols], mem[p], 0, 0) for p in range(held_plots))
                grad = grad.astype(BF16)
                part_keys[2 * pair, which] = as_unit(grad[:rows_part])
                part_keys[2 * pair + 1, which] = as_unit(grad[rows_part:])

        def memory_step(i, carry):
            p, at_rows = i // 2, pl.ds(pl.multiple_of(lax.rem(i, 2) * rows, rows), rows)
            total = 0.0
            for which, back in enumerate((k_back, v_back)):
                for pair in range(n // 2):
                    cols = slice(pair * 2 * rows_part, (pair + 1) * 2 * rows_part)
                    weights = two_units(w_keys, pair, which)
                    total = total + product(back[p, at_rows, cols], weights, 1, 0)
            grad_mem[p, at_rows, :] = total.astype(BF16)
            return carry

        lax.fori_loop(0, held_plots * (mem.shape[1] // rows), memory_step, 0)

    def hook(t):
        for step, work in schedule.items():

            @pl.when(t == step)
            def _(work=work):
                for g, stage in work:
                    reduce.run(g, stage)

        @pl.when(t == n - 1)
        def _():
            loads.wait(9, 10)
            patch_gradients()
            for g in range(count):
                reduce.run(g, 2)

    schedule = {0: [(0, 1), (1, 1), (2, 1)]}

    def before():
        lax.fori_loop(0, heads, clear, 0)
        hidden_gradients()

    exchange = ([do_ref, st_ref], [do_all, st_all], [q_mine], [q_right], [q_left], line)
    line_exchange(n, parts, z, dp, exchange, compute, merge, finish, hook, before)

    loads.wait(*range(11, 17))
    back = 0.0
    for zz in range(n):
        mine = q_mine[z, zz]
        part_query[zz, 0] = as_unit(product(mine, normed_cross[...], 1, 0).astype(BF16))
        part_query[zz, 1] = as_unit(product(cross_mix[zz], grad_rows[...], 1, 0).astype(BF16))
        back = back + product(mine, unit_rows(w_query, zz, 0), 0, 0)
    residual, gain_back = norm_gradient(first_sum[...], cross_gain[...], back)
    total = second_back[...] + residual
    first_back[...] = total
    g_first[...] = total.astype(BF16)
    gain_cross[...] = gain_back
    for g in range(count):
        reduce.end(2, g)
        quarters[g][...] = reduce.acc[g][:, y, x]
    reduce.drain()


def cross_backward(n, ins, shapes):
    do, mem = ins[1], ins[13]
    parts, rows_part, rows = do.shape
    width = parts * rows_part
    heads = width // HD
    held_plots, patches, _ = mem.shape
    count = len(shapes)
    struct = jax.ShapeDtypeStruct
    unit = width // n // 4
    scratch = [pltpu.VMEM((n, 2, 2, 2) + s, BF16) for s in shapes]
    scratch += reduce_scratch(n, 0, shapes, [BF16] * count, [False] * count, [True] * count)
    scratch += [
        pltpu.VMEM((n, parts, rows_part, rows), BF16),
        pltpu.VMEM((n, parts, 8, rows), F32),
        pltpu.VMEM((n, parts, rows_part, rows), BF16),
        pltpu.VMEM((n, parts, rows_part, rows), BF16),
        pltpu.VMEM((n, parts, rows_part, rows), BF16),
        pltpu.VMEM((heads, patches, held_plots * HD), F32),
        pltpu.VMEM((heads, patches, held_plots * HD), F32),
        pltpu.VMEM((held_plots, patches, width), BF16),
        pltpu.VMEM((held_plots, patches, width), BF16),
    ]
    scratch += line_sems(n, parts, 2, 1)
    scratch += [held(i) for i in ins[4:]] + [DMA((len(ins) - 4,))]
    out = pl.pallas_call(
        functools.partial(cross_backward_kernel, n, count),
        out_shape=[struct((n,) + s, BF16) for s in shapes]
        + [
            struct(mem.shape, BF16),
            struct((n, 2, 2, 2, unit, width), BF16),
            struct((n, 2, 2, 2, unit, width), BF16),
            struct((rows, width), F32),
            struct((rows, width), BF16),
            struct((1, width), F32),
        ],
        in_specs=[VMEM] * 4 + [ANY] * 17,
        out_specs=[VMEM] * (count + 6),
        scratch_shapes=scratch,
        compiler_params=pltpu.CompilerParams(
            collective_id=1, has_side_effects=True, vmem_limit_bytes=63 << 20
        ),
        name="cross_backward",
    )(*ins)
    return out[:count], out[count:]


def alone(rows, which):
    zero = jnp.zeros_like(rows)
    return jnp.concatenate([rows, zero] if which == 0 else [zero, rows], axis=0)


def self_backward_kernel(n, extra, halo_chunks, *refs):
    self_gain, gain_cross, gain_hidden = refs[:3]
    late = refs[3:16]
    cross_parts = refs[16:18]
    sums = refs[18:21]
    fin = list(refs[21:30])
    grad_tokens, gain_out = refs[30:32]
    own_parts = refs[32:36]
    gain_part, gain_fin = refs[36:38]
    part = list(cross_parts) + list(own_parts) + [None] * 3 + [gain_part]
    kept = [True, True] + [False] * 8
    quarters = [None] * 6 + list(sums) + [None]
    reduce, rest = take_reduce(n, extra, part, fin + [gain_fin], kept, quarters, refs[38:])
    do_ref, dq_ref, dk_ref, dv_ref, own_back, csend, crecv, gain_rows, hs, hr = rest[:10]
    inside, load_sems = rest[10:23], rest[23]
    (
        g_first, mix, w_vo, k_ref, q_ref, v_ref, kt_ref, bias, logs, w_qk, near, normed, first_back,
    ) = inside
    loads = Moves(list(zip(late, inside)), load_sems)
    loads.start(*range(13))
    dp, z, c, x, y = place()
    rows, width = g_first.shape
    heads = width // HD
    rows_part = width // n
    scale = HD ** (-0.5)
    own_rows = slice(halo_chunks * rows, (halo_chunks + 1) * rows)
    early_groups, late_groups, hidden_groups = (0, 1, 2), (3, 4, 5, 9), (6, 7, 8)
    half = width // 2

    def store_unit(out, zz, grad):
        for cc in range(2):
            columns = grad[:, cc * half : (cc + 1) * half]
            out[zz, :, :, cc] = columns.reshape(2, 2, rows_part // 4, half)

    def all_run(groups, stage):
        for g in groups:
            reduce.run(g, stage)

    greet(reduce.peers())
    all_run((0, 1), 0)
    for g in hidden_groups:
        reduce.begin(3, g)
    loads.wait(0, 1)
    for zz in range(n):
        at_part = slice(zz * rows_part, (zz + 1) * rows_part)
        store_unit(own_parts[0], zz, product(mix[at_part, :], g_first[...], 1, 0).astype(BF16))
    reduce.run(2, 0)
    loads.wait(2)

    def do_part(zz, carry):
        at_part = pl.ds(pl.multiple_of(zz * rows_part, rows_part), rows_part)
        do_ref[at_part, :] = product(unit_rows(w_vo, zz, 1), g_first[...], 1, 1).astype(BF16)
        return carry

    lax.fori_loop(0, n, do_part, 0)
    all_run(early_groups, 1)

    def pair_step(pair, carry):
        cols = pl.ds(pl.multiple_of(pair * 2 * HD, 2 * HD), 2 * HD)
        dk, dv = 0.0, 0.0
        for which in range(2):
            at_head = pl.ds(pl.multiple_of((2 * pair + which) * HD, HD), HD)
            q_pair = alone(q_ref[at_head, :], which)
            do_head = do_ref[at_head, :]
            inner = jnp.sum(
                do_head.astype(F32) * mix[at_head, :].astype(F32), axis=0, keepdims=True
            )
            do_pair = alone(do_head, which)
            scores = jnp.dot(k_ref[:, cols], q_pair, preferred_element_type=F32)
            chances = jnp.exp(scores + bias[...] - logs[pair, which : which + 1, :])
            prob_back = jnp.dot(v_ref[:, cols], do_pair, preferred_element_type=F32)
            score_back = (chances * (prob_back - inner)).astype(BF16)
            q_back = jnp.dot(kt_ref[at_head, :], score_back, preferred_element_type=F32)
            dq_ref[at_head, :] = (q_back * scale).astype(BF16)
            dk = dk + product(score_back, q_pair, 1, 1)
            dv = dv + product(chances.astype(BF16), do_pair, 1, 1)
        dk_ref[:, cols] = dk.astype(BF16)
        dv_ref[:, cols] = dv.astype(BF16)
        return carry

    loads.wait(3, 4, 5, 6, 7, 8)
    lax.fori_loop(0, heads // 2, pair_step, 0)
    loads.wait(9, 10, 11, 12)

    def halo_copy(i):
        dev = (dp, lax.rem(z + n - 1, n))
        return remote(csend.at[i], crecv.at[i], hs.at[i], hr.at[i], dev)

    def halo_send(i):
        if i > 0:
            halo_take(i - 1, csend.at[i])

        @pl.when(z >= halo_chunks - i)
        def _():
            halo_copy(i).start()

    def halo_take(i, onto):
        @pl.when((z + 1 < n) & (z + 1 >= halo_chunks - i))
        def _():
            halo_copy(i).wait_recv()
            onto[...] = (onto[...].astype(F32) + crecv[i].astype(F32)).astype(onto.dtype)

    gain_self = jnp.zeros((1, width), F32)
    for i in range(halo_chunks + 1):
        at_rows = slice(i * rows, (i + 1) * rows)
        back = 0.0
        for pair in range(n // 2):
            cols = slice(pair * 2 * rows_part, (pair + 1) * 2 * rows_part)
            back = back + product(dk_ref[at_rows, cols], two_units(w_qk, pair, 1), 1, 0)
            back = back + product(dv_ref[at_rows, cols], two_units(w_vo, pair, 0), 1, 0)
        if i < halo_chunks:
            csend[i] = back.astype(BF16)
            if i == 0:
                halo_send(0)
        else:
            for zz in range(n):
                at_part = slice(zz * rows_part, (zz + 1) * rows_part)
                back = back + product(dq_ref[at_part, :], unit_rows(w_qk, zz, 0), 0, 0)
            own_back[...] = back
        here = near[at_rows, :].astype(F32)
        inverse = lax.rsqrt(jnp.mean(here * here, axis=-1, keepdims=True) + epsilon)
        gain_self = gain_self + jnp.sum(back * here * inverse, axis=0, keepdims=True)

    lanes = gain_rows.shape[1]
    gain_rows[...] = jnp.zeros(gain_rows.shape, F32)
    for i, gain in enumerate((gain_self, gain_cross[...], gain_hidden[...])):
        for j in range(width // lanes):
            row = i * (width // lanes) + j
            gain_rows[row : row + 1, :] = gain[:, j * lanes : (j + 1) * lanes]
    gain_part[...] = jnp.zeros(gain_part.shape, F32)
    for zz in range(n):
        gain_part[zz, 0, 0, 0] = gain_rows[...]
    for g, back in ((3, dv_ref), (4, dk_ref)):
        for pair in range(n // 2):
            cols = slice(pair * 2 * rows_part, (pair + 1) * 2 * rows_part)
            grad = product(back[:, cols], normed[...], 0, 0).astype(BF16)
            store_unit(own_parts[g - 2], 2 * pair, grad[:rows_part])
            store_unit(own_parts[g - 2], 2 * pair + 1, grad[rows_part:])
        reduce.run(g, 0)
    for zz in range(n):
        at_part = slice(zz * rows_part, (zz + 1) * rows_part)
        grad = product(dq_ref[at_part, :], normed[own_rows, :], 1, 0)
        store_unit(own_parts[3], zz, grad.astype(BF16))
    reduce.run(5, 0)
    reduce.run(9, 0)
    all_run(early_groups, 2)
    all_run(late_groups, 1)
    all_run(early_groups, 3)
    all_run(hidden_groups, 4)
    for i in range(1, halo_chunks):
        halo_send(i)
    all_run(late_groups, 2)
    all_run(hidden_groups, 5)
    all_run(late_groups, 3)
    all_run(early_groups, 4)
    all_run(hidden_groups, 6)
    halo_take(halo_chunks - 1, own_back)
    here = near[own_rows, :].astype(F32)
    residual, _ = norm_gradient(here, self_gain[...], own_back[...])
    grad_tokens[...] = (first_back[...] + residual).astype(BF16)
    all_run(early_groups, 5)
    all_run(late_groups, 4)
    all_run(early_groups, 6)
    all_run(late_groups, 5)
    all_run(late_groups, 6)
    all_run(range(10), 7)
    for i in range(3):
        for j in range(width // lanes):
            row = i * (width // lanes) + j
            cols = slice(j * lanes, (j + 1) * lanes)
            gain_out[i : i + 1, cols] = gain_fin[0, 0, 0, row : row + 1, :]
    gain_out[3:8, :] = jnp.zeros((5, width), F32)
    for i in range(halo_chunks):

        @pl.when(z >= halo_chunks - i)
        def _(i=i):
            halo_copy(i).wait_send()

    reduce.drain()


def self_backward(n, extra, halo_chunks, ins, cross_parts, sums):
    near, g_first = ins[13], ins[3]
    rows, width = g_first.shape
    keys = near.shape[0]
    unit = width // n // 4
    gain_shape = (16, 256)
    single = (unit, width // 2)
    shapes = [(unit, width)] * 2 + [single] * 4 + [p.shape[1:] for p in sums]
    struct = jax.ShapeDtypeStruct
    scratch = [pltpu.VMEM((n, 2, 2, 2) + single, BF16)] * 4
    scratch += [pltpu.VMEM((n, 2, 2, 2) + gain_shape, F32), pltpu.VMEM((2, 2, 2) + gain_shape, F32)]
    scratch += reduce_scratch(
        n, extra, shapes + [gain_shape], [BF16] * 9 + [F32],
        [True, True] + [False] * 8, [True] * 6 + [False] * 3 + [True],
    )
    scratch += [
        pltpu.VMEM((width, rows), BF16),
        pltpu.VMEM((width, rows), BF16),
        pltpu.VMEM((keys, width), BF16),
        pltpu.VMEM((keys, width), BF16),
        pltpu.VMEM((rows, width), F32),
        pltpu.VMEM((halo_chunks, rows, width), BF16),
        pltpu.VMEM((halo_chunks, rows, width), BF16),
        pltpu.VMEM(gain_shape, F32),
        DMA((halo_chunks,)),
        DMA((halo_chunks,)),
    ]
    scratch += [held(i) for i in ins[3:]] + [DMA((len(ins) - 3,))]
    out = pl.pallas_call(
        functools.partial(self_backward_kernel, n, extra, halo_chunks),
        out_shape=[struct((2, 2, 2) + s, BF16) for s in shapes]
        + [struct((rows, width), BF16), struct((8, width), F32)],
        in_specs=[VMEM] * 3 + [ANY] * 15 + [VMEM] * 3,
        out_specs=[VMEM] * 11,
        scratch_shapes=scratch,
        compiler_params=pltpu.CompilerParams(
            collective_id=2, has_side_effects=True, vmem_limit_bytes=63 << 20
        ),
        name="self_backward",
    )(*ins, *cross_parts, *sums)
    return out[:9], out[9], out[10]


def body(
    tokens, memory, table_lengths, table_plots,
    self_gain, self_query, self_key, self_value, self_output,
    cross_gain, cross_query, cross_key, cross_value, cross_output,
    hidden_gain, hidden_gate, hidden_up, hidden_down, cotangent,
):
    n = lax.axis_size("tensor")
    extra = lax.axis_size("dp").bit_length() - 1 - 3
    rows, width = tokens.shape
    halo_chunks = -(-(LONGEST - 1) // rows)

    def pieces(shard):
        return shard.reshape(2, 2, 2, -1, shard.shape[-1])

    shards = [pieces(hidden_gate), pieces(hidden_up), pieces(hidden_down)]
    ins = (
        table_lengths, table_plots, tokens, cotangent,
        self_gain[None], cross_gain[None], hidden_gain[None], memory,
        cross_key.T, cross_value.T, self_query.T, self_key.T, self_value.T, self_output,
        cross_query.T, cross_output,
    )
    full, saved = forward(n, halo_chunks, ins, shards)
    (
        bias, plots, near, normed_near, self_q, self_k, self_kt, self_v, self_mix, self_logs,
        first_sum, normed_cross, q_all, cross_k, cross_kt, cross_v, cross_mix,
        output, normed_hidden, hidden, gate_back, up_back, second_back, grad_rows, mixed_back,
        cross_stats, gain_hidden,
    ) = saved
    ins = (
        plots, mixed_back, cross_stats, cross_gain[None],
        normed_hidden, gate_back, up_back, hidden, cotangent, q_all, cross_k, cross_v, cross_kt,
        memory, full[0], full[3], cross_mix, grad_rows, normed_cross, second_back, first_sum,
    )
    hidden_pieces, rest = cross_backward(n, ins, [s.shape[3:] for s in shards])
    grad_memory, part_keys, part_query, first_back, g_first, gain_cross = rest
    ins = (
        self_gain[None], gain_cross, gain_hidden,
        g_first, self_mix, full[2], self_k, self_q, self_v, self_kt, bias, self_logs, full[1], near,
        normed_near, first_back,
    )
    sums, grad_tokens, gains = self_backward(
        n, extra, halo_chunks, ins, [part_query, part_keys], hidden_pieces
    )

    def pair(summed):
        both = summed.reshape(2, -1, width).astype(F32)
        return both[0], both[1]

    def whole(summed):
        return summed.reshape(-1, summed.shape[-1]).astype(F32)

    def single(summed):
        return summed.transpose(0, 1, 3, 2, 4).reshape(-1, width).astype(F32)

    g_cq, g_co = pair(sums[0])
    g_ck, g_cv = pair(sums[1])
    g_so, g_sv, g_sk, g_sq = (single(summed) for summed in sums[2:6])
    return (
        output, grad_tokens, grad_memory,
        g_sq.T, g_sk.T, g_sv.T, g_so,
        g_cq.T, g_ck.T, g_cv.T, g_co,
        whole(sums[6]), whole(sums[7]), whole(sums[8]),
        gains[0], gains[1], gains[2],
    )


def solution(mesh):
    in_specs = (
        P(("dp", "tensor"), None),
        P("dp", "tensor", None),
        P("dp", None),
        P("dp", None),
        P(),
        P(None, "tensor"),
        P(None, "tensor"),
        P(None, "tensor"),
        P("tensor", None),
        P(),
        P(None, "tensor"),
        P(None, "tensor"),
        P(None, "tensor"),
        P("tensor", None),
        P(),
        P(None, "tensor"),
        P(None, "tensor"),
        P("tensor", None),
        P(("dp", "tensor"), None),
    )
    out_specs = (
        P(("dp", "tensor"), None),
        P(("dp", "tensor"), None),
        P("dp", "tensor", None),
        P(None, "tensor"),
        P(None, "tensor"),
        P(None, "tensor"),
        P("tensor", None),
        P(None, "tensor"),
        P(None, "tensor"),
        P(None, "tensor"),
        P("tensor", None),
        P(None, "tensor"),
        P(None, "tensor"),
        P("tensor", None),
        P(),
        P(),
        P(),
    )
    return jax.shard_map(body, mesh=mesh, in_specs=in_specs, out_specs=out_specs, check_vma=False)
```

```python
import functools

import jax
import jax.numpy as jnp
from jax import lax
from jax.experimental import pallas as pl
from jax.experimental.pallas import tpu as pltpu
from jax.sharding import PartitionSpec as P

HD = 64
LONGEST = 512
F32 = jnp.float32
BF16 = jnp.bfloat16
MESH = pl.DeviceIdType.MESH
ANY = pl.BlockSpec(memory_space=pl.ANY)
VMEM = pl.BlockSpec(memory_space=pltpu.VMEM)
DMA = pltpu.SemaphoreType.DMA

epsilon = 1e-06
masked_value = -1e30


def product(first_op, second_op, first_dim, second_dim):
    return lax.dot_general(
        first_op,
        second_op,
        (((first_dim,), (second_dim,)), ((), ())),
        preferred_element_type=F32,
    )


def remote(src, dst, send_sem, recv_sem, device):
    return pltpu.make_async_remote_copy(
        src_ref=src,
        dst_ref=dst,
        send_sem=send_sem,
        recv_sem=recv_sem,
        device_id=device,
        device_id_type=MESH,
    )


class Moves:
    def __init__(self, pairs, sems):
        self.copies = [
            pltpu.make_async_copy(src, dst, sems.at[i]) for i, (src, dst) in enumerate(pairs)
        ]

    def start(self, *which):
        for i in which:
            self.copies[i].start()

    def wait(self, *which):
        for i in which:
            self.copies[i].wait()


def held(struct):
    return pltpu.VMEM(struct.shape, struct.dtype)


def place():
    dp = lax.axis_index("dp")
    z = lax.axis_index("tensor")
    return dp, z, lax.rem(dp, 2), lax.rem(dp // 2, 2), lax.rem(dp // 4, 2)


def flipped(dp, bit):
    here = lax.rem(dp // (1 << bit), 2)
    return dp + (1 << bit) * (1 - 2 * here)


def greet(devices):
    barrier = pltpu.get_barrier_semaphore()
    for device in devices:
        pl.semaphore_signal(barrier, inc=1, device_id=device, device_id_type=MESH)
    pl.semaphore_wait(barrier, len(devices))


def greet_line(dp, z, n):
    barrier = pltpu.get_barrier_semaphore()

    @pl.when(z > 0)
    def _():
        pl.semaphore_signal(barrier, inc=1, device_id=(dp, z - 1), device_id_type=MESH)

    @pl.when(z < n - 1)
    def _():
        pl.semaphore_signal(barrier, inc=1, device_id=(dp, z + 1), device_id_type=MESH)

    inner = (z > 0) & (z < n - 1)

    @pl.when(inner)
    def _():
        pl.semaphore_wait(barrier, 2)

    @pl.when(jnp.logical_not(inner))
    def _():
        pl.semaphore_wait(barrier, 1)


class Gather:
    def __init__(self, n, mine, full, sems):
        self.n, self.mine, self.full, self.count = n, mine, full, len(full)
        self.zs, self.zr, self.as_, self.ar, self.bs, self.br, self.cs, self.cr, self.loc = sems
        self.dp, self.z, self.c, self.x, self.y = place()
        z = self.z
        inner = [1 + s // 2 if s % 2 == 0 else n - 1 - s // 2 for s in range(n - 1)]
        self.order = [
            jnp.where(z == 0, n - 1 - s, jnp.where(z == n - 1, 1 + s, inner[s]))
            for s in range(n - 1)
        ]

    def peers(self):
        others = [lax.rem(self.z + k, self.n) for k in range(1, self.n)]
        return [(self.dp, o) for o in others] + [(flipped(self.dp, b), self.z) for b in range(3)]

    def own(self, g):
        return pltpu.make_async_copy(self.mine[g], self.full[g].at[self.z], self.loc.at[g])

    def piece(self, g, k):
        zk = lax.rem(self.z + self.n - k, self.n)
        return self.full[g].at[zk, self.y, self.x, self.c]

    def first(self, g, k):
        src = self.piece(g, 0) if self.mine[g] is None else self.mine[g].at[self.y, self.x, self.c]
        dev = (self.dp, lax.rem(self.z + k, self.n))
        return remote(src, self.piece(g, 0), self.zs.at[g, k - 1], self.zr.at[g, k - 1], dev)

    def passed(self, g, up):
        k = self.n - 2 if up else 2
        dev = (self.dp, lax.rem(self.z + (1 if up else self.n - 1), self.n))
        slot = self.n - 2 if up else 0
        piece = self.piece(g, k)
        return remote(piece, piece, self.zs.at[g, self.n - 1], self.zr.at[g, slot], dev)

    def straight(self, k, start):
        ends = ((self.z == 0) & (k == self.n - 1)) | ((self.z == self.n - 1) & (k == 1))
        pl.when(jnp.logical_not(ends) if self.n > 2 else self.z >= 0)(start)

    def arrived(self, g, k):
        piece = self.piece(g, k)
        dev = (self.dp, lax.rem(self.z + k, self.n))
        return remote(piece, piece, self.zs.at[g, 0], self.zr.at[g, k - 1], dev)

    def second(self, g, s, incoming=False):
        k = self.order[s]
        zk = lax.rem(self.z + self.n - k, self.n)
        x, y, c = self.x, self.y, self.c
        if s % 2 == 1:
            there, bit = self.full[g].at[zk, y, 1 - x if incoming else x, c], 1
        else:
            there, bit = self.full[g].at[zk, 1 - y if incoming else y, x, c], 2
        dev = (flipped(self.dp, bit), self.z)
        return remote(there, there, self.as_.at[g, s], self.ar.at[g, s], dev)

    def third(self, g, s, incoming=False):
        k = self.order[s]
        zk = lax.rem(self.z + self.n - k, self.n)
        x, y, c = self.x, self.y, self.c
        if s % 2 == 1:
            there, bit = self.full[g].at[zk, 1 - y if incoming else y, :, c], 2
        else:
            there, bit = self.full[g].at[zk, :, 1 - x if incoming else x, c], 1
        dev = (flipped(self.dp, bit), self.z)
        return remote(there, there, self.bs.at[g, s], self.br.at[g, s], dev)

    def fourth(self, g, s, incoming=False):
        zk = lax.rem(self.z + self.n - self.order[s], self.n)
        there = self.full[g].at[zk, :, :, 1 - self.c if incoming else self.c]
        dev = (flipped(self.dp, 0), self.z)
        return remote(there, there, self.cs.at[g, s], self.cr.at[g, s], dev)

    def run(self, g, stage):
        n = self.n
        steps = range(n - 1)
        if stage == 0:
            if self.mine[g] is not None:
                self.own(g).start()

            for k in sorted(range(1, n), key=lambda k: min(k, n - k)):
                self.straight(k, lambda k=k: self.first(g, k).start())
        elif stage == 1:
            for s in steps:
                k = self.order[s]
                self.arrived(g, k).wait_recv()
                if n > 2:

                    @pl.when((self.z == n - 2) & (k == n - 2))
                    def _():
                        self.passed(g, True).start()

                    @pl.when((self.z == 1) & (k == 2))
                    def _():
                        self.passed(g, False).start()

                self.second(g, s).start()
        elif stage == 2:
            for s in steps:
                self.second(g, s, True).wait_recv()
                self.third(g, s).start()
        elif stage == 3:
            for s in steps:
                self.third(g, s, True).wait_recv()
                self.fourth(g, s).start()
        else:
            if self.mine[g] is not None:
                self.own(g).wait()
            for s in steps:
                self.fourth(g, s, True).wait_recv()

    def drain(self):
        for g in range(self.count):
            if self.n > 2:

                @pl.when((self.z == self.n - 2) | (self.z == 1))
                def _(g=g):
                    self.passed(g, True).wait_send()

            for s in range(self.n - 1):
                self.straight(s + 1, lambda s=s, g=g: self.first(g, s + 1).wait_send())
                self.second(g, s).wait_send()
                self.third(g, s).wait_send()
                self.fourth(g, s).wait_send()


def gather_sems(n, count):
    return [DMA((count, n)) for _ in range(8)] + [DMA((count,))]


class Reduce:
    def __init__(
        self, n, extra, part, acc, rec1, rec2, rec3, rec4, relay, fin, recx, sems, quarters
    ):
        self.relay = relay
        self.n, self.extra, self.count = n, extra, len(rec4)
        self.part, self.fin, self.recx, self.quarters = part, fin, recx, quarters
        self.rec1, self.rec2, self.rec3, self.rec4 = rec1, rec2, rec3, rec4
        self.sems = sems
        self.dp, self.z, self.c, self.x, self.y = place()
        self.ks = range(1, n)
        self.kept = acc
        self.started = []
        self.acc = []
        for g in range(self.count):
            if part[g] is None:
                self.acc.append(None)
            elif acc[g] is None:
                self.acc.append(part[g].at[:, :, :, self.c])
            else:
                self.acc.append(acc[g])

    def peers(self):
        others = [lax.rem(self.z + k, self.n) for k in self.ks]
        bits = range(3 + self.extra)
        return [(self.dp, o) for o in others] + [(flipped(self.dp, b), self.z) for b in bits]

    def lanes(self, g, half):
        width = self.rec4[g].shape[-1]
        if width == 128:
            return slice(0, width)
        middle = width // 256 * 128 + (128 if width % 256 and g % 2 == 0 else 0)
        return slice(0, middle) if half == 0 else slice(middle, width)

    def copies(self, stage, g, incoming=False):
        halves = range(1 if self.rec4[g].shape[-1] == 128 else 2)
        dp, z, c, x, y, n = self.dp, self.z, self.c, self.x, self.y, self.n
        acc, fin = self.acc[g], self.fin[g] if self.fin else None
        found = []
        if stage == 0:
            src, dst, dev = self.part[g].at[:, :, :, 1 - c], self.rec1[g], (flipped(dp, 0), z)
            found.append((src, dst, dev, 0))
        elif stage == 1:
            for half in halves:
                at = self.lanes(g, half)
                src = acc.at[:, :, 1 - x, :, at] if half == 0 else acc.at[:, 1 - y, :, :, at]
                dev = (flipped(dp, 1 if half == 0 else 2), z)
                found.append((src, self.rec2[g].at[:, :, :, at], dev, 1 + half))
        elif stage == 2:
            for half in halves:
                at = self.lanes(g, half)
                src = acc.at[:, 1 - y, x, :, at] if half == 0 else acc.at[:, y, 1 - x, :, at]
                dev = (flipped(dp, 2 if half == 0 else 1), z)
                found.append((src, self.rec3[g].at[:, :, at], dev, 3 + half))
        elif stage == 3:
            for k in self.ks:
                zk = lax.rem(z + k, n)
                slot = lax.rem(z + n - k, n) if incoming else z
                found.append((self.quarter(g, zk), self.rec4[g].at[slot], (dp, zk), 8 + k))
        elif stage == 4:
            for half in halves:
                at = self.lanes(g, half)
                if half == 0:
                    src = fin.at[1 - y if incoming else y, x, c, :, at]
                else:
                    src = fin.at[y, 1 - x if incoming else x, c, :, at]
                found.append((src, src, (flipped(dp, 2 if half == 0 else 1), z), 5 + half))
        elif stage == 5:
            for half in halves:
                at = self.lanes(g, half)
                if half == 0:
                    src = fin.at[:, 1 - x if incoming else x, c, :, at]
                else:
                    src = fin.at[1 - y if incoming else y, :, c, :, at]
                found.append((src, src, (flipped(dp, 1 if half == 0 else 2), z), 7 + half))
        else:
            src = fin.at[:, :, 1 - c if incoming else c]
            found.append((src, src, (flipped(dp, 0), z), 8 + n))
        return [
            remote(src, dst, self.sems[0].at[g, slot], self.sems[1].at[g, slot], dev)
            for src, dst, dev, slot in found
        ]

    def quarter(self, g, zz):
        if self.quarters[g] is not None:
            return self.quarters[g].at[zz]
        return self.acc[g].at[zz, self.y, self.x]

    def own(self, g):
        src = self.part[g].at[:, :, :, self.c]
        return pltpu.make_async_copy(src, self.acc[g], self.sems[4].at[g])

    def further(self, g, e):
        return remote(
            self.fin[g].at[self.y, self.x, self.c],
            self.recx[g].at[e],
            self.sems[2].at[g, e],
            self.sems[3].at[g, e],
            (flipped(self.dp, 3 + e), self.z),
        )

    def add(self, stage, g):
        n, x, y, c, z = self.n, self.x, self.y, self.c, self.z
        acc, fin = self.acc[g], self.fin[g] if self.fin else None
        kind = self.rec4[g].dtype
        if stage == 1:

            def step(i, carry):
                zz, yy, xx = i // 4, lax.rem(i // 2, 2), lax.rem(i, 2)
                total = acc[zz, yy, xx].astype(F32) + self.rec1[g][zz, yy, xx].astype(F32)
                acc[zz, yy, xx] = total.astype(kind)
                return carry

            lax.fori_loop(0, 4 * n, step, 0)
        elif stage == 2:

            def step(i, carry):
                zz, aa = i // 2, lax.rem(i, 2)
                for half in range(1 if self.rec4[g].shape[-1] == 128 else 2):
                    at = self.lanes(g, half)
                    yy, xx = (aa, x) if half == 0 else (y, aa)
                    came = self.rec2[g][zz, aa, :, at].astype(F32)
                    acc[zz, yy, xx, :, at] = (acc[zz, yy, xx, :, at].astype(F32) + came).astype(kind)
                return carry

            lax.fori_loop(0, 2 * n, step, 0)
        elif stage == 3:

            def step(zz, carry):
                total = acc[zz, y, x].astype(F32) + self.rec3[g][zz].astype(F32)
                acc[zz, y, x] = total.astype(kind)
                return carry

            lax.fori_loop(0, n, step, 0)
        else:
            self.rec4[g][z] = self.quarter(g, z)[...]
            total = self.rec4[g][0].astype(F32)
            for k in self.ks:
                total = total + self.rec4[g][k].astype(F32)
            fin[y, x, c] = total.astype(kind)
            for e in range(self.extra):
                self.further(g, e).start()
                self.further(g, e).wait()
                total = fin[y, x, c].astype(F32) + self.recx[g][e].astype(F32)
                fin[y, x, c] = total.astype(kind)

    def to_relay(self, g, up):
        n = self.n
        k, dev = (n - 1, n - 2) if up else (1, 1)
        src = self.quarter(g, n - 1 if up else 0)
        sems = self.sems
        return remote(
            src, self.relay[g], sems[0].at[g, 8 + k], sems[1].at[g, 9 + n], (self.dp, dev)
        )

    def from_relay(self, g, up):
        n = self.n
        k, dev, slot = (1, n - 1, n - 2) if up else (n - 1, 0, 1)
        dst = self.rec4[g].at[slot]
        sems = self.sems
        return remote(
            self.relay[g], dst, sems[0].at[g, 8 + k], sems[1].at[g, 8 + k], (self.dp, dev)
        )

    def relayed(self, g):
        return self.relay[g] is not None

    def begin_line(self, g, act):
        z, n = self.z, self.n
        for k, copy in zip(self.ks, self.copies(3, g)):
            later = (z == 0) & (k == n - 1) | (z == n - 1) & (k == 1)
            later = later | (z == n - 2) & (k == 1) | (z == 1) & (k == n - 1)
            pl.when(jnp.logical_not(later))(functools.partial(act, copy))
        pl.when(z == 0)(lambda: act(self.to_relay(g, True)))
        pl.when(z == n - 1)(lambda: act(self.to_relay(g, False)))

    def pass_on(self, g):
        z, n = self.z, self.n

        def one(up):
            self.to_relay(g, up).wait_recv()
            own = self.quarter(g, n - 1 if up else 0)[...].astype(F32)
            self.relay[g][...] = (self.relay[g][...].astype(F32) + own).astype(BF16)
            self.from_relay(g, up).start()

        pl.when(z == n - 2)(lambda: one(True))
        pl.when(z == 1)(lambda: one(False))

    def end_line(self, g):
        z, n = self.z, self.n
        for k, copy in zip(self.ks, self.copies(3, g, True)):
            never = (z == n - 1) & (k == n - 1) | (z == 0) & (k == 1)
            pl.when(jnp.logical_not(never))(copy.wait_recv)

        @pl.when(z == n - 1)
        def _():
            self.rec4[g][0] = jnp.zeros(self.rec4[g].shape[1:], BF16)

        @pl.when(z == 0)
        def _():
            self.rec4[g][n - 1] = jnp.zeros(self.rec4[g].shape[1:], BF16)

    def begin(self, stage, g):
        if stage == 3 and self.relayed(g):
            self.begin_line(g, lambda copy: copy.start())
        else:
            for copy in self.copies(stage, g):
                copy.start()
        if (stage, g) not in self.started:
            self.started.append((stage, g))

    def end(self, stage, g):
        if stage == 0 and self.kept[g] is not None:
            self.own(g).wait()
        if stage == 3 and self.relayed(g):
            self.end_line(g)
        else:
            for copy in self.copies(stage, g, True):
                copy.wait_recv()
        if stage < 4:
            self.add(stage + 1, g)

    def run(self, g, stage):
        if stage == 0 and self.kept[g] is not None:
            self.own(g).start()
        if stage > 0:
            self.end(stage - 1, g)
        if stage <= 6:
            self.begin(stage, g)

    def drain(self):
        for stage, g in self.started:
            if stage == 3 and self.relayed(g):
                self.begin_line(g, lambda copy: copy.wait_send())
                pl.when(self.z == self.n - 2)(self.from_relay(g, True).wait_send)
                pl.when(self.z == 1)(self.from_relay(g, False).wait_send)
            else:
                for copy in self.copies(stage, g):
                    copy.wait_send()


def reduce_scratch(n, extra, shapes, kinds, kept, from_start, relays):
    count = len(shapes)
    every = list(zip(shapes, kinds))
    used = [s for s, f in zip(every, from_start) if f]
    scratch = [pltpu.VMEM((n, 2, 2) + s, d) for (s, d), k in zip(every, kept) if k]
    scratch += [pltpu.VMEM((n, 2, 2) + s, d) for s, d in used]
    scratch += [pltpu.VMEM((n, 2) + s, d) for s, d in used]
    scratch += [pltpu.VMEM((n,) + s, d) for s, d in used]
    scratch += [pltpu.VMEM((n,) + s, d) for s, d in every]
    if n > 3:
        scratch += [pltpu.VMEM(s, d) for (s, d), r in zip(every, relays) if r]
    if extra:
        scratch += [pltpu.VMEM((extra,) + s, d) for s, d in every]
    scratch += [
        DMA((count, 10 + n)),
        DMA((count, 10 + n)),
        DMA((count, max(extra, 1))),
        DMA((count, max(extra, 1))),
        DMA((count,)),
    ]
    return scratch


def take_reduce(n, extra, part, fin, kept, quarters, relays, refs):
    refs = list(refs)
    acc = [refs.pop(0) if k else None for k in kept]
    recs = []
    for _ in range(3):
        recs.append([refs.pop(0) if p is not None else None for p in part])
    recs.append([refs.pop(0) for _ in part])
    recs.append([refs.pop(0) if n > 3 and r else None for r in relays])
    recx = [refs.pop(0) for _ in part] if extra else None
    sems = [refs.pop(0) for _ in range(5)]
    return Reduce(n, extra, part, acc, *recs, fin, recx, sems, quarters), refs


def both_plots(rows, plot_row):
    wide = rows.astype(F32)
    zero = jnp.zeros_like(wide)
    return jnp.concatenate(
        [jnp.where(plot_row == 0, wide, zero), jnp.where(plot_row == 0, zero, wide)], axis=0
    ).astype(BF16)


def own_plot(pair, plot_row):
    half = pair.shape[0] // 2
    return jnp.where(plot_row == 0, pair[:half], pair[half:])


def line_exchange(n, parts, z, dp, refs, compute, merge, finish, hook, before=None):
    own, spread, mine, from_right, from_left, sems = refs
    ups, upr, dns, dnr, rls, rlr, rrs, rrr = sems

    def up(j, p, i, start):
        src = own[i].at[p] if start else spread[i].at[j, p]
        return remote(
            src, spread[i].at[j, p], ups.at[i, j, p], upr.at[i, j, p], (dp, lax.rem(z + 1, n))
        )

    def down(j, p, i, start):
        src = own[i].at[p] if start else spread[i].at[j, p]
        return remote(
            src,
            spread[i].at[j, p],
            dns.at[i, j, p],
            dnr.at[i, j, p],
            (dp, lax.rem(z + n - 1, n)),
        )

    def back_left(j, p, i):
        return remote(
            mine[i].at[j, p],
            from_right[i].at[j, p],
            rls.at[i, j, p],
            rlr.at[i, j, p],
            (dp, lax.rem(z + n - 1, n)),
        )

    def back_right(j, p, i):
        return remote(
            mine[i].at[j, p],
            from_left[i].at[j, p],
            rrs.at[i, j, p],
            rrr.at[i, j, p],
            (dp, lax.rem(z + 1, n)),
        )

    out_kinds = range(len(own))
    back_kinds = range(len(mine))

    def send_own(p, carry):
        for i in out_kinds:

            @pl.when(z < n - 1)
            def _():
                up(z, p, i, True).start()

            @pl.when(z > 0)
            def _():
                down(z, p, i, True).start()

        return carry

    lax.fori_loop(0, parts, send_own, 0)
    if before is not None:
        before()

    def slot(t, carry):
        def one_part(p, inner):
            low = z - t
            high = z + t

            def one_side(side, done):
                chunk = jnp.where(side == 0, low, high)
                held = jnp.where(side == 0, low >= 0, (high < n) & (t > 0))

                @pl.when((t < n) & held)
                def _():
                    @pl.when(t == 0)
                    def _():
                        for i in out_kinds:
                            spread[i][z, p] = own[i][p]

                    compute(chunk, p)

                    @pl.when((t > 0) & (side == 0) & (z == n - 1))
                    def _():
                        for i in back_kinds:
                            back_left(low, p, i).start()

                    @pl.when((t > 0) & (side == 1) & (z == 0))
                    def _():
                        for i in back_kinds:
                            back_right(high, p, i).start()

                return done

            lax.fori_loop(0, 2, one_side, 0)

            @pl.when((t + 1 < n) & (low - 1 >= 0))
            def _():
                for i in out_kinds:
                    up(low - 1, p, i, False).wait_recv()

                    @pl.when(z < n - 1)
                    def _():
                        up(low - 1, p, i, False).start()

            @pl.when((t + 1 < n) & (high + 1 < n))
            def _():
                for i in out_kinds:
                    down(high + 1, p, i, False).wait_recv()

                    @pl.when(z > 0)
                    def _():
                        down(high + 1, p, i, False).start()

            left_chunk = 2 * (n - 1) - z - t

            @pl.when((t > 0) & (left_chunk >= 0) & (left_chunk < z) & (z < n - 1))
            def _():
                for i in back_kinds:
                    back_left(left_chunk, p, i).wait_recv()
                merge(left_chunk, p, from_right)
                for i in back_kinds:
                    back_left(left_chunk, p, i).start()

            right_chunk = t - z

            @pl.when((t > 0) & (right_chunk < n) & (right_chunk > z) & (z > 0))
            def _():
                for i in back_kinds:
                    back_right(right_chunk, p, i).wait_recv()
                merge(right_chunk, p, from_left)
                for i in back_kinds:
                    back_right(right_chunk, p, i).start()

            return inner

        lax.fori_loop(0, parts, one_part, 0)
        hook(t)
        return carry

    lax.fori_loop(0, 2 * n - 2, slot, 0)

    def last(p, carry):
        @pl.when(z > 0)
        def _():
            for i in back_kinds:
                back_right(z, p, i).wait_recv()
            merge(z, p, from_left)

        @pl.when(z < n - 1)
        def _():
            for i in back_kinds:
                back_left(z, p, i).wait_recv()
            merge(z, p, from_right)

        finish(p)
        return carry

    lax.fori_loop(0, parts, last, 0)

    def drain(p, carry):
        for j in range(n):
            for i in out_kinds:

                @pl.when((z < n - 1) & (z == j))
                def _(i=i, j=j):
                    up(j, p, i, True).wait_send()

                @pl.when((z < n - 1) & (z > j))
                def _(i=i, j=j):
                    up(j, p, i, False).wait_send()

                @pl.when((z > 0) & (z == j))
                def _(i=i, j=j):
                    down(j, p, i, True).wait_send()

                @pl.when((z > 0) & (z < j))
                def _(i=i, j=j):
                    down(j, p, i, False).wait_send()

            for i in back_kinds:

                @pl.when(z > j)
                def _(i=i, j=j):
                    back_left(j, p, i).wait_send()

                @pl.when(z < j)
                def _(i=i, j=j):
                    back_right(j, p, i).wait_send()

        return carry

    return lambda: lax.fori_loop(0, parts, drain, 0)


def line_sems(n, parts, out_kinds, back_kinds):
    return [DMA((out_kinds, n, parts))] * 4 + [DMA((back_kinds, n, parts))] * 4


def as_row(ref):
    return ref[...].reshape(1, -1)


def unit_rows(ref, zz, which):
    block = ref[zz, which]
    return block.reshape(-1, block.shape[-1])


def two_units(ref, pair, which):
    return jnp.concatenate(
        [unit_rows(ref, 2 * pair, which), unit_rows(ref, 2 * pair + 1, which)], axis=0
    )


def normed_rows(rows, gain):
    inverse = lax.rsqrt(jnp.mean(rows * rows, axis=-1, keepdims=True) + epsilon)
    return rows * inverse * gain


def half_lanes(first, second, which):
    lane = lax.broadcasted_iota(jnp.int32, first.shape, 1)
    if which == 0:
        return jnp.where(lane < HD, first, pltpu.roll(second, HD, 1))
    return jnp.where(lane < HD, pltpu.roll(first, HD, 1), second)


def tall(out, rows_in, weights, which, n):
    block = 256
    columns = out.shape[1] * 2 // n
    blocks = out.shape[0] // block

    def step(i, carry):
        pair, at = i // blocks, lax.rem(i, blocks)
        at_rows = pl.ds(pl.multiple_of(at * block, block), block)
        cols = pl.ds(pl.multiple_of(pair * columns, columns), columns)
        both = two_units(weights, pair, which)
        out[at_rows, cols] = product(rows_in[at_rows, :], both, 1, 1).astype(BF16)
        return carry

    lax.fori_loop(0, n // 2 * blocks, step, 0)


def flat(out, rows_in, weights, which, n):
    rows_part = out.shape[0] // n

    def step(zz, carry):
        at_part = pl.ds(pl.multiple_of(zz * rows_part, rows_part), rows_part)
        out[at_part, :] = product(unit_rows(weights, zz, which), rows_in[...], 1, 1).astype(BF16)
        return carry

    lax.fori_loop(0, n, step, 0)


def table_at(position, lengths, count):
    table = jnp.zeros(position.shape, jnp.int32)
    end = 0
    for t in range(count):
        end = end + lengths[0, t]
        table = table + (position >= end).astype(jnp.int32)
    return table


KEPT = 23


def forward_kernel(n, count, halo_chunks, *refs):
    (
        lengths, table_plots, tok, cot, self_gain, cross_gain, hidden_gain, mem,
        w_ck, w_cv, w_sq, w_sk, w_sv, w_so, w_cq, w_co,
    ) = refs[:16]
    mine = [None] * 4 + list(refs[16 : 16 + count - 4])
    at = 12 + count
    full_out = refs[at : at + 4]
    at += 4
    out_refs = refs[at : at + 25]
    at += 25
    kept_refs = refs[at : at + KEPT]
    at += KEPT
    (
        bias, plots, near, normed, self_q, self_k, self_mix, self_logs, first_sum, normed_cross,
        q_all, cross_k, cross_kt, cross_v, o_ref,
        output, normed_hidden, hidden, gate_back, up_back, second_back, grad_rows, do_ref, stats,
        gain_hidden,
    ) = kept_refs + out_refs[KEPT:]
    full = refs[at : at + count]
    at += count
    (
        halo, self_vt, cross_vt, cross_q, o_mine, l_mine, o_right, l_right, o_left, l_left,
        down_sum, back_sum, second_sum,
    ) = refs[at : at + 13]
    at += 13
    line = refs[at : at + 8]
    at += 8
    gather_refs = refs[at : at + 9]
    hs, hr, outs, out_sems = refs[at + 9 :]
    leaving = Moves(list(zip(kept_refs, out_refs[:KEPT])), out_sems)
    rows, width = tok.shape
    heads = width // HD
    parts = n
    heads_part = heads // parts
    rows_part = heads_part * HD
    scale = HD ** (-0.5)
    dp, z, c, x, y = place()
    gather = Gather(n, mine, full, gather_refs)
    greet(gather.peers())

    def halo_copy(i):
        src = tok if i == 0 else halo.at[halo_chunks - i]
        dst = halo.at[halo_chunks - 1 - i]
        return remote(src, dst, hs.at[i], hr.at[i], (dp, lax.rem(z + 1, n)))

    def own_units(g, first, second):
        full[g][z, 0] = as_unit(first[...])
        full[g][z, 1] = as_unit(second[...])

    own_units(0, w_ck, w_cv)
    gather.run(0, 0)
    own_units(1, w_sq, w_sk)
    gather.run(1, 0)
    own_units(2, w_sv, w_so)
    own_units(3, w_cq, w_co)

    halo[halo_chunks] = tok[...]
    for i in range(halo_chunks):

        @pl.when(z <= i)
        def _(i=i):
            halo[halo_chunks - 1 - i] = jnp.zeros((rows, width), BF16)

    keys = bias.shape[0]
    held_tables = lengths.shape[1]
    first_key = z * rows - halo_chunks * rows
    key_at = lax.broadcasted_iota(jnp.int32, (keys, rows), 0) + first_key
    query_at = lax.broadcasted_iota(jnp.int32, (1, rows), 1) + z * rows
    same = table_at(key_at, lengths, held_tables) == table_at(query_at, lengths, held_tables)
    allowed = same & (key_at <= query_at) & (key_at >= 0)
    bias[...] = jnp.where(allowed, 0.0, masked_value)
    for j in range(n):
        tables = table_at(
            lax.broadcasted_iota(jnp.int32, (1, rows), 1) + j * rows, lengths, held_tables
        )
        plot = jnp.zeros((1, rows), jnp.int32)
        for t in range(held_tables):
            plot = jnp.where(tables == t, table_plots[0, t], plot)
        plots[j] = plot

    gather.run(0, 1)

    @pl.when(z < n - 1)
    def _():
        halo_copy(0).start()

    gather.run(2, 0)
    gather.run(0, 2)
    gather.run(1, 1)
    gather.run(0, 3)
    gather.run(1, 2)
    gather.run(3, 0)

    def halo_pass(i):
        @pl.when(z > i)
        def _():
            halo_copy(i).wait_recv()

        if i + 1 < halo_chunks:

            @pl.when((z > i) & (z < n - 1))
            def _():
                halo_copy(i + 1).start()

    halo_pass(0)
    gather.run(2, 1)

    def norm_chunk(i, carry):
        at_rows = pl.ds(pl.multiple_of(i * rows, rows), rows)
        near[at_rows, :] = halo[i]
        normed[at_rows, :] = normed_rows(halo[i].astype(F32), as_row(self_gain)).astype(BF16)
        return carry

    gather.run(0, 4)

    plots_held = mem.shape[0]

    def flat_part(which, out):
        def step(zz, carry):
            for p in range(plots_held):
                rows_t = product(unit_rows(full[0], zz, which), mem[p], 1, 1).astype(BF16)
                for hh in range(heads_part):
                    at_head = slice(hh * HD, (hh + 1) * HD)
                    out[zz * heads_part + hh, p * HD : (p + 1) * HD, :] = rows_t[at_head]
            return carry

        lax.fori_loop(0, n, step, 0)

    def tall_part(which, out):
        def step(pair, carry):
            weights = two_units(full[0], pair, which)
            first = product(mem[0], weights, 1, 1)
            second = product(mem[1], weights, 1, 1)
            for hh in range(2 * heads_part):
                cols = slice((hh // 2) * 2 * HD, (hh // 2 + 1) * 2 * HD)
                both = half_lanes(first[:, cols], second[:, cols], hh % 2)
                out[pair * 2 * heads_part + hh] = both.astype(BF16)
            return carry

        lax.fori_loop(0, n // 2, step, 0)

    flat_part(1, cross_vt)
    gather.run(1, 3)
    gather.run(2, 2)
    flat_part(0, cross_kt)
    gather.run(3, 1)
    gather.run(4, 0)
    tall_part(0, cross_k)
    for i in range(1, halo_chunks):
        halo_pass(i)
    gather.run(1, 4)
    gather.run(2, 3)
    gather.run(3, 2)
    lax.fori_loop(0, halo_chunks + 1, norm_chunk, 0)

    own_rows = slice(halo_chunks * rows, (halo_chunks + 1) * rows)

    def query_part(zz, carry):
        at_part = pl.ds(pl.multiple_of(zz * rows_part, rows_part), rows_part)
        projected = product(unit_rows(full[1], zz, 0), normed[own_rows, :], 1, 1)
        self_q[at_part, :] = (projected.astype(BF16).astype(F32) * scale).astype(BF16)
        return carry

    lax.fori_loop(0, n, query_part, 0)

    tall(self_k, normed, full[1], 1, n)
    gather.run(5, 0)
    gather.run(2, 4)

    flat(self_vt, normed, full[2], 0, n)
    gather.run(3, 3)

    def self_pair(pair, carry):
        cols = pl.ds(pl.multiple_of(pair * 2 * HD, 2 * HD), 2 * HD)
        for which in range(2):
            at_head = pl.ds(pl.multiple_of((2 * pair + which) * HD, HD), HD)
            scores = jnp.dot(
                self_k[:, cols], alone(self_q[at_head, :], which), preferred_element_type=F32
            )
            scores = scores + bias[...]
            top = jnp.max(scores, axis=0, keepdims=True)
            powers = jnp.exp(scores - top)
            total = jnp.sum(powers, axis=0, keepdims=True)
            mixed = jnp.dot(self_vt[at_head, :], powers.astype(BF16), preferred_element_type=F32)
            self_mix[at_head, :] = (mixed / total).astype(BF16)
            self_logs[pair, which : which + 1, :] = top + jnp.log(total)
        return carry

    lax.fori_loop(0, heads // 4, self_pair, 0)
    lax.fori_loop(heads // 4, heads // 2, self_pair, 0)

    first_sum[...] = tok[...].astype(F32)

    def first_part(zz, carry):
        at_part = pl.ds(pl.multiple_of(zz * rows_part, rows_part), rows_part)
        first_sum[...] += product(self_mix[at_part, :], unit_rows(full[2], zz, 1), 0, 0)
        return carry

    lax.fori_loop(0, n, first_part, 0)
    total = first_sum[...]
    normed_cross[...] = normed_rows(total, as_row(cross_gain)).astype(BF16)
    gather.run(3, 4)

    def cross_query_part(zz, carry):
        projected = product(unit_rows(full[3], zz, 0), normed_cross[...], 1, 1)
        cross_q[zz] = (projected.astype(BF16).astype(F32) * scale).astype(BF16)
        return carry

    lax.fori_loop(0, n, cross_query_part, 0)

    def compute(j, p):
        plot_row = plots[j]
        for hh in range(heads_part):
            h = p * heads_part + hh
            q_pair = both_plots(q_all[j, p, hh * HD : (hh + 1) * HD, :], plot_row)
            scores = jnp.dot(cross_k[h], q_pair, preferred_element_type=F32)
            top = jnp.max(scores, axis=0, keepdims=True)
            powers = jnp.exp(scores - top)
            total = jnp.sum(powers, axis=0, keepdims=True)
            mixed = jnp.dot(cross_vt[h], powers.astype(BF16), preferred_element_type=F32)
            mixed = own_plot(mixed, plot_row) / total
            o_mine[j, p, hh * HD : (hh + 1) * HD, :] = mixed.astype(BF16)
            l_mine[j, p, hh : hh + 1, :] = top + jnp.log(total)

    def merge(j, p, arrived):
        for hh in range(heads_part):
            at_head = slice(hh * HD, (hh + 1) * HD)
            log_a = l_mine[j, p, hh : hh + 1, :]
            log_b = arrived[1][j, p, hh : hh + 1, :]
            top = jnp.maximum(log_a, log_b)
            share_a = jnp.exp(log_a - top)
            share_b = jnp.exp(log_b - top)
            total = share_a + share_b
            mixed = o_mine[j, p, at_head, :].astype(F32) * (share_a / total)
            mixed = mixed + arrived[0][j, p, at_head, :].astype(F32) * (share_b / total)
            o_mine[j, p, at_head, :] = mixed.astype(BF16)
            l_mine[j, p, hh : hh + 1, :] = top + jnp.log(total)

    def finish(p):
        o_ref[p] = o_mine[z, p]

    def keep(g):
        return pltpu.make_async_copy(full[g], full_out[g], outs.at[g])

    schedule = {
        0: [(4, 1)],
        1: [(6, 0), (4, 2), (5, 1)],
        2: [(4, 3), (5, 2)],
        3: [(6, 1)],
        4: [(6, 2), (5, 3)],
        5: [(6, 3)],
    }

    def hook(t):
        for step, work in schedule.items():

            @pl.when(t == step)
            def _(step=step, work=work):
                if step == 0:
                    tall_part(1, cross_v)
                for g, stage in work:
                    gather.run(g, stage)
                if step == 0:
                    for g in range(4):
                        keep(g).start()

        @pl.when(t == 2 * n - 3)
        def _():
            leaving.start(*range(14))

    exchange = ([cross_q], [q_all], [o_mine, l_mine], [o_right, l_right], [o_left, l_left], line)
    end_exchange = line_exchange(n, parts, z, dp, exchange, compute, merge, finish, hook)

    second_sum[...] = first_sum[...]

    def second_part(zz, carry):
        second_sum[...] += product(o_ref[zz], unit_rows(full[3], zz, 1), 0, 0)
        return carry

    lax.fori_loop(0, n, second_part, 0)
    total = second_sum[...]
    normed_hidden[...] = normed_rows(total, as_row(hidden_gain)).astype(BF16)
    leaving.start(14, 16)
    down_sum[...] = jnp.zeros((rows, width), F32)
    back_sum[...] = jnp.zeros((rows, width), F32)
    for g in range(4, 7):
        gather.run(g, 4)
    slope = (2.0 / 3.141592653589793) ** 0.5
    bend = 0.044715

    def whole(g, zz):
        block = full[g][zz]
        return block.reshape(-1, block.shape[-1])

    def hidden_part(zz, carry):
        gate = product(normed_hidden[...], whole(4, zz), 1, 0)
        up = product(normed_hidden[...], whole(5, zz), 1, 0)
        act_back = product(cot[...], whole(6, zz), 1, 1).astype(BF16).astype(F32)
        square = gate * gate
        curve = jnp.tanh(slope * (gate + bend * square * gate))
        cdf = 0.5 * (1.0 + curve)
        act = gate * cdf
        turn = cdf + 0.5 * gate * (1.0 - curve * curve) * slope * (1.0 + 3.0 * bend * square)
        here = (act * up).astype(BF16)
        to_gate = (act_back * up * turn).astype(BF16)
        to_up = (act_back * act).astype(BF16)
        hidden[zz] = here
        gate_back[zz] = to_gate
        up_back[zz] = to_up
        down_sum[...] += product(here, whole(6, zz), 1, 0)
        back_sum[...] += product(to_gate, whole(4, zz), 1, 1) + product(to_up, whole(5, zz), 1, 1)
        return carry

    lax.fori_loop(0, n, hidden_part, 0)
    leaving.start(17, 18, 19)
    output[...] = (second_sum[...] + down_sum[...]).astype(BF16)
    leaving.start(15)
    residual, gain_back = norm_gradient(second_sum[...], as_row(hidden_gain), back_sum[...])
    gain_hidden[...] = gain_back
    total = cot[...].astype(F32) + residual
    second_back[...] = total
    grad_rows[...] = total.astype(BF16)
    leaving.start(20, 21)

    def mixed_part(zz, carry):
        mixed = product(unit_rows(full[3], zz, 1), grad_rows[...], 1, 1).astype(BF16)
        do_ref[zz] = mixed
        for hh in range(heads_part):
            at_head = slice(hh * HD, (hh + 1) * HD)
            inner = mixed[at_head].astype(F32) * o_ref[zz, at_head, :].astype(F32)
            row = heads_part + hh
            stats[zz, row : row + 1, :] = jnp.sum(inner, axis=0, keepdims=True)
            stats[zz, hh : hh + 1, :] = l_mine[z, zz, hh : hh + 1, :]
        stats[zz, 2 * heads_part : 8, :] = jnp.zeros((8 - 2 * heads_part, rows), F32)
        return carry

    lax.fori_loop(0, n, mixed_part, 0)
    leaving.start(22)
    end_exchange()
    gather.drain()
    leaving.wait(*range(KEPT))
    for g in range(4):
        keep(g).wait()
    for i in range(halo_chunks):

        @pl.when((z >= i) & (z < n - 1))
        def _(i=i):
            halo_copy(i).wait_send()


def forward(n, halo_chunks, ins, shards):
    tokens, memory = ins[2], ins[7]
    rows, width = tokens.shape
    keys = (halo_chunks + 1) * rows
    heads = width // HD
    parts = n
    rows_part = width // parts
    held_plots, patches, _ = memory.shape
    unit = rows_part // 4
    full = [(n, 2, 2, 2, unit, width)] * 4 + [(n,) + s.shape for s in shards]
    count = len(full)
    struct = jax.ShapeDtypeStruct
    out_shape = [struct(f, BF16) for f in full[:4]] + [
        struct((keys, rows), F32),
        struct((n, 1, rows), jnp.int32),
        struct((keys, width), BF16),
        struct((keys, width), BF16),
        struct((width, rows), BF16),
        struct((keys, width), BF16),
        struct((width, rows), BF16),
        struct((heads // 2, 8, rows), F32),
        struct((rows, width), F32),
        struct((rows, width), BF16),
        struct((n, parts, rows_part, rows), BF16),
        struct((heads, patches, held_plots * HD), BF16),
        struct((heads, held_plots * HD, patches), BF16),
        struct((heads, patches, held_plots * HD), BF16),
        struct((parts, rows_part, rows), BF16),
        struct((rows, width), BF16),
        struct((rows, width), BF16),
        struct((n, rows, shards[0].shape[-1]), BF16),
        struct((n, rows, shards[0].shape[-1]), BF16),
        struct((n, rows, shards[0].shape[-1]), BF16),
        struct((rows, width), F32),
        struct((rows, width), BF16),
        struct((parts, rows_part, rows), BF16),
        struct((parts, 8, rows), F32),
        struct((1, width), F32),
    ]
    scratch = [held(o) for o in out_shape[4 : 4 + KEPT]]
    scratch += [pltpu.VMEM(f, BF16) for f in full]
    scratch += [
        pltpu.VMEM((halo_chunks + 1, rows, width), BF16),
        pltpu.VMEM((width, keys), BF16),
        pltpu.VMEM((heads, held_plots * HD, patches), BF16),
        pltpu.VMEM((parts, rows_part, rows), BF16),
    ]
    for _ in range(3):
        scratch += [
            pltpu.VMEM((n, parts, rows_part, rows), BF16),
            pltpu.VMEM((n, parts, 8, rows), F32),
        ]
    scratch += [pltpu.VMEM((rows, width), F32)] * 3
    scratch += line_sems(n, parts, 1, 2)
    scratch += gather_sems(n, count)
    scratch += [DMA((halo_chunks,)), DMA((halo_chunks,)), DMA((4,)), DMA((KEPT,))]
    smem = pl.BlockSpec(memory_space=pltpu.SMEM)
    out = pl.pallas_call(
        functools.partial(forward_kernel, n, count, halo_chunks),
        out_shape=out_shape,
        in_specs=[smem] * 2 + [VMEM] * 14 + [ANY] * (count - 4),
        out_specs=[ANY] * (4 + KEPT) + [VMEM] * (25 - KEPT),
        scratch_shapes=scratch,
        compiler_params=pltpu.CompilerParams(
            collective_id=0, has_side_effects=True, vmem_limit_bytes=63 << 20
        ),
        name="forward",
    )(*ins, *shards)
    return out[:4], out[4:]


def norm_gradient(rows, gain, back):
    inverse = lax.rsqrt(jnp.mean(rows * rows, axis=-1, keepdims=True) + epsilon)
    unit = rows * inverse
    scaled = back * gain
    inner = jnp.mean(scaled * unit, axis=-1, keepdims=True)
    return inverse * (scaled - unit * inner), jnp.sum(back * unit, axis=0, keepdims=True)


def as_unit(rows_192):
    rows, width = rows_192.shape
    return rows_192.reshape(2, 2, rows // 4, width)


def cross_backward_kernel(n, count, *refs):
    plots, do_ref, st_ref, cross_gain = refs[:4]
    late, at = refs[4:21], 21
    quarters = refs[at : at + count]
    gain_cross, out_refs = refs[at + count], refs[at + count + 1 : at + count + 6]
    rest = refs[at + count + 6 :]
    part, rest = rest[:count], rest[count:]
    none = [False] * count
    reduce, rest = take_reduce(n, 0, part, None, none, [None] * count, none, rest)
    do_all, st_all, q_mine, q_right, q_left, dk_ref, dv_ref, k_back, v_back = rest[:9]
    line = rest[9:17]
    inside, load_sems = rest[17:34], rest[34]
    kept_refs, out_sems = rest[35:40], rest[40]
    grad_mem, part_keys, part_query, first_back, g_first = kept_refs
    leaving = Moves(list(zip(kept_refs, out_refs)), out_sems)
    (
        normed_hidden, gate_back, up_back, hidden, cot, q_all, k_ref, v_ref, kt_ref,
        mem, w_keys, w_query, cross_mix, grad_rows, normed_cross, second_back, first_sum,
    ) = inside
    loads = Moves(list(zip(late, inside)), load_sems)
    loads.start(*range(17))
    dp, z, c, x, y = place()
    parts, rows_part, rows = do_ref.shape
    width = parts * rows_part
    heads_part = rows_part // HD
    heads = parts * heads_part
    held_plots = mem.shape[0]
    scale = HD ** (-0.5)
    greet(reduce.peers())

    def clear(h, carry):
        dk_ref[h] = jnp.zeros(dk_ref.shape[1:], F32)
        dv_ref[h] = jnp.zeros(dv_ref.shape[1:], F32)
        return carry

    def compute(j, p):
        plot_row = plots[j]
        for hh in range(heads_part):
            h = p * heads_part + hh
            at_head = slice(hh * HD, (hh + 1) * HD)
            q_pair = both_plots(q_all[j, p, at_head, :], plot_row)
            do_pair = both_plots(do_all[j, p, at_head, :], plot_row)
            scores = jnp.dot(k_ref[h], q_pair, preferred_element_type=F32)
            chances = jnp.exp(scores - st_all[j, p, hh : hh + 1, :])
            prob_back = jnp.dot(v_ref[h], do_pair, preferred_element_type=F32)
            inner = st_all[j, p, heads_part + hh : heads_part + hh + 1, :]
            score_back = (chances * (prob_back - inner)).astype(BF16)
            q_back = jnp.dot(kt_ref[h], score_back, preferred_element_type=F32)
            q_mine[j, p, at_head, :] = (own_plot(q_back, plot_row) * scale).astype(BF16)
            dk_ref[h] += product(score_back, q_pair, 1, 1)
            dv_ref[h] += product(chances.astype(BF16), do_pair, 1, 1)

    def merge(j, p, arrived):
        total = q_mine[j, p].astype(F32) + arrived[0][j, p].astype(F32)
        q_mine[j, p] = total.astype(BF16)

    def finish(p):
        pass

    def hidden_gradients():
        firsts = (normed_hidden, normed_hidden, None)
        for g, seconds in enumerate((gate_back, up_back, None)):

            def step(zz, carry, g=g, seconds=seconds):
                if seconds is None:
                    grad = product(hidden[zz], cot[...], 0, 0)
                else:
                    grad = product(firsts[g][...], seconds[zz], 0, 0)
                part[g][zz] = grad.astype(BF16).reshape(part[g].shape[1:])
                return carry

            loads.wait(*((0, 1), (2,), (3, 4))[g])
            lax.fori_loop(0, n, step, 0)
            reduce.run(g, 0)

        loads.wait(5, 6, 7, 8)

    def patch_gradients():
        for source, out in ((dk_ref, k_back), (dv_ref, v_back)):

            def pair_step(i, carry, source=source, out=out):
                even, odd = source[2 * i], source[2 * i + 1]
                lane = lax.broadcasted_iota(jnp.int32, even.shape, 1)
                cols = pl.ds(pl.multiple_of(i * 2 * HD, 2 * HD), 2 * HD)
                out[0, :, cols] = jnp.where(lane < HD, even, pltpu.roll(odd, HD, 1)).astype(BF16)
                out[1, :, cols] = jnp.where(lane < HD, pltpu.roll(even, HD, 1), odd).astype(BF16)
                return carry

            lax.fori_loop(0, heads // 2, pair_step, 0)
        for which, back in enumerate((k_back, v_back)):

            def grad_step(pair, carry, which=which, back=back):
                wide = 2 * rows_part
                cols = pl.ds(pl.multiple_of(pair * wide, wide), wide)
                grad = sum(product(back[p, :, cols], mem[p], 0, 0) for p in range(held_plots))
                grad = grad.astype(BF16)
                part_keys[2 * pair, which] = as_unit(grad[:rows_part])
                part_keys[2 * pair + 1, which] = as_unit(grad[rows_part:])
                return carry

            lax.fori_loop(0, n // 2, grad_step, 0)

        def memory_step(i, carry):
            p, at_rows = i // 2, pl.ds(pl.multiple_of(lax.rem(i, 2) * rows, rows), rows)
            total = 0.0
            for which, back in enumerate((k_back, v_back)):
                for pair in range(n // 2):
                    cols = slice(pair * 2 * rows_part, (pair + 1) * 2 * rows_part)
                    weights = two_units(w_keys, pair, which)
                    total = total + product(back[p, at_rows, cols], weights, 1, 0)
            grad_mem[p, at_rows, :] = total.astype(BF16)
            return carry

        lax.fori_loop(0, held_plots * (mem.shape[1] // rows), memory_step, 0)

    def hook(t):
        for step, work in schedule.items():

            @pl.when(t == step)
            def _(work=work):
                for g, stage in work:
                    reduce.run(g, stage)

        @pl.when(t == n - 1)
        def _():
            loads.wait(9, 10)
            patch_gradients()
            leaving.start(0, 1)
            for g in range(count):
                reduce.run(g, 2)

    schedule = {0: [(0, 1), (1, 1), (2, 1)]}

    def before():
        lax.fori_loop(0, heads, clear, 0)
        hidden_gradients()

    exchange = ([do_ref, st_ref], [do_all, st_all], [q_mine], [q_right], [q_left], line)
    end_exchange = line_exchange(n, parts, z, dp, exchange, compute, merge, finish, hook, before)

    loads.wait(*range(11, 17))
    first_back[...] = jnp.zeros(first_back.shape, F32)

    def query_part(zz, carry):
        mine = q_mine[z, zz]
        part_query[zz, 0] = as_unit(product(mine, normed_cross[...], 1, 0).astype(BF16))
        part_query[zz, 1] = as_unit(product(cross_mix[zz], grad_rows[...], 1, 0).astype(BF16))
        first_back[...] += product(mine, unit_rows(w_query, zz, 0), 0, 0)
        return carry

    lax.fori_loop(0, n, query_part, 0)
    leaving.start(2)
    residual, gain_back = norm_gradient(first_sum[...], as_row(cross_gain), first_back[...])
    total = second_back[...] + residual
    first_back[...] = total
    g_first[...] = total.astype(BF16)
    leaving.start(3, 4)
    gain_cross[...] = gain_back
    for g in range(count):
        reduce.end(2, g)
        quarters[g][...] = reduce.acc[g][:, y, x]
    end_exchange()
    reduce.drain()
    leaving.wait(*range(5))


def cross_backward(n, ins, shapes):
    do, mem = ins[1], ins[13]
    parts, rows_part, rows = do.shape
    width = parts * rows_part
    heads = width // HD
    held_plots, patches, _ = mem.shape
    count = len(shapes)
    struct = jax.ShapeDtypeStruct
    unit = width // n // 4
    scratch = [pltpu.VMEM((n, 2, 2, 2) + s, BF16) for s in shapes]
    none = [False] * count
    scratch += reduce_scratch(n, 0, shapes, [BF16] * count, none, [True] * count, none)
    scratch += [
        pltpu.VMEM((n, parts, rows_part, rows), BF16),
        pltpu.VMEM((n, parts, 8, rows), F32),
        pltpu.VMEM((n, parts, rows_part, rows), BF16),
        pltpu.VMEM((n, parts, rows_part, rows), BF16),
        pltpu.VMEM((n, parts, rows_part, rows), BF16),
        pltpu.VMEM((heads, patches, held_plots * HD), F32),
        pltpu.VMEM((heads, patches, held_plots * HD), F32),
        pltpu.VMEM((held_plots, patches, width), BF16),
        pltpu.VMEM((held_plots, patches, width), BF16),
    ]
    scratch += line_sems(n, parts, 2, 1)
    scratch += [held(i) for i in ins[4:]] + [DMA((len(ins) - 4,))]
    kept = [
        struct(mem.shape, BF16),
        struct((n, 2, 2, 2, unit, width), BF16),
        struct((n, 2, 2, 2, unit, width), BF16),
        struct((rows, width), F32),
        struct((rows, width), BF16),
    ]
    scratch += [held(k) for k in kept] + [DMA((len(kept),))]
    out = pl.pallas_call(
        functools.partial(cross_backward_kernel, n, count),
        out_shape=[struct((n,) + s, BF16) for s in shapes] + [struct((1, width), F32)] + kept,
        in_specs=[VMEM] * 4 + [ANY] * 17,
        out_specs=[VMEM] * (count + 1) + [ANY] * 5,
        scratch_shapes=scratch,
        compiler_params=pltpu.CompilerParams(
            collective_id=1, has_side_effects=True, vmem_limit_bytes=63 << 20
        ),
        name="cross_backward",
    )(*ins)
    return out[:count], out[count:]


def alone(rows, which):
    zero = jnp.zeros_like(rows)
    return jnp.concatenate([rows, zero] if which == 0 else [zero, rows], axis=0)


RELAYED = [True] * 3 + [False] * 3 + [True] * 3 + [False]


def self_backward_kernel(n, extra, halo_chunks, *refs):
    self_gain, gain_cross, gain_hidden = refs[:3]
    late = refs[3:14]
    cross_parts = refs[14:16]
    sums = refs[16:19]
    fin_out = refs[19:28]
    grad_tokens, gain_out = refs[28:30]
    own_parts = refs[30:34]
    gain_part, gain_fin = refs[34:36]
    part = list(cross_parts) + list(own_parts) + [None] * 3 + [gain_part]
    kept = [True, True] + [False] * 8
    quarters = [None] * 6 + list(sums) + [None]
    fin = list(refs[-10:-1]) + [gain_fin]
    reduce, rest = take_reduce(n, extra, part, fin, kept, quarters, RELAYED, refs[36:])
    do_ref, dq_ref, dk_ref, dv_ref, own_back, csend, crecv, hs, hr = rest[:9]
    inside, load_sems, v_ref, kt_ref = rest[9:20], rest[20], rest[21], rest[22]
    leaving = Moves(list(zip(fin[:9], fin_out)), rest[33])
    gain_self = rest[23]
    g_first, mix, w_vo, normed, w_qk, k_ref, q_ref, bias, logs, near, first_back = inside
    loads = Moves(list(zip(late, inside)), load_sems)
    loads.start(*range(11))
    dp, z, c, x, y = place()
    rows, width = g_first.shape
    heads = width // HD
    rows_part = width // n
    scale = HD ** (-0.5)
    own_rows = slice(halo_chunks * rows, (halo_chunks + 1) * rows)
    early_groups, late_groups, hidden_groups = (0, 1, 2), (3, 4, 5), (6, 7, 8)
    half = width // 2

    def store_unit(out, zz, grad):
        for cc in range(2):
            columns = grad[:, cc * half : (cc + 1) * half]
            out[zz, :, :, cc] = columns.reshape(2, 2, rows_part // 4, half)

    def all_run(groups, stage):
        for g in groups:
            reduce.run(g, stage)

    greet(reduce.peers())
    all_run((0, 1), 0)
    for g in hidden_groups:
        reduce.begin(3, g)
    loads.wait(0, 1)
    def output_part(zz, carry):
        at_part = pl.ds(pl.multiple_of(zz * rows_part, rows_part), rows_part)
        store_unit(own_parts[0], zz, product(mix[at_part, :], g_first[...], 1, 0).astype(BF16))
        return carry

    lax.fori_loop(0, n, output_part, 0)
    reduce.run(2, 0)
    loads.wait(2)

    def do_part(zz, carry):
        at_part = pl.ds(pl.multiple_of(zz * rows_part, rows_part), rows_part)
        do_ref[at_part, :] = product(unit_rows(w_vo, zz, 1), g_first[...], 1, 1).astype(BF16)
        return carry

    lax.fori_loop(0, n, do_part, 0)
    all_run(early_groups, 1)
    loads.wait(3, 4)
    tall(v_ref, normed, w_vo, 0, n)
    flat(kt_ref, normed, w_qk, 1, n)

    def pair_step(pair, carry):
        cols = pl.ds(pl.multiple_of(pair * 2 * HD, 2 * HD), 2 * HD)
        dk, dv = 0.0, 0.0
        for which in range(2):
            at_head = pl.ds(pl.multiple_of((2 * pair + which) * HD, HD), HD)
            q_pair = alone(q_ref[at_head, :], which)
            do_head = do_ref[at_head, :]
            inner = jnp.sum(
                do_head.astype(F32) * mix[at_head, :].astype(F32), axis=0, keepdims=True
            )
            do_pair = alone(do_head, which)
            scores = jnp.dot(k_ref[:, cols], q_pair, preferred_element_type=F32)
            chances = jnp.exp(scores + bias[...] - logs[pair, which : which + 1, :])
            prob_back = jnp.dot(v_ref[:, cols], do_pair, preferred_element_type=F32)
            score_back = (chances * (prob_back - inner)).astype(BF16)
            q_back = jnp.dot(kt_ref[at_head, :], score_back, preferred_element_type=F32)
            dq_ref[at_head, :] = (q_back * scale).astype(BF16)
            dk = dk + product(score_back, q_pair, 1, 1)
            dv = dv + product(chances.astype(BF16), do_pair, 1, 1)
        dk_ref[:, cols] = dk.astype(BF16)
        dv_ref[:, cols] = dv.astype(BF16)
        return carry

    loads.wait(5, 6, 7, 8)
    lax.fori_loop(0, heads // 2, pair_step, 0)
    for g, back in ((3, dv_ref), (4, dk_ref)):

        def grad_step(pair, carry, g=g, back=back):
            cols = pl.ds(pl.multiple_of(pair * 2 * rows_part, 2 * rows_part), 2 * rows_part)
            grad = product(back[:, cols], normed[...], 0, 0).astype(BF16)
            store_unit(own_parts[g - 2], 2 * pair, grad[:rows_part])
            store_unit(own_parts[g - 2], 2 * pair + 1, grad[rows_part:])
            return carry

        lax.fori_loop(0, n // 2, grad_step, 0)
        reduce.run(g, 0)

    def query_part(zz, carry):
        at_part = pl.ds(pl.multiple_of(zz * rows_part, rows_part), rows_part)
        grad = product(dq_ref[at_part, :], normed[own_rows, :], 1, 0)
        store_unit(own_parts[3], zz, grad.astype(BF16))
        return carry

    lax.fori_loop(0, n, query_part, 0)
    reduce.run(5, 0)
    all_run(early_groups, 2)
    all_run(late_groups, 1)
    for g in hidden_groups:
        reduce.pass_on(g)
    loads.wait(9, 10)

    def halo_copy(i):
        dev = (dp, lax.rem(z + n - 1, n))
        return remote(csend.at[i], crecv.at[i], hs.at[i], hr.at[i], dev)

    def halo_send(i):
        if i > 0:
            halo_take(i - 1, csend.at[i])

        @pl.when(z >= halo_chunks - i)
        def _():
            halo_copy(i).start()

    def halo_take(i, onto):
        @pl.when((z + 1 < n) & (z + 1 >= halo_chunks - i))
        def _():
            halo_copy(i).wait_recv()
            onto[...] = (onto[...].astype(F32) + crecv[i].astype(F32)).astype(onto.dtype)

    def unit_of(at_rows):
        here = near[at_rows, :].astype(F32)
        return here * lax.rsqrt(jnp.mean(here * here, axis=-1, keepdims=True) + epsilon)

    gain_self[...] = jnp.zeros((1, width), F32)

    def near_chunk(i, carry):
        at_rows = pl.ds(pl.multiple_of(i * rows, rows), rows)
        back = 0.0
        for pair in range(n // 2):
            cols = slice(pair * 2 * rows_part, (pair + 1) * 2 * rows_part)
            back = back + product(dk_ref[at_rows, cols], two_units(w_qk, pair, 1), 1, 0)
            back = back + product(dv_ref[at_rows, cols], two_units(w_vo, pair, 0), 1, 0)

        @pl.when(i < halo_chunks)
        def _():
            csend[i] = back.astype(BF16)
            gain_self[...] += jnp.sum(back * unit_of(at_rows), axis=0, keepdims=True)

        @pl.when(i == 0)
        def _():
            halo_send(0)

        @pl.when(i == halo_chunks)
        def _():
            own_back[...] = back

        return carry

    lax.fori_loop(0, halo_chunks + 1, near_chunk, 0)

    def own_part(zz, carry):
        at_part = pl.ds(pl.multiple_of(zz * rows_part, rows_part), rows_part)
        own_back[...] += product(dq_ref[at_part, :], unit_rows(w_qk, zz, 0), 0, 0)
        return carry

    lax.fori_loop(0, n, own_part, 0)
    gain_self[...] += jnp.sum(own_back[...] * unit_of(own_rows), axis=0, keepdims=True)

    deep, lanes = gain_part.shape[4:]
    gain_part[...] = jnp.zeros(gain_part.shape, F32)
    for i, gain in enumerate((gain_self[...], gain_cross[...], gain_hidden[...])):
        for j in range(width // lanes):
            piece, row = divmod(i * (width // lanes) + j, deep)
            for zz in range(n):
                gain_part[zz, piece // 4, piece // 2 % 2, piece % 2, row : row + 1, :] = gain[
                    :, j * lanes : (j + 1) * lanes
                ]

    reduce.run(9, 0)
    all_run(early_groups, 3)
    reduce.run(9, 1)
    all_run(late_groups, 2)
    reduce.run(9, 2)
    for g in early_groups:
        reduce.pass_on(g)
    all_run(late_groups, 3)
    reduce.run(9, 3)
    all_run(hidden_groups, 4)
    for i in range(1, halo_chunks):
        halo_send(i)
    all_run(hidden_groups, 5)
    all_run(early_groups, 4)
    all_run(late_groups + (9,), 4)
    all_run(hidden_groups, 6)
    all_run(early_groups, 5)
    all_run(late_groups + (9,), 5)
    all_run(hidden_groups, 7)
    leaving.start(*hidden_groups)
    all_run(early_groups, 6)
    all_run(late_groups + (9,), 6)
    halo_take(halo_chunks - 1, own_back)
    here = near[own_rows, :].astype(F32)
    residual, _ = norm_gradient(here, as_row(self_gain), own_back[...])
    grad_tokens[...] = (first_back[...] + residual).astype(BF16)
    all_run(early_groups, 7)
    leaving.start(*early_groups)
    all_run(late_groups + (9,), 7)
    leaving.start(*late_groups)
    for i in range(3):
        for j in range(width // lanes):
            piece, row = divmod(i * (width // lanes) + j, deep)
            found = gain_fin[piece // 4, piece // 2 % 2, piece % 2, row : row + 1, :]
            gain_out[i : i + 1, j * lanes : (j + 1) * lanes] = found
    gain_out[3:8, :] = jnp.zeros((5, width), F32)
    for i in range(halo_chunks):

        @pl.when(z >= halo_chunks - i)
        def _(i=i):
            halo_copy(i).wait_send()

    reduce.drain()
    leaving.wait(*range(9))


def self_backward(n, extra, halo_chunks, ins, cross_parts, sums):
    near, g_first = ins[12], ins[3]
    rows, width = g_first.shape
    keys = near.shape[0]
    unit = width // n // 4
    gain_shape = (8, 128)
    single = (unit, width // 2)
    shapes = [(unit, width)] * 2 + [single] * 4 + [p.shape[1:] for p in sums]
    struct = jax.ShapeDtypeStruct
    scratch = [pltpu.VMEM((n, 2, 2, 2) + single, BF16)] * 4
    scratch += [pltpu.VMEM((n, 2, 2, 2) + gain_shape, F32), pltpu.VMEM((2, 2, 2) + gain_shape, F32)]
    scratch += reduce_scratch(
        n, extra, shapes + [gain_shape], [BF16] * 9 + [F32],
        [True, True] + [False] * 8, [True] * 6 + [False] * 3 + [True], RELAYED,
    )
    scratch += [
        pltpu.VMEM((width, rows), BF16),
        pltpu.VMEM((width, rows), BF16),
        pltpu.VMEM((keys, width), BF16),
        pltpu.VMEM((keys, width), BF16),
        pltpu.VMEM((rows, width), F32),
        pltpu.VMEM((halo_chunks, rows, width), BF16),
        pltpu.VMEM((halo_chunks, rows, width), BF16),
        DMA((halo_chunks,)),
        DMA((halo_chunks,)),
    ]
    scratch += [held(i) for i in ins[3:]] + [DMA((len(ins) - 3,))]
    scratch += [pltpu.VMEM((keys, width), BF16), pltpu.VMEM((width, keys), BF16)]
    scratch += [pltpu.VMEM((1, width), F32)]
    scratch += [pltpu.VMEM((2, 2, 2) + s, BF16) for s in shapes] + [DMA((len(shapes),))]
    out = pl.pallas_call(
        functools.partial(self_backward_kernel, n, extra, halo_chunks),
        out_shape=[struct((2, 2, 2) + s, BF16) for s in shapes]
        + [struct((rows, width), BF16), struct((8, width), F32)],
        in_specs=[VMEM] * 3 + [ANY] * 13 + [VMEM] * 3,
        out_specs=[ANY] * 9 + [VMEM] * 2,
        scratch_shapes=scratch,
        compiler_params=pltpu.CompilerParams(
            collective_id=2, has_side_effects=True, vmem_limit_bytes=63 << 20
        ),
        name="self_backward",
    )(*ins, *cross_parts, *sums)
    return out[:9], out[9], out[10]


def results_kernel(*refs):
    ins, outs = refs[:12], refs[12:]
    at = 0
    for g in range(2):
        for u in range(2):
            outs[at][...] = ins[g][u, 0, 0].astype(F32)
            at += 1
    for g in range(2, 6):
        half = ins[g].shape[-1]
        for cc in range(2):
            outs[at][:, cc * half : (cc + 1) * half] = ins[g][0, 0, cc].astype(F32)
        at += 1
    for g in range(6, 9):
        block = ins[g][0, 0]
        outs[at][...] = block.reshape(-1, block.shape[-1]).astype(F32)
        at += 1
    for i in range(9, 12):
        outs[at][...] = ins[i][...]
        at += 1


def results(sums, output, grad_tokens, grad_memory):
    struct = jax.ShapeDtypeStruct
    steps = 4
    in_specs, out_specs, out_shape = [], [], []
    for i, piece in enumerate(sums):
        rows, cols = piece.shape[3:]
        if i < 2:
            in_specs.append(pl.BlockSpec((2, 1, 1, rows, cols), lambda i: (0, i // 2, i % 2, 0, 0)))
            for _ in range(2):
                out_specs.append(pl.BlockSpec((rows, cols), lambda i: (i, 0)))
                out_shape.append(struct((steps * rows, cols), F32))
        else:
            in_specs.append(pl.BlockSpec((1, 1, 2, rows, cols), lambda i: (i // 2, i % 2, 0, 0, 0)))
            shape = (rows, 2 * cols) if i < 6 else (2 * rows, cols)
            out_specs.append(pl.BlockSpec(shape, lambda i: (i, 0)))
            out_shape.append(struct((steps * shape[0], shape[1]), F32))
    for rows in (output, grad_tokens):
        spec = pl.BlockSpec((rows.shape[0] // steps, rows.shape[1]), lambda i: (i, 0))
        in_specs.append(spec)
        out_specs.append(spec)
        out_shape.append(struct(rows.shape, rows.dtype))
    plots, patches, width = grad_memory.shape
    per = steps // plots
    spec = pl.BlockSpec((1, patches // per, width), lambda i: (i // per, i % per, 0))
    in_specs.append(spec)
    out_specs.append(spec)
    out_shape.append(struct(grad_memory.shape, grad_memory.dtype))
    return pl.pallas_call(
        results_kernel,
        grid=(steps,),
        out_shape=out_shape,
        in_specs=in_specs,
        out_specs=out_specs,
        compiler_params=pltpu.CompilerParams(vmem_limit_bytes=63 << 20),
        name="results",
    )(*sums, output, grad_tokens, grad_memory)


def body(
    tokens, memory, table_lengths, table_plots,
    self_gain, self_query, self_key, self_value, self_output,
    cross_gain, cross_query, cross_key, cross_value, cross_output,
    hidden_gain, hidden_gate, hidden_up, hidden_down, cotangent,
):
    n = lax.axis_size("tensor")
    extra = lax.axis_size("dp").bit_length() - 1 - 3
    rows, width = tokens.shape
    halo_chunks = -(-(LONGEST - 1) // rows)

    def pieces(shard):
        return shard.reshape(2, 2, 2, -1, shard.shape[-1])

    shards = [pieces(hidden_gate), pieces(hidden_up), pieces(hidden_down)]
    ins = (
        table_lengths, table_plots, tokens, cotangent,
        self_gain, cross_gain, hidden_gain, memory,
        cross_key.T, cross_value.T, self_query.T, self_key.T, self_value.T, self_output,
        cross_query.T, cross_output,
    )
    full, saved = forward(n, halo_chunks, ins, shards)
    (
        bias, plots, near, normed_near, self_q, self_k, self_mix, self_logs, first_sum,
        normed_cross, q_all, cross_k, cross_kt, cross_v, cross_mix,
        output, normed_hidden, hidden, gate_back, up_back, second_back, grad_rows, mixed_back,
        cross_stats, gain_hidden,
    ) = saved
    ins = (
        plots, mixed_back, cross_stats, cross_gain,
        normed_hidden, gate_back, up_back, hidden, cotangent, q_all, cross_k, cross_v, cross_kt,
        memory, full[0], full[3], cross_mix, grad_rows, normed_cross, second_back, first_sum,
    )
    hidden_pieces, rest = cross_backward(n, ins, [s.shape[3:] for s in shards])
    gain_cross, grad_memory, part_keys, part_query, first_back, g_first = rest
    ins = (
        self_gain, gain_cross, gain_hidden,
        g_first, self_mix, full[2], normed_near, full[1], self_k, self_q, bias, self_logs, near,
        first_back,
    )
    sums, grad_tokens, gains = self_backward(
        n, extra, halo_chunks, ins, [part_query, part_keys], hidden_pieces
    )

    (
        g_cq, g_co, g_ck, g_cv, g_so, g_sv, g_sk, g_sq, g_gate, g_up, g_down,
        output, grad_tokens, grad_memory,
    ) = results(sums, output, grad_tokens, grad_memory)
    return (
        output, grad_tokens, grad_memory,
        g_sq.T, g_sk.T, g_sv.T, g_so,
        g_cq.T, g_ck.T, g_cv.T, g_co,
        g_gate, g_up, g_down,
        gains[0], gains[1], gains[2],
    )


def solution(mesh):
    in_specs = (
        P(("dp", "tensor"), None),
        P("dp", "tensor", None),
        P("dp", None),
        P("dp", None),
        P(),
        P(None, "tensor"),
        P(None, "tensor"),
        P(None, "tensor"),
        P("tensor", None),
        P(),
        P(None, "tensor"),
        P(None, "tensor"),
        P(None, "tensor"),
        P("tensor", None),
        P(),
        P(None, "tensor"),
        P(None, "tensor"),
        P("tensor", None),
        P(("dp", "tensor"), None),
    )
    out_specs = (
        P(("dp", "tensor"), None),
        P(("dp", "tensor"), None),
        P("dp", "tensor", None),
        P(None, "tensor"),
        P(None, "tensor"),
        P(None, "tensor"),
        P("tensor", None),
        P(None, "tensor"),
        P(None, "tensor"),
        P(None, "tensor"),
        P("tensor", None),
        P(None, "tensor"),
        P(None, "tensor"),
        P("tensor", None),
        P(),
        P(),
        P(),
    )
    return jax.shard_map(body, mesh=mesh, in_specs=in_specs, out_specs=out_specs, check_vma=False)
```

```python
import functools

import jax
import jax.numpy as jnp
from jax import lax
from jax.experimental import pallas as pl
from jax.experimental.pallas import tpu as pltpu
from jax.sharding import PartitionSpec as P

HD = 64
LONGEST = 512
F32 = jnp.float32
BF16 = jnp.bfloat16
MESH = pl.DeviceIdType.MESH
ANY = pl.BlockSpec(memory_space=pl.ANY)
VMEM = pl.BlockSpec(memory_space=pltpu.VMEM)
DMA = pltpu.SemaphoreType.DMA

epsilon = 1e-06
masked_value = -1e30


def product(first_op, second_op, first_dim, second_dim):
    return lax.dot_general(
        first_op,
        second_op,
        (((first_dim,), (second_dim,)), ((), ())),
        preferred_element_type=F32,
    )


def remote(src, dst, send_sem, recv_sem, device):
    return pltpu.make_async_remote_copy(
        src_ref=src,
        dst_ref=dst,
        send_sem=send_sem,
        recv_sem=recv_sem,
        device_id=device,
        device_id_type=MESH,
    )


class Moves:
    def __init__(self, pairs, sems):
        self.copies = [
            pltpu.make_async_copy(src, dst, sems.at[i]) for i, (src, dst) in enumerate(pairs)
        ]

    def start(self, *which):
        for i in which:
            self.copies[i].start()

    def wait(self, *which):
        for i in which:
            self.copies[i].wait()


def held(struct):
    return pltpu.VMEM(struct.shape, struct.dtype)


def place():
    dp = lax.axis_index("dp")
    z = lax.axis_index("tensor")
    return dp, z, lax.rem(dp, 2), lax.rem(dp // 2, 2), lax.rem(dp // 4, 2)


def flipped(dp, bit):
    here = lax.rem(dp // (1 << bit), 2)
    return dp + (1 << bit) * (1 - 2 * here)


def greet(devices):
    barrier = pltpu.get_barrier_semaphore()
    for device in devices:
        pl.semaphore_signal(barrier, inc=1, device_id=device, device_id_type=MESH)
    pl.semaphore_wait(barrier, len(devices))


def greet_line(dp, z, n):
    barrier = pltpu.get_barrier_semaphore()

    @pl.when(z > 0)
    def _():
        pl.semaphore_signal(barrier, inc=1, device_id=(dp, z - 1), device_id_type=MESH)

    @pl.when(z < n - 1)
    def _():
        pl.semaphore_signal(barrier, inc=1, device_id=(dp, z + 1), device_id_type=MESH)

    inner = (z > 0) & (z < n - 1)

    @pl.when(inner)
    def _():
        pl.semaphore_wait(barrier, 2)

    @pl.when(jnp.logical_not(inner))
    def _():
        pl.semaphore_wait(barrier, 1)


class Gather:
    def __init__(self, n, mine, full, sems):
        self.n, self.mine, self.full, self.count = n, mine, full, len(full)
        self.zs, self.zr, self.as_, self.ar, self.bs, self.br, self.cs, self.cr, self.loc = sems
        self.dp, self.z, self.c, self.x, self.y = place()
        z = self.z
        inner = [1 + s // 2 if s % 2 == 0 else n - 1 - s // 2 for s in range(n - 1)]
        self.order = [
            jnp.where(z == 0, n - 1 - s, jnp.where(z == n - 1, 1 + s, inner[s]))
            for s in range(n - 1)
        ]

    def peers(self):
        others = [lax.rem(self.z + k, self.n) for k in range(1, self.n)]
        return [(self.dp, o) for o in others] + [(flipped(self.dp, b), self.z) for b in range(3)]

    def own(self, g):
        return pltpu.make_async_copy(self.mine[g], self.full[g].at[self.z], self.loc.at[g])

    def piece(self, g, k):
        zk = lax.rem(self.z + self.n - k, self.n)
        return self.full[g].at[zk, self.y, self.x, self.c]

    def first(self, g, k):
        src = self.piece(g, 0) if self.mine[g] is None else self.mine[g].at[self.y, self.x, self.c]
        dev = (self.dp, lax.rem(self.z + k, self.n))
        return remote(src, self.piece(g, 0), self.zs.at[g, k - 1], self.zr.at[g, k - 1], dev)

    def passed(self, g, up):
        k = self.n - 2 if up else 2
        dev = (self.dp, lax.rem(self.z + (1 if up else self.n - 1), self.n))
        slot = self.n - 2 if up else 0
        piece = self.piece(g, k)
        return remote(piece, piece, self.zs.at[g, self.n - 1], self.zr.at[g, slot], dev)

    def straight(self, k, start):
        ends = ((self.z == 0) & (k == self.n - 1)) | ((self.z == self.n - 1) & (k == 1))
        pl.when(jnp.logical_not(ends) if self.n > 2 else self.z >= 0)(start)

    def arrived(self, g, k):
        piece = self.piece(g, k)
        dev = (self.dp, lax.rem(self.z + k, self.n))
        return remote(piece, piece, self.zs.at[g, 0], self.zr.at[g, k - 1], dev)

    def second(self, g, s, incoming=False):
        k = self.order[s]
        zk = lax.rem(self.z + self.n - k, self.n)
        x, y, c = self.x, self.y, self.c
        if s % 2 == 1:
            there, bit = self.full[g].at[zk, y, 1 - x if incoming else x, c], 1
        else:
            there, bit = self.full[g].at[zk, 1 - y if incoming else y, x, c], 2
        dev = (flipped(self.dp, bit), self.z)
        return remote(there, there, self.as_.at[g, s], self.ar.at[g, s], dev)

    def third(self, g, s, incoming=False):
        k = self.order[s]
        zk = lax.rem(self.z + self.n - k, self.n)
        x, y, c = self.x, self.y, self.c
        if s % 2 == 1:
            there, bit = self.full[g].at[zk, 1 - y if incoming else y, :, c], 2
        else:
            there, bit = self.full[g].at[zk, :, 1 - x if incoming else x, c], 1
        dev = (flipped(self.dp, bit), self.z)
        return remote(there, there, self.bs.at[g, s], self.br.at[g, s], dev)

    def fourth(self, g, s, incoming=False):
        zk = lax.rem(self.z + self.n - self.order[s], self.n)
        there = self.full[g].at[zk, :, :, 1 - self.c if incoming else self.c]
        dev = (flipped(self.dp, 0), self.z)
        return remote(there, there, self.cs.at[g, s], self.cr.at[g, s], dev)

    def run(self, g, stage):
        n = self.n
        steps = range(n - 1)
        if stage == 0:
            if self.mine[g] is not None:
                self.own(g).start()

            for k in sorted(range(1, n), key=lambda k: min(k, n - k)):
                self.straight(k, lambda k=k: self.first(g, k).start())
        elif stage == 1:
            for s in steps:
                k = self.order[s]
                self.arrived(g, k).wait_recv()
                if n > 2:

                    @pl.when((self.z == n - 2) & (k == n - 2))
                    def _():
                        self.passed(g, True).start()

                    @pl.when((self.z == 1) & (k == 2))
                    def _():
                        self.passed(g, False).start()

                self.second(g, s).start()
        elif stage == 2:
            for s in steps:
                self.second(g, s, True).wait_recv()
                self.third(g, s).start()
        elif stage == 3:
            for s in steps:
                self.third(g, s, True).wait_recv()
                self.fourth(g, s).start()
        else:
            if self.mine[g] is not None:
                self.own(g).wait()
            for s in steps:
                self.fourth(g, s, True).wait_recv()

    def drain(self):
        for g in range(self.count):
            if self.n > 2:

                @pl.when((self.z == self.n - 2) | (self.z == 1))
                def _(g=g):
                    self.passed(g, True).wait_send()

            for s in range(self.n - 1):
                self.straight(s + 1, lambda s=s, g=g: self.first(g, s + 1).wait_send())
                self.second(g, s).wait_send()
                self.third(g, s).wait_send()
                self.fourth(g, s).wait_send()


def gather_sems(n, count):
    return [DMA((count, n))] + [DMA((count, n - 1)) for _ in range(7)] + [DMA((count,))]


class Reduce:
    def __init__(
        self, n, extra, part, acc, rec1, rec2, rec3, rec4, relay, fin, recx, sems, quarters
    ):
        self.relay = relay
        self.n, self.extra, self.count = n, extra, len(rec4)
        self.part, self.fin, self.recx, self.quarters = part, fin, recx, quarters
        self.rec1, self.rec2, self.rec3, self.rec4 = rec1, rec2, rec3, rec4
        self.sems = sems
        self.dp, self.z, self.c, self.x, self.y = place()
        self.ks = range(1, n)
        self.kept = acc
        self.started = []
        self.acc = []
        for g in range(self.count):
            if part[g] is None:
                self.acc.append(None)
            elif acc[g] is None:
                self.acc.append(part[g].at[:, :, :, self.c])
            else:
                self.acc.append(acc[g])

    def peers(self):
        others = [lax.rem(self.z + k, self.n) for k in self.ks]
        bits = range(3 + self.extra)
        return [(self.dp, o) for o in others] + [(flipped(self.dp, b), self.z) for b in bits]

    def lanes(self, g, half):
        width = self.rec4[g].shape[-1]
        if width == 128:
            return slice(0, width)
        middle = width // 256 * 128 + (128 if width % 256 and g % 2 == 0 else 0)
        return slice(0, middle) if half == 0 else slice(middle, width)

    def copies(self, stage, g, incoming=False):
        halves = range(1 if self.rec4[g].shape[-1] == 128 else 2)
        dp, z, c, x, y, n = self.dp, self.z, self.c, self.x, self.y, self.n
        acc, fin = self.acc[g], self.fin[g] if self.fin else None
        found = []
        if stage == 0:
            src, dst, dev = self.part[g].at[:, :, :, 1 - c], self.rec1[g], (flipped(dp, 0), z)
            found.append((src, dst, dev, 0))
        elif stage == 1:
            for half in halves:
                at = self.lanes(g, half)
                src = acc.at[:, :, 1 - x, :, at] if half == 0 else acc.at[:, 1 - y, :, :, at]
                dev = (flipped(dp, 1 if half == 0 else 2), z)
                found.append((src, self.rec2[g].at[:, :, :, at], dev, 1 + half))
        elif stage == 2:
            for half in halves:
                at = self.lanes(g, half)
                src = acc.at[:, 1 - y, x, :, at] if half == 0 else acc.at[:, y, 1 - x, :, at]
                dev = (flipped(dp, 2 if half == 0 else 1), z)
                found.append((src, self.rec3[g].at[:, :, at], dev, 3 + half))
        elif stage == 3:
            for k in self.ks:
                zk = lax.rem(z + k, n)
                slot = lax.rem(z + n - k, n) if incoming else z
                found.append((self.quarter(g, zk), self.rec4[g].at[slot], (dp, zk), 8 + k))
        elif stage == 4:
            for half in halves:
                at = self.lanes(g, half)
                if half == 0:
                    src = fin.at[1 - y if incoming else y, x, c, :, at]
                else:
                    src = fin.at[y, 1 - x if incoming else x, c, :, at]
                found.append((src, src, (flipped(dp, 2 if half == 0 else 1), z), 5 + half))
        elif stage == 5:
            for half in halves:
                at = self.lanes(g, half)
                if half == 0:
                    src = fin.at[:, 1 - x if incoming else x, c, :, at]
                else:
                    src = fin.at[1 - y if incoming else y, :, c, :, at]
                found.append((src, src, (flipped(dp, 1 if half == 0 else 2), z), 7 + half))
        else:
            src = fin.at[:, :, 1 - c if incoming else c]
            found.append((src, src, (flipped(dp, 0), z), 8 + n))
        return [
            remote(src, dst, self.sems[0].at[g, slot], self.sems[1].at[g, slot], dev)
            for src, dst, dev, slot in found
        ]

    def quarter(self, g, zz):
        if self.quarters[g] is not None:
            return self.quarters[g].at[zz]
        return self.acc[g].at[zz, self.y, self.x]

    def own(self, g):
        src = self.part[g].at[:, :, :, self.c]
        return pltpu.make_async_copy(src, self.acc[g], self.sems[4].at[g])

    def further(self, g, e):
        return remote(
            self.fin[g].at[self.y, self.x, self.c],
            self.recx[g].at[e],
            self.sems[2].at[g, e],
            self.sems[3].at[g, e],
            (flipped(self.dp, 3 + e), self.z),
        )

    def add(self, stage, g):
        n, x, y, c, z = self.n, self.x, self.y, self.c, self.z
        acc, fin = self.acc[g], self.fin[g] if self.fin else None
        kind = self.rec4[g].dtype
        if stage == 1:

            def step(i, carry):
                zz, yy, xx = i // 4, lax.rem(i // 2, 2), lax.rem(i, 2)
                total = acc[zz, yy, xx].astype(F32) + self.rec1[g][zz, yy, xx].astype(F32)
                acc[zz, yy, xx] = total.astype(kind)
                return carry

            lax.fori_loop(0, 4 * n, step, 0)
        elif stage == 2:

            def step(i, carry):
                zz, aa = i // 2, lax.rem(i, 2)
                for half in range(1 if self.rec4[g].shape[-1] == 128 else 2):
                    at = self.lanes(g, half)
                    yy, xx = (aa, x) if half == 0 else (y, aa)
                    came = self.rec2[g][zz, aa, :, at].astype(F32)
                    acc[zz, yy, xx, :, at] = (acc[zz, yy, xx, :, at].astype(F32) + came).astype(kind)
                return carry

            lax.fori_loop(0, 2 * n, step, 0)
        elif stage == 3:

            def step(zz, carry):
                total = acc[zz, y, x].astype(F32) + self.rec3[g][zz].astype(F32)
                acc[zz, y, x] = total.astype(kind)
                return carry

            lax.fori_loop(0, n, step, 0)
        else:
            self.rec4[g][z] = self.quarter(g, z)[...]
            total = self.rec4[g][0].astype(F32)
            for k in self.ks:
                total = total + self.rec4[g][k].astype(F32)
            fin[y, x, c] = total.astype(kind)
            for e in range(self.extra):
                self.further(g, e).start()
                self.further(g, e).wait()
                total = fin[y, x, c].astype(F32) + self.recx[g][e].astype(F32)
                fin[y, x, c] = total.astype(kind)

    def to_relay(self, g, up):
        n = self.n
        k, dev = (n - 1, n - 2) if up else (1, 1)
        src = self.quarter(g, n - 1 if up else 0)
        sems = self.sems
        return remote(
            src, self.relay[g], sems[0].at[g, 8 + k], sems[1].at[g, 9 + n], (self.dp, dev)
        )

    def from_relay(self, g, up):
        n = self.n
        k, dev, slot = (1, n - 1, n - 2) if up else (n - 1, 0, 1)
        dst = self.rec4[g].at[slot]
        sems = self.sems
        return remote(
            self.relay[g], dst, sems[0].at[g, 8 + k], sems[1].at[g, 8 + k], (self.dp, dev)
        )

    def relayed(self, g):
        return self.relay[g] is not None

    def begin_line(self, g, act):
        z, n = self.z, self.n
        for k, copy in zip(self.ks, self.copies(3, g)):
            later = (z == 0) & (k == n - 1) | (z == n - 1) & (k == 1)
            later = later | (z == n - 2) & (k == 1) | (z == 1) & (k == n - 1)
            pl.when(jnp.logical_not(later))(functools.partial(act, copy))
        pl.when(z == 0)(lambda: act(self.to_relay(g, True)))
        pl.when(z == n - 1)(lambda: act(self.to_relay(g, False)))

    def pass_on(self, g):
        z, n = self.z, self.n

        def one(up):
            self.to_relay(g, up).wait_recv()
            own = self.quarter(g, n - 1 if up else 0)[...].astype(F32)
            self.relay[g][...] = (self.relay[g][...].astype(F32) + own).astype(BF16)
            self.from_relay(g, up).start()

        pl.when(z == n - 2)(lambda: one(True))
        pl.when(z == 1)(lambda: one(False))

    def end_line(self, g):
        z, n = self.z, self.n
        for k, copy in zip(self.ks, self.copies(3, g, True)):
            never = (z == n - 1) & (k == n - 1) | (z == 0) & (k == 1)
            pl.when(jnp.logical_not(never))(copy.wait_recv)

        @pl.when(z == n - 1)
        def _():
            self.rec4[g][0] = jnp.zeros(self.rec4[g].shape[1:], BF16)

        @pl.when(z == 0)
        def _():
            self.rec4[g][n - 1] = jnp.zeros(self.rec4[g].shape[1:], BF16)

    def begin(self, stage, g):
        if stage == 3 and self.relayed(g):
            self.begin_line(g, lambda copy: copy.start())
        else:
            for copy in self.copies(stage, g):
                copy.start()
        if (stage, g) not in self.started:
            self.started.append((stage, g))

    def end(self, stage, g):
        if stage == 0 and self.kept[g] is not None:
            self.own(g).wait()
        if stage == 3 and self.relayed(g):
            self.end_line(g)
        else:
            for copy in self.copies(stage, g, True):
                copy.wait_recv()
        if stage < 4:
            self.add(stage + 1, g)

    def run(self, g, stage):
        if stage == 0 and self.kept[g] is not None:
            self.own(g).start()
        if stage > 0:
            self.end(stage - 1, g)
        if stage <= 6:
            self.begin(stage, g)

    def drain(self):
        for stage, g in self.started:
            if stage == 3 and self.relayed(g):
                self.begin_line(g, lambda copy: copy.wait_send())
                pl.when(self.z == self.n - 2)(self.from_relay(g, True).wait_send)
                pl.when(self.z == 1)(self.from_relay(g, False).wait_send)
            else:
                for copy in self.copies(stage, g):
                    copy.wait_send()


def reduce_scratch(n, extra, shapes, kinds, kept, from_start, relays):
    count = len(shapes)
    every = list(zip(shapes, kinds))
    used = [s for s, f in zip(every, from_start) if f]
    scratch = [pltpu.VMEM((n, 2, 2) + s, d) for (s, d), k in zip(every, kept) if k]
    scratch += [pltpu.VMEM((n, 2, 2) + s, d) for s, d in used]
    scratch += [pltpu.VMEM((n, 2) + s, d) for s, d in used]
    scratch += [pltpu.VMEM((n,) + s, d) for s, d in used]
    scratch += [pltpu.VMEM((n,) + s, d) for s, d in every]
    if n > 3:
        scratch += [pltpu.VMEM(s, d) for (s, d), r in zip(every, relays) if r]
    if extra:
        scratch += [pltpu.VMEM((extra,) + s, d) for s, d in every]
    scratch += [
        DMA((count, 10 + n)),
        DMA((count, 10 + n)),
        DMA((count, extra) if extra else (1, 1)),
        DMA((count, extra) if extra else (1, 1)),
        DMA((count,)),
    ]
    return scratch


def take_reduce(n, extra, part, fin, kept, quarters, relays, refs):
    refs = list(refs)
    acc = [refs.pop(0) if k else None for k in kept]
    recs = []
    for _ in range(3):
        recs.append([refs.pop(0) if p is not None else None for p in part])
    recs.append([refs.pop(0) for _ in part])
    recs.append([refs.pop(0) if n > 3 and r else None for r in relays])
    recx = [refs.pop(0) for _ in part] if extra else None
    sems = [refs.pop(0) for _ in range(5)]
    return Reduce(n, extra, part, acc, *recs, fin, recx, sems, quarters), refs


def both_plots(rows, plot_row):
    wide = rows.astype(F32)
    zero = jnp.zeros_like(wide)
    return jnp.concatenate(
        [jnp.where(plot_row == 0, wide, zero), jnp.where(plot_row == 0, zero, wide)], axis=0
    ).astype(BF16)


def own_plot(pair, plot_row):
    half = pair.shape[0] // 2
    return jnp.where(plot_row == 0, pair[:half], pair[half:])


def line_exchange(n, parts, z, dp, refs, compute, merge, finish, hook, before=None):
    own, spread, mine, from_right, from_left, sems = refs
    out_send, out_recv, back_send, back_recv = sems

    def up(j, p, i, start):
        src = own[i].at[p] if start else spread[i].at[j, p]
        return remote(
            src,
            spread[i].at[j, p],
            out_send.at[i, j, p],
            out_recv.at[i, j, p],
            (dp, lax.rem(z + 1, n)),
        )

    def down(j, p, i, start):
        src = own[i].at[p] if start else spread[i].at[j, p]
        return remote(
            src,
            spread[i].at[j, p],
            out_send.at[i, j + 1, p],
            out_recv.at[i, j, p],
            (dp, lax.rem(z + n - 1, n)),
        )

    def back_left(j, p, i):
        return remote(
            mine[i].at[j, p],
            from_right[i].at[j, p],
            back_send.at[i, j, p],
            back_recv.at[i, j, p],
            (dp, lax.rem(z + n - 1, n)),
        )

    def back_right(j, p, i):
        return remote(
            mine[i].at[j, p],
            from_left[i].at[j, p],
            back_send.at[i, j, p],
            back_recv.at[i, j + 1, p],
            (dp, lax.rem(z + 1, n)),
        )

    out_kinds = range(len(own))
    back_kinds = range(len(mine))

    def send_own(p, carry):
        for i in out_kinds:

            @pl.when(z < n - 1)
            def _():
                up(z, p, i, True).start()

            @pl.when(z > 0)
            def _():
                down(z, p, i, True).start()

        return carry

    lax.fori_loop(0, parts, send_own, 0)
    if before is not None:
        before()

    def slot(t, carry):
        def one_part(p, inner):
            low = z - t
            high = z + t

            def one_side(side, done):
                chunk = jnp.where(side == 0, low, high)
                held = jnp.where(side == 0, low >= 0, (high < n) & (t > 0))

                @pl.when((t < n) & held)
                def _():
                    @pl.when(t == 0)
                    def _():
                        for i in out_kinds:
                            spread[i][z, p] = own[i][p]

                    compute(chunk, p)

                    @pl.when((t > 0) & (side == 0) & (z == n - 1))
                    def _():
                        for i in back_kinds:
                            back_left(low, p, i).start()

                    @pl.when((t > 0) & (side == 1) & (z == 0))
                    def _():
                        for i in back_kinds:
                            back_right(high, p, i).start()

                return done

            lax.fori_loop(0, 2, one_side, 0)

            @pl.when((t + 1 < n) & (low - 1 >= 0))
            def _():
                for i in out_kinds:
                    up(low - 1, p, i, False).wait_recv()

                    @pl.when(z < n - 1)
                    def _():
                        up(low - 1, p, i, False).start()

            @pl.when((t + 1 < n) & (high + 1 < n))
            def _():
                for i in out_kinds:
                    down(high + 1, p, i, False).wait_recv()

                    @pl.when(z > 0)
                    def _():
                        down(high + 1, p, i, False).start()

            left_chunk = 2 * (n - 1) - z - t

            @pl.when((t > 0) & (left_chunk >= 0) & (left_chunk < z) & (z < n - 1))
            def _():
                for i in back_kinds:
                    back_left(left_chunk, p, i).wait_recv()
                merge(left_chunk, p, from_right)
                for i in back_kinds:
                    back_left(left_chunk, p, i).start()

            right_chunk = t - z

            @pl.when((t > 0) & (right_chunk < n) & (right_chunk > z) & (z > 0))
            def _():
                for i in back_kinds:
                    back_right(right_chunk, p, i).wait_recv()
                merge(right_chunk, p, from_left)
                for i in back_kinds:
                    back_right(right_chunk, p, i).start()

            return inner

        lax.fori_loop(0, parts, one_part, 0)
        hook(t)
        return carry

    lax.fori_loop(0, 2 * n - 2, slot, 0)

    def last(p, carry):
        @pl.when(z > 0)
        def _():
            for i in back_kinds:
                back_right(z, p, i).wait_recv()
            merge(z, p, from_left)

        @pl.when(z < n - 1)
        def _():
            for i in back_kinds:
                back_left(z, p, i).wait_recv()
            merge(z, p, from_right)

        finish(p)
        return carry

    lax.fori_loop(0, parts, last, 0)

    def drain(p, carry):
        for j in range(n):
            for i in out_kinds:

                @pl.when((z < n - 1) & (z == j))
                def _(i=i, j=j):
                    up(j, p, i, True).wait_send()

                @pl.when((z < n - 1) & (z > j))
                def _(i=i, j=j):
                    up(j, p, i, False).wait_send()

                @pl.when((z > 0) & (z == j))
                def _(i=i, j=j):
                    down(j, p, i, True).wait_send()

                @pl.when((z > 0) & (z < j))
                def _(i=i, j=j):
                    down(j, p, i, False).wait_send()

            for i in back_kinds:

                @pl.when(z > j)
                def _(i=i, j=j):
                    back_left(j, p, i).wait_send()

                @pl.when(z < j)
                def _(i=i, j=j):
                    back_right(j, p, i).wait_send()

        return carry

    return lambda: lax.fori_loop(0, parts, drain, 0)


def line_sems(n, parts, out_kinds, back_kinds):
    return [
        DMA((out_kinds, n + 1, parts)),
        DMA((out_kinds, n, parts)),
        DMA((back_kinds, n, parts)),
        DMA((back_kinds, n + 1, parts)),
    ]


def as_row(ref):
    return ref[...].reshape(1, -1)


def unit_rows(ref, zz, which):
    block = ref[zz, which]
    return block.reshape(-1, block.shape[-1])


def two_units(ref, pair, which):
    return jnp.concatenate(
        [unit_rows(ref, 2 * pair, which), unit_rows(ref, 2 * pair + 1, which)], axis=0
    )


def normed_rows(rows, gain):
    inverse = lax.rsqrt(jnp.mean(rows * rows, axis=-1, keepdims=True) + epsilon)
    return rows * inverse * gain


def half_lanes(first, second, which):
    lane = lax.broadcasted_iota(jnp.int32, first.shape, 1)
    if which == 0:
        return jnp.where(lane < HD, first, pltpu.roll(second, HD, 1))
    return jnp.where(lane < HD, pltpu.roll(first, HD, 1), second)


def tall(out, rows_in, weights, which, n):
    block = 256
    columns = out.shape[1] * 2 // n
    blocks = out.shape[0] // block

    def step(i, carry):
        pair, at = i // blocks, lax.rem(i, blocks)
        at_rows = pl.ds(pl.multiple_of(at * block, block), block)
        cols = pl.ds(pl.multiple_of(pair * columns, columns), columns)
        both = two_units(weights, pair, which)
        out[at_rows, cols] = product(rows_in[at_rows, :], both, 1, 1).astype(BF16)
        return carry

    lax.fori_loop(0, n // 2 * blocks, step, 0)


def flat(out, rows_in, weights, which, n):
    rows_part = out.shape[0] // n

    def step(zz, carry):
        at_part = pl.ds(pl.multiple_of(zz * rows_part, rows_part), rows_part)
        out[at_part, :] = product(unit_rows(weights, zz, which), rows_in[...], 1, 1).astype(BF16)
        return carry

    lax.fori_loop(0, n, step, 0)


def table_at(position, lengths, count):
    table = jnp.zeros(position.shape, jnp.int32)
    end = 0
    for t in range(count):
        end = end + lengths[0, t]
        table = table + (position >= end).astype(jnp.int32)
    return table


KEPT = 23


def forward_kernel(n, count, halo_chunks, *refs):
    (
        lengths, table_plots, tok, cot, self_gain, cross_gain, hidden_gain, mem,
        w_ck, w_cv, w_sq, w_sk, w_sv, w_so, w_cq, w_co,
    ) = refs[:16]
    mine = [None] * 4 + list(refs[16 : 16 + count - 4])
    at = 12 + count
    full_out = refs[at : at + 4]
    at += 4
    out_refs = refs[at : at + 25]
    at += 25
    kept_refs = refs[at : at + KEPT]
    at += KEPT
    (
        bias, plots, near, normed, self_q, self_k, self_mix, self_logs, first_sum, normed_cross,
        q_all, cross_k, cross_kt, cross_v, o_ref,
        output, normed_hidden, hidden, gate_back, up_back, second_back, grad_rows, do_ref, stats,
        gain_hidden,
    ) = kept_refs + out_refs[KEPT:]
    full = refs[at : at + count]
    at += count
    (
        halo, self_vt, cross_vt, cross_q, o_mine, l_mine, o_right, l_right, o_left, l_left,
        down_sum, back_sum, second_sum,
    ) = refs[at : at + 13]
    at += 13
    line = refs[at : at + 4]
    at += 4
    gather_refs = refs[at : at + 9]
    hs, hr, outs, out_sems = refs[at + 9 :]
    leaving = Moves(list(zip(kept_refs, out_refs[:KEPT])), out_sems)
    rows, width = tok.shape
    heads = width // HD
    parts = n
    heads_part = heads // parts
    rows_part = heads_part * HD
    scale = HD ** (-0.5)
    dp, z, c, x, y = place()
    gather = Gather(n, mine, full, gather_refs)
    greet(gather.peers())

    def halo_copy(i):
        src = tok if i == 0 else halo.at[halo_chunks - i]
        dst = halo.at[halo_chunks - 1 - i]
        return remote(src, dst, hs.at[i], hr.at[i], (dp, lax.rem(z + 1, n)))

    def own_units(g, first, second):
        full[g][z, 0] = as_unit(first[...])
        full[g][z, 1] = as_unit(second[...])

    own_units(0, w_ck, w_cv)
    gather.run(0, 0)
    own_units(1, w_sq, w_sk)
    gather.run(1, 0)
    own_units(2, w_sv, w_so)
    own_units(3, w_cq, w_co)

    halo[halo_chunks] = tok[...]
    for i in range(halo_chunks):

        @pl.when(z <= i)
        def _(i=i):
            halo[halo_chunks - 1 - i] = jnp.zeros((rows, width), BF16)

    keys = bias.shape[0]
    held_tables = lengths.shape[1]
    first_key = z * rows - halo_chunks * rows
    key_at = lax.broadcasted_iota(jnp.int32, (keys, rows), 0) + first_key
    query_at = lax.broadcasted_iota(jnp.int32, (1, rows), 1) + z * rows
    same = table_at(key_at, lengths, held_tables) == table_at(query_at, lengths, held_tables)
    allowed = same & (key_at <= query_at) & (key_at >= 0)
    bias[...] = jnp.where(allowed, 0.0, masked_value)
    for j in range(n):
        tables = table_at(
            lax.broadcasted_iota(jnp.int32, (1, rows), 1) + j * rows, lengths, held_tables
        )
        plot = jnp.zeros((1, rows), jnp.int32)
        for t in range(held_tables):
            plot = jnp.where(tables == t, table_plots[0, t], plot)
        plots[j] = plot

    gather.run(0, 1)

    @pl.when(z < n - 1)
    def _():
        halo_copy(0).start()

    gather.run(2, 0)
    gather.run(0, 2)
    gather.run(1, 1)
    gather.run(0, 3)
    gather.run(1, 2)
    gather.run(3, 0)

    def halo_pass(i):
        @pl.when(z > i)
        def _():
            halo_copy(i).wait_recv()

        if i + 1 < halo_chunks:

            @pl.when((z > i) & (z < n - 1))
            def _():
                halo_copy(i + 1).start()

    halo_pass(0)
    gather.run(2, 1)

    def norm_chunk(i, carry):
        at_rows = pl.ds(pl.multiple_of(i * rows, rows), rows)
        near[at_rows, :] = halo[i]
        normed[at_rows, :] = normed_rows(halo[i].astype(F32), as_row(self_gain)).astype(BF16)
        return carry

    gather.run(0, 4)

    plots_held = mem.shape[0]

    def flat_part(which, out):
        def step(zz, carry):
            for p in range(plots_held):
                rows_t = product(unit_rows(full[0], zz, which), mem[p], 1, 1).astype(BF16)
                for hh in range(heads_part):
                    at_head = slice(hh * HD, (hh + 1) * HD)
                    out[zz * heads_part + hh, p * HD : (p + 1) * HD, :] = rows_t[at_head]
            return carry

        lax.fori_loop(0, n, step, 0)

    def tall_part(which, out):
        def step(pair, carry):
            weights = two_units(full[0], pair, which)
            first = product(mem[0], weights, 1, 1)
            second = product(mem[1], weights, 1, 1)
            for hh in range(2 * heads_part):
                cols = slice((hh // 2) * 2 * HD, (hh // 2 + 1) * 2 * HD)
                both = half_lanes(first[:, cols], second[:, cols], hh % 2)
                out[pair * 2 * heads_part + hh] = both.astype(BF16)
            return carry

        lax.fori_loop(0, n // 2, step, 0)

    flat_part(1, cross_vt)
    gather.run(1, 3)
    gather.run(2, 2)
    flat_part(0, cross_kt)
    gather.run(3, 1)
    gather.run(4, 0)
    tall_part(0, cross_k)
    for i in range(1, halo_chunks):
        halo_pass(i)
    gather.run(1, 4)
    gather.run(2, 3)
    gather.run(3, 2)
    lax.fori_loop(0, halo_chunks + 1, norm_chunk, 0)

    own_rows = slice(halo_chunks * rows, (halo_chunks + 1) * rows)

    def query_part(zz, carry):
        at_part = pl.ds(pl.multiple_of(zz * rows_part, rows_part), rows_part)
        projected = product(unit_rows(full[1], zz, 0), normed[own_rows, :], 1, 1)
        self_q[at_part, :] = (projected.astype(BF16).astype(F32) * scale).astype(BF16)
        return carry

    lax.fori_loop(0, n, query_part, 0)

    tall(self_k, normed, full[1], 1, n)
    gather.run(5, 0)
    gather.run(2, 4)

    flat(self_vt, normed, full[2], 0, n)
    gather.run(3, 3)

    def self_pair(pair, carry):
        cols = pl.ds(pl.multiple_of(pair * 2 * HD, 2 * HD), 2 * HD)
        for which in range(2):
            at_head = pl.ds(pl.multiple_of((2 * pair + which) * HD, HD), HD)
            scores = jnp.dot(
                self_k[:, cols], alone(self_q[at_head, :], which), preferred_element_type=F32
            )
            scores = scores + bias[...]
            top = jnp.max(scores, axis=0, keepdims=True)
            powers = jnp.exp(scores - top)
            total = jnp.sum(powers, axis=0, keepdims=True)
            mixed = jnp.dot(self_vt[at_head, :], powers.astype(BF16), preferred_element_type=F32)
            self_mix[at_head, :] = (mixed / total).astype(BF16)
            self_logs[pair, which : which + 1, :] = top + jnp.log(total)
        return carry

    lax.fori_loop(0, heads // 4, self_pair, 0)
    lax.fori_loop(heads // 4, heads // 2, self_pair, 0)

    first_sum[...] = tok[...].astype(F32)

    def first_part(zz, carry):
        at_part = pl.ds(pl.multiple_of(zz * rows_part, rows_part), rows_part)
        first_sum[...] += product(self_mix[at_part, :], unit_rows(full[2], zz, 1), 0, 0)
        return carry

    lax.fori_loop(0, n, first_part, 0)
    total = first_sum[...]
    normed_cross[...] = normed_rows(total, as_row(cross_gain)).astype(BF16)
    gather.run(3, 4)

    def cross_query_part(zz, carry):
        projected = product(unit_rows(full[3], zz, 0), normed_cross[...], 1, 1)
        cross_q[zz] = (projected.astype(BF16).astype(F32) * scale).astype(BF16)
        return carry

    lax.fori_loop(0, n, cross_query_part, 0)

    def compute(j, p):
        plot_row = plots[j]
        for hh in range(heads_part):
            h = p * heads_part + hh
            q_pair = both_plots(q_all[j, p, hh * HD : (hh + 1) * HD, :], plot_row)
            scores = jnp.dot(cross_k[h], q_pair, preferred_element_type=F32)
            top = jnp.max(scores, axis=0, keepdims=True)
            powers = jnp.exp(scores - top)
            total = jnp.sum(powers, axis=0, keepdims=True)
            mixed = jnp.dot(cross_vt[h], powers.astype(BF16), preferred_element_type=F32)
            mixed = own_plot(mixed, plot_row) / total
            o_mine[j, p, hh * HD : (hh + 1) * HD, :] = mixed.astype(BF16)
            l_mine[j, p, hh : hh + 1, :] = top + jnp.log(total)

    def merge(j, p, arrived):
        for hh in range(heads_part):
            at_head = slice(hh * HD, (hh + 1) * HD)
            log_a = l_mine[j, p, hh : hh + 1, :]
            log_b = arrived[1][j, p, hh : hh + 1, :]
            top = jnp.maximum(log_a, log_b)
            share_a = jnp.exp(log_a - top)
            share_b = jnp.exp(log_b - top)
            total = share_a + share_b
            mixed = o_mine[j, p, at_head, :].astype(F32) * (share_a / total)
            mixed = mixed + arrived[0][j, p, at_head, :].astype(F32) * (share_b / total)
            o_mine[j, p, at_head, :] = mixed.astype(BF16)
            l_mine[j, p, hh : hh + 1, :] = top + jnp.log(total)

    def finish(p):
        o_ref[p] = o_mine[z, p]

    def keep(g):
        return pltpu.make_async_copy(full[g], full_out[g], outs.at[g])

    schedule = {
        0: [(4, 1)],
        1: [(6, 0), (4, 2), (5, 1)],
        2: [(4, 3), (5, 2)],
        3: [(6, 1)],
        4: [(6, 2), (5, 3)],
        5: [(6, 3)],
    }

    def hook(t):
        for step, work in schedule.items():

            @pl.when(t == step)
            def _(step=step, work=work):
                if step == 0:
                    tall_part(1, cross_v)
                for g, stage in work:
                    gather.run(g, stage)
                if step == 0:
                    for g in range(4):
                        keep(g).start()

        @pl.when(t == 2 * n - 3)
        def _():
            leaving.start(*range(14))

    exchange = ([cross_q], [q_all], [o_mine, l_mine], [o_right, l_right], [o_left, l_left], line)
    end_exchange = line_exchange(n, parts, z, dp, exchange, compute, merge, finish, hook)

    second_sum[...] = first_sum[...]

    def second_part(zz, carry):
        second_sum[...] += product(o_ref[zz], unit_rows(full[3], zz, 1), 0, 0)
        return carry

    lax.fori_loop(0, n, second_part, 0)
    total = second_sum[...]
    normed_hidden[...] = normed_rows(total, as_row(hidden_gain)).astype(BF16)
    leaving.start(14, 16)
    down_sum[...] = jnp.zeros((rows, width), F32)
    back_sum[...] = jnp.zeros((rows, width), F32)
    for g in range(4, 7):
        gather.run(g, 4)
    slope = (2.0 / 3.141592653589793) ** 0.5
    bend = 0.044715

    def whole(g, zz):
        block = full[g][zz]
        return block.reshape(-1, block.shape[-1])

    def hidden_part(zz, carry):
        gate = product(normed_hidden[...], whole(4, zz), 1, 0)
        up = product(normed_hidden[...], whole(5, zz), 1, 0)
        act_back = product(cot[...], whole(6, zz), 1, 1).astype(BF16).astype(F32)
        square = gate * gate
        curve = jnp.tanh(slope * (gate + bend * square * gate))
        cdf = 0.5 * (1.0 + curve)
        act = gate * cdf
        turn = cdf + 0.5 * gate * (1.0 - curve * curve) * slope * (1.0 + 3.0 * bend * square)
        here = (act * up).astype(BF16)
        to_gate = (act_back * up * turn).astype(BF16)
        to_up = (act_back * act).astype(BF16)
        hidden[zz] = here
        gate_back[zz] = to_gate
        up_back[zz] = to_up
        down_sum[...] += product(here, whole(6, zz), 1, 0)
        back_sum[...] += product(to_gate, whole(4, zz), 1, 1) + product(to_up, whole(5, zz), 1, 1)
        return carry

    lax.fori_loop(0, n, hidden_part, 0)
    leaving.start(17, 18, 19)
    output[...] = (second_sum[...] + down_sum[...]).astype(BF16)
    leaving.start(15)
    residual, gain_back = norm_gradient(second_sum[...], as_row(hidden_gain), back_sum[...])
    gain_hidden[...] = gain_back
    total = cot[...].astype(F32) + residual
    second_back[...] = total
    grad_rows[...] = total.astype(BF16)
    leaving.start(20, 21)

    def mixed_part(zz, carry):
        mixed = product(unit_rows(full[3], zz, 1), grad_rows[...], 1, 1).astype(BF16)
        do_ref[zz] = mixed
        for hh in range(heads_part):
            at_head = slice(hh * HD, (hh + 1) * HD)
            inner = mixed[at_head].astype(F32) * o_ref[zz, at_head, :].astype(F32)
            row = heads_part + hh
            stats[zz, row : row + 1, :] = jnp.sum(inner, axis=0, keepdims=True)
            stats[zz, hh : hh + 1, :] = l_mine[z, zz, hh : hh + 1, :]
        stats[zz, 2 * heads_part : 8, :] = jnp.zeros((8 - 2 * heads_part, rows), F32)
        return carry

    lax.fori_loop(0, n, mixed_part, 0)
    leaving.start(22)
    end_exchange()
    gather.drain()
    leaving.wait(*range(KEPT))
    for g in range(4):
        keep(g).wait()
    for i in range(halo_chunks):

        @pl.when((z >= i) & (z < n - 1))
        def _(i=i):
            halo_copy(i).wait_send()


def forward(n, halo_chunks, ins, shards):
    tokens, memory = ins[2], ins[7]
    rows, width = tokens.shape
    keys = (halo_chunks + 1) * rows
    heads = width // HD
    parts = n
    rows_part = width // parts
    held_plots, patches, _ = memory.shape
    unit = rows_part // 4
    full = [(n, 2, 2, 2, unit, width)] * 4 + [(n,) + s.shape for s in shards]
    count = len(full)
    struct = jax.ShapeDtypeStruct
    out_shape = [struct(f, BF16) for f in full[:4]] + [
        struct((keys, rows), F32),
        struct((n, 1, rows), jnp.int32),
        struct((keys, width), BF16),
        struct((keys, width), BF16),
        struct((width, rows), BF16),
        struct((keys, width), BF16),
        struct((width, rows), BF16),
        struct((heads // 2, 8, rows), F32),
        struct((rows, width), F32),
        struct((rows, width), BF16),
        struct((n, parts, rows_part, rows), BF16),
        struct((heads, patches, held_plots * HD), BF16),
        struct((heads, held_plots * HD, patches), BF16),
        struct((heads, patches, held_plots * HD), BF16),
        struct((parts, rows_part, rows), BF16),
        struct((rows, width), BF16),
        struct((rows, width), BF16),
        struct((n, rows, shards[0].shape[-1]), BF16),
        struct((n, rows, shards[0].shape[-1]), BF16),
        struct((n, rows, shards[0].shape[-1]), BF16),
        struct((rows, width), F32),
        struct((rows, width), BF16),
        struct((parts, rows_part, rows), BF16),
        struct((parts, 8, rows), F32),
        struct((1, width), F32),
    ]
    scratch = [held(o) for o in out_shape[4 : 4 + KEPT]]
    scratch += [pltpu.VMEM(f, BF16) for f in full]
    scratch += [
        pltpu.VMEM((halo_chunks + 1, rows, width), BF16),
        pltpu.VMEM((width, keys), BF16),
        pltpu.VMEM((heads, held_plots * HD, patches), BF16),
        pltpu.VMEM((parts, rows_part, rows), BF16),
    ]
    for _ in range(3):
        scratch += [
            pltpu.VMEM((n, parts, rows_part, rows), BF16),
            pltpu.VMEM((n, parts, 8, rows), F32),
        ]
    scratch += [pltpu.VMEM((rows, width), F32)] * 3
    scratch += line_sems(n, parts, 1, 2)
    scratch += gather_sems(n, count)
    scratch += [DMA((halo_chunks,)), DMA((halo_chunks,)), DMA((4,)), DMA((KEPT,))]
    smem = pl.BlockSpec(memory_space=pltpu.SMEM)
    out = pl.pallas_call(
        functools.partial(forward_kernel, n, count, halo_chunks),
        out_shape=out_shape,
        in_specs=[smem] * 2 + [VMEM] * 14 + [ANY] * (count - 4),
        out_specs=[ANY] * (4 + KEPT) + [VMEM] * (25 - KEPT),
        scratch_shapes=scratch,
        compiler_params=pltpu.CompilerParams(
            collective_id=0, has_side_effects=True, vmem_limit_bytes=63 << 20
        ),
        name="forward",
    )(*ins, *shards)
    return out[:4], out[4:]


def norm_gradient(rows, gain, back):
    inverse = lax.rsqrt(jnp.mean(rows * rows, axis=-1, keepdims=True) + epsilon)
    unit = rows * inverse
    scaled = back * gain
    inner = jnp.mean(scaled * unit, axis=-1, keepdims=True)
    return inverse * (scaled - unit * inner), jnp.sum(back * unit, axis=0, keepdims=True)


def as_unit(rows_192):
    rows, width = rows_192.shape
    return rows_192.reshape(2, 2, rows // 4, width)


def cross_backward_kernel(n, count, *refs):
    plots, do_ref, st_ref, cross_gain = refs[:4]
    late, at = refs[4:21], 21
    quarters = refs[at : at + count]
    gain_cross, out_refs = refs[at + count], refs[at + count + 1 : at + count + 6]
    rest = refs[at + count + 6 :]
    part, rest = rest[:count], rest[count:]
    none = [False] * count
    reduce, rest = take_reduce(n, 0, part, None, none, [None] * count, none, rest)
    do_all, st_all, q_mine, q_right, q_left, dk_ref, dv_ref, k_back, v_back = rest[:9]
    line = rest[9:13]
    inside, load_sems = rest[13:30], rest[30]
    kept_refs, out_sems = rest[31:36], rest[36]
    grad_mem, part_keys, part_query, first_back, g_first = kept_refs
    leaving = Moves(list(zip(kept_refs, out_refs)), out_sems)
    (
        normed_hidden, gate_back, up_back, hidden, cot, q_all, k_ref, v_ref, kt_ref,
        mem, w_keys, w_query, cross_mix, grad_rows, normed_cross, second_back, first_sum,
    ) = inside
    loads = Moves(list(zip(late, inside)), load_sems)
    loads.start(*range(17))
    dp, z, c, x, y = place()
    parts, rows_part, rows = do_ref.shape
    width = parts * rows_part
    heads_part = rows_part // HD
    heads = parts * heads_part
    held_plots = mem.shape[0]
    scale = HD ** (-0.5)
    greet(reduce.peers())

    def clear(h, carry):
        dk_ref[h] = jnp.zeros(dk_ref.shape[1:], F32)
        dv_ref[h] = jnp.zeros(dv_ref.shape[1:], F32)
        return carry

    def compute(j, p):
        plot_row = plots[j]
        for hh in range(heads_part):
            h = p * heads_part + hh
            at_head = slice(hh * HD, (hh + 1) * HD)
            q_pair = both_plots(q_all[j, p, at_head, :], plot_row)
            do_pair = both_plots(do_all[j, p, at_head, :], plot_row)
            scores = jnp.dot(k_ref[h], q_pair, preferred_element_type=F32)
            chances = jnp.exp(scores - st_all[j, p, hh : hh + 1, :])
            prob_back = jnp.dot(v_ref[h], do_pair, preferred_element_type=F32)
            inner = st_all[j, p, heads_part + hh : heads_part + hh + 1, :]
            score_back = (chances * (prob_back - inner)).astype(BF16)
            q_back = jnp.dot(kt_ref[h], score_back, preferred_element_type=F32)
            q_mine[j, p, at_head, :] = (own_plot(q_back, plot_row) * scale).astype(BF16)
            dk_ref[h] += product(score_back, q_pair, 1, 1)
            dv_ref[h] += product(chances.astype(BF16), do_pair, 1, 1)

    def merge(j, p, arrived):
        total = q_mine[j, p].astype(F32) + arrived[0][j, p].astype(F32)
        q_mine[j, p] = total.astype(BF16)

    def finish(p):
        pass

    def hidden_gradients():
        firsts = (normed_hidden, normed_hidden, None)
        for g, seconds in enumerate((gate_back, up_back, None)):

            def step(zz, carry, g=g, seconds=seconds):
                if seconds is None:
                    grad = product(hidden[zz], cot[...], 0, 0)
                else:
                    grad = product(firsts[g][...], seconds[zz], 0, 0)
                part[g][zz] = grad.astype(BF16).reshape(part[g].shape[1:])
                return carry

            loads.wait(*((0, 1), (2,), (3, 4))[g])
            lax.fori_loop(0, n, step, 0)
            reduce.run(g, 0)

        loads.wait(5, 6, 7, 8)

    def patch_gradients():
        for source, out in ((dk_ref, k_back), (dv_ref, v_back)):

            def pair_step(i, carry, source=source, out=out):
                even, odd = source[2 * i], source[2 * i + 1]
                lane = lax.broadcasted_iota(jnp.int32, even.shape, 1)
                cols = pl.ds(pl.multiple_of(i * 2 * HD, 2 * HD), 2 * HD)
                out[0, :, cols] = jnp.where(lane < HD, even, pltpu.roll(odd, HD, 1)).astype(BF16)
                out[1, :, cols] = jnp.where(lane < HD, pltpu.roll(even, HD, 1), odd).astype(BF16)
                return carry

            lax.fori_loop(0, heads // 2, pair_step, 0)
        for which, back in enumerate((k_back, v_back)):

            def grad_step(pair, carry, which=which, back=back):
                wide = 2 * rows_part
                cols = pl.ds(pl.multiple_of(pair * wide, wide), wide)
                grad = sum(product(back[p, :, cols], mem[p], 0, 0) for p in range(held_plots))
                grad = grad.astype(BF16)
                part_keys[2 * pair, which] = as_unit(grad[:rows_part])
                part_keys[2 * pair + 1, which] = as_unit(grad[rows_part:])
                return carry

            lax.fori_loop(0, n // 2, grad_step, 0)

        def memory_step(i, carry):
            p, at_rows = i // 2, pl.ds(pl.multiple_of(lax.rem(i, 2) * rows, rows), rows)
            total = 0.0
            for which, back in enumerate((k_back, v_back)):
                for pair in range(n // 2):
                    cols = slice(pair * 2 * rows_part, (pair + 1) * 2 * rows_part)
                    weights = two_units(w_keys, pair, which)
                    total = total + product(back[p, at_rows, cols], weights, 1, 0)
            grad_mem[p, at_rows, :] = total.astype(BF16)
            return carry

        lax.fori_loop(0, held_plots * (mem.shape[1] // rows), memory_step, 0)

    def hook(t):
        for step, work in schedule.items():

            @pl.when(t == step)
            def _(work=work):
                for g, stage in work:
                    reduce.run(g, stage)

        @pl.when(t == n - 1)
        def _():
            loads.wait(9, 10)
            patch_gradients()
            leaving.start(0, 1)
            for g in range(count):
                reduce.run(g, 2)

    schedule = {0: [(0, 1), (1, 1), (2, 1)]}

    def before():
        lax.fori_loop(0, heads, clear, 0)
        hidden_gradients()

    exchange = ([do_ref, st_ref], [do_all, st_all], [q_mine], [q_right], [q_left], line)
    end_exchange = line_exchange(n, parts, z, dp, exchange, compute, merge, finish, hook, before)

    loads.wait(*range(11, 17))
    first_back[...] = jnp.zeros(first_back.shape, F32)

    def query_part(zz, carry):
        mine = q_mine[z, zz]
        part_query[zz, 0] = as_unit(product(mine, normed_cross[...], 1, 0).astype(BF16))
        part_query[zz, 1] = as_unit(product(cross_mix[zz], grad_rows[...], 1, 0).astype(BF16))
        first_back[...] += product(mine, unit_rows(w_query, zz, 0), 0, 0)
        return carry

    lax.fori_loop(0, n, query_part, 0)
    leaving.start(2)
    residual, gain_back = norm_gradient(first_sum[...], as_row(cross_gain), first_back[...])
    total = second_back[...] + residual
    first_back[...] = total
    g_first[...] = total.astype(BF16)
    leaving.start(3, 4)
    gain_cross[...] = gain_back
    for g in range(count):
        reduce.end(2, g)
        quarters[g][...] = reduce.acc[g][:, y, x]
    end_exchange()
    reduce.drain()
    leaving.wait(*range(5))


def cross_backward(n, ins, shapes):
    do, mem = ins[1], ins[13]
    parts, rows_part, rows = do.shape
    width = parts * rows_part
    heads = width // HD
    held_plots, patches, _ = mem.shape
    count = len(shapes)
    struct = jax.ShapeDtypeStruct
    unit = width // n // 4
    scratch = [pltpu.VMEM((n, 2, 2, 2) + s, BF16) for s in shapes]
    none = [False] * count
    scratch += reduce_scratch(n, 0, shapes, [BF16] * count, none, [True] * count, none)
    scratch += [
        pltpu.VMEM((n, parts, rows_part, rows), BF16),
        pltpu.VMEM((n, parts, 8, rows), F32),
        pltpu.VMEM((n, parts, rows_part, rows), BF16),
        pltpu.VMEM((n, parts, rows_part, rows), BF16),
        pltpu.VMEM((n, parts, rows_part, rows), BF16),
        pltpu.VMEM((heads, patches, held_plots * HD), F32),
        pltpu.VMEM((heads, patches, held_plots * HD), F32),
        pltpu.VMEM((held_plots, patches, width), BF16),
        pltpu.VMEM((held_plots, patches, width), BF16),
    ]
    scratch += line_sems(n, parts, 2, 1)
    scratch += [held(i) for i in ins[4:]] + [DMA((len(ins) - 4,))]
    kept = [
        struct(mem.shape, BF16),
        struct((n, 2, 2, 2, unit, width), BF16),
        struct((n, 2, 2, 2, unit, width), BF16),
        struct((rows, width), F32),
        struct((rows, width), BF16),
    ]
    scratch += [held(k) for k in kept] + [DMA((len(kept),))]
    out = pl.pallas_call(
        functools.partial(cross_backward_kernel, n, count),
        out_shape=[struct((n,) + s, BF16) for s in shapes] + [struct((1, width), F32)] + kept,
        in_specs=[VMEM] * 4 + [ANY] * 17,
        out_specs=[VMEM] * (count + 1) + [ANY] * 5,
        scratch_shapes=scratch,
        compiler_params=pltpu.CompilerParams(
            collective_id=1, has_side_effects=True, vmem_limit_bytes=63 << 20
        ),
        name="cross_backward",
    )(*ins)
    return out[:count], out[count:]


def alone(rows, which):
    zero = jnp.zeros_like(rows)
    return jnp.concatenate([rows, zero] if which == 0 else [zero, rows], axis=0)


RELAYED = [True] * 3 + [False] * 3 + [True] * 3 + [False]


def self_backward_kernel(n, extra, halo_chunks, *refs):
    self_gain, gain_cross, gain_hidden = refs[:3]
    late = refs[3:14]
    cross_parts = refs[14:16]
    sums = refs[16:19]
    fin_out = refs[19:28]
    grad_tokens, gain_out = refs[28:30]
    own_parts = refs[30:34]
    gain_part, gain_fin = refs[34:36]
    part = list(cross_parts) + list(own_parts) + [None] * 3 + [gain_part]
    kept = [True, True] + [False] * 8
    quarters = [None] * 6 + list(sums) + [None]
    fin = list(refs[-10:-1]) + [gain_fin]
    reduce, rest = take_reduce(n, extra, part, fin, kept, quarters, RELAYED, refs[36:])
    do_ref, dq_ref, dk_ref, dv_ref, own_back, csend, crecv, hs, hr = rest[:9]
    inside, load_sems, v_ref, kt_ref = rest[9:20], rest[20], rest[21], rest[22]
    leaving = Moves(list(zip(fin[:9], fin_out)), rest[33])
    gain_self = rest[23]
    g_first, mix, w_vo, normed, w_qk, k_ref, q_ref, bias, logs, near, first_back = inside
    loads = Moves(list(zip(late, inside)), load_sems)
    loads.start(*range(11))
    dp, z, c, x, y = place()
    rows, width = g_first.shape
    heads = width // HD
    rows_part = width // n
    scale = HD ** (-0.5)
    own_rows = slice(halo_chunks * rows, (halo_chunks + 1) * rows)
    early_groups, late_groups, hidden_groups = (0, 1, 2), (3, 4, 5), (6, 7, 8)
    half = width // 2

    def store_unit(out, zz, grad):
        for cc in range(2):
            columns = grad[:, cc * half : (cc + 1) * half]
            out[zz, :, :, cc] = columns.reshape(2, 2, rows_part // 4, half)

    def all_run(groups, stage):
        for g in groups:
            reduce.run(g, stage)

    greet(reduce.peers())
    all_run((0, 1), 0)
    for g in hidden_groups:
        reduce.begin(3, g)
    loads.wait(0, 1)
    def output_part(zz, carry):
        at_part = pl.ds(pl.multiple_of(zz * rows_part, rows_part), rows_part)
        store_unit(own_parts[0], zz, product(mix[at_part, :], g_first[...], 1, 0).astype(BF16))
        return carry

    lax.fori_loop(0, n, output_part, 0)
    reduce.run(2, 0)
    loads.wait(2)

    def do_part(zz, carry):
        at_part = pl.ds(pl.multiple_of(zz * rows_part, rows_part), rows_part)
        do_ref[at_part, :] = product(unit_rows(w_vo, zz, 1), g_first[...], 1, 1).astype(BF16)
        return carry

    lax.fori_loop(0, n, do_part, 0)
    all_run(early_groups, 1)
    loads.wait(3, 4)
    tall(v_ref, normed, w_vo, 0, n)
    flat(kt_ref, normed, w_qk, 1, n)

    def pair_step(pair, carry):
        cols = pl.ds(pl.multiple_of(pair * 2 * HD, 2 * HD), 2 * HD)
        dk, dv = 0.0, 0.0
        for which in range(2):
            at_head = pl.ds(pl.multiple_of((2 * pair + which) * HD, HD), HD)
            q_pair = alone(q_ref[at_head, :], which)
            do_head = do_ref[at_head, :]
            inner = jnp.sum(
                do_head.astype(F32) * mix[at_head, :].astype(F32), axis=0, keepdims=True
            )
            do_pair = alone(do_head, which)
            scores = jnp.dot(k_ref[:, cols], q_pair, preferred_element_type=F32)
            chances = jnp.exp(scores + bias[...] - logs[pair, which : which + 1, :])
            prob_back = jnp.dot(v_ref[:, cols], do_pair, preferred_element_type=F32)
            score_back = (chances * (prob_back - inner)).astype(BF16)
            q_back = jnp.dot(kt_ref[at_head, :], score_back, preferred_element_type=F32)
            dq_ref[at_head, :] = (q_back * scale).astype(BF16)
            dk = dk + product(score_back, q_pair, 1, 1)
            dv = dv + product(chances.astype(BF16), do_pair, 1, 1)
        dk_ref[:, cols] = dk.astype(BF16)
        dv_ref[:, cols] = dv.astype(BF16)
        return carry

    loads.wait(5, 6, 7, 8)
    lax.fori_loop(0, heads // 2, pair_step, 0)
    for g, back in ((3, dv_ref), (4, dk_ref)):

        def grad_step(pair, carry, g=g, back=back):
            cols = pl.ds(pl.multiple_of(pair * 2 * rows_part, 2 * rows_part), 2 * rows_part)
            grad = product(back[:, cols], normed[...], 0, 0).astype(BF16)
            store_unit(own_parts[g - 2], 2 * pair, grad[:rows_part])
            store_unit(own_parts[g - 2], 2 * pair + 1, grad[rows_part:])
            return carry

        lax.fori_loop(0, n // 2, grad_step, 0)
        reduce.run(g, 0)

    def query_part(zz, carry):
        at_part = pl.ds(pl.multiple_of(zz * rows_part, rows_part), rows_part)
        grad = product(dq_ref[at_part, :], normed[own_rows, :], 1, 0)
        store_unit(own_parts[3], zz, grad.astype(BF16))
        return carry

    lax.fori_loop(0, n, query_part, 0)
    reduce.run(5, 0)
    all_run(early_groups, 2)
    all_run(late_groups, 1)
    for g in hidden_groups:
        reduce.pass_on(g)
    loads.wait(9, 10)

    def halo_copy(i):
        dev = (dp, lax.rem(z + n - 1, n))
        return remote(csend.at[i], crecv.at[i], hs.at[i], hr.at[i], dev)

    def halo_send(i):
        if i > 0:
            halo_take(i - 1, csend.at[i])

        @pl.when(z >= halo_chunks - i)
        def _():
            halo_copy(i).start()

    def halo_take(i, onto):
        @pl.when((z + 1 < n) & (z + 1 >= halo_chunks - i))
        def _():
            halo_copy(i).wait_recv()
            onto[...] = (onto[...].astype(F32) + crecv[i].astype(F32)).astype(onto.dtype)

    def unit_of(at_rows):
        here = near[at_rows, :].astype(F32)
        return here * lax.rsqrt(jnp.mean(here * here, axis=-1, keepdims=True) + epsilon)

    gain_self[...] = jnp.zeros((1, width), F32)

    def near_chunk(i, carry):
        at_rows = pl.ds(pl.multiple_of(i * rows, rows), rows)
        back = 0.0
        for pair in range(n // 2):
            cols = slice(pair * 2 * rows_part, (pair + 1) * 2 * rows_part)
            back = back + product(dk_ref[at_rows, cols], two_units(w_qk, pair, 1), 1, 0)
            back = back + product(dv_ref[at_rows, cols], two_units(w_vo, pair, 0), 1, 0)

        @pl.when(i < halo_chunks)
        def _():
            csend[i] = back.astype(BF16)
            gain_self[...] += jnp.sum(back * unit_of(at_rows), axis=0, keepdims=True)

        @pl.when(i == 0)
        def _():
            halo_send(0)

        @pl.when(i == halo_chunks)
        def _():
            own_back[...] = back

        return carry

    lax.fori_loop(0, halo_chunks + 1, near_chunk, 0)

    def own_part(zz, carry):
        at_part = pl.ds(pl.multiple_of(zz * rows_part, rows_part), rows_part)
        own_back[...] += product(dq_ref[at_part, :], unit_rows(w_qk, zz, 0), 0, 0)
        return carry

    lax.fori_loop(0, n, own_part, 0)
    gain_self[...] += jnp.sum(own_back[...] * unit_of(own_rows), axis=0, keepdims=True)

    deep, lanes = gain_part.shape[4:]
    gain_part[...] = jnp.zeros(gain_part.shape, F32)
    for i, gain in enumerate((gain_self[...], gain_cross[...], gain_hidden[...])):
        for j in range(width // lanes):
            piece, row = divmod(i * (width // lanes) + j, deep)
            for zz in range(n):
                gain_part[zz, piece // 4, piece // 2 % 2, piece % 2, row : row + 1, :] = gain[
                    :, j * lanes : (j + 1) * lanes
                ]

    reduce.run(9, 0)
    all_run(early_groups, 3)
    reduce.run(9, 1)
    all_run(late_groups, 2)
    reduce.run(9, 2)
    for g in early_groups:
        reduce.pass_on(g)
    all_run(late_groups, 3)
    reduce.run(9, 3)
    all_run(hidden_groups, 4)
    for i in range(1, halo_chunks):
        halo_send(i)
    all_run(hidden_groups, 5)
    all_run(early_groups, 4)
    all_run(late_groups + (9,), 4)
    all_run(hidden_groups, 6)
    all_run(early_groups, 5)
    all_run(late_groups + (9,), 5)
    all_run(hidden_groups, 7)
    leaving.start(*hidden_groups)
    all_run(early_groups, 6)
    all_run(late_groups + (9,), 6)
    halo_take(halo_chunks - 1, own_back)
    here = near[own_rows, :].astype(F32)
    residual, _ = norm_gradient(here, as_row(self_gain), own_back[...])
    grad_tokens[...] = (first_back[...] + residual).astype(BF16)
    all_run(early_groups, 7)
    leaving.start(*early_groups)
    all_run(late_groups + (9,), 7)
    leaving.start(*late_groups)
    for i in range(3):
        for j in range(width // lanes):
            piece, row = divmod(i * (width // lanes) + j, deep)
            found = gain_fin[piece // 4, piece // 2 % 2, piece % 2, row : row + 1, :]
            gain_out[i : i + 1, j * lanes : (j + 1) * lanes] = found
    gain_out[3:8, :] = jnp.zeros((5, width), F32)
    for i in range(halo_chunks):

        @pl.when(z >= halo_chunks - i)
        def _(i=i):
            halo_copy(i).wait_send()

    reduce.drain()
    leaving.wait(*range(9))


def self_backward(n, extra, halo_chunks, ins, cross_parts, sums):
    near, g_first = ins[12], ins[3]
    rows, width = g_first.shape
    keys = near.shape[0]
    unit = width // n // 4
    gain_shape = (8, 128)
    single = (unit, width // 2)
    shapes = [(unit, width)] * 2 + [single] * 4 + [p.shape[1:] for p in sums]
    struct = jax.ShapeDtypeStruct
    scratch = [pltpu.VMEM((n, 2, 2, 2) + single, BF16)] * 4
    scratch += [pltpu.VMEM((n, 2, 2, 2) + gain_shape, F32), pltpu.VMEM((2, 2, 2) + gain_shape, F32)]
    scratch += reduce_scratch(
        n, extra, shapes + [gain_shape], [BF16] * 9 + [F32],
        [True, True] + [False] * 8, [True] * 6 + [False] * 3 + [True], RELAYED,
    )
    scratch += [
        pltpu.VMEM((width, rows), BF16),
        pltpu.VMEM((width, rows), BF16),
        pltpu.VMEM((keys, width), BF16),
        pltpu.VMEM((keys, width), BF16),
        pltpu.VMEM((rows, width), F32),
        pltpu.VMEM((halo_chunks, rows, width), BF16),
        pltpu.VMEM((halo_chunks, rows, width), BF16),
        DMA((halo_chunks,)),
        DMA((halo_chunks,)),
    ]
    scratch += [held(i) for i in ins[3:]] + [DMA((len(ins) - 3,))]
    scratch += [pltpu.VMEM((keys, width), BF16), pltpu.VMEM((width, keys), BF16)]
    scratch += [pltpu.VMEM((1, width), F32)]
    scratch += [pltpu.VMEM((2, 2, 2) + s, BF16) for s in shapes] + [DMA((len(shapes),))]
    out = pl.pallas_call(
        functools.partial(self_backward_kernel, n, extra, halo_chunks),
        out_shape=[struct((2, 2, 2) + s, BF16) for s in shapes]
        + [struct((rows, width), BF16), struct((8, width), F32)],
        in_specs=[VMEM] * 3 + [ANY] * 13 + [VMEM] * 3,
        out_specs=[ANY] * 9 + [VMEM] * 2,
        scratch_shapes=scratch,
        compiler_params=pltpu.CompilerParams(
            collective_id=2, has_side_effects=True, vmem_limit_bytes=63 << 20
        ),
        name="self_backward",
    )(*ins, *cross_parts, *sums)
    return out[:9], out[9], out[10]


def results_kernel(*refs):
    ins, gains, outs = refs[:12], refs[12], refs[13:]
    at = 0
    for g in range(2):
        for u in range(2):
            outs[at][...] = ins[g][u, 0, 0].astype(F32)
            at += 1
    for g in range(2, 6):
        half = ins[g].shape[-1]
        for cc in range(2):
            outs[at][:, cc * half : (cc + 1) * half] = ins[g][0, 0, cc].astype(F32)
        at += 1
    for g in range(6, 9):
        block = ins[g][0, 0]
        outs[at][...] = block.reshape(-1, block.shape[-1]).astype(F32)
        at += 1
    for i in range(9, 12):
        outs[at][...] = ins[i][...]
        at += 1
    for i in range(3):
        outs[at][...] = gains[i, :]
        at += 1


def results(sums, output, grad_tokens, grad_memory, gains):
    struct = jax.ShapeDtypeStruct
    steps = 4
    in_specs, out_specs, out_shape = [], [], []
    for i, piece in enumerate(sums):
        rows, cols = piece.shape[3:]
        if i < 2:
            in_specs.append(pl.BlockSpec((2, 1, 1, rows, cols), lambda i: (0, i // 2, i % 2, 0, 0)))
            for _ in range(2):
                out_specs.append(pl.BlockSpec((rows, cols), lambda i: (i, 0)))
                out_shape.append(struct((steps * rows, cols), F32))
        else:
            in_specs.append(pl.BlockSpec((1, 1, 2, rows, cols), lambda i: (i // 2, i % 2, 0, 0, 0)))
            shape = (rows, 2 * cols) if i < 6 else (2 * rows, cols)
            out_specs.append(pl.BlockSpec(shape, lambda i: (i, 0)))
            out_shape.append(struct((steps * shape[0], shape[1]), F32))
    for rows in (output, grad_tokens):
        spec = pl.BlockSpec((rows.shape[0] // steps, rows.shape[1]), lambda i: (i, 0))
        in_specs.append(spec)
        out_specs.append(spec)
        out_shape.append(struct(rows.shape, rows.dtype))
    plots, patches, width = grad_memory.shape
    per = steps // plots
    spec = pl.BlockSpec((1, patches // per, width), lambda i: (i // per, i % per, 0))
    in_specs.append(spec)
    out_specs.append(spec)
    out_shape.append(struct(grad_memory.shape, grad_memory.dtype))
    in_specs.append(pl.BlockSpec(gains.shape, lambda i: (0, 0)))
    for _ in range(3):
        out_specs.append(pl.BlockSpec((width,), lambda i: (0,)))
        out_shape.append(struct((width,), F32))
    return pl.pallas_call(
        results_kernel,
        grid=(steps,),
        out_shape=out_shape,
        in_specs=in_specs,
        out_specs=out_specs,
        compiler_params=pltpu.CompilerParams(vmem_limit_bytes=63 << 20),
        name="results",
    )(*sums, output, grad_tokens, grad_memory, gains)


def body(
    tokens, memory, table_lengths, table_plots,
    self_gain, self_query, self_key, self_value, self_output,
    cross_gain, cross_query, cross_key, cross_value, cross_output,
    hidden_gain, hidden_gate, hidden_up, hidden_down, cotangent,
):
    n = lax.axis_size("tensor")
    extra = lax.axis_size("dp").bit_length() - 1 - 3
    rows, width = tokens.shape
    halo_chunks = -(-(LONGEST - 1) // rows)

    def pieces(shard):
        return shard.reshape(2, 2, 2, -1, shard.shape[-1])

    shards = [pieces(hidden_gate), pieces(hidden_up), pieces(hidden_down)]
    ins = (
        table_lengths, table_plots, tokens, cotangent,
        self_gain, cross_gain, hidden_gain, memory,
        cross_key.T, cross_value.T, self_query.T, self_key.T, self_value.T, self_output,
        cross_query.T, cross_output,
    )
    full, saved = forward(n, halo_chunks, ins, shards)
    (
        bias, plots, near, normed_near, self_q, self_k, self_mix, self_logs, first_sum,
        normed_cross, q_all, cross_k, cross_kt, cross_v, cross_mix,
        output, normed_hidden, hidden, gate_back, up_back, second_back, grad_rows, mixed_back,
        cross_stats, gain_hidden,
    ) = saved
    ins = (
        plots, mixed_back, cross_stats, cross_gain,
        normed_hidden, gate_back, up_back, hidden, cotangent, q_all, cross_k, cross_v, cross_kt,
        memory, full[0], full[3], cross_mix, grad_rows, normed_cross, second_back, first_sum,
    )
    hidden_pieces, rest = cross_backward(n, ins, [s.shape[3:] for s in shards])
    gain_cross, grad_memory, part_keys, part_query, first_back, g_first = rest
    ins = (
        self_gain, gain_cross, gain_hidden,
        g_first, self_mix, full[2], normed_near, full[1], self_k, self_q, bias, self_logs, near,
        first_back,
    )
    sums, grad_tokens, gains = self_backward(
        n, extra, halo_chunks, ins, [part_query, part_keys], hidden_pieces
    )

    (
        g_cq, g_co, g_ck, g_cv, g_so, g_sv, g_sk, g_sq, g_gate, g_up, g_down,
        output, grad_tokens, grad_memory, gain_s, gain_c, gain_h,
    ) = results(sums, output, grad_tokens, grad_memory, gains)
    return (
        output, grad_tokens, grad_memory,
        g_sq.T, g_sk.T, g_sv.T, g_so,
        g_cq.T, g_ck.T, g_cv.T, g_co,
        g_gate, g_up, g_down,
        gain_s, gain_c, gain_h,
    )


def solution(mesh):
    in_specs = (
        P(("dp", "tensor"), None),
        P("dp", "tensor", None),
        P("dp", None),
        P("dp", None),
        P(),
        P(None, "tensor"),
        P(None, "tensor"),
        P(None, "tensor"),
        P("tensor", None),
        P(),
        P(None, "tensor"),
        P(None, "tensor"),
        P(None, "tensor"),
        P("tensor", None),
        P(),
        P(None, "tensor"),
        P(None, "tensor"),
        P("tensor", None),
        P(("dp", "tensor"), None),
    )
    out_specs = (
        P(("dp", "tensor"), None),
        P(("dp", "tensor"), None),
        P("dp", "tensor", None),
        P(None, "tensor"),
        P(None, "tensor"),
        P(None, "tensor"),
        P("tensor", None),
        P(None, "tensor"),
        P(None, "tensor"),
        P(None, "tensor"),
        P("tensor", None),
        P(None, "tensor"),
        P(None, "tensor"),
        P("tensor", None),
        P(),
        P(),
        P(),
    )
    return jax.shard_map(body, mesh=mesh, in_specs=in_specs, out_specs=out_specs, check_vma=False)
```

```python
import functools

import jax
import jax.numpy as jnp
from jax import lax
from jax.experimental import pallas as pl
from jax.experimental.pallas import tpu as pltpu
from jax.sharding import PartitionSpec as P

HD = 64
LONGEST = 512
F32 = jnp.float32
BF16 = jnp.bfloat16
MESH = pl.DeviceIdType.MESH
ANY = pl.BlockSpec(memory_space=pl.ANY)
VMEM = pl.BlockSpec(memory_space=pltpu.VMEM)
DMA = pltpu.SemaphoreType.DMA

epsilon = 1e-06
masked_value = -1e30


def product(first_op, second_op, first_dim, second_dim):
    return lax.dot_general(
        first_op,
        second_op,
        (((first_dim,), (second_dim,)), ((), ())),
        preferred_element_type=F32,
    )


def remote(src, dst, send_sem, recv_sem, device):
    return pltpu.make_async_remote_copy(
        src_ref=src,
        dst_ref=dst,
        send_sem=send_sem,
        recv_sem=recv_sem,
        device_id=device,
        device_id_type=MESH,
    )


class Moves:
    def __init__(self, pairs, sems):
        self.copies = [
            pltpu.make_async_copy(src, dst, sems.at[i]) for i, (src, dst) in enumerate(pairs)
        ]

    def start(self, *which):
        for i in which:
            self.copies[i].start()

    def wait(self, *which):
        for i in which:
            self.copies[i].wait()


def held(struct):
    return pltpu.VMEM(struct.shape, struct.dtype)


def place():
    dp = lax.axis_index("dp")
    z = lax.axis_index("tensor")
    return dp, z, lax.rem(dp, 2), lax.rem(dp // 2, 2), lax.rem(dp // 4, 2)


def flipped(dp, bit):
    here = lax.rem(dp // (1 << bit), 2)
    return dp + (1 << bit) * (1 - 2 * here)


def greet(devices):
    barrier = pltpu.get_barrier_semaphore()
    for device in devices:
        pl.semaphore_signal(barrier, inc=1, device_id=device, device_id_type=MESH)
    pl.semaphore_wait(barrier, len(devices))


def greet_line(dp, z, n):
    barrier = pltpu.get_barrier_semaphore()

    @pl.when(z > 0)
    def _():
        pl.semaphore_signal(barrier, inc=1, device_id=(dp, z - 1), device_id_type=MESH)

    @pl.when(z < n - 1)
    def _():
        pl.semaphore_signal(barrier, inc=1, device_id=(dp, z + 1), device_id_type=MESH)

    inner = (z > 0) & (z < n - 1)

    @pl.when(inner)
    def _():
        pl.semaphore_wait(barrier, 2)

    @pl.when(jnp.logical_not(inner))
    def _():
        pl.semaphore_wait(barrier, 1)


class Gather:
    def __init__(self, n, mine, full, sems):
        self.n, self.mine, self.full, self.count = n, mine, full, len(full)
        self.zs, self.zr, self.as_, self.ar, self.bs, self.br, self.cs, self.cr, self.loc = sems
        self.dp, self.z, self.c, self.x, self.y = place()
        z = self.z
        inner = [1 + s // 2 if s % 2 == 0 else n - 1 - s // 2 for s in range(n - 1)]
        self.order = [
            jnp.where(z == 0, n - 1 - s, jnp.where(z == n - 1, 1 + s, inner[s]))
            for s in range(n - 1)
        ]

    def peers(self):
        others = [lax.rem(self.z + k, self.n) for k in range(1, self.n)]
        return [(self.dp, o) for o in others] + [(flipped(self.dp, b), self.z) for b in range(3)]

    def own(self, g):
        return pltpu.make_async_copy(self.mine[g], self.full[g].at[self.z], self.loc.at[g])

    def piece(self, g, k):
        zk = lax.rem(self.z + self.n - k, self.n)
        return self.full[g].at[zk, self.y, self.x, self.c]

    def first(self, g, k):
        src = self.piece(g, 0) if self.mine[g] is None else self.mine[g].at[self.y, self.x, self.c]
        dev = (self.dp, lax.rem(self.z + k, self.n))
        return remote(src, self.piece(g, 0), self.zs.at[g, k - 1], self.zr.at[g, k - 1], dev)

    def passed(self, g, up):
        k = self.n - 2 if up else 2
        dev = (self.dp, lax.rem(self.z + (1 if up else self.n - 1), self.n))
        slot = self.n - 2 if up else 0
        piece = self.piece(g, k)
        return remote(piece, piece, self.zs.at[g, self.n - 1], self.zr.at[g, slot], dev)

    def straight(self, k, start):
        ends = ((self.z == 0) & (k == self.n - 1)) | ((self.z == self.n - 1) & (k == 1))
        pl.when(jnp.logical_not(ends) if self.n > 2 else self.z >= 0)(start)

    def arrived(self, g, k):
        piece = self.piece(g, k)
        dev = (self.dp, lax.rem(self.z + k, self.n))
        return remote(piece, piece, self.zs.at[g, 0], self.zr.at[g, k - 1], dev)

    def second(self, g, s, incoming=False):
        k = self.order[s]
        zk = lax.rem(self.z + self.n - k, self.n)
        x, y, c = self.x, self.y, self.c
        if s % 2 == 1:
            there, bit = self.full[g].at[zk, y, 1 - x if incoming else x, c], 1
        else:
            there, bit = self.full[g].at[zk, 1 - y if incoming else y, x, c], 2
        dev = (flipped(self.dp, bit), self.z)
        return remote(there, there, self.as_.at[g, s], self.ar.at[g, s], dev)

    def third(self, g, s, incoming=False):
        k = self.order[s]
        zk = lax.rem(self.z + self.n - k, self.n)
        x, y, c = self.x, self.y, self.c
        if s % 2 == 1:
            there, bit = self.full[g].at[zk, 1 - y if incoming else y, :, c], 2
        else:
            there, bit = self.full[g].at[zk, :, 1 - x if incoming else x, c], 1
        dev = (flipped(self.dp, bit), self.z)
        return remote(there, there, self.bs.at[g, s], self.br.at[g, s], dev)

    def fourth(self, g, s, incoming=False):
        zk = lax.rem(self.z + self.n - self.order[s], self.n)
        there = self.full[g].at[zk, :, :, 1 - self.c if incoming else self.c]
        dev = (flipped(self.dp, 0), self.z)
        return remote(there, there, self.cs.at[g, s], self.cr.at[g, s], dev)

    def run(self, g, stage):
        n = self.n
        steps = range(n - 1)
        if stage == 0:
            if self.mine[g] is not None:
                self.own(g).start()

            for k in sorted(range(1, n), key=lambda k: min(k, n - k)):
                self.straight(k, lambda k=k: self.first(g, k).start())
        elif stage == 1:
            for s in steps:
                k = self.order[s]
                self.arrived(g, k).wait_recv()
                if n > 2:

                    @pl.when((self.z == n - 2) & (k == n - 2))
                    def _():
                        self.passed(g, True).start()

                    @pl.when((self.z == 1) & (k == 2))
                    def _():
                        self.passed(g, False).start()

                self.second(g, s).start()
        elif stage == 2:
            for s in steps:
                self.second(g, s, True).wait_recv()
                self.third(g, s).start()
        elif stage == 3:
            for s in steps:
                self.third(g, s, True).wait_recv()
                self.fourth(g, s).start()
        else:
            if self.mine[g] is not None:
                self.own(g).wait()
            for s in steps:
                self.fourth(g, s, True).wait_recv()

    def drain(self):
        for g in range(self.count):
            if self.n > 2:

                @pl.when((self.z == self.n - 2) | (self.z == 1))
                def _(g=g):
                    self.passed(g, True).wait_send()

            for s in range(self.n - 1):
                self.straight(s + 1, lambda s=s, g=g: self.first(g, s + 1).wait_send())
                self.second(g, s).wait_send()
                self.third(g, s).wait_send()
                self.fourth(g, s).wait_send()


def gather_sems(n, count):
    return [DMA((count, n))] + [DMA((count, n - 1)) for _ in range(7)] + [DMA((count,))]


class Reduce:
    def __init__(
        self, n, extra, part, acc, rec1, rec2, rec3, rec4, relay, fin, recx, sems, quarters
    ):
        self.relay = relay
        self.n, self.extra, self.count = n, extra, len(rec4)
        self.part, self.fin, self.recx, self.quarters = part, fin, recx, quarters
        self.rec1, self.rec2, self.rec3, self.rec4 = rec1, rec2, rec3, rec4
        self.sems = sems
        self.dp, self.z, self.c, self.x, self.y = place()
        self.ks = range(1, n)
        self.kept = acc
        self.started = []
        self.acc = []
        for g in range(self.count):
            if part[g] is None:
                self.acc.append(None)
            elif acc[g] is None:
                self.acc.append(part[g].at[:, :, :, self.c])
            else:
                self.acc.append(acc[g])

    def peers(self):
        others = [lax.rem(self.z + k, self.n) for k in self.ks]
        bits = range(3 + self.extra)
        return [(self.dp, o) for o in others] + [(flipped(self.dp, b), self.z) for b in bits]

    def at(self, g, slot):
        spans = [slots_of(self.n, p is not None, bool(self.fin)) for p in self.part]
        return sum(high - low for low, high in spans[:g]) + slot - spans[g][0]

    def lanes(self, g, half):
        width = self.rec4[g].shape[-1]
        if width == 128:
            return slice(0, width)
        middle = width // 256 * 128 + (128 if width % 256 and g % 2 == 0 else 0)
        return slice(0, middle) if half == 0 else slice(middle, width)

    def copies(self, stage, g, incoming=False):
        halves = range(1 if self.rec4[g].shape[-1] == 128 else 2)
        dp, z, c, x, y, n = self.dp, self.z, self.c, self.x, self.y, self.n
        acc, fin = self.acc[g], self.fin[g] if self.fin else None
        found = []
        if stage == 0:
            src, dst, dev = self.part[g].at[:, :, :, 1 - c], self.rec1[g], (flipped(dp, 0), z)
            found.append((src, dst, dev, 0))
        elif stage == 1:
            for half in halves:
                at = self.lanes(g, half)
                src = acc.at[:, :, 1 - x, :, at] if half == 0 else acc.at[:, 1 - y, :, :, at]
                dev = (flipped(dp, 1 if half == 0 else 2), z)
                found.append((src, self.rec2[g].at[:, :, :, at], dev, 1 + half))
        elif stage == 2:
            for half in halves:
                at = self.lanes(g, half)
                src = acc.at[:, 1 - y, x, :, at] if half == 0 else acc.at[:, y, 1 - x, :, at]
                dev = (flipped(dp, 2 if half == 0 else 1), z)
                found.append((src, self.rec3[g].at[:, :, at], dev, 3 + half))
        elif stage == 3:
            for k in self.ks:
                zk = lax.rem(z + k, n)
                slot = lax.rem(z + n - k, n) if incoming else z
                found.append((self.quarter(g, zk), self.rec4[g].at[slot], (dp, zk), 8 + k))
        elif stage == 4:
            for half in halves:
                at = self.lanes(g, half)
                if half == 0:
                    src = fin.at[1 - y if incoming else y, x, c, :, at]
                else:
                    src = fin.at[y, 1 - x if incoming else x, c, :, at]
                found.append((src, src, (flipped(dp, 2 if half == 0 else 1), z), 5 + half))
        elif stage == 5:
            for half in halves:
                at = self.lanes(g, half)
                if half == 0:
                    src = fin.at[:, 1 - x if incoming else x, c, :, at]
                else:
                    src = fin.at[1 - y if incoming else y, :, c, :, at]
                found.append((src, src, (flipped(dp, 1 if half == 0 else 2), z), 7 + half))
        else:
            src = fin.at[:, :, 1 - c if incoming else c]
            found.append((src, src, (flipped(dp, 0), z), 8 + n))
        return [
            remote(src, dst, self.sems[0].at[self.at(g, slot)], self.sems[1].at[self.at(g, slot)], dev)
            for src, dst, dev, slot in found
        ]

    def quarter(self, g, zz):
        if self.quarters[g] is not None:
            return self.quarters[g].at[zz]
        return self.acc[g].at[zz, self.y, self.x]

    def own(self, g):
        src = self.part[g].at[:, :, :, self.c]
        return pltpu.make_async_copy(src, self.acc[g], self.sems[4].at[g])

    def further(self, g, e):
        return remote(
            self.fin[g].at[self.y, self.x, self.c],
            self.recx[g].at[e],
            self.sems[2].at[g, e],
            self.sems[3].at[g, e],
            (flipped(self.dp, 3 + e), self.z),
        )

    def add(self, stage, g):
        n, x, y, c, z = self.n, self.x, self.y, self.c, self.z
        acc, fin = self.acc[g], self.fin[g] if self.fin else None
        kind = self.rec4[g].dtype
        if stage == 1:

            def step(i, carry):
                zz, yy, xx = i // 4, lax.rem(i // 2, 2), lax.rem(i, 2)
                total = acc[zz, yy, xx].astype(F32) + self.rec1[g][zz, yy, xx].astype(F32)
                acc[zz, yy, xx] = total.astype(kind)
                return carry

            lax.fori_loop(0, 4 * n, step, 0)
        elif stage == 2:

            def step(i, carry):
                zz, aa = i // 2, lax.rem(i, 2)
                for half in range(1 if self.rec4[g].shape[-1] == 128 else 2):
                    at = self.lanes(g, half)
                    yy, xx = (aa, x) if half == 0 else (y, aa)
                    came = self.rec2[g][zz, aa, :, at].astype(F32)
                    acc[zz, yy, xx, :, at] = (acc[zz, yy, xx, :, at].astype(F32) + came).astype(kind)
                return carry

            lax.fori_loop(0, 2 * n, step, 0)
        elif stage == 3:

            def step(zz, carry):
                total = acc[zz, y, x].astype(F32) + self.rec3[g][zz].astype(F32)
                acc[zz, y, x] = total.astype(kind)
                return carry

            lax.fori_loop(0, n, step, 0)
        else:
            self.rec4[g][z] = self.quarter(g, z)[...]
            total = self.rec4[g][0].astype(F32)
            for k in self.ks:
                total = total + self.rec4[g][k].astype(F32)
            fin[y, x, c] = total.astype(kind)
            for e in range(self.extra):
                self.further(g, e).start()
                self.further(g, e).wait()
                total = fin[y, x, c].astype(F32) + self.recx[g][e].astype(F32)
                fin[y, x, c] = total.astype(kind)

    def to_relay(self, g, up):
        n = self.n
        k, dev = (n - 1, n - 2) if up else (1, 1)
        src = self.quarter(g, n - 1 if up else 0)
        sems = self.sems
        return remote(
            src,
            self.relay[g],
            sems[0].at[self.at(g, 8 + k)],
            sems[1].at[self.at(g, 9 + n)],
            (self.dp, dev),
        )

    def from_relay(self, g, up):
        n = self.n
        k, dev, slot = (1, n - 1, n - 2) if up else (n - 1, 0, 1)
        dst = self.rec4[g].at[slot]
        sems = self.sems
        return remote(
            self.relay[g],
            dst,
            sems[0].at[self.at(g, 8 + k)],
            sems[1].at[self.at(g, 8 + k)],
            (self.dp, dev),
        )

    def relayed(self, g):
        return self.relay[g] is not None

    def begin_line(self, g, act):
        z, n = self.z, self.n
        for k, copy in zip(self.ks, self.copies(3, g)):
            later = (z == 0) & (k == n - 1) | (z == n - 1) & (k == 1)
            later = later | (z == n - 2) & (k == 1) | (z == 1) & (k == n - 1)
            pl.when(jnp.logical_not(later))(functools.partial(act, copy))
        pl.when(z == 0)(lambda: act(self.to_relay(g, True)))
        pl.when(z == n - 1)(lambda: act(self.to_relay(g, False)))

    def pass_on(self, g):
        z, n = self.z, self.n

        def one(up):
            self.to_relay(g, up).wait_recv()
            own = self.quarter(g, n - 1 if up else 0)[...].astype(F32)
            self.relay[g][...] = (self.relay[g][...].astype(F32) + own).astype(BF16)
            self.from_relay(g, up).start()

        pl.when(z == n - 2)(lambda: one(True))
        pl.when(z == 1)(lambda: one(False))

    def end_line(self, g):
        z, n = self.z, self.n
        for k, copy in zip(self.ks, self.copies(3, g, True)):
            never = (z == n - 1) & (k == n - 1) | (z == 0) & (k == 1)
            pl.when(jnp.logical_not(never))(copy.wait_recv)

        @pl.when(z == n - 1)
        def _():
            self.rec4[g][0] = jnp.zeros(self.rec4[g].shape[1:], BF16)

        @pl.when(z == 0)
        def _():
            self.rec4[g][n - 1] = jnp.zeros(self.rec4[g].shape[1:], BF16)

    def begin(self, stage, g):
        if stage == 3 and self.relayed(g):
            self.begin_line(g, lambda copy: copy.start())
        else:
            for copy in self.copies(stage, g):
                copy.start()
        if (stage, g) not in self.started:
            self.started.append((stage, g))

    def end(self, stage, g):
        if stage == 0 and self.kept[g] is not None:
            self.own(g).wait()
        if stage == 3 and self.relayed(g):
            self.end_line(g)
        else:
            for copy in self.copies(stage, g, True):
                copy.wait_recv()
        if stage < 4:
            self.add(stage + 1, g)

    def run(self, g, stage):
        if stage == 0 and self.kept[g] is not None:
            self.own(g).start()
        if stage > 0:
            self.end(stage - 1, g)
        if stage <= 6:
            self.begin(stage, g)

    def drain(self):
        for stage, g in self.started:
            if stage == 3 and self.relayed(g):
                self.begin_line(g, lambda copy: copy.wait_send())
                pl.when(self.z == self.n - 2)(self.from_relay(g, True).wait_send)
                pl.when(self.z == 1)(self.from_relay(g, False).wait_send)
            else:
                for copy in self.copies(stage, g):
                    copy.wait_send()


def slots_of(n, from_start, to_end):
    return (0 if from_start else 5), (10 + n if to_end else 5)


def reduce_scratch(n, extra, shapes, kinds, kept, from_start, relays, to_end):
    count = len(shapes)
    every = list(zip(shapes, kinds))
    spans = [slots_of(n, f, to_end) for f in from_start]
    slots = sum(high - low for low, high in spans)
    used = [s for s, f in zip(every, from_start) if f]
    scratch = [pltpu.VMEM((n, 2, 2) + s, d) for (s, d), k in zip(every, kept) if k]
    scratch += [pltpu.VMEM((n, 2, 2) + s, d) for s, d in used]
    scratch += [pltpu.VMEM((n, 2) + s, d) for s, d in used]
    scratch += [pltpu.VMEM((n,) + s, d) for s, d in used]
    scratch += [pltpu.VMEM((n,) + s, d) for s, d in every]
    if n > 3:
        scratch += [pltpu.VMEM(s, d) for (s, d), r in zip(every, relays) if r]
    if extra:
        scratch += [pltpu.VMEM((extra,) + s, d) for s, d in every]
    scratch += [
        DMA((slots,)),
        DMA((slots,)),
        DMA((count, extra) if extra else (1, 1)),
        DMA((count, extra) if extra else (1, 1)),
        DMA((count,)),
    ]
    return scratch


def take_reduce(n, extra, part, fin, kept, quarters, relays, refs):
    refs = list(refs)
    acc = [refs.pop(0) if k else None for k in kept]
    recs = []
    for _ in range(3):
        recs.append([refs.pop(0) if p is not None else None for p in part])
    recs.append([refs.pop(0) for _ in part])
    recs.append([refs.pop(0) if n > 3 and r else None for r in relays])
    recx = [refs.pop(0) for _ in part] if extra else None
    sems = [refs.pop(0) for _ in range(5)]
    return Reduce(n, extra, part, acc, *recs, fin, recx, sems, quarters), refs


def both_plots(rows, plot_row):
    wide = rows.astype(F32)
    zero = jnp.zeros_like(wide)
    return jnp.concatenate(
        [jnp.where(plot_row == 0, wide, zero), jnp.where(plot_row == 0, zero, wide)], axis=0
    ).astype(BF16)


def own_plot(pair, plot_row):
    half = pair.shape[0] // 2
    return jnp.where(plot_row == 0, pair[:half], pair[half:])


def line_exchange(n, parts, z, dp, refs, compute, merge, finish, hook, before=None):
    own, spread, mine, from_right, from_left, sems = refs
    out_send, out_recv, back_send, back_recv = sems

    def up(j, p, i, start):
        src = own[i].at[p] if start else spread[i].at[j, p]
        return remote(
            src,
            spread[i].at[j, p],
            out_send.at[i, j, p],
            out_recv.at[i, j, p],
            (dp, lax.rem(z + 1, n)),
        )

    def down(j, p, i, start):
        src = own[i].at[p] if start else spread[i].at[j, p]
        return remote(
            src,
            spread[i].at[j, p],
            out_send.at[i, j + 1, p],
            out_recv.at[i, j, p],
            (dp, lax.rem(z + n - 1, n)),
        )

    def back_left(j, p, i):
        return remote(
            mine[i].at[j, p],
            from_right[i].at[j, p],
            back_send.at[i, j, p],
            back_recv.at[i, j, p],
            (dp, lax.rem(z + n - 1, n)),
        )

    def back_right(j, p, i):
        return remote(
            mine[i].at[j, p],
            from_left[i].at[j, p],
            back_send.at[i, j, p],
            back_recv.at[i, j + 1, p],
            (dp, lax.rem(z + 1, n)),
        )

    out_kinds = range(len(own))
    back_kinds = range(len(mine))

    def send_own(p, carry):
        for i in out_kinds:

            @pl.when(z < n - 1)
            def _():
                up(z, p, i, True).start()

            @pl.when(z > 0)
            def _():
                down(z, p, i, True).start()

        return carry

    lax.fori_loop(0, parts, send_own, 0)
    if before is not None:
        before()

    def slot(t, carry):
        def one_part(p, inner):
            low = z - t
            high = z + t

            def one_side(side, done):
                chunk = jnp.where(side == 0, low, high)
                held = jnp.where(side == 0, low >= 0, (high < n) & (t > 0))

                @pl.when((t < n) & held)
                def _():
                    @pl.when(t == 0)
                    def _():
                        for i in out_kinds:
                            spread[i][z, p] = own[i][p]

                    compute(chunk, p)

                    @pl.when((t > 0) & (side == 0) & (z == n - 1))
                    def _():
                        for i in back_kinds:
                            back_left(low, p, i).start()

                    @pl.when((t > 0) & (side == 1) & (z == 0))
                    def _():
                        for i in back_kinds:
                            back_right(high, p, i).start()

                return done

            lax.fori_loop(0, 2, one_side, 0)

            @pl.when((t + 1 < n) & (low - 1 >= 0))
            def _():
                for i in out_kinds:
                    up(low - 1, p, i, False).wait_recv()

                    @pl.when(z < n - 1)
                    def _():
                        up(low - 1, p, i, False).start()

            @pl.when((t + 1 < n) & (high + 1 < n))
            def _():
                for i in out_kinds:
                    down(high + 1, p, i, False).wait_recv()

                    @pl.when(z > 0)
                    def _():
                        down(high + 1, p, i, False).start()

            left_chunk = 2 * (n - 1) - z - t

            @pl.when((t > 0) & (left_chunk >= 0) & (left_chunk < z) & (z < n - 1))
            def _():
                for i in back_kinds:
                    back_left(left_chunk, p, i).wait_recv()
                merge(left_chunk, p, from_right)
                for i in back_kinds:
                    back_left(left_chunk, p, i).start()

            right_chunk = t - z

            @pl.when((t > 0) & (right_chunk < n) & (right_chunk > z) & (z > 0))
            def _():
                for i in back_kinds:
                    back_right(right_chunk, p, i).wait_recv()
                merge(right_chunk, p, from_left)
                for i in back_kinds:
                    back_right(right_chunk, p, i).start()

            return inner

        lax.fori_loop(0, parts, one_part, 0)
        hook(t)
        return carry

    lax.fori_loop(0, 2 * n - 2, slot, 0)

    def last(p, carry):
        @pl.when(z > 0)
        def _():
            for i in back_kinds:
                back_right(z, p, i).wait_recv()
            merge(z, p, from_left)

        @pl.when(z < n - 1)
        def _():
            for i in back_kinds:
                back_left(z, p, i).wait_recv()
            merge(z, p, from_right)

        finish(p)
        return carry

    lax.fori_loop(0, parts, last, 0)

    def drain(p, carry):
        for j in range(n):
            for i in out_kinds:

                @pl.when((z < n - 1) & (z == j))
                def _(i=i, j=j):
                    up(j, p, i, True).wait_send()

                @pl.when((z < n - 1) & (z > j))
                def _(i=i, j=j):
                    up(j, p, i, False).wait_send()

                @pl.when((z > 0) & (z == j))
                def _(i=i, j=j):
                    down(j, p, i, True).wait_send()

                @pl.when((z > 0) & (z < j))
                def _(i=i, j=j):
                    down(j, p, i, False).wait_send()

            for i in back_kinds:

                @pl.when(z > j)
                def _(i=i, j=j):
                    back_left(j, p, i).wait_send()

                @pl.when(z < j)
                def _(i=i, j=j):
                    back_right(j, p, i).wait_send()

        return carry

    return lambda: lax.fori_loop(0, parts, drain, 0)


def line_sems(n, parts, out_kinds, back_kinds):
    return [
        DMA((out_kinds, n + 1, parts)),
        DMA((out_kinds, n, parts)),
        DMA((back_kinds, n, parts)),
        DMA((back_kinds, n + 1, parts)),
    ]


def as_row(ref):
    return ref[...].reshape(1, -1)


def unit_rows(ref, zz, which):
    block = ref[zz, which]
    return block.reshape(-1, block.shape[-1])


def two_units(ref, pair, which):
    return jnp.concatenate(
        [unit_rows(ref, 2 * pair, which), unit_rows(ref, 2 * pair + 1, which)], axis=0
    )


def normed_rows(rows, gain):
    inverse = lax.rsqrt(jnp.mean(rows * rows, axis=-1, keepdims=True) + epsilon)
    return rows * inverse * gain


def half_lanes(first, second, which):
    lane = lax.broadcasted_iota(jnp.int32, first.shape, 1)
    if which == 0:
        return jnp.where(lane < HD, first, pltpu.roll(second, HD, 1))
    return jnp.where(lane < HD, pltpu.roll(first, HD, 1), second)


def tall(out, rows_in, weights, which, n):
    block = 256
    columns = out.shape[1] * 2 // n
    blocks = out.shape[0] // block

    def step(i, carry):
        pair, at = i // blocks, lax.rem(i, blocks)
        at_rows = pl.ds(pl.multiple_of(at * block, block), block)
        cols = pl.ds(pl.multiple_of(pair * columns, columns), columns)
        both = two_units(weights, pair, which)
        out[at_rows, cols] = product(rows_in[at_rows, :], both, 1, 1).astype(BF16)
        return carry

    lax.fori_loop(0, n // 2 * blocks, step, 0)


def flat(out, rows_in, weights, which, n):
    rows_part = out.shape[0] // n

    def step(zz, carry):
        at_part = pl.ds(pl.multiple_of(zz * rows_part, rows_part), rows_part)
        out[at_part, :] = product(unit_rows(weights, zz, which), rows_in[...], 1, 1).astype(BF16)
        return carry

    lax.fori_loop(0, n, step, 0)


def table_at(position, lengths, count):
    table = jnp.zeros(position.shape, jnp.int32)
    end = 0
    for t in range(count):
        end = end + lengths[0, t]
        table = table + (position >= end).astype(jnp.int32)
    return table


KEPT = 23


def forward_kernel(n, count, halo_chunks, *refs):
    (
        lengths, table_plots, tok, cot, self_gain, cross_gain, hidden_gain, mem,
        w_ck, w_cv, w_sq, w_sk, w_sv, w_so, w_cq, w_co,
    ) = refs[:16]
    mine = [None] * 4 + list(refs[16 : 16 + count - 4])
    at = 12 + count
    full_out = refs[at : at + 4]
    at += 4
    out_refs = refs[at : at + 25]
    at += 25
    kept_refs = refs[at : at + KEPT]
    at += KEPT
    (
        bias, plots, near, normed, self_q, self_k, self_mix, self_logs, first_sum, normed_cross,
        q_all, cross_k, cross_kt, cross_v, o_ref,
        output, normed_hidden, hidden, gate_back, up_back, second_back, grad_rows, do_ref, stats,
        gain_hidden,
    ) = kept_refs + out_refs[KEPT:]
    full = refs[at : at + count]
    at += count
    (
        halo, self_vt, cross_vt, cross_q, o_mine, l_mine, o_right, l_right, o_left, l_left,
        down_sum, back_sum, second_sum,
    ) = refs[at : at + 13]
    at += 13
    line = refs[at : at + 4]
    at += 4
    gather_refs = refs[at : at + 9]
    hs, hr, outs, out_sems = refs[at + 9 :]
    leaving = Moves(list(zip(kept_refs, out_refs[:KEPT])), out_sems)
    rows, width = tok.shape
    heads = width // HD
    parts = n
    heads_part = heads // parts
    rows_part = heads_part * HD
    scale = HD ** (-0.5)
    dp, z, c, x, y = place()
    gather = Gather(n, mine, full, gather_refs)
    greet(gather.peers())

    def halo_copy(i):
        src = tok if i == 0 else halo.at[halo_chunks - i]
        dst = halo.at[halo_chunks - 1 - i]
        return remote(src, dst, hs.at[i], hr.at[i], (dp, lax.rem(z + 1, n)))

    def own_units(g, first, second):
        full[g][z, 0] = as_unit(first[...])
        full[g][z, 1] = as_unit(second[...])

    own_units(0, w_ck, w_cv)
    gather.run(0, 0)
    own_units(1, w_sq, w_sk)
    gather.run(1, 0)
    own_units(2, w_sv, w_so)
    own_units(3, w_cq, w_co)
    @pl.when(z < n - 1)
    def _():
        halo_copy(0).start()


    halo[halo_chunks] = tok[...]
    for i in range(halo_chunks):

        @pl.when(z <= i)
        def _(i=i):
            halo[halo_chunks - 1 - i] = jnp.zeros((rows, width), BF16)

    keys = bias.shape[0]
    held_tables = lengths.shape[1]
    first_key = z * rows - halo_chunks * rows
    key_at = lax.broadcasted_iota(jnp.int32, (keys, rows), 0) + first_key
    query_at = lax.broadcasted_iota(jnp.int32, (1, rows), 1) + z * rows
    same = table_at(key_at, lengths, held_tables) == table_at(query_at, lengths, held_tables)
    allowed = same & (key_at <= query_at) & (key_at >= 0)
    bias[...] = jnp.where(allowed, 0.0, masked_value)
    for j in range(n):
        tables = table_at(
            lax.broadcasted_iota(jnp.int32, (1, rows), 1) + j * rows, lengths, held_tables
        )
        plot = jnp.zeros((1, rows), jnp.int32)
        for t in range(held_tables):
            plot = jnp.where(tables == t, table_plots[0, t], plot)
        plots[j] = plot

    gather.run(0, 1)

    gather.run(2, 0)
    gather.run(0, 2)
    gather.run(1, 1)
    gather.run(0, 3)
    gather.run(1, 2)
    gather.run(3, 0)

    def halo_pass(i):
        @pl.when(z > i)
        def _():
            halo_copy(i).wait_recv()

        if i + 1 < halo_chunks:

            @pl.when((z > i) & (z < n - 1))
            def _():
                halo_copy(i + 1).start()

    halo_pass(0)
    gather.run(2, 1)

    def norm_chunk(i, carry):
        at_rows = pl.ds(pl.multiple_of(i * rows, rows), rows)
        near[at_rows, :] = halo[i]
        normed[at_rows, :] = normed_rows(halo[i].astype(F32), as_row(self_gain)).astype(BF16)
        return carry

    gather.run(0, 4)

    plots_held = mem.shape[0]

    def flat_part(which, out):
        def step(zz, carry):
            for p in range(plots_held):
                rows_t = product(unit_rows(full[0], zz, which), mem[p], 1, 1).astype(BF16)
                for hh in range(heads_part):
                    at_head = slice(hh * HD, (hh + 1) * HD)
                    out[zz * heads_part + hh, p * HD : (p + 1) * HD, :] = rows_t[at_head]
            return carry

        lax.fori_loop(0, n, step, 0)

    def tall_part(which, out):
        def step(pair, carry):
            weights = two_units(full[0], pair, which)
            first = product(mem[0], weights, 1, 1)
            second = product(mem[1], weights, 1, 1)
            for hh in range(2 * heads_part):
                cols = slice((hh // 2) * 2 * HD, (hh // 2 + 1) * 2 * HD)
                both = half_lanes(first[:, cols], second[:, cols], hh % 2)
                out[pair * 2 * heads_part + hh] = both.astype(BF16)
            return carry

        lax.fori_loop(0, n // 2, step, 0)

    flat_part(1, cross_vt)
    gather.run(1, 3)
    gather.run(2, 2)
    flat_part(0, cross_kt)
    gather.run(3, 1)
    gather.run(4, 0)
    tall_part(0, cross_k)
    for i in range(1, halo_chunks):
        halo_pass(i)
    gather.run(1, 4)
    gather.run(2, 3)
    gather.run(3, 2)
    lax.fori_loop(0, halo_chunks + 1, norm_chunk, 0)

    own_rows = slice(halo_chunks * rows, (halo_chunks + 1) * rows)

    def query_part(zz, carry):
        at_part = pl.ds(pl.multiple_of(zz * rows_part, rows_part), rows_part)
        projected = product(unit_rows(full[1], zz, 0), normed[own_rows, :], 1, 1)
        self_q[at_part, :] = (projected.astype(BF16).astype(F32) * scale).astype(BF16)
        return carry

    lax.fori_loop(0, n, query_part, 0)

    tall(self_k, normed, full[1], 1, n)
    gather.run(5, 0)
    gather.run(2, 4)

    flat(self_vt, normed, full[2], 0, n)
    gather.run(3, 3)

    def self_pair(pair, carry):
        cols = pl.ds(pl.multiple_of(pair * 2 * HD, 2 * HD), 2 * HD)
        for which in range(2):
            at_head = pl.ds(pl.multiple_of((2 * pair + which) * HD, HD), HD)
            scores = jnp.dot(
                self_k[:, cols], alone(self_q[at_head, :], which), preferred_element_type=F32
            )
            scores = scores + bias[...]
            top = jnp.max(scores, axis=0, keepdims=True)
            powers = jnp.exp(scores - top)
            total = jnp.sum(powers, axis=0, keepdims=True)
            mixed = jnp.dot(self_vt[at_head, :], powers.astype(BF16), preferred_element_type=F32)
            self_mix[at_head, :] = (mixed / total).astype(BF16)
            self_logs[pair, which : which + 1, :] = top + jnp.log(total)
        return carry

    lax.fori_loop(0, heads // 4, self_pair, 0)
    lax.fori_loop(heads // 4, heads // 2, self_pair, 0)

    first_sum[...] = tok[...].astype(F32)

    def first_part(zz, carry):
        at_part = pl.ds(pl.multiple_of(zz * rows_part, rows_part), rows_part)
        first_sum[...] += product(self_mix[at_part, :], unit_rows(full[2], zz, 1), 0, 0)
        return carry

    lax.fori_loop(0, n, first_part, 0)
    total = first_sum[...]
    normed_cross[...] = normed_rows(total, as_row(cross_gain)).astype(BF16)
    gather.run(3, 4)

    def cross_query_part(zz, carry):
        projected = product(unit_rows(full[3], zz, 0), normed_cross[...], 1, 1)
        cross_q[zz] = (projected.astype(BF16).astype(F32) * scale).astype(BF16)
        return carry

    lax.fori_loop(0, n, cross_query_part, 0)

    def compute(j, p):
        plot_row = plots[j]
        for hh in range(heads_part):
            h = p * heads_part + hh
            q_pair = both_plots(q_all[j, p, hh * HD : (hh + 1) * HD, :], plot_row)
            scores = jnp.dot(cross_k[h], q_pair, preferred_element_type=F32)
            top = jnp.max(scores, axis=0, keepdims=True)
            powers = jnp.exp(scores - top)
            total = jnp.sum(powers, axis=0, keepdims=True)
            mixed = jnp.dot(cross_vt[h], powers.astype(BF16), preferred_element_type=F32)
            mixed = own_plot(mixed, plot_row) / total
            o_mine[j, p, hh * HD : (hh + 1) * HD, :] = mixed.astype(BF16)
            l_mine[j, p, hh : hh + 1, :] = top + jnp.log(total)

    def merge(j, p, arrived):
        for hh in range(heads_part):
            at_head = slice(hh * HD, (hh + 1) * HD)
            log_a = l_mine[j, p, hh : hh + 1, :]
            log_b = arrived[1][j, p, hh : hh + 1, :]
            top = jnp.maximum(log_a, log_b)
            share_a = jnp.exp(log_a - top)
            share_b = jnp.exp(log_b - top)
            total = share_a + share_b
            mixed = o_mine[j, p, at_head, :].astype(F32) * (share_a / total)
            mixed = mixed + arrived[0][j, p, at_head, :].astype(F32) * (share_b / total)
            o_mine[j, p, at_head, :] = mixed.astype(BF16)
            l_mine[j, p, hh : hh + 1, :] = top + jnp.log(total)

    def finish(p):
        o_ref[p] = o_mine[z, p]

    def keep(g):
        return pltpu.make_async_copy(full[g], full_out[g], outs.at[g])

    schedule = {
        0: [(4, 1)],
        1: [(6, 0), (4, 2), (5, 1)],
        2: [(4, 3), (5, 2)],
        3: [(6, 1)],
        4: [(6, 2), (5, 3)],
        5: [(6, 3)],
    }

    def hook(t):
        for step, work in schedule.items():

            @pl.when(t == step)
            def _(step=step, work=work):
                if step == 0:
                    tall_part(1, cross_v)
                for g, stage in work:
                    gather.run(g, stage)
                if step == 0:
                    for g in range(4):
                        keep(g).start()

        @pl.when(t == 2 * n - 3)
        def _():
            leaving.start(*range(14))

    exchange = ([cross_q], [q_all], [o_mine, l_mine], [o_right, l_right], [o_left, l_left], line)
    end_exchange = line_exchange(n, parts, z, dp, exchange, compute, merge, finish, hook)

    second_sum[...] = first_sum[...]

    def second_part(zz, carry):
        second_sum[...] += product(o_ref[zz], unit_rows(full[3], zz, 1), 0, 0)
        return carry

    lax.fori_loop(0, n, second_part, 0)
    total = second_sum[...]
    normed_hidden[...] = normed_rows(total, as_row(hidden_gain)).astype(BF16)
    leaving.start(14, 16)
    down_sum[...] = jnp.zeros((rows, width), F32)
    back_sum[...] = jnp.zeros((rows, width), F32)
    for g in range(4, 7):
        gather.run(g, 4)
    slope = (2.0 / 3.141592653589793) ** 0.5
    bend = 0.044715

    def whole(g, zz):
        block = full[g][zz]
        return block.reshape(-1, block.shape[-1])

    def hidden_part(zz, carry):
        gate = product(normed_hidden[...], whole(4, zz), 1, 0)
        up = product(normed_hidden[...], whole(5, zz), 1, 0)
        act_back = product(cot[...], whole(6, zz), 1, 1).astype(BF16).astype(F32)
        square = gate * gate
        curve = jnp.tanh(slope * (gate + bend * square * gate))
        cdf = 0.5 * (1.0 + curve)
        act = gate * cdf
        turn = cdf + 0.5 * gate * (1.0 - curve * curve) * slope * (1.0 + 3.0 * bend * square)
        here = (act * up).astype(BF16)
        to_gate = (act_back * up * turn).astype(BF16)
        to_up = (act_back * act).astype(BF16)
        hidden[zz] = here
        gate_back[zz] = to_gate
        up_back[zz] = to_up
        down_sum[...] += product(here, whole(6, zz), 1, 0)
        back_sum[...] += product(to_gate, whole(4, zz), 1, 1) + product(to_up, whole(5, zz), 1, 1)
        return carry

    lax.fori_loop(0, n, hidden_part, 0)
    leaving.start(17, 18, 19)
    output[...] = (second_sum[...] + down_sum[...]).astype(BF16)
    leaving.start(15)
    residual, gain_back = norm_gradient(second_sum[...], as_row(hidden_gain), back_sum[...])
    gain_hidden[...] = gain_back
    total = cot[...].astype(F32) + residual
    second_back[...] = total
    grad_rows[...] = total.astype(BF16)
    leaving.start(20, 21)

    def mixed_part(zz, carry):
        mixed = product(unit_rows(full[3], zz, 1), grad_rows[...], 1, 1).astype(BF16)
        do_ref[zz] = mixed
        for hh in range(heads_part):
            at_head = slice(hh * HD, (hh + 1) * HD)
            inner = mixed[at_head].astype(F32) * o_ref[zz, at_head, :].astype(F32)
            row = heads_part + hh
            stats[zz, row : row + 1, :] = jnp.sum(inner, axis=0, keepdims=True)
            stats[zz, hh : hh + 1, :] = l_mine[z, zz, hh : hh + 1, :]
        stats[zz, 2 * heads_part : 8, :] = jnp.zeros((8 - 2 * heads_part, rows), F32)
        return carry

    lax.fori_loop(0, n, mixed_part, 0)
    leaving.start(22)
    end_exchange()
    gather.drain()
    leaving.wait(*range(KEPT))
    for g in range(4):
        keep(g).wait()
    for i in range(halo_chunks):

        @pl.when((z >= i) & (z < n - 1))
        def _(i=i):
            halo_copy(i).wait_send()


def forward(n, halo_chunks, ins, shards):
    tokens, memory = ins[2], ins[7]
    rows, width = tokens.shape
    keys = (halo_chunks + 1) * rows
    heads = width // HD
    parts = n
    rows_part = width // parts
    held_plots, patches, _ = memory.shape
    unit = rows_part // 4
    full = [(n, 2, 2, 2, unit, width)] * 4 + [(n,) + s.shape for s in shards]
    count = len(full)
    struct = jax.ShapeDtypeStruct
    out_shape = [struct(f, BF16) for f in full[:4]] + [
        struct((keys, rows), F32),
        struct((n, 1, rows), jnp.int32),
        struct((keys, width), BF16),
        struct((keys, width), BF16),
        struct((width, rows), BF16),
        struct((keys, width), BF16),
        struct((width, rows), BF16),
        struct((heads // 2, 8, rows), F32),
        struct((rows, width), F32),
        struct((rows, width), BF16),
        struct((n, parts, rows_part, rows), BF16),
        struct((heads, patches, held_plots * HD), BF16),
        struct((heads, held_plots * HD, patches), BF16),
        struct((heads, patches, held_plots * HD), BF16),
        struct((parts, rows_part, rows), BF16),
        struct((rows, width), BF16),
        struct((rows, width), BF16),
        struct((n, rows, shards[0].shape[-1]), BF16),
        struct((n, rows, shards[0].shape[-1]), BF16),
        struct((n, rows, shards[0].shape[-1]), BF16),
        struct((rows, width), F32),
        struct((rows, width), BF16),
        struct((parts, rows_part, rows), BF16),
        struct((parts, 8, rows), F32),
        struct((1, width), F32),
    ]
    scratch = [held(o) for o in out_shape[4 : 4 + KEPT]]
    scratch += [pltpu.VMEM(f, BF16) for f in full]
    scratch += [
        pltpu.VMEM((halo_chunks + 1, rows, width), BF16),
        pltpu.VMEM((width, keys), BF16),
        pltpu.VMEM((heads, held_plots * HD, patches), BF16),
        pltpu.VMEM((parts, rows_part, rows), BF16),
    ]
    for _ in range(3):
        scratch += [
            pltpu.VMEM((n, parts, rows_part, rows), BF16),
            pltpu.VMEM((n, parts, 8, rows), F32),
        ]
    scratch += [pltpu.VMEM((rows, width), F32)] * 3
    scratch += line_sems(n, parts, 1, 2)
    scratch += gather_sems(n, count)
    scratch += [DMA((halo_chunks,)), DMA((halo_chunks,)), DMA((4,)), DMA((KEPT,))]
    smem = pl.BlockSpec(memory_space=pltpu.SMEM)
    out = pl.pallas_call(
        functools.partial(forward_kernel, n, count, halo_chunks),
        out_shape=out_shape,
        in_specs=[smem] * 2 + [VMEM] * 14 + [ANY] * (count - 4),
        out_specs=[ANY] * (4 + KEPT) + [VMEM] * (25 - KEPT),
        scratch_shapes=scratch,
        compiler_params=pltpu.CompilerParams(
            collective_id=0, has_side_effects=True, vmem_limit_bytes=63 << 20
        ),
        name="forward",
    )(*ins, *shards)
    return out[:4], out[4:]


def norm_gradient(rows, gain, back):
    inverse = lax.rsqrt(jnp.mean(rows * rows, axis=-1, keepdims=True) + epsilon)
    unit = rows * inverse
    scaled = back * gain
    inner = jnp.mean(scaled * unit, axis=-1, keepdims=True)
    return inverse * (scaled - unit * inner), jnp.sum(back * unit, axis=0, keepdims=True)


def as_unit(rows_192):
    rows, width = rows_192.shape
    return rows_192.reshape(2, 2, rows // 4, width)


def cross_backward_kernel(n, count, *refs):
    plots, do_ref, st_ref, cross_gain = refs[:4]
    late, at = refs[4:21], 21
    quarters = refs[at : at + count]
    gain_cross, out_refs = refs[at + count], refs[at + count + 1 : at + count + 6]
    rest = refs[at + count + 6 :]
    part, rest = rest[:count], rest[count:]
    none = [False] * count
    reduce, rest = take_reduce(n, 0, part, None, none, [None] * count, none, rest)
    do_all, st_all, q_mine, q_right, q_left, dk_ref, dv_ref, k_back, v_back = rest[:9]
    line = rest[9:13]
    inside, load_sems = rest[13:30], rest[30]
    kept_refs, out_sems = rest[31:36], rest[36]
    grad_mem, part_keys, part_query, first_back, g_first = kept_refs
    leaving = Moves(list(zip(kept_refs, out_refs)), out_sems)
    (
        normed_hidden, gate_back, up_back, hidden, cot, q_all, k_ref, v_ref, kt_ref,
        mem, w_keys, w_query, cross_mix, grad_rows, normed_cross, second_back, first_sum,
    ) = inside
    loads = Moves(list(zip(late, inside)), load_sems)
    loads.start(*range(17))
    dp, z, c, x, y = place()
    parts, rows_part, rows = do_ref.shape
    width = parts * rows_part
    heads_part = rows_part // HD
    heads = parts * heads_part
    held_plots = mem.shape[0]
    scale = HD ** (-0.5)
    greet(reduce.peers())

    def clear(h, carry):
        dk_ref[h] = jnp.zeros(dk_ref.shape[1:], F32)
        dv_ref[h] = jnp.zeros(dv_ref.shape[1:], F32)
        return carry

    def compute(j, p):
        plot_row = plots[j]
        for hh in range(heads_part):
            h = p * heads_part + hh
            at_head = slice(hh * HD, (hh + 1) * HD)
            q_pair = both_plots(q_all[j, p, at_head, :], plot_row)
            do_pair = both_plots(do_all[j, p, at_head, :], plot_row)
            scores = jnp.dot(k_ref[h], q_pair, preferred_element_type=F32)
            chances = jnp.exp(scores - st_all[j, p, hh : hh + 1, :])
            prob_back = jnp.dot(v_ref[h], do_pair, preferred_element_type=F32)
            inner = st_all[j, p, heads_part + hh : heads_part + hh + 1, :]
            score_back = (chances * (prob_back - inner)).astype(BF16)
            q_back = jnp.dot(kt_ref[h], score_back, preferred_element_type=F32)
            q_mine[j, p, at_head, :] = (own_plot(q_back, plot_row) * scale).astype(BF16)
            dk_ref[h] += product(score_back, q_pair, 1, 1)
            dv_ref[h] += product(chances.astype(BF16), do_pair, 1, 1)

    def merge(j, p, arrived):
        total = q_mine[j, p].astype(F32) + arrived[0][j, p].astype(F32)
        q_mine[j, p] = total.astype(BF16)

    def finish(p):
        pass

    def hidden_gradients():
        firsts = (normed_hidden, normed_hidden, None)
        for g, seconds in enumerate((gate_back, up_back, None)):

            def step(zz, carry, g=g, seconds=seconds):
                if seconds is None:
                    grad = product(hidden[zz], cot[...], 0, 0)
                else:
                    grad = product(firsts[g][...], seconds[zz], 0, 0)
                part[g][zz] = grad.astype(BF16).reshape(part[g].shape[1:])
                return carry

            loads.wait(*((0, 1), (2,), (3, 4))[g])
            lax.fori_loop(0, n, step, 0)
            reduce.run(g, 0)

        loads.wait(5, 6, 7, 8)

    def patch_gradients():
        for source, out in ((dk_ref, k_back), (dv_ref, v_back)):

            def pair_step(i, carry, source=source, out=out):
                even, odd = source[2 * i], source[2 * i + 1]
                lane = lax.broadcasted_iota(jnp.int32, even.shape, 1)
                cols = pl.ds(pl.multiple_of(i * 2 * HD, 2 * HD), 2 * HD)
                out[0, :, cols] = jnp.where(lane < HD, even, pltpu.roll(odd, HD, 1)).astype(BF16)
                out[1, :, cols] = jnp.where(lane < HD, pltpu.roll(even, HD, 1), odd).astype(BF16)
                return carry

            lax.fori_loop(0, heads // 2, pair_step, 0)
        for which, back in enumerate((k_back, v_back)):

            def grad_step(pair, carry, which=which, back=back):
                wide = 2 * rows_part
                cols = pl.ds(pl.multiple_of(pair * wide, wide), wide)
                grad = sum(product(back[p, :, cols], mem[p], 0, 0) for p in range(held_plots))
                grad = grad.astype(BF16)
                part_keys[2 * pair, which] = as_unit(grad[:rows_part])
                part_keys[2 * pair + 1, which] = as_unit(grad[rows_part:])
                return carry

            lax.fori_loop(0, n // 2, grad_step, 0)

        def memory_step(i, carry):
            p, at_rows = i // 2, pl.ds(pl.multiple_of(lax.rem(i, 2) * rows, rows), rows)
            total = 0.0
            for which, back in enumerate((k_back, v_back)):
                for pair in range(n // 2):
                    cols = slice(pair * 2 * rows_part, (pair + 1) * 2 * rows_part)
                    weights = two_units(w_keys, pair, which)
                    total = total + product(back[p, at_rows, cols], weights, 1, 0)
            grad_mem[p, at_rows, :] = total.astype(BF16)
            return carry

        lax.fori_loop(0, held_plots * (mem.shape[1] // rows), memory_step, 0)

    def hook(t):
        for step, work in schedule.items():

            @pl.when(t == step)
            def _(work=work):
                for g, stage in work:
                    reduce.run(g, stage)

        @pl.when(t == n - 1)
        def _():
            loads.wait(9, 10)
            patch_gradients()
            leaving.start(0, 1)
            for g in range(count):
                reduce.run(g, 2)

    schedule = {0: [(0, 1), (1, 1), (2, 1)]}

    def before():
        lax.fori_loop(0, heads, clear, 0)
        hidden_gradients()

    exchange = ([do_ref, st_ref], [do_all, st_all], [q_mine], [q_right], [q_left], line)
    end_exchange = line_exchange(n, parts, z, dp, exchange, compute, merge, finish, hook, before)

    loads.wait(*range(11, 17))
    first_back[...] = jnp.zeros(first_back.shape, F32)

    def query_part(zz, carry):
        mine = q_mine[z, zz]
        part_query[zz, 0] = as_unit(product(mine, normed_cross[...], 1, 0).astype(BF16))
        part_query[zz, 1] = as_unit(product(cross_mix[zz], grad_rows[...], 1, 0).astype(BF16))
        first_back[...] += product(mine, unit_rows(w_query, zz, 0), 0, 0)
        return carry

    lax.fori_loop(0, n, query_part, 0)
    leaving.start(2)
    residual, gain_back = norm_gradient(first_sum[...], as_row(cross_gain), first_back[...])
    total = second_back[...] + residual
    first_back[...] = total
    g_first[...] = total.astype(BF16)
    leaving.start(3, 4)
    gain_cross[...] = gain_back
    for g in range(count):
        reduce.end(2, g)
        quarters[g][...] = reduce.acc[g][:, y, x]
    end_exchange()
    reduce.drain()
    leaving.wait(*range(5))


def cross_backward(n, ins, shapes):
    do, mem = ins[1], ins[13]
    parts, rows_part, rows = do.shape
    width = parts * rows_part
    heads = width // HD
    held_plots, patches, _ = mem.shape
    count = len(shapes)
    struct = jax.ShapeDtypeStruct
    unit = width // n // 4
    scratch = [pltpu.VMEM((n, 2, 2, 2) + s, BF16) for s in shapes]
    none = [False] * count
    scratch += reduce_scratch(n, 0, shapes, [BF16] * count, none, [True] * count, none, False)
    scratch += [
        pltpu.VMEM((n, parts, rows_part, rows), BF16),
        pltpu.VMEM((n, parts, 8, rows), F32),
        pltpu.VMEM((n, parts, rows_part, rows), BF16),
        pltpu.VMEM((n, parts, rows_part, rows), BF16),
        pltpu.VMEM((n, parts, rows_part, rows), BF16),
        pltpu.VMEM((heads, patches, held_plots * HD), F32),
        pltpu.VMEM((heads, patches, held_plots * HD), F32),
        pltpu.VMEM((held_plots, patches, width), BF16),
        pltpu.VMEM((held_plots, patches, width), BF16),
    ]
    scratch += line_sems(n, parts, 2, 1)
    scratch += [held(i) for i in ins[4:]] + [DMA((len(ins) - 4,))]
    kept = [
        struct(mem.shape, BF16),
        struct((n, 2, 2, 2, unit, width), BF16),
        struct((n, 2, 2, 2, unit, width), BF16),
        struct((rows, width), F32),
        struct((rows, width), BF16),
    ]
    scratch += [held(k) for k in kept] + [DMA((len(kept),))]
    out = pl.pallas_call(
        functools.partial(cross_backward_kernel, n, count),
        out_shape=[struct((n,) + s, BF16) for s in shapes] + [struct((1, width), F32)] + kept,
        in_specs=[VMEM] * 4 + [ANY] * 17,
        out_specs=[VMEM] * (count + 1) + [ANY] * 5,
        scratch_shapes=scratch,
        compiler_params=pltpu.CompilerParams(
            collective_id=1, has_side_effects=True, vmem_limit_bytes=63 << 20
        ),
        name="cross_backward",
    )(*ins)
    return out[:count], out[count:]


def alone(rows, which):
    zero = jnp.zeros_like(rows)
    return jnp.concatenate([rows, zero] if which == 0 else [zero, rows], axis=0)


RELAYED = [True] * 3 + [False] * 3 + [True] * 3 + [False]


def self_backward_kernel(n, extra, halo_chunks, *refs):
    self_gain, gain_cross, gain_hidden = refs[:3]
    late = refs[3:14]
    cross_parts = refs[14:16]
    sums = refs[16:19]
    fin_out = refs[19:28]
    grad_tokens, gain_out = refs[28:30]
    own_parts = refs[30:34]
    gain_part, gain_fin = refs[34:36]
    part = list(cross_parts) + list(own_parts) + [None] * 3 + [gain_part]
    kept = [True, True] + [False] * 8
    quarters = [None] * 6 + list(sums) + [None]
    fin = list(refs[-10:-1]) + [gain_fin]
    reduce, rest = take_reduce(n, extra, part, fin, kept, quarters, RELAYED, refs[36:])
    do_ref, dq_ref, dk_ref, dv_ref, own_back, csend, crecv, hs, hr = rest[:9]
    inside, load_sems, v_ref, kt_ref = rest[9:20], rest[20], rest[21], rest[22]
    leaving = Moves(list(zip(fin[:9], fin_out)), rest[33])
    gain_self = rest[23]
    g_first, mix, w_vo, normed, w_qk, k_ref, q_ref, bias, logs, near, first_back = inside
    loads = Moves(list(zip(late, inside)), load_sems)
    loads.start(*range(11))
    dp, z, c, x, y = place()
    rows, width = g_first.shape
    heads = width // HD
    rows_part = width // n
    scale = HD ** (-0.5)
    own_rows = slice(halo_chunks * rows, (halo_chunks + 1) * rows)
    early_groups, late_groups, hidden_groups = (0, 1, 2), (3, 4, 5), (6, 7, 8)
    half = width // 2

    def store_unit(out, zz, grad):
        for cc in range(2):
            columns = grad[:, cc * half : (cc + 1) * half]
            out[zz, :, :, cc] = columns.reshape(2, 2, rows_part // 4, half)

    def all_run(groups, stage):
        for g in groups:
            reduce.run(g, stage)

    greet(reduce.peers())
    all_run((0, 1), 0)
    for g in hidden_groups:
        reduce.begin(3, g)
    loads.wait(0, 1)
    def output_part(zz, carry):
        at_part = pl.ds(pl.multiple_of(zz * rows_part, rows_part), rows_part)
        store_unit(own_parts[0], zz, product(mix[at_part, :], g_first[...], 1, 0).astype(BF16))
        return carry

    lax.fori_loop(0, n, output_part, 0)
    reduce.run(2, 0)
    loads.wait(2)

    def do_part(zz, carry):
        at_part = pl.ds(pl.multiple_of(zz * rows_part, rows_part), rows_part)
        do_ref[at_part, :] = product(unit_rows(w_vo, zz, 1), g_first[...], 1, 1).astype(BF16)
        return carry

    lax.fori_loop(0, n, do_part, 0)
    all_run(early_groups, 1)
    loads.wait(3, 4)
    tall(v_ref, normed, w_vo, 0, n)
    flat(kt_ref, normed, w_qk, 1, n)

    def pair_step(pair, carry):
        cols = pl.ds(pl.multiple_of(pair * 2 * HD, 2 * HD), 2 * HD)
        dk, dv = 0.0, 0.0
        for which in range(2):
            at_head = pl.ds(pl.multiple_of((2 * pair + which) * HD, HD), HD)
            q_pair = alone(q_ref[at_head, :], which)
            do_head = do_ref[at_head, :]
            inner = jnp.sum(
                do_head.astype(F32) * mix[at_head, :].astype(F32), axis=0, keepdims=True
            )
            do_pair = alone(do_head, which)
            scores = jnp.dot(k_ref[:, cols], q_pair, preferred_element_type=F32)
            chances = jnp.exp(scores + bias[...] - logs[pair, which : which + 1, :])
            prob_back = jnp.dot(v_ref[:, cols], do_pair, preferred_element_type=F32)
            score_back = (chances * (prob_back - inner)).astype(BF16)
            q_back = jnp.dot(kt_ref[at_head, :], score_back, preferred_element_type=F32)
            dq_ref[at_head, :] = (q_back * scale).astype(BF16)
            dk = dk + product(score_back, q_pair, 1, 1)
            dv = dv + product(chances.astype(BF16), do_pair, 1, 1)
        dk_ref[:, cols] = dk.astype(BF16)
        dv_ref[:, cols] = dv.astype(BF16)
        return carry

    loads.wait(5, 6, 7, 8)
    lax.fori_loop(0, heads // 2, pair_step, 0)
    for g, back in ((3, dv_ref), (4, dk_ref)):

        def grad_step(pair, carry, g=g, back=back):
            cols = pl.ds(pl.multiple_of(pair * 2 * rows_part, 2 * rows_part), 2 * rows_part)
            grad = product(back[:, cols], normed[...], 0, 0).astype(BF16)
            store_unit(own_parts[g - 2], 2 * pair, grad[:rows_part])
            store_unit(own_parts[g - 2], 2 * pair + 1, grad[rows_part:])
            return carry

        lax.fori_loop(0, n // 2, grad_step, 0)
        reduce.run(g, 0)

    def query_part(zz, carry):
        at_part = pl.ds(pl.multiple_of(zz * rows_part, rows_part), rows_part)
        grad = product(dq_ref[at_part, :], normed[own_rows, :], 1, 0)
        store_unit(own_parts[3], zz, grad.astype(BF16))
        return carry

    lax.fori_loop(0, n, query_part, 0)
    reduce.run(5, 0)
    all_run(early_groups, 2)
    all_run(late_groups, 1)
    for g in hidden_groups:
        reduce.pass_on(g)
    loads.wait(9, 10)

    def halo_copy(i):
        dev = (dp, lax.rem(z + n - 1, n))
        return remote(csend.at[i], crecv.at[i], hs.at[i], hr.at[i], dev)

    def halo_send(i):
        if i > 0:
            halo_take(i - 1, csend.at[i])

        @pl.when(z >= halo_chunks - i)
        def _():
            halo_copy(i).start()

    def halo_take(i, onto):
        @pl.when((z + 1 < n) & (z + 1 >= halo_chunks - i))
        def _():
            halo_copy(i).wait_recv()
            onto[...] = (onto[...].astype(F32) + crecv[i].astype(F32)).astype(onto.dtype)

    def unit_of(at_rows):
        here = near[at_rows, :].astype(F32)
        return here * lax.rsqrt(jnp.mean(here * here, axis=-1, keepdims=True) + epsilon)

    gain_self[...] = jnp.zeros((1, width), F32)

    def near_chunk(i, carry):
        at_rows = pl.ds(pl.multiple_of(i * rows, rows), rows)
        back = 0.0
        for pair in range(n // 2):
            cols = slice(pair * 2 * rows_part, (pair + 1) * 2 * rows_part)
            back = back + product(dk_ref[at_rows, cols], two_units(w_qk, pair, 1), 1, 0)
            back = back + product(dv_ref[at_rows, cols], two_units(w_vo, pair, 0), 1, 0)

        @pl.when(i < halo_chunks)
        def _():
            csend[i] = back.astype(BF16)
            gain_self[...] += jnp.sum(back * unit_of(at_rows), axis=0, keepdims=True)

        @pl.when(i == 0)
        def _():
            halo_send(0)

        @pl.when(i == halo_chunks)
        def _():
            own_back[...] = back

        return carry

    lax.fori_loop(0, halo_chunks + 1, near_chunk, 0)

    def own_part(zz, carry):
        at_part = pl.ds(pl.multiple_of(zz * rows_part, rows_part), rows_part)
        own_back[...] += product(dq_ref[at_part, :], unit_rows(w_qk, zz, 0), 0, 0)
        return carry

    lax.fori_loop(0, n, own_part, 0)
    gain_self[...] += jnp.sum(own_back[...] * unit_of(own_rows), axis=0, keepdims=True)

    deep, lanes = gain_part.shape[4:]
    gain_part[...] = jnp.zeros(gain_part.shape, F32)
    for i, gain in enumerate((gain_self[...], gain_cross[...], gain_hidden[...])):
        for j in range(width // lanes):
            piece, row = divmod(i * (width // lanes) + j, deep)
            for zz in range(n):
                gain_part[zz, piece // 4, piece // 2 % 2, piece % 2, row : row + 1, :] = gain[
                    :, j * lanes : (j + 1) * lanes
                ]

    reduce.run(9, 0)
    all_run(early_groups, 3)
    reduce.run(9, 1)
    all_run(late_groups, 2)
    reduce.run(9, 2)
    for g in early_groups:
        reduce.pass_on(g)
    all_run(late_groups, 3)
    reduce.run(9, 3)
    all_run(hidden_groups, 4)
    for i in range(1, halo_chunks):
        halo_send(i)
    all_run(hidden_groups, 5)
    all_run(early_groups, 4)
    all_run(late_groups + (9,), 4)
    all_run(hidden_groups, 6)
    all_run(early_groups, 5)
    all_run(late_groups + (9,), 5)
    all_run(hidden_groups, 7)
    leaving.start(*hidden_groups)
    all_run(early_groups, 6)
    all_run(late_groups + (9,), 6)
    halo_take(halo_chunks - 1, own_back)
    here = near[own_rows, :].astype(F32)
    residual, _ = norm_gradient(here, as_row(self_gain), own_back[...])
    grad_tokens[...] = (first_back[...] + residual).astype(BF16)
    all_run(early_groups, 7)
    leaving.start(*early_groups)
    all_run(late_groups + (9,), 7)
    leaving.start(*late_groups)
    for i in range(3):
        for j in range(width // lanes):
            piece, row = divmod(i * (width // lanes) + j, deep)
            found = gain_fin[piece // 4, piece // 2 % 2, piece % 2, row : row + 1, :]
            gain_out[i : i + 1, j * lanes : (j + 1) * lanes] = found
    gain_out[3:8, :] = jnp.zeros((5, width), F32)
    for i in range(halo_chunks):

        @pl.when(z >= halo_chunks - i)
        def _(i=i):
            halo_copy(i).wait_send()

    reduce.drain()
    leaving.wait(*range(9))


def self_backward(n, extra, halo_chunks, ins, cross_parts, sums):
    near, g_first = ins[12], ins[3]
    rows, width = g_first.shape
    keys = near.shape[0]
    unit = width // n // 4
    gain_shape = (8, 128)
    single = (unit, width // 2)
    shapes = [(unit, width)] * 2 + [single] * 4 + [p.shape[1:] for p in sums]
    struct = jax.ShapeDtypeStruct
    scratch = [pltpu.VMEM((n, 2, 2, 2) + single, BF16)] * 4
    scratch += [pltpu.VMEM((n, 2, 2, 2) + gain_shape, F32), pltpu.VMEM((2, 2, 2) + gain_shape, F32)]
    scratch += reduce_scratch(
        n, extra, shapes + [gain_shape], [BF16] * 9 + [F32],
        [True, True] + [False] * 8, [True] * 6 + [False] * 3 + [True], RELAYED, True,
    )
    scratch += [
        pltpu.VMEM((width, rows), BF16),
        pltpu.VMEM((width, rows), BF16),
        pltpu.VMEM((keys, width), BF16),
        pltpu.VMEM((keys, width), BF16),
        pltpu.VMEM((rows, width), F32),
        pltpu.VMEM((halo_chunks, rows, width), BF16),
        pltpu.VMEM((halo_chunks, rows, width), BF16),
        DMA((halo_chunks,)),
        DMA((halo_chunks,)),
    ]
    scratch += [held(i) for i in ins[3:]] + [DMA((len(ins) - 3,))]
    scratch += [pltpu.VMEM((keys, width), BF16), pltpu.VMEM((width, keys), BF16)]
    scratch += [pltpu.VMEM((1, width), F32)]
    scratch += [pltpu.VMEM((2, 2, 2) + s, BF16) for s in shapes] + [DMA((len(shapes),))]
    out = pl.pallas_call(
        functools.partial(self_backward_kernel, n, extra, halo_chunks),
        out_shape=[struct((2, 2, 2) + s, BF16) for s in shapes]
        + [struct((rows, width), BF16), struct((8, width), F32)],
        in_specs=[VMEM] * 3 + [ANY] * 13 + [VMEM] * 3,
        out_specs=[ANY] * 9 + [VMEM] * 2,
        scratch_shapes=scratch,
        compiler_params=pltpu.CompilerParams(
            collective_id=2, has_side_effects=True, vmem_limit_bytes=63 << 20
        ),
        name="self_backward",
    )(*ins, *cross_parts, *sums)
    return out[:9], out[9], out[10]


def results_kernel(*refs):
    ins, gains, outs = refs[:12], refs[12], refs[13:]
    at = 0
    for g in range(2):
        for u in range(2):
            outs[at][...] = ins[g][u, 0, 0].astype(F32)
            at += 1
    for g in range(2, 6):
        half = ins[g].shape[-1]
        for cc in range(2):
            outs[at][:, cc * half : (cc + 1) * half] = ins[g][0, 0, cc].astype(F32)
        at += 1
    for g in range(6, 9):
        block = ins[g][0, 0]
        outs[at][...] = block.reshape(-1, block.shape[-1]).astype(F32)
        at += 1
    for i in range(9, 12):
        outs[at][...] = ins[i][...]
        at += 1
    for i in range(3):
        outs[at][...] = gains[i, :]
        at += 1


def results(sums, output, grad_tokens, grad_memory, gains):
    struct = jax.ShapeDtypeStruct
    steps = 4
    in_specs, out_specs, out_shape = [], [], []
    for i, piece in enumerate(sums):
        rows, cols = piece.shape[3:]
        if i < 2:
            in_specs.append(pl.BlockSpec((2, 1, 1, rows, cols), lambda i: (0, i // 2, i % 2, 0, 0)))
            for _ in range(2):
                out_specs.append(pl.BlockSpec((rows, cols), lambda i: (i, 0)))
                out_shape.append(struct((steps * rows, cols), F32))
        else:
            in_specs.append(pl.BlockSpec((1, 1, 2, rows, cols), lambda i: (i // 2, i % 2, 0, 0, 0)))
            shape = (rows, 2 * cols) if i < 6 else (2 * rows, cols)
            out_specs.append(pl.BlockSpec(shape, lambda i: (i, 0)))
            out_shape.append(struct((steps * shape[0], shape[1]), F32))
    for rows in (output, grad_tokens):
        spec = pl.BlockSpec((rows.shape[0] // steps, rows.shape[1]), lambda i: (i, 0))
        in_specs.append(spec)
        out_specs.append(spec)
        out_shape.append(struct(rows.shape, rows.dtype))
    plots, patches, width = grad_memory.shape
    per = steps // plots
    spec = pl.BlockSpec((1, patches // per, width), lambda i: (i // per, i % per, 0))
    in_specs.append(spec)
    out_specs.append(spec)
    out_shape.append(struct(grad_memory.shape, grad_memory.dtype))
    in_specs.append(pl.BlockSpec(gains.shape, lambda i: (0, 0)))
    for _ in range(3):
        out_specs.append(pl.BlockSpec((width,), lambda i: (0,)))
        out_shape.append(struct((width,), F32))
    return pl.pallas_call(
        results_kernel,
        grid=(steps,),
        out_shape=out_shape,
        in_specs=in_specs,
        out_specs=out_specs,
        compiler_params=pltpu.CompilerParams(vmem_limit_bytes=63 << 20),
        name="results",
    )(*sums, output, grad_tokens, grad_memory, gains)


def body(
    tokens, memory, table_lengths, table_plots,
    self_gain, self_query, self_key, self_value, self_output,
    cross_gain, cross_query, cross_key, cross_value, cross_output,
    hidden_gain, hidden_gate, hidden_up, hidden_down, cotangent,
):
    n = lax.axis_size("tensor")
    extra = lax.axis_size("dp").bit_length() - 1 - 3
    rows, width = tokens.shape
    halo_chunks = -(-(LONGEST - 1) // rows)

    def pieces(shard):
        return shard.reshape(2, 2, 2, -1, shard.shape[-1])

    shards = [pieces(hidden_gate), pieces(hidden_up), pieces(hidden_down)]
    ins = (
        table_lengths, table_plots, tokens, cotangent,
        self_gain, cross_gain, hidden_gain, memory,
        cross_key.T, cross_value.T, self_query.T, self_key.T, self_value.T, self_output,
        cross_query.T, cross_output,
    )
    full, saved = forward(n, halo_chunks, ins, shards)
    (
        bias, plots, near, normed_near, self_q, self_k, self_mix, self_logs, first_sum,
        normed_cross, q_all, cross_k, cross_kt, cross_v, cross_mix,
        output, normed_hidden, hidden, gate_back, up_back, second_back, grad_rows, mixed_back,
        cross_stats, gain_hidden,
    ) = saved
    ins = (
        plots, mixed_back, cross_stats, cross_gain,
        normed_hidden, gate_back, up_back, hidden, cotangent, q_all, cross_k, cross_v, cross_kt,
        memory, full[0], full[3], cross_mix, grad_rows, normed_cross, second_back, first_sum,
    )
    hidden_pieces, rest = cross_backward(n, ins, [s.shape[3:] for s in shards])
    gain_cross, grad_memory, part_keys, part_query, first_back, g_first = rest
    ins = (
        self_gain, gain_cross, gain_hidden,
        g_first, self_mix, full[2], normed_near, full[1], self_k, self_q, bias, self_logs, near,
        first_back,
    )
    sums, grad_tokens, gains = self_backward(
        n, extra, halo_chunks, ins, [part_query, part_keys], hidden_pieces
    )

    (
        g_cq, g_co, g_ck, g_cv, g_so, g_sv, g_sk, g_sq, g_gate, g_up, g_down,
        output, grad_tokens, grad_memory, gain_s, gain_c, gain_h,
    ) = results(sums, output, grad_tokens, grad_memory, gains)
    return (
        output, grad_tokens, grad_memory,
        g_sq.T, g_sk.T, g_sv.T, g_so,
        g_cq.T, g_ck.T, g_cv.T, g_co,
        g_gate, g_up, g_down,
        gain_s, gain_c, gain_h,
    )


def solution(mesh):
    in_specs = (
        P(("dp", "tensor"), None),
        P("dp", "tensor", None),
        P("dp", None),
        P("dp", None),
        P(),
        P(None, "tensor"),
        P(None, "tensor"),
        P(None, "tensor"),
        P("tensor", None),
        P(),
        P(None, "tensor"),
        P(None, "tensor"),
        P(None, "tensor"),
        P("tensor", None),
        P(),
        P(None, "tensor"),
        P(None, "tensor"),
        P("tensor", None),
        P(("dp", "tensor"), None),
    )
    out_specs = (
        P(("dp", "tensor"), None),
        P(("dp", "tensor"), None),
        P("dp", "tensor", None),
        P(None, "tensor"),
        P(None, "tensor"),
        P(None, "tensor"),
        P("tensor", None),
        P(None, "tensor"),
        P(None, "tensor"),
        P(None, "tensor"),
        P("tensor", None),
        P(None, "tensor"),
        P(None, "tensor"),
        P("tensor", None),
        P(),
        P(),
        P(),
    )
    return jax.shard_map(body, mesh=mesh, in_specs=in_specs, out_specs=out_specs, check_vma=False)
```
